128 devices in a mesh: wide: 16 (over y_lo, x, core), narrow: 8 (over y_hi, z).
Axes of the slice: x: 4, y: 4 (y_hi: 2, y_lo: 2; y = y_hi * 2 + y_lo), z: 4, core: 2. Of those that a mesh axis runs over, the one named last changes fastest.
Arguments:
- fine_input: bfloat16 [4, 512, 128, 256], P(None, 'wide', 'narrow'), may hold values from -8 to 8
- gain_fine: float32 [256], replicated, may hold values from 0.1 to 1.9
- kernel_fine: bfloat16 [3, 3, 256, 256], replicated, may hold values from -0.125 to 0.125
- down_mid: bfloat16 [256, 512], replicated, may hold values from -1.5 to 1.5
- gain_mid: float32 [512], replicated, may hold values from 0.1 to 1.9
- kernel_mid: bfloat16 [3, 3, 512, 512], replicated, may hold values from -0.09375 to 0.09375
- down_coarse: bfloat16 [512, 512], replicated, may hold values from -1 to 1
- gain_coarse: float32 [512], replicated, may hold values from 0.1 to 1.9
- kernel_coarse: bfloat16 [3, 3, 512, 512], replicated, may hold values from -0.09375 to 0.09375
- up_coarse: bfloat16 [512, 512], replicated, may hold values from -0.25 to 0.25
- up_mid: bfloat16 [512, 256], replicated, may hold values from -0.25 to 0.25
- grad_out: bfloat16 [4, 512, 128, 256], P(None, 'wide', 'narrow'), may hold values from -6 to 6
Outputs:
- fine_output: bfloat16 [4, 512, 128, 256], P(None, 'wide', 'narrow')
- grad_input: float32 [4, 512, 128, 256], P(None, 'wide', 'narrow')
The draws below stay inside these ranges and needn't reach their ends.
All inputs are finite; a program needn't handle non-finite values.
Results may differ from the reference program's by a relative error of at most 0.022.
Values may be sent and summed in bfloat16 or wider, within the bound.
A program may use at most 128 MiB of HBM per device.

```python
import jax
import jax.numpy as jnp
from jax import lax

C1 = 256
C2 = 512
C3 = 512
GROUPS = 32
FRAMES = 4
H1 = 512
W1 = 128


def draw_fine_input(key, part):
    key = jax.random.fold_in(key, 7)
    noise_key, channel_key = jax.random.split(key)
    height_pos = jnp.arange(H1, dtype=jnp.float32) / max(H1 - 1, 1)
    channel_scale = jnp.exp(jax.random.uniform(channel_key, (C1,), jnp.float32, -0.5, 0.5))
    fluctuation = jax.random.normal(noise_key, (FRAMES, H1, W1, C1), jnp.float32)
    envelope = 0.5 * 3.0 ** height_pos
    values = fluctuation * envelope[None, :, None, None] * channel_scale
    return jnp.clip(values, -8.0, 8.0).astype(jnp.bfloat16)


def draw_grad_out(key, part):
    key = jax.random.fold_in(key, 11)
    noise_key, sign_key = jax.random.split(key, 2)
    signs = 2.0 * jax.random.randint(sign_key, (C1,), 0, 2).astype(jnp.float32) - 1.0
    fluctuation = jax.random.normal(noise_key, (FRAMES, H1, W1, C1), jnp.float32)
    values = fluctuation + 0.3 * signs
    return jnp.clip(values, -6.0, 6.0).astype(jnp.bfloat16)


def gaussian(key, shape, deviation, most, kind=jnp.bfloat16):
    array = deviation * jax.random.normal(key, shape, jnp.float32)
    return jnp.clip(array, min=-most, max=most).astype(kind)


def setup_inputs(seed: int = 0) -> dict:
    key_of = jax.random.split(jax.random.key(seed), 13)
    fine_input = draw_fine_input(jax.random.fold_in(key_of[12], 71), 0)
    gain_fine = jnp.clip(1.0 + 0.18 * jax.random.normal(key_of[1], (C1,), jnp.float32), 0.1, 1.9)
    kernel_fine = gaussian(key_of[2], (3, 3, C1, C1), (9 * C1) ** -0.5, 0.125)
    down_mid = gaussian(key_of[3], (C1, C2), (C1 // 16) ** -0.5, 1.5)
    gain_mid = jnp.clip(1.0 + 0.18 * jax.random.normal(key_of[4], (C2,), jnp.float32), 0.1, 1.9)
    kernel_mid = gaussian(key_of[5], (3, 3, C2, C2), (9 * C2) ** -0.5, 0.09375)
    down_coarse = gaussian(key_of[6], (C2, C3), (C2 // 16) ** -0.5, 1.0)
    gain_coarse = jnp.clip(1.0 + 0.18 * jax.random.normal(key_of[7], (C3,), jnp.float32), 0.1, 1.9)
    kernel_coarse = gaussian(key_of[8], (3, 3, C3, C3), (9 * C3) ** -0.5, 0.09375)
    up_coarse = gaussian(key_of[9], (C3, C2), C3 ** -0.5, 0.25)
    up_mid = gaussian(key_of[10], (C2, C1), C2 ** -0.5, 0.25)
    grad_out = draw_grad_out(jax.random.fold_in(key_of[12], 71), 0)
    return {"fine_input": fine_input, "gain_fine": gain_fine, "kernel_fine": kernel_fine, "down_mid": down_mid, "gain_mid": gain_mid, "kernel_mid": kernel_mid, "down_coarse": down_coarse, "gain_coarse": gain_coarse, "kernel_coarse": kernel_coarse, "up_coarse": up_coarse, "up_mid": up_mid, "grad_out": grad_out}


epsilon = 1e-05

def convolve(padded, kernel):
    return lax.conv_general_dilated(padded, kernel, (1, 1), 'VALID', dimension_numbers=('NHWC', 'HWIO', 'NHWC'), preferred_element_type=jnp.float32)

def pad_cells(tensor):
    return jnp.pad(tensor, ((0, 0), (1, 1), (1, 1), (0, 0)))

def group_sums(values):
    per_channel = lax.optimization_barrier(jnp.sum(values, axis=(0, 1, 2)))
    return lax.optimization_barrier(jnp.sum(per_channel.reshape(GROUPS, -1), axis=1))

def spread(vector, channels):
    return jnp.broadcast_to(vector[:, None], (GROUPS, channels // GROUPS)).reshape(channels)

def average_blocks(tensor):
    frames, height, breadth, channels = tensor.shape
    return lax.optimization_barrier(jnp.mean(tensor.astype(jnp.float32).reshape(frames, height // 4, 4, breadth // 4, 4, channels), axis=(2, 4)))

def sum_blocks(tensor):
    frames, height, breadth, channels = tensor.shape
    return lax.optimization_barrier(jnp.sum(tensor.astype(jnp.float32).reshape(frames, height // 4, 4, breadth // 4, 4, channels), axis=(2, 4)))

def enlarge(tensor):
    frames, height, breadth, channels = tensor.shape
    return jnp.broadcast_to(tensor[:, :, None, :, None, :], (frames, height, 4, breadth, 4, channels)).reshape(frames, height * 4, breadth * 4, channels)

def project(tensor, matrix):
    return jnp.dot(tensor, matrix, preferred_element_type=jnp.float32)

def block_forward(inputs, scaling, kernel):
    values = inputs.astype(jnp.float32)
    channels = inputs.shape[-1]
    number = values.size // GROUPS
    totals = group_sums(values)
    square = group_sums(values * values)
    center = totals / number
    inverse = lax.rsqrt(square / number - center * center + epsilon)
    scaled = (values - spread(center, channels)) * spread(inverse, channels)
    normed = scaled * scaling
    activated = jax.nn.silu(normed).astype(jnp.bfloat16)
    result = (values + convolve(pad_cells(activated), kernel)).astype(jnp.bfloat16)
    return (result, center, inverse)

def block_backward(inputs, scaling, kernel, center, inverse, upstream):
    values = inputs.astype(jnp.float32)
    channels = inputs.shape[-1]
    number = values.size // GROUPS
    flipped = jnp.transpose(kernel[::-1, ::-1], (0, 1, 3, 2))
    act_grad = convolve(pad_cells(upstream), flipped)
    scaled = (values - spread(center, channels)) * spread(inverse, channels)
    normed = scaled * scaling
    logistic = jax.nn.sigmoid(normed)
    normed_grad = act_grad * logistic * (1.0 + normed * (1.0 - logistic)) * scaling
    first_sum = group_sums(normed_grad)
    second_sum = group_sums(normed_grad * scaled)
    return upstream.astype(jnp.float32) + spread(inverse, channels) * (normed_grad - spread(first_sum / number, channels) - scaled * spread(second_sum / number, channels))

def reference(fine_input, gain_fine, kernel_fine, down_mid, gain_mid, kernel_mid, down_coarse, gain_coarse, kernel_coarse, up_coarse, up_mid, grad_out):
    fine_block, fine_center, fine_inverse = block_forward(fine_input, gain_fine, kernel_fine)
    mid_in = project(average_blocks(fine_block).astype(jnp.bfloat16), down_mid).astype(jnp.bfloat16)
    mid_block, mid_center, mid_inverse = block_forward(mid_in, gain_mid, kernel_mid)
    coarse_in = project(average_blocks(mid_block).astype(jnp.bfloat16), down_coarse).astype(jnp.bfloat16)
    coarse_block, coarse_center, coarse_inverse = block_forward(coarse_in, gain_coarse, kernel_coarse)
    coarse_up = project(coarse_block, up_coarse).astype(jnp.bfloat16)
    mid_sum = (mid_block.astype(jnp.float32) + enlarge(coarse_up.astype(jnp.float32))).astype(jnp.bfloat16)
    mid_up = project(mid_sum, up_mid).astype(jnp.bfloat16)
    fine_output = (fine_block.astype(jnp.float32) + enlarge(mid_up.astype(jnp.float32))).astype(jnp.bfloat16)
    upstream = grad_out.astype(jnp.float32)
    up_mid_grad = sum_blocks(upstream).astype(jnp.bfloat16)
    mid_sum_grad = project(up_mid_grad, up_mid.T)
    up_coarse_grad = sum_blocks(mid_sum_grad).astype(jnp.bfloat16)
    coarse_grad = project(up_coarse_grad, up_coarse.T).astype(jnp.bfloat16)
    coarse_in_grad = block_backward(coarse_in, gain_coarse, kernel_coarse, coarse_center, coarse_inverse, coarse_grad)
    mid_pool_grad = project(coarse_in_grad.astype(jnp.bfloat16), down_coarse.T)
    mid_grad = (mid_sum_grad + 0.0625 * enlarge(mid_pool_grad)).astype(jnp.bfloat16)
    mid_in_grad = block_backward(mid_in, gain_mid, kernel_mid, mid_center, mid_inverse, mid_grad)
    fine_pool_grad = project(mid_in_grad.astype(jnp.bfloat16), down_mid.T)
    fine_grad = (upstream + 0.0625 * enlarge(fine_pool_grad)).astype(jnp.bfloat16)
    grad_input = block_backward(fine_input, gain_fine, kernel_fine, fine_center, fine_inverse, fine_grad)
    return (fine_output, grad_input)
```

```python
import functools

import jax
import jax.numpy as jnp
import numpy as np
from jax import lax
from jax.experimental import pallas as pl
from jax.experimental.pallas import tpu as pltpu
from jax.sharding import PartitionSpec as P

MESH = pl.DeviceIdType.MESH
GROUPS = 32
epsilon = 1e-05
F32 = jnp.float32
BF16 = jnp.bfloat16

DIRS = ((0, 0), (-1, 0), (1, 0), (0, -1), (0, 1), (-1, -1), (-1, 1), (1, -1), (1, 1))

ABOVE, BELOW, LEFT, RIGHT, CORNER = 128, 144, 160, 192, 224


def mid_row(f, i, j):
    if 0 <= i < 8 and 0 <= j < 4:
        return 32 * f + 4 * i + j
    if i < 0 and 0 <= j < 4:
        return ABOVE + 4 * f + j
    if i > 7 and 0 <= j < 4:
        return BELOW + 4 * f + j
    if 0 <= i < 8:
        return (LEFT if j < 0 else RIGHT) + 8 * f + i
    return CORNER + 4 * (2 * (i > 7) + (j > 3)) + f


def coarse_row(f, i, side):
    down = -1 if i < 0 else (1 if i > 1 else 0)
    return 8 * DIRS.index((down, side)) + 2 * f + i % 2


def tables():
    pick = np.zeros((96, 512), np.float32)
    for i in range(32):
        for j in range(16):
            pick[4 * (i // 4) + j // 4, 16 * i + j] = 1
        pick[32 + i, 16 * i + 15] = 1
        pick[64 + i, 16 * i] = 1
    enlarge = np.zeros((912, 256), np.float32)
    taps = np.zeros((1152, 256), np.float32)
    ends = np.zeros((16, 256), np.float32)
    pack = np.zeros((112, 128), np.float32)
    pool = np.zeros((16, 128), np.float32)
    coarse_taps = np.zeros((144, 128), np.float32)
    spread = np.zeros((256, 128), np.float32)
    for f in range(4):
        for i in range(8):
            for j in range(16):
                enlarge[128 * f + 16 * i + j, mid_row(f, i, j // 4)] = 1
        for j in range(16):
            enlarge[512 + 16 * f + j, ABOVE + 4 * f + j // 4] = 1
            enlarge[576 + 16 * f + j, BELOW + 4 * f + j // 4] = 1
        for i in range(32):
            enlarge[640 + 32 * f + i, LEFT + 8 * f + i // 4] = 1
            enlarge[768 + 32 * f + i, RIGHT + 8 * f + i // 4] = 1
        for c in range(4):
            enlarge[896 + 4 * c + f, CORNER + 4 * c + f] = 1
            low, first = c < 2, c % 2 == 1
            ends[4 * c + f, 128 * first + 32 * f + 31 * low] = 1
            pack[96 + 4 * c + f, mid_row(f, 7 * low, 3 * (not first))] = 1
        for i in range(8):
            for j in range(4):
                here = 32 * f + 4 * i + j
                pool[2 * f + i // 4, here] = 1
                for t in range(9):
                    taps[128 * t + here, mid_row(f, i + t // 3 - 1, j + t % 3 - 1)] = 1
            pack[32 + 8 * f + i, mid_row(f, i, 3)] = 1
            pack[64 + 8 * f + i, mid_row(f, i, 0)] = 1
        for j in range(4):
            pack[4 * f + j, mid_row(f, 7, j)] = 1
            pack[16 + 4 * f + j, mid_row(f, 0, j)] = 1
        for i in range(2):
            for t in range(9):
                coarse_taps[16 * t + 2 * f + i, coarse_row(f, i + t // 3 - 1, t % 3 - 1)] = 1
        for i in range(-1, 9):
            for j in range(-1, 5):
                side = -1 if j < 0 else (1 if j > 3 else 0)
                spread[mid_row(f, i, j), coarse_row(f, i // 4 if i < 8 else 2, side)] = 1
    sides = np.zeros((512, 128), np.float32)
    for i in range(32):
        sides[16 * i, i] = 1
        sides[16 * i + 15, 64 + i] = 1
    wide_table = np.concatenate([pick, np.concatenate([enlarge, enlarge], axis=1)])
    middle_table = np.concatenate([taps, ends])
    narrow_table = np.concatenate([pack, pool, coarse_taps, spread, sides])
    return [jnp.asarray(t, BF16) for t in (wide_table, middle_table, narrow_table)]


def dot(a, b):
    return jnp.dot(a, b, preferred_element_type=F32)


def dot_t(a, b):
    return lax.dot_general(a, b, (((1,), (1,)), ((), ())), preferred_element_type=F32)


def group_lanes(t, size):
    lane = lax.broadcasted_iota(jnp.int32, t.shape, 1)
    step = 1
    while step < size:
        t = t + jnp.where(
            (lane & step) != 0, pltpu.roll(t, step, 1), pltpu.roll(t, 128 - step, 1)
        )
        step *= 2
    return t


def halves(t):
    high = t.astype(BF16)
    return high, (t - high.astype(F32)).astype(BF16)


def kernel(
    wide_count,
    narrow_count,
    x_in,
    gain_fine_in,
    kernel_fine_in,
    down_mid_in,
    gain_mid_in,
    kernel_mid_in,
    down_coarse_in,
    gain_coarse_in,
    kernel_coarse_in,
    up_coarse_in,
    up_mid_in,
    grad_in,
    wide_table_in,
    middle_table_in,
    narrow_table_in,
    out_ref,
    part_ref,
    tail_ref,
    xg,
    kernel_fine,
    flipped_fine,
    down_mid,
    kernel_mid,
    down_coarse,
    kernel_coarse,
    up_coarse,
    up_mid,
    gain_fine,
    gain_mid,
    gain_coarse,
    wide_table,
    middle_table,
    narrow_table,
    taps_buf,
    columns,
    fine_block,
    part,
    pooled,
    edge_rows,
    edge_sides,
    edge_ends,
    pool_grad,
    summed_grad,
    first,
    second,
    col_pack,
    cor_pack,
    row_in,
    col_in,
    cor_in,
    sum_pack,
    sum_in,
    sum_cor,
    cgrad_own,
    cgrad_in,
    mid_pack,
    mid_halo,
    mid_cor,
    coarse_own,
    coarse_halo,
    coarse_u,
    coarse_u_halo,
    u_pack,
    u_halo,
    u_cor,
    load_sem,
    out_sem,
    total_send,
    total_recv,
    halo_send,
    halo_recv,
):
    wide, narrow = lax.axis_index("wide"), lax.axis_index("narrow")

    def device(down, side):
        return (
            lax.rem(wide + down + wide_count, wide_count),
            lax.rem(narrow + side + narrow_count, narrow_count),
        )

    loads = {}
    pairs = (
        ("x", x_in, xg.at[0]),
        ("grad", grad_in, xg.at[1]),
        ("wide_table", wide_table_in, wide_table),
        ("middle_table", middle_table_in, middle_table),
        ("narrow_table", narrow_table_in, narrow_table),
        ("gain_fine", gain_fine_in, gain_fine),
        ("kernel_fine", kernel_fine_in, kernel_fine),
        ("up_mid", up_mid_in, up_mid),
        ("up_coarse", up_coarse_in, up_coarse),
        ("down_mid", down_mid_in, down_mid),
        ("gain_mid", gain_mid_in, gain_mid),
        ("kernel_coarse", kernel_coarse_in, kernel_coarse),
        ("kernel_mid", kernel_mid_in, kernel_mid),
        ("down_coarse", down_coarse_in, down_coarse),
        ("gain_coarse", gain_coarse_in, gain_coarse),
    )
    for number, (name, source, target) in enumerate(pairs):
        loads[name] = pltpu.make_async_copy(source, target, load_sem.at[number])
        loads[name].start()

    barrier = pltpu.get_barrier_semaphore()
    greeted = 0
    for down in range(wide_count):
        for side in range(-2, narrow_count - 2):
            near = (down <= 1 or down == wide_count - 1) and abs(side) <= 1
            if (down, side) != (0, 0) and (down == 0 or side == 0 or near):
                pl.semaphore_signal(
                    barrier, inc=1, device_id=device(down, side), device_id_type=MESH
                )
                greeted += 1

    def send(source, target, which, down, side):
        pltpu.make_async_remote_copy(
            src_ref=source,
            dst_ref=target,
            send_sem=halo_send.at[which],
            recv_sem=halo_recv.at[which],
            device_id=device(down, side),
            device_id_type=MESH,
        ).start()

    def arrived(buffer, which):
        pltpu.make_async_copy(buffer, buffer, halo_recv.at[which]).wait()

    def sent(buffer, which):
        pltpu.make_async_copy(buffer, buffer, halo_send.at[which]).wait()

    def total_begin(phase, one, two):
        blank = jnp.zeros((8, 128), F32)
        first[phase, wide] = blank
        for k in range(one.shape[1] // 128):
            first[phase, wide, k : k + 1, :] = one[:, 128 * k : 128 * k + 128]
            first[phase, wide, 4 + k : 5 + k, :] = two[:, 128 * k : 128 * k + 128]
        for step in range(1, wide_count):
            pltpu.make_async_remote_copy(
                src_ref=first.at[phase, wide],
                dst_ref=first.at[phase, wide],
                send_sem=total_send.at[2 * phase],
                recv_sem=total_recv.at[2 * phase],
                device_id=device(step, 0),
                device_id_type=MESH,
            ).start()

    def total_middle(phase):
        whole = first.at[phase, pl.ds(0, wide_count - 1)]
        pltpu.make_async_copy(whole, whole, total_recv.at[2 * phase]).wait()
        second[phase, narrow] = jnp.sum(first[phase], axis=0)
        for step in range(1, narrow_count):
            pltpu.make_async_remote_copy(
                src_ref=second.at[phase, narrow],
                dst_ref=second.at[phase, narrow],
                send_sem=total_send.at[2 * phase + 1],
                recv_sem=total_recv.at[2 * phase + 1],
                device_id=device(0, step),
                device_id_type=MESH,
            ).start()

    def total_end(phase, channels, cells):
        whole = second.at[phase, pl.ds(0, narrow_count - 1)]
        pltpu.make_async_copy(whole, whole, total_recv.at[2 * phase + 1]).wait()
        size = channels // GROUPS
        t = group_lanes(jnp.sum(second[phase], axis=0), size) * (1.0 / (size * cells))
        count = channels // 128
        return (
            jnp.concatenate([t[k : k + 1] for k in range(count)], axis=1),
            jnp.concatenate([t[4 + k : 5 + k] for k in range(count)], axis=1),
        )

    has_above, has_below = wide > 0, wide < wide_count - 1
    has_left, has_right = narrow > 0, narrow < narrow_count - 1
    has_corner = (
        jnp.logical_and(has_above, has_left),
        jnp.logical_and(has_above, has_right),
        jnp.logical_and(has_below, has_left),
        jnp.logical_and(has_below, has_right),
    )
    exists = (None, has_above, has_below, has_left, has_right) + has_corner

    def only(condition, value):
        return value * jnp.where(condition, 1.0, 0.0).astype(F32)

    def corners(read, change, masked):
        result = None
        for c in range(4):
            value = change(read(c).astype(F32))
            if masked:
                value = only(has_corner[c], value)
            quarter = lax.broadcasted_iota(jnp.int32, value.shape, 0) // 4
            result = value if result is None else jnp.where(quarter == c, value, result)
        return result

    def mid_extended(own, read_halo, read_cor, change, masked):
        pieces = [change(own)]
        halo = change(read_halo.astype(F32))
        for low, high, d in ((0, 16, 1), (16, 32, 2), (32, 64, 3), (64, 96, 4)):
            piece = halo[low:high]
            pieces.append(only(exists[d], piece) if masked else piece)
        pieces.append(corners(read_cor, change, masked))
        pieces.append(jnp.zeros((16, own.shape[1]), F32))
        return jnp.concatenate(pieces, axis=0)

    def send_mid(pack, halo, cor, which):
        send(pack.at[pl.ds(0, 16)], halo.at[pl.ds(0, 16)], which, 1, 0)
        send(pack.at[pl.ds(16, 16)], halo.at[pl.ds(16, 16)], which, -1, 0)
        send(pack.at[pl.ds(32, 32)], halo.at[pl.ds(32, 32)], which, 0, 1)
        send(pack.at[pl.ds(64, 32)], halo.at[pl.ds(64, 32)], which, 0, -1)
        for c in range(4):
            down, side = DIRS[5 + c]
            send(pack.at[pl.ds(96, 16)], cor.at[c], which + 1, -down, -side)

    def send_coarse(own, halo, which):
        for d in range(1, 9):
            down, side = DIRS[d]
            send(own, halo.at[d - 1], which, -down, -side)

    def coarse_extended(own, halo, change, masked):
        pieces = [change(own)]
        for d in range(1, 9):
            piece = change(halo(d - 1))
            pieces.append(only(exists[d], piece) if masked else piece)
        pieces.append(jnp.zeros((56, own.shape[1]), F32))
        return jnp.concatenate(pieces, axis=0)

    PICK = wide_table.at[pl.ds(0, 96)]
    ENLARGE = wide_table.at[pl.ds(96, 912)]
    TAPS = middle_table.at[pl.ds(0, 1152)]
    ENDS = middle_table.at[pl.ds(1152, 16)]
    PACK = narrow_table.at[pl.ds(0, 112)]
    POOL = narrow_table.at[pl.ds(112, 16)]
    COARSE_TAPS = narrow_table.at[pl.ds(128, 144)]
    SPREAD = narrow_table.at[pl.ds(272, 256)]
    SIDES = narrow_table.at[pl.ds(528, 512)]

    def frame(which, f):
        return xg[which, f].reshape(512, 256)

    loads["x"].wait()

    def add_frame(f, carry):
        value = frame(0, f).astype(F32)
        return (
            carry[0] + jnp.sum(value.reshape(64, 8, 256), axis=0),
            carry[1] + jnp.sum((value * value).reshape(64, 8, 256), axis=0),
        )

    blank = jnp.zeros((8, 256), F32)
    one, two = lax.fori_loop(0, 4, add_frame, (blank, blank))
    pl.semaphore_wait(barrier, greeted)
    total_begin(0, jnp.sum(one, axis=0, keepdims=True), jnp.sum(two, axis=0, keepdims=True))

    loads["grad"].wait()
    send(xg.at[:, :, 31], row_in.at[0], 0, 1, 0)
    send(xg.at[:, :, 0], row_in.at[1], 0, -1, 0)
    loads["wide_table"].wait()
    for which in range(2):
        for f in range(4):
            picked = dot(PICK[...], frame(which, f)).astype(BF16)
            col_pack[0, which, 32 * f : 32 * f + 32] = picked[32:64]
            col_pack[1, which, 32 * f : 32 * f + 32] = picked[64:96]
            if which == 1:
                pooled[32 * f : 32 * f + 32] = picked[0:32]
    send(col_pack.at[0], col_in.at[0], 1, 0, 1)
    send(col_pack.at[1], col_in.at[1], 1, 0, -1)
    loads["middle_table"].wait()
    for which in range(2):
        ends = jnp.concatenate([col_pack[0, which], col_pack[1, which]], axis=0)
        cor_pack[which] = dot(ENDS[...], ends).astype(BF16)
    for c in range(4):
        down, side = DIRS[5 + c]
        send(cor_pack, cor_in.at[c], 2, -down, -side)
    total_middle(0)

    loads["narrow_table"].wait()
    up_mid_grad = pooled[...]
    sum_pack[...] = dot(PACK[...], up_mid_grad).astype(BF16)
    send_mid(sum_pack, sum_in, sum_cor, 3)
    loads["up_mid"].wait()
    mid_sum_grad = dot_t(up_mid_grad, up_mid[...])
    high, low = halves(mid_sum_grad)
    up_coarse_grad = (dot(POOL[...], high) + dot(POOL[...], low)).astype(BF16)
    loads["up_coarse"].wait()
    cgrad_own[...] = dot_t(up_coarse_grad, up_coarse[...]).astype(BF16)
    send_coarse(cgrad_own, cgrad_in, 5)
    loads["gain_fine"].wait()
    loads["kernel_fine"].wait()
    for a in range(3):
        for b in range(3):
            flipped_fine[a, 256 * b : 256 * b + 256, :] = kernel_fine[
                2 - a, 256 * (2 - b) : 256 * (2 - b) + 256, :
            ].T

    fine_center, fine_square = total_end(0, 256, 2048 * wide_count * narrow_count)
    fine_inverse = lax.rsqrt(fine_square - fine_center * fine_center + epsilon)
    s_fine = gain_fine[...]

    def silu(value, center, inverse, scaling):
        normed = (value - center) * inverse * scaling
        return normed / (1.0 + jnp.exp(-normed))

    def fine_act(value):
        return silu(value, fine_center, fine_inverse, s_fine)

    arrived(row_in, 0)
    arrived(col_in, 1)
    arrived(cor_in, 2)

    def set_edges(above, below, left, right, ends):
        edge_rows[0] = only(has_above, above)
        edge_rows[1] = only(has_below, below)
        left = only(has_left, left).astype(BF16)
        right = only(has_right, right).astype(BF16)
        for f in range(4):
            edge_sides[f, 0:32] = left[32 * f : 32 * f + 32]
            edge_sides[f, 32:64] = right[32 * f : 32 * f + 32]
        edge_ends[...] = ends

    def place(f, own):
        column = lax.broadcasted_iota(jnp.int32, (512, 256), 0) % 16
        sides = edge_sides[f]
        low = jnp.where(
            column == 0, dot(SIDES[:, 0:64], sides), pltpu.roll(own, 1, 0)
        )
        columns[f, 16:528, 0:256] = low.astype(BF16)
        columns[f, 16:528, 256:512] = own.astype(BF16)
        high = jnp.where(
            column == 15, dot(SIDES[:, 32:96], sides), pltpu.roll(own, 511, 0)
        )
        columns[f, 16:528, 512:768] = high.astype(BF16)
        cell = lax.broadcasted_iota(jnp.int32, (16, 256), 0)
        for k in range(2):
            row = edge_rows[k, f]
            at = slice(528 * k, 528 * k + 16)
            west = edge_ends[pl.ds(8 * k + f, 1), :]
            east = edge_ends[pl.ds(8 * k + 4 + f, 1), :]
            columns[f, at, 0:256] = jnp.where(cell == 0, west, pltpu.roll(row, 1, 0)).astype(BF16)
            columns[f, at, 256:512] = row.astype(BF16)
            columns[f, at, 512:768] = jnp.where(cell == 15, east, pltpu.roll(row, 15, 0)).astype(BF16)

    def fine_convolve(f, weights):
        total = dot(columns[f, 0:512, :], weights[0])
        total += dot(columns[f, 16:528, :], weights[1])
        return total + dot(columns[f, 32:544, :], weights[2])

    set_edges(
        fine_act(row_in[0, 0].astype(F32)),
        fine_act(row_in[1, 0].astype(F32)),
        fine_act(col_in[0, 0].astype(F32)),
        fine_act(col_in[1, 0].astype(F32)),
        corners(lambda c: cor_in[c, 0], fine_act, True),
    )

    def fine_forward(f, carry):
        value = frame(0, f).astype(F32)
        place(f, fine_act(value))
        block = (value + fine_convolve(f, kernel_fine)).astype(BF16)
        fine_block[f] = block
        pooled[pl.ds(pl.multiple_of(32 * f, 32), 32), :] = (
            dot(PICK[0:32, :], block) * 0.0625
        ).astype(BF16)
        return carry

    lax.fori_loop(0, 4, fine_forward, 0)

    loads["down_mid"].wait()
    mid_in = dot(pooled[...], down_mid[...]).astype(BF16)
    mid_value = mid_in.astype(F32)

    def column_sums(value):
        return jnp.sum(value, axis=0, keepdims=True)

    total_begin(1, column_sums(mid_value), column_sums(mid_value * mid_value))
    mid_pack[...] = dot(PACK[...], mid_in).astype(BF16)
    send_mid(mid_pack, mid_halo, mid_cor, 6)
    total_middle(1)

    arrived(cgrad_in, 5)
    loads["kernel_coarse"].wait()

    def coarse_convolve(extended, weights):
        spread_out = dot(COARSE_TAPS[...], extended.astype(BF16)).astype(BF16)
        total = None
        for t in range(9):
            term = weights(t, spread_out[16 * t : 16 * t + 16])
            total = term if total is None else total + term
        return total

    def same(value):
        return value

    cgrad = cgrad_own[...].astype(F32)[0:8]
    coarse_act_grad = coarse_convolve(
        coarse_extended(cgrad, lambda d: cgrad_in[d].astype(F32)[0:8], same, True),
        lambda t, part_: dot_t(part_, kernel_coarse[8 - t]),
    )[0:8]

    loads["gain_mid"].wait()
    loads["kernel_mid"].wait()
    mid_center, mid_square = total_end(1, 512, 128 * wide_count * narrow_count)
    mid_inverse = lax.rsqrt(mid_square - mid_center * mid_center + epsilon)
    s_mid = gain_mid[...]

    def mid_act(value):
        return silu(value, mid_center, mid_inverse, s_mid)

    def mid_scaled(value):
        return (value - mid_center) * mid_inverse

    def mid_convolve(extended, weights):
        taps_buf[...] = dot(TAPS[...], extended.astype(BF16)).astype(BF16)
        total = None
        for t in range(9):
            term = weights(t, taps_buf[128 * t : 128 * t + 128, :])
            total = term if total is None else total + term
        return total

    arrived(mid_halo, 6)
    arrived(mid_cor, 7)
    mid_block = (
        mid_value
        + mid_convolve(
            mid_extended(mid_value, mid_halo[...], lambda c: mid_cor[c], mid_act, True),
            lambda t, part_: dot(part_, kernel_mid[t]),
        )
    ).astype(BF16)

    loads["down_coarse"].wait()
    mid_pooled = (dot(POOL[...], mid_block) * 0.0625).astype(BF16)
    coarse_in = dot(mid_pooled, down_coarse[...]).astype(BF16)
    coarse_own[...] = coarse_in
    coarse_value = coarse_in.astype(F32)[0:8]
    total_begin(2, column_sums(coarse_value), column_sums(coarse_value * coarse_value))
    send_coarse(coarse_own, coarse_halo, 8)
    total_middle(2)

    arrived(sum_in, 3)
    arrived(sum_cor, 4)
    sum_extended = mid_extended(
        up_mid_grad.astype(F32), sum_in[...], lambda c: sum_cor[c], same, True
    )
    summed_grad[...] = dot_t(sum_extended.astype(BF16), up_mid[...])

    loads["gain_coarse"].wait()
    coarse_center, coarse_square = total_end(2, 512, 8 * wide_count * narrow_count)
    coarse_inverse = lax.rsqrt(coarse_square - coarse_center * coarse_center + epsilon)
    s_coarse = gain_coarse[...]

    def coarse_scaled(value):
        return (value - coarse_center) * coarse_inverse

    def slope(scaled, scaling):
        normed = scaled * scaling
        logistic = 1.0 / (1.0 + jnp.exp(-normed))
        return logistic * (1.0 + normed * (1.0 - logistic)) * scaling

    scaled = coarse_scaled(coarse_value)
    normed_grad = coarse_act_grad * slope(scaled, s_coarse)
    total_begin(3, column_sums(normed_grad), column_sums(normed_grad * scaled))
    coarse_u[...] = cgrad + coarse_inverse * normed_grad
    send_coarse(coarse_u, coarse_u_halo, 9)
    total_middle(3)

    arrived(coarse_halo, 8)
    coarse_block = (
        coarse_in.astype(F32)
        + coarse_convolve(
            coarse_extended(
                coarse_value,
                lambda d: coarse_halo[d].astype(F32)[0:8],
                lambda v: silu(v, coarse_center, coarse_inverse, s_coarse),
                True,
            ),
            lambda t, part_: dot(part_, kernel_coarse[t]),
        )
    ).astype(BF16)
    coarse_up = dot(coarse_block, up_coarse[...]).astype(BF16)
    mid_sum = (mid_block.astype(F32) + dot(SPREAD[0:128, 0:16], coarse_up)).astype(BF16)
    mid_up = dot(mid_sum, up_mid[...]).astype(BF16)

    first_mean, second_mean = total_end(3, 512, 8 * wide_count * narrow_count)
    arrived(coarse_u_halo, 9)
    offset = coarse_inverse * first_mean
    factor = coarse_inverse * second_mean
    pieces = [coarse_u[...] - offset - scaled * factor]
    for d in range(8):
        piece = coarse_scaled(coarse_halo[d].astype(F32)[0:8])
        pieces.append(coarse_u_halo[d] - offset - piece * factor)
    pieces.append(jnp.zeros((56, 512), F32))
    coarse_in_grad = jnp.concatenate(pieces, axis=0).astype(BF16)

    mid_pool_grad = dot_t(dot(SPREAD[...], coarse_in_grad).astype(BF16), down_coarse[...])
    row = lax.broadcasted_iota(jnp.int32, (256, 512), 0)
    keep = jnp.where(row < ABOVE, 1.0, 0.0)
    bounds = ((ABOVE, 16, 1), (BELOW, 16, 2), (LEFT, 32, 3), (RIGHT, 32, 4)) + tuple(
        (CORNER + 4 * c, 4, 5 + c) for c in range(4)
    )
    for start, size, d in bounds:
        inside = jnp.logical_and(row >= start, row < start + size)
        keep = jnp.where(inside, jnp.where(exists[d], 1.0, 0.0).astype(F32), keep)
    mid_grad = (summed_grad[...] + 0.0625 * mid_pool_grad) * keep
    mid_act_grad = mid_convolve(mid_grad, lambda t, part_: dot_t(part_, kernel_mid[8 - t]))
    scaled = mid_scaled(mid_value)
    normed_grad = mid_act_grad * slope(scaled, s_mid)
    total_begin(4, column_sums(normed_grad), column_sums(normed_grad * scaled))
    mid_u = mid_grad[0:128].astype(BF16).astype(F32) + mid_inverse * normed_grad
    u_pack[...] = dot(PACK[...], mid_u.astype(BF16)).astype(BF16)
    send_mid(u_pack, u_halo, u_cor, 10)
    total_middle(4)

    mid_up = dot(ENLARGE[0:512, 0:128], mid_up).reshape(4, 8, 1, 16, 256)
    for f in range(4):
        block = fine_block[f].astype(F32).reshape(8, 4, 16, 256)
        fine_block[f] = (block + mid_up[f]).astype(BF16).reshape(512, 256)
    out_copy = pltpu.make_async_copy(fine_block, out_ref, out_sem.at[0])
    out_copy.start()

    first_mean, second_mean = total_end(4, 512, 128 * wide_count * narrow_count)
    arrived(u_halo, 10)
    arrived(u_cor, 11)
    offset = mid_inverse * first_mean
    factor = mid_inverse * second_mean
    mid_in_grad = mid_extended(
        mid_u, u_halo[...], lambda c: u_cor[c], lambda v: v - offset, False
    ) - factor * mid_extended(
        mid_value, mid_halo[...], lambda c: mid_cor[c], mid_scaled, False
    )

    high, low = halves(0.0625 * dot_t(mid_in_grad.astype(BF16), down_mid[...]))
    pool_grad[...] = dot(ENLARGE[...], jnp.concatenate([high, low], axis=0))

    def rounded(value):
        return value.astype(BF16).astype(F32)

    set_edges(
        rounded(row_in[0, 1].astype(F32) + pool_grad[512:576, :].reshape(4, 16, 256)),
        rounded(row_in[1, 1].astype(F32) + pool_grad[576:640, :].reshape(4, 16, 256)),
        rounded(col_in[0, 1].astype(F32) + pool_grad[640:768, :]),
        rounded(col_in[1, 1].astype(F32) + pool_grad[768:896, :]),
        corners(lambda c: cor_in[c, 1], lambda v: v + pool_grad[896:912, :], True),
    )

    def fine_backward(f, carry):
        added = pool_grad[pl.ds(pl.multiple_of(128 * f, 128), 128), :].reshape(8, 1, 16, 256)
        grad = xg[1, f].astype(F32).reshape(8, 4, 16, 256) + added
        grad = rounded(grad.reshape(512, 256))
        place(f, grad)
        act_grad = fine_convolve(f, flipped_fine)
        scaled = (frame(0, f).astype(F32) - fine_center) * fine_inverse
        normed_grad = act_grad * slope(scaled, s_fine)
        part[f] = grad + fine_inverse * normed_grad
        return (
            carry[0] + jnp.sum(normed_grad.reshape(64, 8, 256), axis=0),
            carry[1] + jnp.sum((normed_grad * scaled).reshape(64, 8, 256), axis=0),
        )

    one, two = lax.fori_loop(0, 4, fine_backward, (blank, blank))
    total_begin(5, jnp.sum(one, axis=0, keepdims=True), jnp.sum(two, axis=0, keepdims=True))
    part_copy = pltpu.make_async_copy(part, part_ref, out_sem.at[1])
    part_copy.start()
    total_middle(5)

    sent(row_in, 0)
    sent(col_in, 1)
    sent(cor_in, 2)
    sent(sum_in, 3)
    sent(sum_cor, 4)
    sent(cgrad_in, 5)
    sent(mid_halo, 6)
    sent(mid_cor, 7)
    sent(coarse_halo, 8)
    sent(coarse_u_halo, 9)
    sent(u_halo, 10)
    sent(u_cor, 11)
    for phase in range(6):
        whole = first.at[phase, pl.ds(0, wide_count - 1)]
        pltpu.make_async_copy(whole, whole, total_send.at[2 * phase]).wait()
    first_mean, second_mean = total_end(5, 256, 2048 * wide_count * narrow_count)
    for phase in range(6):
        whole = second.at[phase, pl.ds(0, narrow_count - 1)]
        pltpu.make_async_copy(whole, whole, total_send.at[2 * phase + 1]).wait()
    slant = -fine_inverse * fine_inverse * second_mean
    tail_ref[...] = jnp.zeros((8, 256), F32)
    tail_ref[0:1, :] = -fine_inverse * first_mean - fine_center * slant
    tail_ref[1:2, :] = slant
    out_copy.wait()
    part_copy.wait()


def shards(*arguments):
    (
        fine_input,
        gain_fine,
        kernel_fine,
        down_mid,
        gain_mid,
        kernel_mid,
        down_coarse,
        gain_coarse,
        kernel_coarse,
        up_coarse,
        up_mid,
        grad_out,
    ) = arguments
    wide_count, narrow_count = lax.axis_size("wide"), lax.axis_size("narrow")
    anywhere = pl.BlockSpec(memory_space=pl.ANY)
    vmem = pltpu.VMEM
    scratch = [
        vmem((2, 4, 32, 16, 256), BF16),
        vmem((3, 768, 256), BF16),
        vmem((3, 768, 256), BF16),
        vmem((256, 512), BF16),
        vmem((9, 512, 512), BF16),
        vmem((512, 512), BF16),
        vmem((9, 512, 512), BF16),
        vmem((512, 512), BF16),
        vmem((512, 256), BF16),
        vmem((1, 256), F32),
        vmem((1, 512), F32),
        vmem((1, 512), F32),
        vmem((1008, 512), BF16),
        vmem((1168, 256), BF16),
        vmem((1040, 128), BF16),
        vmem((1152, 512), BF16),
        vmem((4, 544, 768), BF16),
        vmem((4, 512, 256), BF16),
        vmem((4, 512, 256), F32),
        vmem((128, 256), BF16),
        vmem((2, 4, 16, 256), F32),
        vmem((4, 64, 256), BF16),
        vmem((16, 256), F32),
        vmem((912, 256), F32),
        vmem((256, 512), F32),
        vmem((6, wide_count, 8, 128), F32),
        vmem((6, narrow_count, 8, 128), F32),
        vmem((2, 2, 128, 256), BF16),
        vmem((2, 16, 256), BF16),
        vmem((2, 2, 4, 16, 256), BF16),
        vmem((2, 2, 128, 256), BF16),
        vmem((4, 2, 16, 256), BF16),
        vmem((112, 256), BF16),
        vmem((96, 256), BF16),
        vmem((4, 16, 256), BF16),
        vmem((16, 512), BF16),
        vmem((8, 16, 512), BF16),
        vmem((112, 512), BF16),
        vmem((96, 512), BF16),
        vmem((4, 16, 512), BF16),
        vmem((16, 512), BF16),
        vmem((8, 16, 512), BF16),
        vmem((8, 512), F32),
        vmem((8, 8, 512), F32),
        vmem((112, 512), BF16),
        vmem((96, 512), BF16),
        vmem((4, 16, 512), BF16),
        pltpu.SemaphoreType.DMA((15,)),
        pltpu.SemaphoreType.DMA((2,)),
        pltpu.SemaphoreType.DMA((12,)),
        pltpu.SemaphoreType.DMA((12,)),
        pltpu.SemaphoreType.DMA((12,)),
        pltpu.SemaphoreType.DMA((12,)),
    ]
    output, part, tail = pl.pallas_call(
        functools.partial(kernel, wide_count, narrow_count),
        out_shape=(
            jax.ShapeDtypeStruct((4, 512, 256), BF16),
            jax.ShapeDtypeStruct((4, 512, 256), F32),
            jax.ShapeDtypeStruct((8, 256), F32),
        ),
        in_specs=[anywhere] * 15,
        out_specs=(anywhere, anywhere, pl.BlockSpec(memory_space=pltpu.VMEM)),
        scratch_shapes=scratch,
        compiler_params=pltpu.CompilerParams(
            collective_id=0, has_side_effects=True, vmem_limit_bytes=56 * 2**20
        ),
        name="whole_net",
    )(
        fine_input,
        gain_fine.reshape(1, 256),
        kernel_fine.reshape(3, 768, 256),
        down_mid,
        gain_mid.reshape(1, 512),
        kernel_mid.reshape(9, 512, 512),
        down_coarse,
        gain_coarse.reshape(1, 512),
        kernel_coarse.reshape(9, 512, 512),
        up_coarse,
        up_mid,
        grad_out,
        *tables(),
    )
    grad = part.reshape(4, 32, 16, 256) + (tail[0] + fine_input.astype(F32) * tail[1])
    return output.reshape(4, 32, 16, 256), grad


def solution(mesh):
    tile = P(None, "wide", "narrow", None)
    return jax.shard_map(
        shards,
        mesh=mesh,
        in_specs=(tile,) + (P(),) * 10 + (tile,),
        out_specs=(tile, tile),
        check_vma=False,
    )
```

```python
import functools

import jax
import jax.numpy as jnp
import numpy as np
from jax import lax
from jax.experimental import pallas as pl
from jax.experimental.pallas import tpu as pltpu
from jax.sharding import PartitionSpec as P

MESH = pl.DeviceIdType.MESH
GROUPS = 32
epsilon = 1e-05
F32 = jnp.float32
BF16 = jnp.bfloat16

DIRS = ((0, 0), (-1, 0), (1, 0), (0, -1), (0, 1), (-1, -1), (-1, 1), (1, -1), (1, 1))

ABOVE, BELOW, LEFT, RIGHT, CORNER = 128, 144, 160, 192, 224


def mid_row(f, i, j):
    if 0 <= i < 8 and 0 <= j < 4:
        return 32 * f + 4 * i + j
    if i < 0 and 0 <= j < 4:
        return ABOVE + 4 * f + j
    if i > 7 and 0 <= j < 4:
        return BELOW + 4 * f + j
    if 0 <= i < 8:
        return (LEFT if j < 0 else RIGHT) + 8 * f + i
    return CORNER + 4 * (2 * (i > 7) + (j > 3)) + f


def coarse_row(f, i, side):
    down = -1 if i < 0 else (1 if i > 1 else 0)
    return 8 * DIRS.index((down, side)) + 2 * f + i % 2


def tables():
    pick = np.zeros((96, 512), np.float32)
    for i in range(32):
        for j in range(16):
            pick[4 * (i // 4) + j // 4, 16 * i + j] = 1
        pick[32 + i, 16 * i + 15] = 1
        pick[64 + i, 16 * i] = 1
    enlarge = np.zeros((912, 256), np.float32)
    taps = np.zeros((1152, 256), np.float32)
    ends = np.zeros((16, 256), np.float32)
    pack = np.zeros((112, 128), np.float32)
    pool = np.zeros((16, 128), np.float32)
    coarse_taps = np.zeros((144, 128), np.float32)
    spread = np.zeros((256, 128), np.float32)
    for f in range(4):
        for i in range(8):
            for j in range(16):
                enlarge[128 * f + 16 * i + j, mid_row(f, i, j // 4)] = 1
        for j in range(16):
            enlarge[512 + 16 * f + j, ABOVE + 4 * f + j // 4] = 1
            enlarge[576 + 16 * f + j, BELOW + 4 * f + j // 4] = 1
        for i in range(32):
            enlarge[640 + 32 * f + i, LEFT + 8 * f + i // 4] = 1
            enlarge[768 + 32 * f + i, RIGHT + 8 * f + i // 4] = 1
        for c in range(4):
            enlarge[896 + 4 * c + f, CORNER + 4 * c + f] = 1
            low, first = c < 2, c % 2 == 1
            ends[4 * c + f, 128 * first + 32 * f + 31 * low] = 1
            pack[96 + 4 * c + f, mid_row(f, 7 * low, 3 * (not first))] = 1
        for i in range(8):
            for j in range(4):
                here = 32 * f + 4 * i + j
                pool[2 * f + i // 4, here] = 1
                for t in range(9):
                    taps[128 * t + here, mid_row(f, i + t // 3 - 1, j + t % 3 - 1)] = 1
            pack[32 + 8 * f + i, mid_row(f, i, 3)] = 1
            pack[64 + 8 * f + i, mid_row(f, i, 0)] = 1
        for j in range(4):
            pack[4 * f + j, mid_row(f, 7, j)] = 1
            pack[16 + 4 * f + j, mid_row(f, 0, j)] = 1
        for i in range(2):
            for t in range(9):
                coarse_taps[16 * t + 2 * f + i, coarse_row(f, i + t // 3 - 1, t % 3 - 1)] = 1
        for i in range(-1, 9):
            for j in range(-1, 5):
                side = -1 if j < 0 else (1 if j > 3 else 0)
                spread[mid_row(f, i, j), coarse_row(f, i // 4 if i < 8 else 2, side)] = 1
    sides = np.zeros((512, 128), np.float32)
    for i in range(32):
        sides[16 * i, i] = 1
        sides[16 * i + 15, 64 + i] = 1
    wide_table = np.concatenate([pick, np.concatenate([enlarge, enlarge], axis=1)])
    middle_table = np.concatenate([taps, ends])
    narrow_table = np.concatenate([pack, pool, coarse_taps, spread, sides])
    return [jnp.asarray(t, BF16) for t in (wide_table, middle_table, narrow_table)]


def dot(a, b):
    return jnp.dot(a, b, preferred_element_type=F32)


def dot_t(a, b):
    return lax.dot_general(a, b, (((1,), (1,)), ((), ())), preferred_element_type=F32)


def group_lanes(t, size):
    lane = lax.broadcasted_iota(jnp.int32, t.shape, 1)
    step = 1
    while step < size:
        t = t + jnp.where(
            (lane & step) != 0, pltpu.roll(t, step, 1), pltpu.roll(t, 128 - step, 1)
        )
        step *= 2
    return t


def halves(t):
    high = t.astype(BF16)
    return high, (t - high.astype(F32)).astype(BF16)


def kernel(
    wide_count,
    narrow_count,
    x_in,
    gain_fine_in,
    kernel_fine_in,
    down_mid_in,
    gain_mid_in,
    kernel_mid_in,
    down_coarse_in,
    gain_coarse_in,
    kernel_coarse_in,
    up_coarse_in,
    up_mid_in,
    grad_in,
    wide_table_in,
    middle_table_in,
    narrow_table_in,
    out_ref,
    part_ref,
    shift_ref,
    slant_ref,
    xg,
    kernel_fine,
    flipped_fine,
    down_mid,
    kernel_mid,
    down_coarse,
    kernel_coarse,
    up_coarse,
    up_mid,
    gain_fine,
    gain_mid,
    gain_coarse,
    wide_table,
    middle_table,
    narrow_table,
    taps_buf,
    coarse_taps,
    columns,
    fine_block,
    part,
    pooled,
    summed,
    fine_slope,
    edge_rows,
    edge_sides,
    edge_ends,
    pool_grad,
    summed_grad,
    first,
    second,
    col_pack,
    cor_pack,
    row_in,
    col_in,
    cor_in,
    sum_pack,
    sum_in,
    sum_cor,
    cgrad_own,
    cgrad_in,
    mid_pack,
    mid_halo,
    mid_cor,
    coarse_own,
    coarse_halo,
    coarse_u,
    coarse_u_halo,
    u_pack,
    u_halo,
    u_cor,
    load_sem,
    out_sem,
    total_send,
    total_recv,
    halo_send,
    halo_recv,
):
    wide, narrow = lax.axis_index("wide"), lax.axis_index("narrow")

    def device(down, side):
        return (
            lax.rem(wide + down + wide_count, wide_count),
            lax.rem(narrow + side + narrow_count, narrow_count),
        )

    loads = {}
    pairs = (
        ("x", x_in, xg.at[0]),
        ("grad", grad_in, xg.at[1]),
        ("wide_table", wide_table_in, wide_table),
        ("middle_table", middle_table_in, middle_table),
        ("narrow_table", narrow_table_in, narrow_table),
        ("gain_fine", gain_fine_in, gain_fine),
        ("kernel_fine", kernel_fine_in, kernel_fine),
        ("up_mid", up_mid_in, up_mid),
        ("up_coarse", up_coarse_in, up_coarse),
        ("down_mid", down_mid_in, down_mid),
        ("gain_mid", gain_mid_in, gain_mid),
        ("kernel_coarse", kernel_coarse_in, kernel_coarse),
        ("kernel_mid", kernel_mid_in, kernel_mid),
        ("down_coarse", down_coarse_in, down_coarse),
        ("gain_coarse", gain_coarse_in, gain_coarse),
    )
    for number, (name, source, target) in enumerate(pairs):
        loads[name] = pltpu.make_async_copy(source, target, load_sem.at[number])
    loads["x"].start()

    barrier = pltpu.get_barrier_semaphore()
    greeted = 0
    for down in range(wide_count):
        for side in range(-2, narrow_count - 2):
            near = (down <= 1 or down == wide_count - 1) and abs(side) <= 1
            if (down, side) != (0, 0) and (down == 0 or side == 0 or near):
                pl.semaphore_signal(
                    barrier, inc=1, device_id=device(down, side), device_id_type=MESH
                )
                greeted += 1

    def send(source, target, which, down, side):
        pltpu.make_async_remote_copy(
            src_ref=source,
            dst_ref=target,
            send_sem=halo_send.at[which],
            recv_sem=halo_recv.at[which],
            device_id=device(down, side),
            device_id_type=MESH,
        ).start()

    def arrived(buffer, which):
        pltpu.make_async_copy(buffer, buffer, halo_recv.at[which]).wait()

    def sent(buffer, which):
        pltpu.make_async_copy(buffer, buffer, halo_send.at[which]).wait()

    def total_begin(phase, one, two):
        blank = jnp.zeros((8, 128), F32)
        first[phase, wide] = blank
        for k in range(one.shape[1] // 128):
            first[phase, wide, k : k + 1, :] = one[:, 128 * k : 128 * k + 128]
            first[phase, wide, 4 + k : 5 + k, :] = two[:, 128 * k : 128 * k + 128]
        @pl.loop(1, wide_count)
        def _(step):
            pltpu.make_async_remote_copy(
                src_ref=first.at[phase, wide],
                dst_ref=first.at[phase, wide],
                send_sem=total_send.at[2 * phase],
                recv_sem=total_recv.at[2 * phase],
                device_id=device(step, 0),
                device_id_type=MESH,
            ).start()

    def total_middle(phase):
        whole = first.at[phase, pl.ds(0, wide_count - 1)]
        pltpu.make_async_copy(whole, whole, total_recv.at[2 * phase]).wait()
        second[phase, narrow] = jnp.sum(first[phase], axis=0)
        @pl.loop(1, narrow_count)
        def _(step):
            pltpu.make_async_remote_copy(
                src_ref=second.at[phase, narrow],
                dst_ref=second.at[phase, narrow],
                send_sem=total_send.at[2 * phase + 1],
                recv_sem=total_recv.at[2 * phase + 1],
                device_id=device(0, step),
                device_id_type=MESH,
            ).start()

    def total_end(phase, channels, cells):
        whole = second.at[phase, pl.ds(0, narrow_count - 1)]
        pltpu.make_async_copy(whole, whole, total_recv.at[2 * phase + 1]).wait()
        size = channels // GROUPS
        t = group_lanes(jnp.sum(second[phase], axis=0), size) * (1.0 / (size * cells))
        count = channels // 128
        return (
            jnp.concatenate([t[k : k + 1] for k in range(count)], axis=1),
            jnp.concatenate([t[4 + k : 5 + k] for k in range(count)], axis=1),
        )

    has_above, has_below = wide > 0, wide < wide_count - 1
    has_left, has_right = narrow > 0, narrow < narrow_count - 1
    has_corner = (
        jnp.logical_and(has_above, has_left),
        jnp.logical_and(has_above, has_right),
        jnp.logical_and(has_below, has_left),
        jnp.logical_and(has_below, has_right),
    )
    exists = (None, has_above, has_below, has_left, has_right) + has_corner

    def only(condition, value):
        return value * jnp.where(condition, 1.0, 0.0).astype(F32)

    def corners(read, change, masked):
        result = None
        for c in range(4):
            value = change(read(c).astype(F32))
            if masked:
                value = only(has_corner[c], value)
            quarter = lax.broadcasted_iota(jnp.int32, value.shape, 0) // 4
            result = value if result is None else jnp.where(quarter == c, value, result)
        return result

    def mid_extended(own, read_halo, read_cor, change, masked):
        pieces = [change(own)]
        halo = change(read_halo.astype(F32))
        for low, high, d in ((0, 16, 1), (16, 32, 2), (32, 64, 3), (64, 96, 4)):
            piece = halo[low:high]
            pieces.append(only(exists[d], piece) if masked else piece)
        pieces.append(corners(read_cor, change, masked))
        pieces.append(jnp.zeros((16, own.shape[1]), F32))
        return jnp.concatenate(pieces, axis=0)

    def send_mid(pack, halo, cor, which):
        send(pack.at[pl.ds(0, 16)], halo.at[pl.ds(0, 16)], which, 1, 0)
        send(pack.at[pl.ds(16, 16)], halo.at[pl.ds(16, 16)], which, -1, 0)
        send(pack.at[pl.ds(32, 32)], halo.at[pl.ds(32, 32)], which, 0, 1)
        send(pack.at[pl.ds(64, 32)], halo.at[pl.ds(64, 32)], which, 0, -1)
        for c in range(4):
            down, side = DIRS[5 + c]
            send(pack.at[pl.ds(96, 16)], cor.at[c], which + 1, -down, -side)

    def send_coarse(own, halo, which):
        for d in range(1, 9):
            down, side = DIRS[d]
            send(own, halo.at[d - 1], which, -down, -side)

    def coarse_extended(own, halo, change, masked):
        pieces = [change(own)]
        for d in range(1, 9):
            piece = change(halo(d - 1))
            pieces.append(only(exists[d], piece) if masked else piece)
        pieces.append(jnp.zeros((56, own.shape[1]), F32))
        return jnp.concatenate(pieces, axis=0)

    PICK = wide_table.at[pl.ds(0, 96)]
    ENLARGE = wide_table.at[pl.ds(96, 912)]
    TAPS = middle_table.at[pl.ds(0, 1152)]
    ENDS = middle_table.at[pl.ds(1152, 16)]
    PACK = narrow_table.at[pl.ds(0, 112)]
    POOL = narrow_table.at[pl.ds(112, 16)]
    COARSE_TAPS = narrow_table.at[pl.ds(128, 144)]
    SPREAD = narrow_table.at[pl.ds(272, 256)]
    SIDES = narrow_table.at[pl.ds(528, 512)]

    def frame(which, f):
        return xg[which, f].reshape(512, 256)

    loads["x"].wait()
    for name in loads:
        if name != "x":
            loads[name].start()

    def add_frame(f, carry):
        value = frame(0, f).astype(F32)
        return (
            carry[0] + jnp.sum(value.reshape(64, 8, 256), axis=0),
            carry[1] + jnp.sum((value * value).reshape(64, 8, 256), axis=0),
        )

    blank = jnp.zeros((8, 256), F32)
    one, two = lax.fori_loop(0, 4, add_frame, (blank, blank))
    pl.semaphore_wait(barrier, greeted)
    total_begin(0, jnp.sum(one, axis=0, keepdims=True), jnp.sum(two, axis=0, keepdims=True))

    def rim(which):
        sem = 13 * which
        send(xg.at[which, :, 31], row_in.at[0, which], sem, 1, 0)
        send(xg.at[which, :, 0], row_in.at[1, which], sem, -1, 0)
        for f in range(4):
            picked = dot(PICK[...], frame(which, f)).astype(BF16)
            col_pack[0, which, 32 * f : 32 * f + 32] = picked[32:64]
            col_pack[1, which, 32 * f : 32 * f + 32] = picked[64:96]
            if which == 1:
                summed[32 * f : 32 * f + 32] = picked[0:32]
        send(col_pack.at[0, which], col_in.at[0, which], sem + 1, 0, 1)
        send(col_pack.at[1, which], col_in.at[1, which], sem + 1, 0, -1)
        ends = jnp.concatenate([col_pack[0, which], col_pack[1, which]], axis=0)
        cor_pack[which] = dot(ENDS[...], ends).astype(BF16)
        for c in range(4):
            down, side = DIRS[5 + c]
            send(cor_pack.at[which], cor_in.at[which, c], sem + 2, -down, -side)

    loads["wide_table"].wait()
    loads["middle_table"].wait()
    rim(0)
    total_middle(0)
    loads["grad"].wait()
    rim(1)
    loads["narrow_table"].wait()
    loads["gain_fine"].wait()
    loads["kernel_fine"].wait()

    fine_center, fine_square = total_end(0, 256, 2048 * wide_count * narrow_count)
    fine_inverse = lax.rsqrt(fine_square - fine_center * fine_center + epsilon)
    s_fine = gain_fine[...]

    def silu(value, center, inverse, scaling):
        normed = (value - center) * inverse * scaling
        return normed / (1.0 + jnp.exp(-normed))

    def slope(scaled, scaling):
        normed = scaled * scaling
        logistic = 1.0 / (1.0 + jnp.exp(-normed))
        return logistic * (1.0 + normed * (1.0 - logistic)) * scaling

    def fine_act(value):
        return silu(value, fine_center, fine_inverse, s_fine)

    arrived(row_in.at[:, 0], 0)
    arrived(col_in.at[:, 0], 1)
    arrived(cor_in.at[0], 2)

    def set_edges(above, below, left, right, ends):
        edge_rows[0] = only(has_above, above)
        edge_rows[1] = only(has_below, below)
        left = only(has_left, left).astype(BF16)
        right = only(has_right, right).astype(BF16)
        for f in range(4):
            edge_sides[f, 0:32] = left[32 * f : 32 * f + 32]
            edge_sides[f, 32:64] = right[32 * f : 32 * f + 32]
        edge_ends[...] = ends

    def place(f, own):
        column = lax.broadcasted_iota(jnp.int32, (512, 256), 0) % 16
        sides = edge_sides[f]
        low = jnp.where(
            column == 0, dot(SIDES[:, 0:64], sides), pltpu.roll(own, 1, 0)
        )
        columns[f, 16:528, 0:256] = low.astype(BF16)
        columns[f, 16:528, 256:512] = own.astype(BF16)
        high = jnp.where(
            column == 15, dot(SIDES[:, 32:96], sides), pltpu.roll(own, 511, 0)
        )
        columns[f, 16:528, 512:768] = high.astype(BF16)
        cell = lax.broadcasted_iota(jnp.int32, (16, 256), 0)
        for k in range(2):
            row = edge_rows[k, f]
            at = slice(528 * k, 528 * k + 16)
            west = edge_ends[pl.ds(8 * k + f, 1), :]
            east = edge_ends[pl.ds(8 * k + 4 + f, 1), :]
            columns[f, at, 0:256] = jnp.where(cell == 0, west, pltpu.roll(row, 1, 0)).astype(BF16)
            columns[f, at, 256:512] = row.astype(BF16)
            columns[f, at, 512:768] = jnp.where(cell == 15, east, pltpu.roll(row, 15, 0)).astype(BF16)

    def fine_convolve(f, weights):
        total = dot(columns[f, 0:512, :], weights[0])
        total += dot(columns[f, 16:528, :], weights[1])
        return total + dot(columns[f, 32:544, :], weights[2])

    set_edges(
        fine_act(row_in[0, 0].astype(F32)),
        fine_act(row_in[1, 0].astype(F32)),
        fine_act(col_in[0, 0].astype(F32)),
        fine_act(col_in[1, 0].astype(F32)),
        corners(lambda c: cor_in[0, c], fine_act, True),
    )

    def fine_value(f):
        return frame(0, f).astype(F32)

    @pl.loop(0, 4)
    def _(f):
        value = fine_value(f)
        place(f, fine_act(value))
        block = (value + fine_convolve(f, kernel_fine)).astype(BF16)
        fine_block[f] = block
        pooled[pl.ds(pl.multiple_of(32 * f, 32), 32), :] = (
            dot(PICK[0:32, :], block) * 0.0625
        ).astype(BF16)

    loads["down_mid"].wait()
    mid_in = dot(pooled[...], down_mid[...]).astype(BF16)
    mid_value = mid_in.astype(F32)

    def column_sums(value):
        return jnp.sum(value, axis=0, keepdims=True)

    total_begin(1, column_sums(mid_value), column_sums(mid_value * mid_value))
    mid_pack[...] = dot(PACK[...], mid_in).astype(BF16)
    send_mid(mid_pack, mid_halo, mid_cor, 6)

    up_mid_grad = summed[...]
    sum_pack[...] = dot(PACK[...], up_mid_grad).astype(BF16)
    send_mid(sum_pack, sum_in, sum_cor, 3)
    loads["up_mid"].wait()
    high, low = halves(dot_t(up_mid_grad, up_mid[...]))
    up_coarse_grad = (dot(POOL[...], high) + dot(POOL[...], low)).astype(BF16)
    loads["up_coarse"].wait()
    cgrad_own[...] = dot_t(up_coarse_grad, up_coarse[...]).astype(BF16)
    send_coarse(cgrad_own, cgrad_in, 5)
    total_middle(1)

    for a in range(3):
        for b in range(3):
            flipped_fine[a, 256 * b : 256 * b + 256, :] = kernel_fine[
                2 - a, 256 * (2 - b) : 256 * (2 - b) + 256, :
            ].T


    loads["gain_mid"].wait()
    loads["kernel_mid"].wait()
    mid_center, mid_square = total_end(1, 512, 128 * wide_count * narrow_count)
    mid_inverse = lax.rsqrt(mid_square - mid_center * mid_center + epsilon)
    s_mid = gain_mid[...]

    def mid_act(value):
        return silu(value, mid_center, mid_inverse, s_mid)

    def mid_scaled(value):
        return (value - mid_center) * mid_inverse

    def mid_convolve(extended, weights):
        taps_buf[...] = dot(TAPS[...], extended.astype(BF16)).astype(BF16).reshape(9, 128, 512)
        total = None
        for t in range(9):
            term = weights(t, taps_buf[t])
            total = term if total is None else total + term
        return total

    arrived(mid_halo, 6)
    arrived(mid_cor, 7)
    mid_block = (
        mid_value
        + mid_convolve(
            mid_extended(mid_value, mid_halo[...], lambda c: mid_cor[c], mid_act, True),
            lambda t, part_: dot(part_, kernel_mid[t]),
        )
    ).astype(BF16)

    loads["down_coarse"].wait()
    mid_pooled = (dot(POOL[...], mid_block) * 0.0625).astype(BF16)
    coarse_in = dot(mid_pooled, down_coarse[...]).astype(BF16)
    coarse_own[...] = coarse_in
    coarse_value = coarse_in.astype(F32)[0:8]
    total_begin(2, column_sums(coarse_value), column_sums(coarse_value * coarse_value))
    send_coarse(coarse_own, coarse_halo, 8)
    total_middle(2)

    arrived(cgrad_in, 5)
    loads["kernel_coarse"].wait()

    def coarse_convolve(extended, weights):
        spread_out = dot(COARSE_TAPS[...], extended.astype(BF16)).astype(BF16)
        coarse_taps[...] = spread_out.reshape(9, 16, 512)
        return lax.fori_loop(
            0, 9, lambda t, total: total + weights(t, coarse_taps[t]), jnp.zeros((16, 512), F32)
        )

    def same(value):
        return value

    cgrad = cgrad_own[...].astype(F32)[0:8]
    coarse_act_grad = coarse_convolve(
        coarse_extended(cgrad, lambda d: cgrad_in[d].astype(F32)[0:8], same, True),
        lambda t, part_: dot_t(part_, kernel_coarse[8 - t]),
    )[0:8]

    arrived(sum_in, 3)
    arrived(sum_cor, 4)
    sum_extended = mid_extended(
        up_mid_grad.astype(F32), sum_in[...], lambda c: sum_cor[c], same, True
    )
    summed_grad[...] = dot_t(sum_extended.astype(BF16), up_mid[...])

    loads["gain_coarse"].wait()
    coarse_center, coarse_square = total_end(2, 512, 8 * wide_count * narrow_count)
    coarse_inverse = lax.rsqrt(coarse_square - coarse_center * coarse_center + epsilon)
    s_coarse = gain_coarse[...]

    def coarse_scaled(value):
        return (value - coarse_center) * coarse_inverse

    scaled = coarse_scaled(coarse_value)
    normed_grad = coarse_act_grad * slope(scaled, s_coarse)
    total_begin(3, column_sums(normed_grad), column_sums(normed_grad * scaled))
    coarse_u[...] = cgrad + coarse_inverse * normed_grad
    send_coarse(coarse_u, coarse_u_halo, 9)
    total_middle(3)

    arrived(coarse_halo, 8)
    coarse_block = (
        coarse_in.astype(F32)
        + coarse_convolve(
            coarse_extended(
                coarse_value,
                lambda d: coarse_halo[d].astype(F32)[0:8],
                lambda v: silu(v, coarse_center, coarse_inverse, s_coarse),
                True,
            ),
            lambda t, part_: dot(part_, kernel_coarse[t]),
        )
    ).astype(BF16)
    coarse_up = dot(coarse_block, up_coarse[...]).astype(BF16)
    mid_sum = (mid_block.astype(F32) + dot(SPREAD[0:128, 0:16], coarse_up)).astype(BF16)
    mid_up = dot(mid_sum, up_mid[...]).astype(BF16)

    first_mean, second_mean = total_end(3, 512, 8 * wide_count * narrow_count)
    arrived(coarse_u_halo, 9)
    offset = coarse_inverse * first_mean
    factor = coarse_inverse * second_mean
    pieces = [coarse_u[...] - offset - scaled * factor]
    for d in range(8):
        piece = coarse_scaled(coarse_halo[d].astype(F32)[0:8])
        pieces.append(coarse_u_halo[d] - offset - piece * factor)
    pieces.append(jnp.zeros((56, 512), F32))
    coarse_in_grad = jnp.concatenate(pieces, axis=0).astype(BF16)

    mid_pool_grad = dot_t(dot(SPREAD[...], coarse_in_grad).astype(BF16), down_coarse[...])
    row = lax.broadcasted_iota(jnp.int32, (256, 512), 0)
    keep = jnp.where(row < ABOVE, 1.0, 0.0)
    bounds = ((ABOVE, 16, 1), (BELOW, 16, 2), (LEFT, 32, 3), (RIGHT, 32, 4)) + tuple(
        (CORNER + 4 * c, 4, 5 + c) for c in range(4)
    )
    for start, size, d in bounds:
        inside = jnp.logical_and(row >= start, row < start + size)
        keep = jnp.where(inside, jnp.where(exists[d], 1.0, 0.0).astype(F32), keep)
    mid_grad = (summed_grad[...] + 0.0625 * mid_pool_grad) * keep
    mid_act_grad = mid_convolve(mid_grad, lambda t, part_: dot_t(part_, kernel_mid[8 - t]))
    scaled = mid_scaled(mid_value)
    normed_grad = mid_act_grad * slope(scaled, s_mid)
    total_begin(4, column_sums(normed_grad), column_sums(normed_grad * scaled))
    mid_u = mid_grad[0:128].astype(BF16).astype(F32) + mid_inverse * normed_grad
    u_pack[...] = dot(PACK[...], mid_u.astype(BF16)).astype(BF16)
    send_mid(u_pack, u_halo, u_cor, 10)
    total_middle(4)

    mid_up = dot(ENLARGE[0:512, 0:128], mid_up).reshape(4, 8, 1, 16, 256)
    for f in range(4):
        block = fine_block[f].astype(F32).reshape(8, 4, 16, 256)
        fine_block[f] = (block + mid_up[f]).astype(BF16).reshape(512, 256)
    out_copy = pltpu.make_async_copy(fine_block, out_ref, out_sem.at[0])
    out_copy.start()

    def fine_scaled(f):
        return (fine_value(f) - fine_center) * fine_inverse

    @pl.loop(0, 4)
    def _(f):
        fine_slope[f] = slope(fine_scaled(f), s_fine)

    arrived(row_in.at[:, 1], 13)
    arrived(col_in.at[:, 1], 14)
    arrived(cor_in.at[1], 15)

    first_mean, second_mean = total_end(4, 512, 128 * wide_count * narrow_count)
    arrived(u_halo, 10)
    arrived(u_cor, 11)
    offset = mid_inverse * first_mean
    factor = mid_inverse * second_mean
    mid_in_grad = mid_extended(
        mid_u, u_halo[...], lambda c: u_cor[c], lambda v: v - offset, False
    ) - factor * mid_extended(
        mid_value, mid_halo[...], lambda c: mid_cor[c], mid_scaled, False
    )

    high, low = halves(0.0625 * dot_t(mid_in_grad.astype(BF16), down_mid[...]))
    pool_grad[...] = dot(ENLARGE[...], jnp.concatenate([high, low], axis=0))

    def rounded(value):
        return value.astype(BF16).astype(F32)

    set_edges(
        rounded(row_in[0, 1].astype(F32) + pool_grad[512:576, :].reshape(4, 16, 256)),
        rounded(row_in[1, 1].astype(F32) + pool_grad[576:640, :].reshape(4, 16, 256)),
        rounded(col_in[0, 1].astype(F32) + pool_grad[640:768, :]),
        rounded(col_in[1, 1].astype(F32) + pool_grad[768:896, :]),
        corners(lambda c: cor_in[1, c], lambda v: v + pool_grad[896:912, :], True),
    )

    def fine_backward(f, carry):
        added = pool_grad[pl.ds(pl.multiple_of(128 * f, 128), 128), :].reshape(8, 1, 16, 256)
        grad = xg[1, f].astype(F32).reshape(8, 4, 16, 256) + added
        grad = rounded(grad.reshape(512, 256))
        place(f, grad)
        normed_grad = fine_convolve(f, flipped_fine) * fine_slope[f]
        part[f] = (grad + fine_inverse * normed_grad).astype(BF16)
        return (
            carry[0] + jnp.sum(normed_grad.reshape(64, 8, 256), axis=0),
            carry[1] + jnp.sum((normed_grad * fine_scaled(f)).reshape(64, 8, 256), axis=0),
        )

    one, two = lax.fori_loop(0, 4, fine_backward, (blank, blank))
    total_begin(5, jnp.sum(one, axis=0, keepdims=True), jnp.sum(two, axis=0, keepdims=True))
    part_copy = pltpu.make_async_copy(part, part_ref, out_sem.at[1])
    part_copy.start()
    total_middle(5)

    for which in range(2):
        sent(row_in.at[:, which], 13 * which)
        sent(col_in.at[:, which], 13 * which + 1)
        sent(cor_in.at[which], 13 * which + 2)
    sent(sum_in, 3)
    sent(sum_cor, 4)
    sent(cgrad_in, 5)
    sent(mid_halo, 6)
    sent(mid_cor, 7)
    sent(coarse_halo, 8)
    sent(coarse_u_halo, 9)
    sent(u_halo, 10)
    sent(u_cor, 11)
    for phase in range(6):
        whole = first.at[phase, pl.ds(0, wide_count - 1)]
        pltpu.make_async_copy(whole, whole, total_send.at[2 * phase]).wait()
    first_mean, second_mean = total_end(5, 256, 2048 * wide_count * narrow_count)
    for phase in range(6):
        whole = second.at[phase, pl.ds(0, narrow_count - 1)]
        pltpu.make_async_copy(whole, whole, total_send.at[2 * phase + 1]).wait()
    slant = -fine_inverse * fine_inverse * second_mean
    shift_ref[...] = -fine_inverse * first_mean - fine_center * slant
    slant_ref[...] = slant
    out_copy.wait()
    part_copy.wait()


def finish(output_in, part, value, shift, slant, output, grad):
    output[...] = output_in[...]
    grad[0] = part[0].astype(F32) + (shift[...] + value[0].astype(F32) * slant[...])


def shards(*arguments):
    (
        fine_input,
        gain_fine,
        kernel_fine,
        down_mid,
        gain_mid,
        kernel_mid,
        down_coarse,
        gain_coarse,
        kernel_coarse,
        up_coarse,
        up_mid,
        grad_out,
    ) = arguments
    wide_count, narrow_count = lax.axis_size("wide"), lax.axis_size("narrow")
    anywhere = pl.BlockSpec(memory_space=pl.ANY)
    vmem = pltpu.VMEM
    scratch = [
        vmem((2, 4, 32, 16, 256), BF16),
        vmem((3, 768, 256), BF16),
        vmem((3, 768, 256), BF16),
        vmem((256, 512), BF16),
        vmem((9, 512, 512), BF16),
        vmem((512, 512), BF16),
        vmem((9, 512, 512), BF16),
        vmem((512, 512), BF16),
        vmem((512, 256), BF16),
        vmem((1, 256), F32),
        vmem((1, 512), F32),
        vmem((1, 512), F32),
        vmem((1008, 512), BF16),
        vmem((1168, 256), BF16),
        vmem((1040, 128), BF16),
        vmem((9, 128, 512), BF16),
        vmem((9, 16, 512), BF16),
        vmem((4, 544, 768), BF16),
        vmem((4, 512, 256), BF16),
        vmem((4, 512, 256), BF16),
        vmem((128, 256), BF16),
        vmem((128, 256), BF16),
        vmem((4, 512, 256), F32),
        vmem((2, 4, 16, 256), F32),
        vmem((4, 64, 256), BF16),
        vmem((16, 256), F32),
        vmem((912, 256), F32),
        vmem((256, 512), F32),
        vmem((6, wide_count, 8, 128), F32),
        vmem((6, narrow_count, 8, 128), F32),
        vmem((2, 2, 128, 256), BF16),
        vmem((2, 16, 256), BF16),
        vmem((2, 2, 4, 16, 256), BF16),
        vmem((2, 2, 128, 256), BF16),
        vmem((2, 4, 16, 256), BF16),
        vmem((112, 256), BF16),
        vmem((96, 256), BF16),
        vmem((4, 16, 256), BF16),
        vmem((16, 512), BF16),
        vmem((8, 16, 512), BF16),
        vmem((112, 512), BF16),
        vmem((96, 512), BF16),
        vmem((4, 16, 512), BF16),
        vmem((16, 512), BF16),
        vmem((8, 16, 512), BF16),
        vmem((8, 512), F32),
        vmem((8, 8, 512), F32),
        vmem((112, 512), BF16),
        vmem((96, 512), BF16),
        vmem((4, 16, 512), BF16),
        pltpu.SemaphoreType.DMA((15,)),
        pltpu.SemaphoreType.DMA((2,)),
        pltpu.SemaphoreType.DMA((12,)),
        pltpu.SemaphoreType.DMA((12,)),
        pltpu.SemaphoreType.DMA((16,)),
        pltpu.SemaphoreType.DMA((16,)),
    ]
    output, part, shift, slant = pl.pallas_call(
        functools.partial(kernel, wide_count, narrow_count),
        out_shape=(
            jax.ShapeDtypeStruct((4, 512, 256), BF16),
            jax.ShapeDtypeStruct((4, 512, 256), BF16),
            jax.ShapeDtypeStruct((1, 256), F32),
            jax.ShapeDtypeStruct((1, 256), F32),
        ),
        in_specs=[anywhere] * 15,
        out_specs=(anywhere, anywhere) + (pl.BlockSpec(memory_space=pltpu.VMEM),) * 2,
        scratch_shapes=scratch,
        compiler_params=pltpu.CompilerParams(
            collective_id=0, has_side_effects=True, vmem_limit_bytes=56 * 2**20
        ),
        name="whole_net",
    )(
        fine_input,
        gain_fine.reshape(1, 256),
        kernel_fine.reshape(3, 768, 256),
        down_mid,
        gain_mid.reshape(1, 512),
        kernel_mid.reshape(9, 512, 512),
        down_coarse,
        gain_coarse.reshape(1, 512),
        kernel_coarse.reshape(9, 512, 512),
        up_coarse,
        up_mid,
        grad_out,
        *tables(),
    )
    cells = pl.BlockSpec((1, 512, 256), lambda f: (f, 0, 0))
    vector = pl.BlockSpec((1, 256), lambda f: (0, 0))
    output, grad = pl.pallas_call(
        finish,
        grid=(4,),
        out_shape=(
            jax.ShapeDtypeStruct((4, 512, 256), BF16),
            jax.ShapeDtypeStruct((4, 512, 256), F32),
        ),
        in_specs=[cells, cells, cells, vector, vector],
        out_specs=(cells, cells),
        name="finish",
    )(output, part, fine_input.reshape(4, 512, 256), shift, slant)
    return output.reshape(4, 32, 16, 256), grad.reshape(4, 32, 16, 256)


def solution(mesh):
    tile = P(None, "wide", "narrow", None)
    return jax.shard_map(
        shards,
        mesh=mesh,
        in_specs=(tile,) + (P(),) * 10 + (tile,),
        out_specs=(tile, tile),
        check_vma=False,
    )
```

```python
import functools

import jax
import jax.numpy as jnp
import numpy as np
from jax import lax
from jax.experimental import pallas as pl
from jax.experimental.pallas import tpu as pltpu
from jax.sharding import PartitionSpec as P

MESH = pl.DeviceIdType.MESH
GROUPS = 32
epsilon = 1e-05
F32 = jnp.float32
BF16 = jnp.bfloat16

DIRS = ((0, 0), (-1, 0), (1, 0), (0, -1), (0, 1), (-1, -1), (-1, 1), (1, -1), (1, 1))

ABOVE, BELOW, LEFT, RIGHT, CORNER = 128, 144, 160, 192, 224


def mid_row(f, i, j):
    if 0 <= i < 8 and 0 <= j < 4:
        return 32 * f + 4 * i + j
    if i < 0 and 0 <= j < 4:
        return ABOVE + 4 * f + j
    if i > 7 and 0 <= j < 4:
        return BELOW + 4 * f + j
    if 0 <= i < 8:
        return (LEFT if j < 0 else RIGHT) + 8 * f + i
    return CORNER + 4 * (2 * (i > 7) + (j > 3)) + f


def coarse_row(f, i, side):
    down = -1 if i < 0 else (1 if i > 1 else 0)
    return 8 * DIRS.index((down, side)) + 2 * f + i % 2


def tables():
    pick = np.zeros((96, 512), np.float32)
    for i in range(32):
        for j in range(16):
            pick[4 * (i // 4) + j // 4, 16 * i + j] = 1
        pick[32 + i, 16 * i + 15] = 1
        pick[64 + i, 16 * i] = 1
    enlarge = np.zeros((512, 256), np.float32)
    taps = np.zeros((1152, 256), np.float32)
    ends = np.zeros((16, 256), np.float32)
    pack = np.zeros((112, 128), np.float32)
    pool = np.zeros((16, 128), np.float32)
    coarse_taps = np.zeros((144, 128), np.float32)
    spread = np.zeros((256, 128), np.float32)
    for f in range(4):
        for i in range(8):
            for j in range(16):
                enlarge[128 * f + 16 * i + j, mid_row(f, i, j // 4)] = 1
        for c in range(4):
            low, first = c < 2, c % 2 == 1
            ends[4 * c + f, 128 * first + 32 * f + 31 * low] = 1
            pack[96 + 4 * c + f, mid_row(f, 7 * low, 3 * (not first))] = 1
        for i in range(8):
            for j in range(4):
                here = 32 * f + 4 * i + j
                pool[2 * f + i // 4, here] = 1
                for t in range(9):
                    taps[128 * t + here, mid_row(f, i + t // 3 - 1, j + t % 3 - 1)] = 1
            pack[32 + 8 * f + i, mid_row(f, i, 3)] = 1
            pack[64 + 8 * f + i, mid_row(f, i, 0)] = 1
        for j in range(4):
            pack[4 * f + j, mid_row(f, 7, j)] = 1
            pack[16 + 4 * f + j, mid_row(f, 0, j)] = 1
        for i in range(2):
            for t in range(9):
                coarse_taps[16 * t + 2 * f + i, coarse_row(f, i + t // 3 - 1, t % 3 - 1)] = 1
        for i in range(-1, 9):
            for j in range(-1, 5):
                side = -1 if j < 0 else (1 if j > 3 else 0)
                spread[mid_row(f, i, j), coarse_row(f, i // 4 if i < 8 else 2, side)] = 1
    windows = np.zeros((288, 640), np.float32)
    for t in range(9):
        for i in range(32):
            for j in range(16):
                p, q = i + 1 - t // 3, j + 1 - t % 3
                row = 32 * t + 4 * (i // 4) + j // 4
                if 0 <= p < 32 and 0 <= q < 16:
                    at = 16 * p + q
                elif 0 <= q < 16:
                    at = (512 if p < 0 else 528) + q
                elif 0 <= p < 32:
                    at = (544 if q < 0 else 576) + p
                else:
                    at = 608 + 2 * (p > 31) + (q > 15)
                windows[row, at] = 1
    stretch = np.zeros((640, 768), np.float32)
    for f in range(4):
        for i in range(10):
            for j in range(16):
                for b in range(3):
                    at = 256 * b + mid_row(f, i - 1, (j + b - 1) // 4)
                    stretch[160 * f + 16 * i + j, at] = 1
    by_frame = np.zeros((128, 128), np.float32)
    for f in range(4):
        for c in range(4):
            by_frame[32 * f + c, 4 * c + f] = 1
    sides = np.zeros((512, 128), np.float32)
    for i in range(32):
        sides[16 * i, i] = 1
        sides[16 * i + 15, 64 + i] = 1
    wide_table = np.concatenate([pick, np.concatenate([enlarge, enlarge], axis=1)])
    middle_table = np.concatenate([taps, ends])
    narrow_table = np.concatenate([pack, pool, coarse_taps, spread, sides, by_frame])
    result = (wide_table, middle_table, narrow_table, windows, stretch)
    return [jnp.asarray(t, BF16) for t in result]


def dot(a, b):
    return jnp.dot(a, b, preferred_element_type=F32)


def dot_t(a, b):
    return lax.dot_general(a, b, (((1,), (1,)), ((), ())), preferred_element_type=F32)


def dot_first(a, b):
    return lax.dot_general(a, b, (((0,), (0,)), ((), ())), preferred_element_type=F32)


def group_lanes(t, size):
    lane = lax.broadcasted_iota(jnp.int32, t.shape, 1)
    step = 1
    while step < size:
        t = t + jnp.where(
            (lane & step) != 0, pltpu.roll(t, step, 1), pltpu.roll(t, 128 - step, 1)
        )
        step *= 2
    return t


def halves(t):
    high = t.astype(BF16)
    return high, (t - high.astype(F32)).astype(BF16)


def kernel(
    wide_count,
    narrow_count,
    x_in,
    gain_fine_in,
    kernel_fine_in,
    down_mid_in,
    gain_mid_in,
    kernel_mid_in,
    down_coarse_in,
    gain_coarse_in,
    kernel_coarse_in,
    up_coarse_in,
    up_mid_in,
    grad_in,
    wide_table_in,
    middle_table_in,
    narrow_table_in,
    windows_in,
    stretch_in,
    out_ref,
    grad_ref,
    xg,
    kernel_fine,
    down_mid,
    kernel_mid,
    down_coarse,
    kernel_coarse,
    up_coarse,
    up_mid,
    gain_fine,
    gain_mid,
    gain_coarse,
    wide_table,
    middle_table,
    narrow_table,
    windows,
    stretch,
    taps_buf,
    coarse_taps,
    columns,
    fine_block,
    grad_buf,
    conv_grad,
    pooled,
    summed,
    fine_slope,
    edge_rows,
    edge_sides,
    edge_ends,
    summed_grad,
    first,
    second,
    first_joint,
    second_joint,
    first_matrix,
    second_matrix,
    window_sums,
    slope_rows,
    slope_sides,
    slope_ends,
    matrix_sum,
    stretched,
    col_pack,
    cor_pack,
    row_in,
    col_in,
    cor_in,
    sum_pack,
    sum_in,
    sum_cor,
    cgrad_own,
    cgrad_in,
    mid_pack,
    mid_halo,
    mid_cor,
    coarse_own,
    coarse_halo,
    coarse_u,
    coarse_u_halo,
    u_pack,
    u_halo,
    u_cor,
    load_sem,
    out_sem,
    total_send,
    total_recv,
    halo_send,
    halo_recv,
):
    wide, narrow = lax.axis_index("wide"), lax.axis_index("narrow")

    def around(index, step, count):
        moved = index + step
        if isinstance(step, int) and step < 0:
            return jnp.where(moved < 0, moved + count, moved)
        return jnp.where(moved >= count, moved - count, moved)

    def device(down, side):
        return (
            wide if isinstance(down, int) and down == 0 else around(wide, down, wide_count),
            narrow if isinstance(side, int) and side == 0 else around(narrow, side, narrow_count),
        )

    loads = {}
    pairs = (
        ("x", x_in, xg.at[0]),
        ("grad", grad_in, xg.at[1]),
        ("wide_table", wide_table_in, wide_table),
        ("middle_table", middle_table_in, middle_table),
        ("narrow_table", narrow_table_in, narrow_table),
        ("gain_fine", gain_fine_in, gain_fine),
        ("kernel_fine", kernel_fine_in, kernel_fine),
        ("up_mid", up_mid_in, up_mid),
        ("up_coarse", up_coarse_in, up_coarse),
        ("down_mid", down_mid_in, down_mid),
        ("gain_mid", gain_mid_in, gain_mid),
        ("kernel_coarse", kernel_coarse_in, kernel_coarse),
        ("kernel_mid", kernel_mid_in, kernel_mid),
        ("down_coarse", down_coarse_in, down_coarse),
        ("gain_coarse", gain_coarse_in, gain_coarse),
        ("windows", windows_in, windows),
        ("stretch", stretch_in, stretch),
    )
    for number, (name, source, target) in enumerate(pairs):
        loads[name] = pltpu.make_async_copy(source, target, load_sem.at[number])
    loads["x"].start()

    barrier = pltpu.get_barrier_semaphore()
    greeted = 0
    for down in range(wide_count):
        for side in range(-2, narrow_count - 2):
            near = (down <= 1 or down == wide_count - 1) and abs(side) <= 1
            if (down, side) != (0, 0) and (down == 0 or side == 0 or near):
                pl.semaphore_signal(
                    barrier, inc=1, device_id=device(down, side), device_id_type=MESH
                )
                greeted += 1

    def send(source, target, which, down, side):
        pltpu.make_async_remote_copy(
            src_ref=source,
            dst_ref=target,
            send_sem=halo_send.at[which],
            recv_sem=halo_recv.at[which],
            device_id=device(down, side),
            device_id_type=MESH,
        ).start()

    def arrived(buffer, which):
        pltpu.make_async_copy(buffer, buffer, halo_recv.at[which]).wait()

    def sent(buffer, which):
        pltpu.make_async_copy(buffer, buffer, halo_send.at[which]).wait()

    firsts = tuple(first.at[p] for p in range(4)) + (first_joint, first_matrix)
    seconds = tuple(second.at[p] for p in range(4)) + (second_joint, second_matrix)

    def total_send_wide(phase):
        mine = firsts[phase].at[wide]

        @pl.loop(1, wide_count)
        def _(step):
            pltpu.make_async_remote_copy(
                src_ref=mine,
                dst_ref=mine,
                send_sem=total_send.at[2 * phase],
                recv_sem=total_recv.at[2 * phase],
                device_id=device(step, 0),
                device_id_type=MESH,
            ).start()

    def total_fill(phase, start, values):
        for n, value in enumerate(values):
            for k in range(value.shape[1] // 128):
                at = start + 4 * n + k
                firsts[phase][wide, at : at + 1, :] = value[:, 128 * k : 128 * k + 128]

    def total_begin(phase, one, two):
        if one.shape[1] < 512:
            firsts[phase][wide] = jnp.zeros((8, 128), F32)
        total_fill(phase, 0, (one, two))
        total_send_wide(phase)

    def total_middle(phase):
        whole = firsts[phase].at[pl.ds(0, wide_count - 1)]
        pltpu.make_async_copy(whole, whole, total_recv.at[2 * phase]).wait()
        seconds[phase][narrow] = jnp.sum(firsts[phase][...], axis=0)
        mine = seconds[phase].at[narrow]

        @pl.loop(1, narrow_count)
        def _(step):
            pltpu.make_async_remote_copy(
                src_ref=mine,
                dst_ref=mine,
                send_sem=total_send.at[2 * phase + 1],
                recv_sem=total_recv.at[2 * phase + 1],
                device_id=device(0, step),
                device_id_type=MESH,
            ).start()

    def total_sum(phase):
        whole = seconds[phase].at[pl.ds(0, narrow_count - 1)]
        pltpu.make_async_copy(whole, whole, total_recv.at[2 * phase + 1]).wait()
        return jnp.sum(seconds[phase][...], axis=0)

    def row_of(t, start, channels):
        return jnp.concatenate([t[start + k : start + k + 1] for k in range(channels // 128)], axis=1)

    def total_end(phase, channels, cells):
        size = channels // GROUPS
        t = group_lanes(total_sum(phase), size) * (1.0 / (size * cells))
        return row_of(t, 0, channels), row_of(t, 4, channels)

    has_above, has_below = wide > 0, wide < wide_count - 1
    has_left, has_right = narrow > 0, narrow < narrow_count - 1
    has_corner = (
        jnp.logical_and(has_above, has_left),
        jnp.logical_and(has_above, has_right),
        jnp.logical_and(has_below, has_left),
        jnp.logical_and(has_below, has_right),
    )
    exists = (None, has_above, has_below, has_left, has_right) + has_corner

    def only(condition, value):
        return value * jnp.where(condition, 1.0, 0.0).astype(F32)

    def corners(read, change, masked):
        result = None
        for c in range(4):
            value = change(read(c).astype(F32))
            if masked:
                value = only(has_corner[c], value)
            cell = lax.broadcasted_iota(jnp.int32, value.shape, 0)
            result = value if result is None else jnp.where(cell >= 4 * c, value, result)
        return result

    def mid_extended(own, read_halo, read_cor, change, masked):
        pieces = [change(own)]
        halo = change(read_halo.astype(F32))
        for low, high, d in ((0, 16, 1), (16, 32, 2), (32, 64, 3), (64, 96, 4)):
            piece = halo[low:high]
            pieces.append(only(exists[d], piece) if masked else piece)
        pieces.append(corners(read_cor, change, masked))
        pieces.append(jnp.zeros((16, own.shape[1]), F32))
        return jnp.concatenate(pieces, axis=0)

    def send_mid(pack, halo, cor, which):
        send(pack.at[pl.ds(0, 16)], halo.at[pl.ds(0, 16)], which, 1, 0)
        send(pack.at[pl.ds(16, 16)], halo.at[pl.ds(16, 16)], which, -1, 0)
        send(pack.at[pl.ds(32, 32)], halo.at[pl.ds(32, 32)], which, 0, 1)
        send(pack.at[pl.ds(64, 32)], halo.at[pl.ds(64, 32)], which, 0, -1)
        for c in range(4):
            down, side = DIRS[5 + c]
            send(pack.at[pl.ds(96, 16)], cor.at[c], which + 1, -down, -side)

    def send_coarse(own, halo, which):
        for d in range(1, 9):
            down, side = DIRS[d]
            send(own, halo.at[d - 1], which, -down, -side)

    def coarse_extended(own, halo, change, masked):
        pieces = [change(own)]
        for d in range(1, 9):
            piece = change(halo(d - 1))
            pieces.append(only(exists[d], piece) if masked else piece)
        pieces.append(jnp.zeros((56, own.shape[1]), F32))
        return jnp.concatenate(pieces, axis=0)

    PICK = wide_table.at[pl.ds(0, 96)]
    ENLARGE = wide_table.at[pl.ds(96, 512)]
    TAPS = middle_table.at[pl.ds(0, 1152)]
    ENDS = middle_table.at[pl.ds(1152, 16)]
    PACK = narrow_table.at[pl.ds(0, 112)]
    POOL = narrow_table.at[pl.ds(112, 16)]
    COARSE_TAPS = narrow_table.at[pl.ds(128, 144)]
    SPREAD = narrow_table.at[pl.ds(272, 256)]
    SIDES = narrow_table.at[pl.ds(528, 512)]
    BY_FRAME = narrow_table.at[pl.ds(1040, 128)]

    def frame(which, f):
        return xg[which, f].reshape(512, 256)

    loads["x"].wait()
    for name in loads:
        if name != "x":
            loads[name].start()

    def add_frame(f, carry):
        value = frame(0, f).astype(F32)
        return (
            carry[0] + jnp.sum(value.reshape(64, 8, 256), axis=0),
            carry[1] + jnp.sum((value * value).reshape(64, 8, 256), axis=0),
        )

    blank = jnp.zeros((8, 256), F32)
    one, two = lax.fori_loop(0, 4, add_frame, (blank, blank))
    pl.semaphore_wait(barrier, greeted)
    total_begin(0, jnp.sum(one, axis=0, keepdims=True), jnp.sum(two, axis=0, keepdims=True))

    def rim(which):
        sem = 13 * which
        send(xg.at[which, :, 31], row_in.at[0, which], sem, 1, 0)
        send(xg.at[which, :, 0], row_in.at[1, which], sem, -1, 0)
        for f in range(4):
            picked = dot(PICK[...], frame(which, f)).astype(BF16)
            col_pack[0, which, 32 * f : 32 * f + 32] = picked[32:64]
            col_pack[1, which, 32 * f : 32 * f + 32] = picked[64:96]
            if which == 1:
                summed[32 * f : 32 * f + 32] = picked[0:32]
        send(col_pack.at[0, which], col_in.at[0, which], sem + 1, 0, 1)
        send(col_pack.at[1, which], col_in.at[1, which], sem + 1, 0, -1)
        ends = jnp.concatenate([col_pack[0, which], col_pack[1, which]], axis=0)
        cor_pack[which] = dot(ENDS[...], ends).astype(BF16)
        for c in range(4):
            down, side = DIRS[5 + c]
            send(cor_pack.at[which], cor_in.at[which, c], sem + 2, -down, -side)

    loads["wide_table"].wait()
    loads["middle_table"].wait()
    rim(0)
    total_middle(0)
    loads["grad"].wait()
    rim(1)
    loads["narrow_table"].wait()
    loads["gain_fine"].wait()
    loads["kernel_fine"].wait()

    fine_center, fine_square = total_end(0, 256, 2048 * wide_count * narrow_count)
    fine_inverse = lax.rsqrt(fine_square - fine_center * fine_center + epsilon)
    s_fine = gain_fine[...]

    def silu(center, inverse, scaling):
        gain = 0.5 * inverse * scaling
        shift = -center * gain

        def change(value):
            half = value * gain + shift
            return half * jnp.tanh(half) + half

        return change

    def slope(scaled, scaling):
        half = scaled * (0.5 * scaling)
        bend = jnp.tanh(half)
        return (0.5 * scaling) * (1.0 + bend) * (1.0 + half * (1.0 - bend))

    fine_act = silu(fine_center, fine_inverse, s_fine)

    arrived(row_in.at[:, 0], 0)
    arrived(col_in.at[:, 0], 1)
    arrived(cor_in.at[0], 2)

    def set_edges(above, below, left, right, ends):
        edge_rows[0] = only(has_above, above)
        edge_rows[1] = only(has_below, below)
        left = only(has_left, left).astype(BF16)
        right = only(has_right, right).astype(BF16)
        for f in range(4):
            edge_sides[f, 0:32] = left[32 * f : 32 * f + 32]
            edge_sides[f, 32:64] = right[32 * f : 32 * f + 32]
        edge_ends[...] = ends

    def place(f, own):
        column = lax.broadcasted_iota(jnp.int32, (512, 256), 0) & 15
        sides = edge_sides[f]
        low = jnp.where(
            column == 0, dot(SIDES[:, 0:64], sides), pltpu.roll(own, 1, 0)
        )
        columns[f, 16:528, 0:256] = low.astype(BF16)
        columns[f, 16:528, 256:512] = own.astype(BF16)
        high = jnp.where(
            column == 15, dot(SIDES[:, 32:96], sides), pltpu.roll(own, 511, 0)
        )
        columns[f, 16:528, 512:768] = high.astype(BF16)
        cell = lax.broadcasted_iota(jnp.int32, (16, 256), 0)
        for k in range(2):
            row = edge_rows[k, f]
            at = slice(528 * k, 528 * k + 16)
            west = edge_ends[pl.ds(8 * k + f, 1), :]
            east = edge_ends[pl.ds(8 * k + 4 + f, 1), :]
            columns[f, at, 0:256] = jnp.where(cell == 0, west, pltpu.roll(row, 1, 0)).astype(BF16)
            columns[f, at, 256:512] = row.astype(BF16)
            columns[f, at, 512:768] = jnp.where(cell == 15, east, pltpu.roll(row, 15, 0)).astype(BF16)

    def fine_convolve(f):
        total = dot(columns[f, 0:512, :], kernel_fine[0:3].reshape(768, 256))
        total += dot(columns[f, 16:528, :], kernel_fine[3:6].reshape(768, 256))
        return total + dot(columns[f, 32:544, :], kernel_fine[6:9].reshape(768, 256))

    def fine_convolve_back(f):
        total = None
        for a in range(3):
            for b in range(3):
                term = dot_t(
                    columns[f, 16 * a : 16 * a + 512, 256 * b : 256 * b + 256],
                    kernel_fine[8 - 3 * a - b],
                )
                total = term if total is None else total + term
        return total

    def fine_scaled(value):
        return (value - fine_center) * fine_inverse

    set_edges(
        fine_act(row_in[0, 0].astype(F32)),
        fine_act(row_in[1, 0].astype(F32)),
        fine_act(col_in[0, 0].astype(F32)),
        fine_act(col_in[1, 0].astype(F32)),
        corners(lambda c: cor_in[0, c], fine_act, True),
    )

    def fine_value(f):
        return frame(0, f).astype(F32)

    @pl.loop(0, 4)
    def _(f):
        value = fine_value(f)
        place(f, fine_act(value))
        block = (value + fine_convolve(f)).astype(BF16)
        fine_block[f] = block
        pooled[pl.ds(pl.multiple_of(32 * f, 32), 32), :] = (
            dot(PICK[0:32, :], block) * 0.0625
        ).astype(BF16)

    def same(value):
        return value

    loads["down_mid"].wait()
    mid_in = dot(pooled[...], down_mid[...]).astype(BF16)
    mid_value = mid_in.astype(F32)

    def column_sums(value):
        return jnp.sum(value, axis=0, keepdims=True)

    total_begin(1, column_sums(mid_value), column_sums(mid_value * mid_value))
    mid_pack[...] = dot(PACK[...], mid_in).astype(BF16)
    send_mid(mid_pack, mid_halo, mid_cor, 6)

    @pl.loop(0, 4)
    def _(f):
        fine_slope[f] = slope(fine_scaled(fine_value(f)), s_fine)

    def pair_of(value, condition):
        scaled = fine_scaled(value.astype(F32))
        bent = slope(scaled, s_fine)
        if condition is not None:
            bent = only(condition, bent)
        return bent.astype(BF16), (bent * scaled).astype(BF16)

    for k in range(2):
        for n, value in enumerate(pair_of(row_in[k, 0], exists[1 + k])):
            slope_rows[n, k] = value
        for n, value in enumerate(pair_of(col_in[k, 0], exists[3 + k])):
            slope_sides[n, k] = value.reshape(4, 32, 256)
    bent = corners(lambda c: cor_in[0, c], lambda v: slope(fine_scaled(v), s_fine), True)
    scaled = corners(lambda c: cor_in[0, c], fine_scaled, False)
    for n, value in enumerate((bent, bent * scaled)):
        slope_ends[n] = dot(BY_FRAME[:, 0:16], value.astype(BF16)).astype(BF16).reshape(4, 32, 256)

    up_mid_grad = summed[...]
    sum_pack[...] = dot(PACK[...], up_mid_grad).astype(BF16)
    send_mid(sum_pack, sum_in, sum_cor, 3)
    loads["up_mid"].wait()
    high, low = halves(dot_t(up_mid_grad, up_mid[...]))
    up_coarse_grad = (dot(POOL[...], high) + dot(POOL[...], low)).astype(BF16)
    loads["up_coarse"].wait()
    cgrad_own[...] = dot_t(up_coarse_grad, up_coarse[...]).astype(BF16)
    send_coarse(cgrad_own, cgrad_in, 5)
    total_middle(1)

    loads["gain_mid"].wait()
    loads["kernel_mid"].wait()
    mid_center, mid_square = total_end(1, 512, 128 * wide_count * narrow_count)
    mid_inverse = lax.rsqrt(mid_square - mid_center * mid_center + epsilon)
    s_mid = gain_mid[...]

    mid_act = silu(mid_center, mid_inverse, s_mid)

    def mid_scaled(value):
        return (value - mid_center) * mid_inverse

    def mid_convolve(extended, weights):
        taps_buf[...] = dot(TAPS[...], extended.astype(BF16)).astype(BF16).reshape(9, 128, 512)
        total = None
        for t in range(9):
            term = weights(t, taps_buf[t])
            total = term if total is None else total + term
        return total

    arrived(mid_halo, 6)
    arrived(mid_cor, 7)
    mid_block = (
        mid_value
        + mid_convolve(
            mid_extended(mid_value, mid_halo[...], lambda c: mid_cor[c], mid_act, True),
            lambda t, part_: dot(part_, kernel_mid[t]),
        )
    ).astype(BF16)

    loads["down_coarse"].wait()
    mid_pooled = (dot(POOL[...], mid_block) * 0.0625).astype(BF16)
    coarse_in = dot(mid_pooled, down_coarse[...]).astype(BF16)
    coarse_own[...] = coarse_in
    coarse_value = coarse_in.astype(F32)[0:8]
    total_begin(2, column_sums(coarse_value), column_sums(coarse_value * coarse_value))
    send_coarse(coarse_own, coarse_halo, 8)

    arrived(row_in.at[:, 1], 13)
    arrived(col_in.at[:, 1], 14)
    arrived(cor_in.at[1], 15)
    set_edges(
        row_in[0, 1].astype(F32),
        row_in[1, 1].astype(F32),
        col_in[0, 1].astype(F32),
        col_in[1, 1].astype(F32),
        corners(lambda c: cor_in[1, c], same, True),
    )

    def convolve_grad(f, carry):
        place(f, frame(1, f).astype(F32))
        result = fine_convolve_back(f)
        conv_grad[f] = result
        weighted = result * fine_slope[f]
        scaled = fine_scaled(fine_value(f))
        return (
            carry[0] + jnp.sum(weighted.reshape(64, 8, 256), axis=0),
            carry[1] + jnp.sum((weighted * scaled).reshape(64, 8, 256), axis=0),
        )

    grad_sums = lax.fori_loop(0, 2, convolve_grad, (blank, blank))
    total_middle(2)

    arrived(cgrad_in, 5)
    loads["kernel_coarse"].wait()

    def coarse_convolve(extended, weights):
        spread_out = dot(COARSE_TAPS[...], extended.astype(BF16)).astype(BF16)
        coarse_taps[...] = spread_out.reshape(9, 16, 512)
        return lax.fori_loop(
            0, 9, lambda t, total: total + weights(t, coarse_taps[t]), jnp.zeros((16, 512), F32)
        )

    cgrad = cgrad_own[...].astype(F32)[0:8]
    coarse_act_grad = coarse_convolve(
        coarse_extended(cgrad, lambda d: cgrad_in[d].astype(F32)[0:8], same, True),
        lambda t, part_: dot_t(part_, kernel_coarse[8 - t]),
    )[0:8]

    arrived(sum_in, 3)
    arrived(sum_cor, 4)
    sum_extended = mid_extended(
        up_mid_grad.astype(F32), sum_in[...], lambda c: sum_cor[c], same, True
    )
    summed_grad[...] = dot_t(sum_extended.astype(BF16), up_mid[...])

    loads["gain_coarse"].wait()
    coarse_center, coarse_square = total_end(2, 512, 8 * wide_count * narrow_count)
    coarse_inverse = lax.rsqrt(coarse_square - coarse_center * coarse_center + epsilon)
    s_coarse = gain_coarse[...]

    def coarse_scaled(value):
        return (value - coarse_center) * coarse_inverse

    scaled = coarse_scaled(coarse_value)
    normed_grad = coarse_act_grad * slope(scaled, s_coarse)
    total_begin(3, column_sums(normed_grad), column_sums(normed_grad * scaled))
    coarse_u[...] = cgrad + coarse_inverse * normed_grad
    send_coarse(coarse_u, coarse_u_halo, 9)
    grad_sums = lax.fori_loop(2, 4, convolve_grad, grad_sums)

    loads["windows"].wait()

    @pl.loop(0, 4)
    def _(f):
        for n in range(2):
            bent = fine_slope[f]
            if n == 1:
                bent = bent * fine_scaled(fine_value(f))
            field = jnp.concatenate(
                [
                    bent.astype(BF16),
                    slope_rows[n, 0, f],
                    slope_rows[n, 1, f],
                    slope_sides[n, 0, f],
                    slope_sides[n, 1, f],
                    slope_ends[n, f],
                ],
                axis=0,
            )
            window_sums[n, :, f] = dot(windows[...], field).astype(BF16).reshape(9, 32, 256)

    total_middle(3)

    mid_mix = jnp.concatenate(
        [mid_scaled(mid_value).astype(BF16), jnp.ones((128, 128), BF16)], axis=1
    )
    matrix_sum[...] = jnp.zeros((4, 256, 512), F32)

    @pl.loop(0, 9)
    def _(t):
        through = 0.0625 * dot(kernel_fine[8 - t], down_mid[...])
        for n in range(2):
            mixed = dot_first(window_sums[n, t].reshape(128, 256), mid_mix)
            plain = jnp.concatenate([mixed[:, 512:640]] * 4, axis=1)
            matrix_sum[2 * n] += through * plain
            matrix_sum[2 * n + 1] += through * mixed[:, 0:512]

    def iota(shape, axis):
        return lax.broadcasted_iota(jnp.int32, shape, axis)

    def one_hot(condition):
        return jnp.where(condition, 1.0, 0.0).astype(BF16)

    by_group = one_hot((iota((32, 256), 1) >> 3) == iota((32, 256), 0))
    matrix = jnp.zeros((32, 128), F32)
    for n in range(4):
        high, low = halves(matrix_sum[n] * mid_inverse)
        high, low = halves(dot(by_group, high) + dot(by_group, low))
        to_lane = one_hot(iota((512, 128), 1) == 32 * n + (iota((512, 128), 0) >> 4))
        matrix += dot(high, to_lane) + dot(low, to_lane)
    first_matrix[wide] = matrix
    total_send_wide(5)

    first_mean, second_mean = total_end(3, 512, 8 * wide_count * narrow_count)
    arrived(coarse_halo, 8)
    arrived(coarse_u_halo, 9)
    offset = coarse_inverse * first_mean
    factor = coarse_inverse * second_mean
    pieces = [coarse_u[...] - offset - scaled * factor]
    for d in range(8):
        piece = coarse_scaled(coarse_halo[d].astype(F32)[0:8])
        pieces.append(coarse_u_halo[d] - offset - piece * factor)
    pieces.append(jnp.zeros((56, 512), F32))
    coarse_in_grad = jnp.concatenate(pieces, axis=0).astype(BF16)

    mid_pool_grad = dot_t(dot(SPREAD[...], coarse_in_grad).astype(BF16), down_coarse[...])
    row = lax.broadcasted_iota(jnp.int32, (256, 128), 0)
    keep = jnp.where(row < ABOVE, 1.0, 0.0)
    bounds = ((ABOVE, 16, 1), (BELOW, 16, 2), (LEFT, 32, 3), (RIGHT, 32, 4)) + tuple(
        (CORNER + 4 * c, 4, 5 + c) for c in range(4)
    )
    for start, size, d in bounds:
        inside = jnp.logical_and(row >= start, row < start + size)
        keep = jnp.where(inside, jnp.where(exists[d], 1.0, 0.0).astype(F32), keep)
    mid_grad = (summed_grad[...] + 0.0625 * mid_pool_grad) * jnp.concatenate([keep] * 4, axis=1)
    mid_act_grad = mid_convolve(mid_grad, lambda t, part_: dot_t(part_, kernel_mid[8 - t]))
    scaled = mid_scaled(mid_value)
    normed_grad = mid_act_grad * slope(scaled, s_mid)
    mid_u = mid_grad[0:128].astype(BF16).astype(F32) + mid_inverse * normed_grad
    u_pack[...] = dot(PACK[...], mid_u.astype(BF16)).astype(BF16)
    send_mid(u_pack, u_halo, u_cor, 10)
    pulled = (0.0625 * dot_t(mid_u.astype(BF16), down_mid[...])).astype(BF16)
    fine_sums = [jnp.sum(value, axis=0, keepdims=True) for value in grad_sums]
    for t in range(9):
        term = dot_t(pulled, kernel_fine[8 - t])
        for n in range(2):
            fine_sums[n] += column_sums(window_sums[n, t].reshape(128, 256).astype(F32) * term)
    first_joint[wide, 8:16, :] = jnp.zeros((8, 128), F32)
    total_fill(4, 0, (column_sums(normed_grad), column_sums(normed_grad * scaled)))
    total_fill(4, 8, fine_sums)
    total_send_wide(4)
    total_middle(5)

    coarse_block = (
        coarse_in.astype(F32)
        + coarse_convolve(
            coarse_extended(
                coarse_value,
                lambda d: coarse_halo[d].astype(F32)[0:8],
                silu(coarse_center, coarse_inverse, s_coarse),
                True,
            ),
            lambda t, part_: dot(part_, kernel_coarse[t]),
        )
    ).astype(BF16)
    coarse_up = dot(coarse_block, up_coarse[...]).astype(BF16)
    mid_sum = (mid_block.astype(F32) + dot(SPREAD[0:128, 0:16], coarse_up)).astype(BF16)
    mid_up = dot(mid_sum, up_mid[...]).astype(BF16)
    total_middle(4)

    mid_up = dot(ENLARGE[:, 0:128], mid_up).reshape(4, 8, 1, 16, 256)
    for f in range(4):
        block = fine_block[f].astype(F32).reshape(8, 4, 16, 256)
        fine_block[f] = (block + mid_up[f]).astype(BF16).reshape(512, 256)
    out_copy = pltpu.make_async_copy(fine_block, out_ref, out_sem.at[0])
    out_copy.start()
    matrix = total_sum(5)

    joint = total_sum(4)
    t = group_lanes(joint[0:8], 16) * (1.0 / (16 * 128 * wide_count * narrow_count))
    first_mean, second_mean = row_of(t, 0, 512), row_of(t, 4, 512)
    arrived(u_halo, 10)
    arrived(u_cor, 11)
    offset = mid_inverse * first_mean
    factor = mid_inverse * second_mean
    mid_in_grad = mid_extended(
        mid_u, u_halo[...], lambda c: u_cor[c], lambda v: v - offset, False
    ) - factor * mid_extended(
        mid_value, mid_halo[...], lambda c: mid_cor[c], mid_scaled, False
    )

    pool_grad = 0.0625 * dot_t(mid_in_grad.astype(BF16), down_mid[...])
    pool_grad = pool_grad * jnp.concatenate([keep] * 2, axis=1)
    high, low = halves(pool_grad)
    added = dot(ENLARGE[...], jnp.concatenate([high[0:256], low[0:256]], axis=0))
    loads["stretch"].wait()
    for a in range(3):
        fields = [dot_t(high, kernel_fine[8 - 3 * a - b]).astype(BF16) for b in range(3)]
        stretched[a] = dot(stretch[...], jnp.concatenate(fields, axis=0)).reshape(4, 10, 16, 256)

    means = jnp.zeros((8, 128), F32)
    for n, mean in enumerate((first_mean, second_mean)):
        lane, row = iota((512, 128), 1), iota((512, 128), 0)
        inside = jnp.logical_and((lane & 31) == (row >> 4), ((lane >> 5) & 1) == n)
        to_lane = jnp.where(inside, 0.0625, 0.0).astype(BF16)
        high, low = halves(jnp.broadcast_to(mean, (8, 512)))
        means += dot(high, to_lane) + dot(low, to_lane)
    matrix_high, matrix_low = halves(matrix)
    spread_groups = one_hot((iota((256, 32), 0) >> 3) == iota((256, 32), 1))
    t = group_lanes(joint[8:16], 8)
    fine_means = []
    for n in range(2):
        half = jnp.where((iota((8, 128), 1) >> 6) == n, means, 0.0)
        high, low = halves(half)
        change = dot_t(high, matrix_high) + dot_t(low, matrix_high) + dot_t(high, matrix_low)
        high, low = halves(change)
        change = dot_t(high, spread_groups) + dot_t(low, spread_groups)
        fine_means.append(
            (row_of(t, 4 * n, 256) - change[0:1]) * (1.0 / (8 * 2048 * wide_count * narrow_count))
        )
    slant = -fine_inverse * fine_inverse * fine_means[1]
    shift = -fine_inverse * fine_means[0] - fine_center * slant

    added = added.reshape(4, 8, 1, 16, 256)
    grad_copies = []
    for f in range(4):
        above, here, below = stretched[0, f], stretched[1, f], stretched[2, f]
        centre = here[1:9] + above[1:9] + below[1:9]
        top = here[1:9] + above[0:8] + below[1:9]
        bottom = here[1:9] + above[1:9] + below[2:10]
        back = jnp.stack([top, centre, centre, bottom], axis=1).reshape(512, 256)
        normed_grad = (conv_grad[f] + back) * fine_slope[f]
        grad = xg[1, f].astype(F32).reshape(8, 4, 16, 256) + added[f]
        grad = grad.reshape(512, 256).astype(BF16).astype(F32)
        grad_buf[f] = grad + fine_inverse * normed_grad + (shift + fine_value(f) * slant)
        grad_copies.append(
            pltpu.make_async_copy(grad_buf.at[f], grad_ref.at[f], out_sem.at[1 + f])
        )
        grad_copies[f].start()

    for which in range(2):
        sent(row_in.at[:, which], 13 * which)
        sent(col_in.at[:, which], 13 * which + 1)
        sent(cor_in.at[which], 13 * which + 2)
    sent(sum_in, 3)
    sent(sum_cor, 4)
    sent(cgrad_in, 5)
    sent(mid_halo, 6)
    sent(mid_cor, 7)
    sent(coarse_halo, 8)
    sent(coarse_u_halo, 9)
    sent(u_halo, 10)
    sent(u_cor, 11)
    for phase in range(6):
        whole = firsts[phase].at[pl.ds(0, wide_count - 1)]
        pltpu.make_async_copy(whole, whole, total_send.at[2 * phase]).wait()
        whole = seconds[phase].at[pl.ds(0, narrow_count - 1)]
        pltpu.make_async_copy(whole, whole, total_send.at[2 * phase + 1]).wait()
    out_copy.wait()
    for copy in grad_copies:
        copy.wait()


def shards(*arguments):
    (
        fine_input,
        gain_fine,
        kernel_fine,
        down_mid,
        gain_mid,
        kernel_mid,
        down_coarse,
        gain_coarse,
        kernel_coarse,
        up_coarse,
        up_mid,
        grad_out,
    ) = arguments
    wide_count, narrow_count = lax.axis_size("wide"), lax.axis_size("narrow")
    anywhere = pl.BlockSpec(memory_space=pl.ANY)
    vmem = pltpu.VMEM
    scratch = [
        vmem((2, 4, 32, 16, 256), BF16),
        vmem((9, 256, 256), BF16),
        vmem((256, 512), BF16),
        vmem((9, 512, 512), BF16),
        vmem((512, 512), BF16),
        vmem((9, 512, 512), BF16),
        vmem((512, 512), BF16),
        vmem((512, 256), BF16),
        vmem((1, 256), F32),
        vmem((1, 512), F32),
        vmem((1, 512), F32),
        vmem((608, 512), BF16),
        vmem((1168, 256), BF16),
        vmem((1168, 128), BF16),
        vmem((288, 640), BF16),
        vmem((640, 768), BF16),
        vmem((9, 128, 512), BF16),
        vmem((9, 16, 512), BF16),
        vmem((4, 544, 768), BF16),
        vmem((4, 512, 256), BF16),
        vmem((4, 512, 256), F32),
        vmem((4, 512, 256), F32),
        vmem((128, 256), BF16),
        vmem((128, 256), BF16),
        vmem((4, 512, 256), F32),
        vmem((2, 4, 16, 256), F32),
        vmem((4, 64, 256), BF16),
        vmem((16, 256), F32),
        vmem((256, 512), F32),
        vmem((4, wide_count, 8, 128), F32),
        vmem((4, narrow_count, 8, 128), F32),
        vmem((wide_count, 16, 128), F32),
        vmem((narrow_count, 16, 128), F32),
        vmem((wide_count, 32, 128), F32),
        vmem((narrow_count, 32, 128), F32),
        vmem((2, 9, 4, 32, 256), BF16),
        vmem((2, 2, 4, 16, 256), BF16),
        vmem((2, 2, 4, 32, 256), BF16),
        vmem((2, 4, 32, 256), BF16),
        vmem((4, 256, 512), F32),
        vmem((3, 4, 10, 16, 256), F32),
        vmem((2, 2, 128, 256), BF16),
        vmem((2, 16, 256), BF16),
        vmem((2, 2, 4, 16, 256), BF16),
        vmem((2, 2, 128, 256), BF16),
        vmem((2, 4, 16, 256), BF16),
        vmem((112, 256), BF16),
        vmem((96, 256), BF16),
        vmem((4, 16, 256), BF16),
        vmem((16, 512), BF16),
        vmem((8, 16, 512), BF16),
        vmem((112, 512), BF16),
        vmem((96, 512), BF16),
        vmem((4, 16, 512), BF16),
        vmem((16, 512), BF16),
        vmem((8, 16, 512), BF16),
        vmem((8, 512), F32),
        vmem((8, 8, 512), F32),
        vmem((112, 512), BF16),
        vmem((96, 512), BF16),
        vmem((4, 16, 512), BF16),
        pltpu.SemaphoreType.DMA((17,)),
        pltpu.SemaphoreType.DMA((5,)),
        pltpu.SemaphoreType.DMA((12,)),
        pltpu.SemaphoreType.DMA((12,)),
        pltpu.SemaphoreType.DMA((16,)),
        pltpu.SemaphoreType.DMA((16,)),
    ]
    output, grad = pl.pallas_call(
        functools.partial(kernel, wide_count, narrow_count),
        out_shape=(
            jax.ShapeDtypeStruct((4, 512, 256), BF16),
            jax.ShapeDtypeStruct((4, 512, 256), F32),
        ),
        in_specs=[anywhere] * 17,
        out_specs=(anywhere, anywhere),
        scratch_shapes=scratch,
        compiler_params=pltpu.CompilerParams(
            collective_id=0, has_side_effects=True, vmem_limit_bytes=56 * 2**20
        ),
        name="whole_net",
    )(
        fine_input,
        gain_fine.reshape(1, 256),
        kernel_fine.reshape(9, 256, 256),
        down_mid,
        gain_mid.reshape(1, 512),
        kernel_mid.reshape(9, 512, 512),
        down_coarse,
        gain_coarse.reshape(1, 512),
        kernel_coarse.reshape(9, 512, 512),
        up_coarse,
        up_mid,
        grad_out,
        *tables(),
    )
    return output.reshape(4, 32, 16, 256), grad.reshape(4, 32, 16, 256)


def solution(mesh):
    tile = P(None, "wide", "narrow", None)
    return jax.shard_map(
        shards,
        mesh=mesh,
        in_specs=(tile,) + (P(),) * 10 + (tile,),
        out_specs=(tile, tile),
        check_vma=False,
    )
```

```python
import functools

import jax
import jax.numpy as jnp
import numpy as np
from jax import lax
from jax.experimental import pallas as pl
from jax.experimental.pallas import tpu as pltpu
from jax.sharding import PartitionSpec as P

MESH = pl.DeviceIdType.MESH
GROUPS = 32
epsilon = 1e-05
F32 = jnp.float32
BF16 = jnp.bfloat16

DIRS = ((0, 0), (-1, 0), (1, 0), (0, -1), (0, 1), (-1, -1), (-1, 1), (1, -1), (1, 1))

ABOVE, BELOW, LEFT, RIGHT, CORNER = 128, 144, 160, 192, 224


def mid_row(f, i, j):
    if 0 <= i < 8 and 0 <= j < 4:
        return 32 * f + 4 * i + j
    if i < 0 and 0 <= j < 4:
        return ABOVE + 4 * f + j
    if i > 7 and 0 <= j < 4:
        return BELOW + 4 * f + j
    if 0 <= i < 8:
        return (LEFT if j < 0 else RIGHT) + 8 * f + i
    return CORNER + 4 * (2 * (i > 7) + (j > 3)) + f


def coarse_row(f, i, side):
    down = -1 if i < 0 else (1 if i > 1 else 0)
    return 8 * DIRS.index((down, side)) + 2 * f + i % 2


def tables():
    pick = np.zeros((96, 512), np.float32)
    for i in range(32):
        for j in range(16):
            pick[4 * (i // 4) + j // 4, 16 * i + j] = 1
        pick[32 + i, 16 * i + 15] = 1
        pick[64 + i, 16 * i] = 1
    enlarge = np.zeros((512, 256), np.float32)
    taps = np.zeros((1152, 256), np.float32)
    ends = np.zeros((16, 256), np.float32)
    pack = np.zeros((112, 128), np.float32)
    pool = np.zeros((16, 128), np.float32)
    coarse_taps = np.zeros((144, 128), np.float32)
    spread = np.zeros((256, 128), np.float32)
    for f in range(4):
        for i in range(8):
            for j in range(16):
                enlarge[128 * f + 16 * i + j, mid_row(f, i, j // 4)] = 1
        for c in range(4):
            low, first = c < 2, c % 2 == 1
            ends[4 * c + f, 128 * first + 32 * f + 31 * low] = 1
            pack[96 + 4 * c + f, mid_row(f, 7 * low, 3 * (not first))] = 1
        for i in range(8):
            for j in range(4):
                here = 32 * f + 4 * i + j
                pool[2 * f + i // 4, here] = 1
                for t in range(9):
                    taps[128 * t + here, mid_row(f, i + t // 3 - 1, j + t % 3 - 1)] = 1
            pack[32 + 8 * f + i, mid_row(f, i, 3)] = 1
            pack[64 + 8 * f + i, mid_row(f, i, 0)] = 1
        for j in range(4):
            pack[4 * f + j, mid_row(f, 7, j)] = 1
            pack[16 + 4 * f + j, mid_row(f, 0, j)] = 1
        for i in range(2):
            for t in range(9):
                coarse_taps[16 * t + 2 * f + i, coarse_row(f, i + t // 3 - 1, t % 3 - 1)] = 1
        for i in range(-1, 9):
            for j in range(-1, 5):
                side = -1 if j < 0 else (1 if j > 3 else 0)
                spread[mid_row(f, i, j), coarse_row(f, i // 4 if i < 8 else 2, side)] = 1
    windows = np.zeros((288, 640), np.float32)
    for t in range(9):
        for i in range(32):
            for j in range(16):
                p, q = i + 1 - t // 3, j + 1 - t % 3
                row = 32 * t + 4 * (i // 4) + j // 4
                if 0 <= p < 32 and 0 <= q < 16:
                    at = 16 * p + q
                elif 0 <= q < 16:
                    at = (512 if p < 0 else 528) + q
                elif 0 <= p < 32:
                    at = (544 if q < 0 else 576) + p
                else:
                    at = 608 + 2 * (p > 31) + (q > 15)
                windows[row, at] = 1
    stretch = np.zeros((640, 768), np.float32)
    for f in range(4):
        for i in range(10):
            for j in range(16):
                for b in range(3):
                    at = 256 * b + mid_row(f, i - 1, (j + b - 1) // 4)
                    stretch[160 * f + 16 * i + j, at] = 1
    by_frame = np.zeros((128, 128), np.float32)
    for f in range(4):
        for c in range(4):
            by_frame[32 * f + c, 4 * c + f] = 1
    sides = np.zeros((512, 128), np.float32)
    for i in range(32):
        sides[16 * i, i] = 1
        sides[16 * i + 15, 64 + i] = 1
    wide_table = np.concatenate([pick, np.concatenate([enlarge, enlarge], axis=1)])
    middle_table = np.concatenate([taps, ends])
    narrow_table = np.concatenate([pack, pool, coarse_taps, spread, sides, by_frame])
    result = (wide_table, middle_table, narrow_table, windows, stretch)
    return [jnp.asarray(t, BF16) for t in result]


def dot(a, b):
    return jnp.dot(a, b, preferred_element_type=F32)


def dot_t(a, b):
    return lax.dot_general(a, b, (((1,), (1,)), ((), ())), preferred_element_type=F32)


def dot_first(a, b):
    return lax.dot_general(a, b, (((0,), (0,)), ((), ())), preferred_element_type=F32)


def group_lanes(t, size):
    lane = lax.broadcasted_iota(jnp.int32, t.shape, 1)
    step = 1
    while step < size:
        t = t + jnp.where(
            (lane & step) != 0, pltpu.roll(t, step, 1), pltpu.roll(t, 128 - step, 1)
        )
        step *= 2
    return t


def halves(t):
    high = t.astype(BF16)
    return high, (t - high.astype(F32)).astype(BF16)


def kernel(
    wide_count,
    narrow_count,
    x_in,
    gain_fine_in,
    kernel_fine_in,
    down_mid_in,
    gain_mid_in,
    kernel_mid_in,
    down_coarse_in,
    gain_coarse_in,
    kernel_coarse_in,
    up_coarse_in,
    up_mid_in,
    grad_in,
    wide_table_in,
    middle_table_in,
    narrow_table_in,
    windows_in,
    stretch_in,
    out_ref,
    grad_ref,
    xg,
    kernel_fine,
    down_mid,
    kernel_mid,
    down_coarse,
    kernel_coarse,
    up_coarse,
    up_mid,
    gain_fine,
    gain_mid,
    gain_coarse,
    wide_table,
    middle_table,
    narrow_table,
    windows,
    stretch,
    taps_buf,
    coarse_taps,
    columns,
    fine_block,
    grad_buf,
    conv_grad,
    pooled_x,
    summed,
    fine_slope,
    edge_rows,
    edge_sides,
    edge_ends,
    summed_grad,
    first,
    second,
    first_joint,
    second_joint,
    first_matrix,
    second_matrix,
    window_sums,
    rim_rows,
    rim_sides,
    rim_ends,
    matrix_sum,
    stretched,
    col_pack,
    cor_pack,
    row_in,
    col_in,
    cor_in,
    sum_pack,
    sum_in,
    sum_cor,
    cgrad_own,
    cgrad_in,
    mid_pack,
    mid_halo,
    mid_cor,
    coarse_own,
    coarse_halo,
    coarse_u,
    coarse_u_halo,
    u_pack,
    u_halo,
    u_cor,
    load_sem,
    out_sem,
    total_send,
    total_recv,
    halo_send,
    halo_recv,
):
    wide, narrow = lax.axis_index("wide"), lax.axis_index("narrow")

    def around(index, step, count):
        moved = index + step
        if isinstance(step, int) and step < 0:
            return jnp.where(moved < 0, moved + count, moved)
        return jnp.where(moved >= count, moved - count, moved)

    def device(down, side):
        return (
            wide if isinstance(down, int) and down == 0 else around(wide, down, wide_count),
            narrow if isinstance(side, int) and side == 0 else around(narrow, side, narrow_count),
        )

    loads = {}
    pairs = (
        ("x", x_in, xg.at[0]),
        ("grad", grad_in, xg.at[1]),
        ("wide_table", wide_table_in, wide_table),
        ("middle_table", middle_table_in, middle_table),
        ("narrow_table", narrow_table_in, narrow_table),
        ("gain_fine", gain_fine_in, gain_fine),
        ("windows", windows_in, windows),
        ("kernel_fine", kernel_fine_in, kernel_fine),
        ("up_mid", up_mid_in, up_mid),
        ("up_coarse", up_coarse_in, up_coarse),
        ("down_mid", down_mid_in, down_mid),
        ("gain_mid", gain_mid_in, gain_mid),
        ("kernel_coarse", kernel_coarse_in, kernel_coarse),
        ("kernel_mid", kernel_mid_in, kernel_mid),
        ("down_coarse", down_coarse_in, down_coarse),
        ("gain_coarse", gain_coarse_in, gain_coarse),
        ("stretch", stretch_in, stretch),
    )
    for number, (name, source, target) in enumerate(pairs):
        loads[name] = pltpu.make_async_copy(source, target, load_sem.at[number])
    loads["x"].start()

    barrier = pltpu.get_barrier_semaphore()
    greeted = 0
    for down in range(wide_count):
        for side in range(-2, narrow_count - 2):
            near = (down <= 1 or down == wide_count - 1) and abs(side) <= 1
            if (down, side) != (0, 0) and (down == 0 or side == 0 or near):
                pl.semaphore_signal(
                    barrier, inc=1, device_id=device(down, side), device_id_type=MESH
                )
                greeted += 1

    def send(source, target, which, down, side):
        pltpu.make_async_remote_copy(
            src_ref=source,
            dst_ref=target,
            send_sem=halo_send.at[which],
            recv_sem=halo_recv.at[which],
            device_id=device(down, side),
            device_id_type=MESH,
        ).start()

    def arrived(buffer, which):
        pltpu.make_async_copy(buffer, buffer, halo_recv.at[which]).wait()

    def sent(buffer, which):
        pltpu.make_async_copy(buffer, buffer, halo_send.at[which]).wait()

    firsts = tuple(first.at[p] for p in range(4)) + (first_joint, first_matrix)
    seconds = tuple(second.at[p] for p in range(4)) + (second_joint, second_matrix)

    def total_send_wide(phase):
        mine = firsts[phase].at[wide]

        @pl.loop(1, wide_count)
        def _(step):
            pltpu.make_async_remote_copy(
                src_ref=mine,
                dst_ref=mine,
                send_sem=total_send.at[2 * phase],
                recv_sem=total_recv.at[2 * phase],
                device_id=device(step, 0),
                device_id_type=MESH,
            ).start()

    def total_fill(phase, start, values):
        for n, value in enumerate(values):
            for k in range(value.shape[1] // 128):
                at = start + 4 * n + k
                firsts[phase][wide, at : at + 1, :] = value[:, 128 * k : 128 * k + 128]

    def total_begin(phase, one, two):
        if one.shape[1] < 512:
            firsts[phase][wide] = jnp.zeros((8, 128), F32)
        total_fill(phase, 0, (one, two))
        total_send_wide(phase)

    def total_middle(phase):
        whole = firsts[phase].at[pl.ds(0, wide_count - 1)]
        pltpu.make_async_copy(whole, whole, total_recv.at[2 * phase]).wait()
        seconds[phase][narrow] = jnp.sum(firsts[phase][...], axis=0)
        mine = seconds[phase].at[narrow]

        @pl.loop(1, narrow_count)
        def _(step):
            pltpu.make_async_remote_copy(
                src_ref=mine,
                dst_ref=mine,
                send_sem=total_send.at[2 * phase + 1],
                recv_sem=total_recv.at[2 * phase + 1],
                device_id=device(0, step),
                device_id_type=MESH,
            ).start()

    def total_sum(phase):
        whole = seconds[phase].at[pl.ds(0, narrow_count - 1)]
        pltpu.make_async_copy(whole, whole, total_recv.at[2 * phase + 1]).wait()
        return jnp.sum(seconds[phase][...], axis=0)

    def row_of(t, start, channels):
        return jnp.concatenate([t[start + k : start + k + 1] for k in range(channels // 128)], axis=1)

    def total_end(phase, channels, cells):
        size = channels // GROUPS
        t = group_lanes(total_sum(phase), size) * (1.0 / (size * cells))
        return row_of(t, 0, channels), row_of(t, 4, channels)

    has_above, has_below = wide > 0, wide < wide_count - 1
    has_left, has_right = narrow > 0, narrow < narrow_count - 1
    has_corner = (
        jnp.logical_and(has_above, has_left),
        jnp.logical_and(has_above, has_right),
        jnp.logical_and(has_below, has_left),
        jnp.logical_and(has_below, has_right),
    )
    exists = (None, has_above, has_below, has_left, has_right) + has_corner

    def only(condition, value):
        return value * jnp.where(condition, 1.0, 0.0).astype(F32)

    def corners(read, change, masked):
        result = None
        for c in range(4):
            value = change(read(c).astype(F32))
            if masked:
                value = only(has_corner[c], value)
            cell = lax.broadcasted_iota(jnp.int32, value.shape, 0)
            result = value if result is None else jnp.where(cell >= 4 * c, value, result)
        return result

    def mid_extended(own, read_halo, read_cor, change, masked):
        pieces = [change(own)]
        halo = change(read_halo.astype(F32))
        for low, high, d in ((0, 16, 1), (16, 32, 2), (32, 64, 3), (64, 96, 4)):
            piece = halo[low:high]
            pieces.append(only(exists[d], piece) if masked else piece)
        pieces.append(corners(read_cor, change, masked))
        pieces.append(jnp.zeros((16, own.shape[1]), F32))
        return jnp.concatenate(pieces, axis=0)

    def send_mid(pack, halo, cor, which):
        send(pack.at[pl.ds(0, 16)], halo.at[pl.ds(0, 16)], which, 1, 0)
        send(pack.at[pl.ds(16, 16)], halo.at[pl.ds(16, 16)], which, -1, 0)
        send(pack.at[pl.ds(32, 32)], halo.at[pl.ds(32, 32)], which, 0, 1)
        send(pack.at[pl.ds(64, 32)], halo.at[pl.ds(64, 32)], which, 0, -1)
        for c in range(4):
            down, side = DIRS[5 + c]
            send(pack.at[pl.ds(96, 16)], cor.at[c], which + 1, -down, -side)

    def send_coarse(own, halo, which):
        for d in range(1, 9):
            down, side = DIRS[d]
            send(own, halo.at[d - 1], which, -down, -side)

    def coarse_extended(own, halo, change, masked):
        pieces = [change(own)]
        for d in range(1, 9):
            piece = change(halo(d - 1))
            pieces.append(only(exists[d], piece) if masked else piece)
        pieces.append(jnp.zeros((56, own.shape[1]), F32))
        return jnp.concatenate(pieces, axis=0)

    PICK = wide_table.at[pl.ds(0, 96)]
    ENLARGE = wide_table.at[pl.ds(96, 512)]
    TAPS = middle_table.at[pl.ds(0, 1152)]
    ENDS = middle_table.at[pl.ds(1152, 16)]
    PACK = narrow_table.at[pl.ds(0, 112)]
    POOL = narrow_table.at[pl.ds(112, 16)]
    COARSE_TAPS = narrow_table.at[pl.ds(128, 144)]
    SPREAD = narrow_table.at[pl.ds(272, 256)]
    SIDES = narrow_table.at[pl.ds(528, 512)]
    BY_FRAME = narrow_table.at[pl.ds(1040, 128)]

    def frame(which, f):
        return xg[which, f].reshape(512, 256)

    loads["x"].wait()
    for name in loads:
        if name != "x":
            loads[name].start()

    def add_frame(f, carry):
        value = frame(0, f).astype(F32)
        return (
            carry[0] + jnp.sum(value.reshape(64, 8, 256), axis=0),
            carry[1] + jnp.sum((value * value).reshape(64, 8, 256), axis=0),
        )

    blank = jnp.zeros((8, 256), F32)
    one, two = lax.fori_loop(0, 4, add_frame, (blank, blank))
    pl.semaphore_wait(barrier, greeted)
    total_begin(0, jnp.sum(one, axis=0, keepdims=True), jnp.sum(two, axis=0, keepdims=True))

    def rim(which):
        sem = 13 * which
        send(xg.at[which, :, 31], row_in.at[0, which], sem, 1, 0)
        send(xg.at[which, :, 0], row_in.at[1, which], sem, -1, 0)
        for f in range(4):
            picked = dot(PICK[...], frame(which, f))
            if which == 0:
                pooled_x[32 * f : 32 * f + 32] = picked[0:32]
            picked = picked.astype(BF16)
            col_pack[0, which, 32 * f : 32 * f + 32] = picked[32:64]
            col_pack[1, which, 32 * f : 32 * f + 32] = picked[64:96]
            if which == 1:
                summed[32 * f : 32 * f + 32] = picked[0:32]
        send(col_pack.at[0, which], col_in.at[0, which], sem + 1, 0, 1)
        send(col_pack.at[1, which], col_in.at[1, which], sem + 1, 0, -1)
        ends = jnp.concatenate([col_pack[0, which], col_pack[1, which]], axis=0)
        cor_pack[which] = dot(ENDS[...], ends).astype(BF16)
        for c in range(4):
            down, side = DIRS[5 + c]
            send(cor_pack.at[which], cor_in.at[which, c], sem + 2, -down, -side)

    loads["wide_table"].wait()
    loads["middle_table"].wait()
    rim(0)
    total_middle(0)
    loads["grad"].wait()
    rim(1)
    loads["narrow_table"].wait()
    loads["gain_fine"].wait()
    loads["kernel_fine"].wait()

    fine_center, fine_square = total_end(0, 256, 2048 * wide_count * narrow_count)
    fine_inverse = lax.rsqrt(fine_square - fine_center * fine_center + epsilon)
    s_fine = gain_fine[...]

    def silu(center, inverse, scaling):
        gain = 0.5 * inverse * scaling
        shift = -center * gain

        def change(value):
            half = value * gain + shift
            return half * jnp.tanh(half) + half

        return change

    def slope(scaled, scaling):
        half = scaled * (0.5 * scaling)
        bend = jnp.tanh(half)
        return (0.5 * scaling) * (1.0 + bend) * (1.0 + half * (1.0 - bend))

    fine_act = silu(fine_center, fine_inverse, s_fine)

    arrived(row_in.at[:, 0], 0)
    arrived(col_in.at[:, 0], 1)
    arrived(cor_in.at[0], 2)

    def set_edges(above, below, left, right, ends):
        edge_rows[0] = only(has_above, above)
        edge_rows[1] = only(has_below, below)
        left = only(has_left, left).astype(BF16)
        right = only(has_right, right).astype(BF16)
        for f in range(4):
            edge_sides[f, 0:32] = left[32 * f : 32 * f + 32]
            edge_sides[f, 32:64] = right[32 * f : 32 * f + 32]
        edge_ends[...] = ends

    def place(f, own):
        column = lax.broadcasted_iota(jnp.int32, (512, 256), 0) & 15
        sides = edge_sides[f]
        low = jnp.where(
            column == 0, dot(SIDES[:, 0:64], sides), pltpu.roll(own, 1, 0)
        )
        columns[f, 16:528, 0:256] = low.astype(BF16)
        columns[f, 16:528, 256:512] = own.astype(BF16)
        high = jnp.where(
            column == 15, dot(SIDES[:, 32:96], sides), pltpu.roll(own, 511, 0)
        )
        columns[f, 16:528, 512:768] = high.astype(BF16)
        cell = lax.broadcasted_iota(jnp.int32, (16, 256), 0)
        for k in range(2):
            row = edge_rows[k, f]
            at = slice(528 * k, 528 * k + 16)
            west = edge_ends[pl.ds(8 * k + f, 1), :]
            east = edge_ends[pl.ds(8 * k + 4 + f, 1), :]
            columns[f, at, 0:256] = jnp.where(cell == 0, west, pltpu.roll(row, 1, 0)).astype(BF16)
            columns[f, at, 256:512] = row.astype(BF16)
            columns[f, at, 512:768] = jnp.where(cell == 15, east, pltpu.roll(row, 15, 0)).astype(BF16)

    def fine_convolve(f):
        total = dot(columns[f, 0:512, :], kernel_fine[0:3].reshape(768, 256))
        total += dot(columns[f, 16:528, :], kernel_fine[3:6].reshape(768, 256))
        return total + dot(columns[f, 32:544, :], kernel_fine[6:9].reshape(768, 256))

    def fine_convolve_back(f):
        total = None
        for a in range(3):
            for b in range(3):
                term = dot_t(
                    columns[f, 16 * a : 16 * a + 512, 256 * b : 256 * b + 256],
                    kernel_fine[8 - 3 * a - b],
                )
                total = term if total is None else total + term
        return total

    def fine_scaled(value):
        return (value - fine_center) * fine_inverse

    def fine_value(f):
        return frame(0, f).astype(F32)

    def set_fields(n, change):
        for k in range(2):
            rim_rows[n, k] = only(exists[1 + k], change(row_in[k, 0].astype(F32))).astype(BF16)
            sides = only(exists[3 + k], change(col_in[k, 0].astype(F32))).astype(BF16)
            rim_sides[n, k] = sides.reshape(4, 32, 256)
        ends = corners(lambda c: cor_in[0, c], change, True)
        ends = dot(BY_FRAME[:, 0:16], ends.astype(BF16)).astype(BF16)
        rim_ends[n] = ends.reshape(4, 32, 256)

    def window(n, f, own):
        field = jnp.concatenate(
            [
                own.astype(BF16),
                rim_rows[n, 0, f],
                rim_rows[n, 1, f],
                rim_sides[n, 0, f],
                rim_sides[n, 1, f],
                rim_ends[n, f],
            ],
            axis=0,
        )
        return dot(windows[...], field)

    set_fields(0, fine_act)
    loads["windows"].wait()

    @pl.loop(0, 4)
    def _(f):
        sums = window(0, f, fine_act(fine_value(f)))
        high, low = halves(sums)
        window_sums[0, :, f] = high.reshape(9, 32, 256)
        window_sums[1, :, f] = low.reshape(9, 32, 256)

    pooled = pooled_x[...]
    for t in range(9):
        both = jnp.concatenate(
            [window_sums[0, t].reshape(128, 256), window_sums[1, t].reshape(128, 256)], axis=0
        )
        both = dot(both, kernel_fine[8 - t])
        pooled += both[0:128] + both[128:256]
    pooled = (pooled * 0.0625).astype(BF16)

    def fine_forward(f):
        value = fine_value(f)
        place(f, fine_act(value))
        fine_block[f] = (value + fine_convolve(f)).astype(BF16)

    def same(value):
        return value

    loads["down_mid"].wait()
    mid_in = dot(pooled, down_mid[...]).astype(BF16)
    mid_value = mid_in.astype(F32)

    def column_sums(value):
        return jnp.sum(value, axis=0, keepdims=True)

    total_begin(1, column_sums(mid_value), column_sums(mid_value * mid_value))
    mid_pack[...] = dot(PACK[...], mid_in).astype(BF16)
    send_mid(mid_pack, mid_halo, mid_cor, 6)

    @pl.loop(0, 4)
    def _(f):
        fine_slope[f] = slope(fine_scaled(fine_value(f)), s_fine)

    set_fields(0, lambda v: slope(fine_scaled(v), s_fine))
    set_fields(1, lambda v: slope(fine_scaled(v), s_fine) * fine_scaled(v))

    total_middle(1)

    up_mid_grad = summed[...]
    sum_pack[...] = dot(PACK[...], up_mid_grad).astype(BF16)
    send_mid(sum_pack, sum_in, sum_cor, 3)
    loads["up_mid"].wait()
    high, low = halves(dot_t(up_mid_grad, up_mid[...]))
    up_coarse_grad = (dot(POOL[...], high) + dot(POOL[...], low)).astype(BF16)
    loads["up_coarse"].wait()
    cgrad_own[...] = dot_t(up_coarse_grad, up_coarse[...]).astype(BF16)
    send_coarse(cgrad_own, cgrad_in, 5)

    @pl.loop(0, 4)
    def _(f):
        bent = fine_slope[f]
        window_sums[0, :, f] = window(0, f, bent).astype(BF16).reshape(9, 32, 256)
        bent = bent * fine_scaled(fine_value(f))
        window_sums[1, :, f] = window(1, f, bent).astype(BF16).reshape(9, 32, 256)

    loads["gain_mid"].wait()
    loads["kernel_mid"].wait()
    mid_center, mid_square = total_end(1, 512, 128 * wide_count * narrow_count)
    mid_inverse = lax.rsqrt(mid_square - mid_center * mid_center + epsilon)
    s_mid = gain_mid[...]

    mid_act = silu(mid_center, mid_inverse, s_mid)

    def mid_scaled(value):
        return (value - mid_center) * mid_inverse

    def mid_convolve(extended, weights):
        taps_buf[...] = dot(TAPS[...], extended.astype(BF16)).astype(BF16).reshape(9, 128, 512)
        total = None
        for t in range(9):
            term = weights(t, taps_buf[t])
            total = term if total is None else total + term
        return total

    arrived(mid_halo, 6)
    arrived(mid_cor, 7)
    mid_block = (
        mid_value
        + mid_convolve(
            mid_extended(mid_value, mid_halo[...], lambda c: mid_cor[c], mid_act, True),
            lambda t, part_: dot(part_, kernel_mid[t]),
        )
    ).astype(BF16)

    loads["down_coarse"].wait()
    mid_pooled = (dot(POOL[...], mid_block) * 0.0625).astype(BF16)
    coarse_in = dot(mid_pooled, down_coarse[...]).astype(BF16)
    coarse_own[...] = coarse_in
    coarse_value = coarse_in.astype(F32)[0:8]
    total_begin(2, column_sums(coarse_value), column_sums(coarse_value * coarse_value))
    send_coarse(coarse_own, coarse_halo, 8)

    arrived(row_in.at[:, 1], 13)
    arrived(col_in.at[:, 1], 14)
    arrived(cor_in.at[1], 15)
    set_edges(
        row_in[0, 1].astype(F32),
        row_in[1, 1].astype(F32),
        col_in[0, 1].astype(F32),
        col_in[1, 1].astype(F32),
        corners(lambda c: cor_in[1, c], same, True),
    )

    def convolve_grad(f, carry):
        place(f, frame(1, f).astype(F32))
        result = fine_convolve_back(f)
        conv_grad[f] = result
        weighted = result * fine_slope[f]
        scaled = fine_scaled(fine_value(f))
        return (
            carry[0] + jnp.sum(weighted.reshape(64, 8, 256), axis=0),
            carry[1] + jnp.sum((weighted * scaled).reshape(64, 8, 256), axis=0),
        )

    grad_sums = lax.fori_loop(0, 2, convolve_grad, (blank, blank))
    total_middle(2)

    arrived(cgrad_in, 5)
    loads["kernel_coarse"].wait()

    def coarse_convolve(extended, weights):
        spread_out = dot(COARSE_TAPS[...], extended.astype(BF16)).astype(BF16)
        coarse_taps[...] = spread_out.reshape(9, 16, 512)
        return lax.fori_loop(
            0, 9, lambda t, total: total + weights(t, coarse_taps[t]), jnp.zeros((16, 512), F32)
        )

    cgrad = cgrad_own[...].astype(F32)[0:8]
    coarse_act_grad = coarse_convolve(
        coarse_extended(cgrad, lambda d: cgrad_in[d].astype(F32)[0:8], same, True),
        lambda t, part_: dot_t(part_, kernel_coarse[8 - t]),
    )[0:8]

    arrived(sum_in, 3)
    arrived(sum_cor, 4)
    sum_extended = mid_extended(
        up_mid_grad.astype(F32), sum_in[...], lambda c: sum_cor[c], same, True
    )
    summed_grad[...] = dot_t(sum_extended.astype(BF16), up_mid[...])

    loads["gain_coarse"].wait()
    coarse_center, coarse_square = total_end(2, 512, 8 * wide_count * narrow_count)
    coarse_inverse = lax.rsqrt(coarse_square - coarse_center * coarse_center + epsilon)
    s_coarse = gain_coarse[...]

    def coarse_scaled(value):
        return (value - coarse_center) * coarse_inverse

    scaled = coarse_scaled(coarse_value)
    normed_grad = coarse_act_grad * slope(scaled, s_coarse)
    total_begin(3, column_sums(normed_grad), column_sums(normed_grad * scaled))
    coarse_u[...] = cgrad + coarse_inverse * normed_grad
    send_coarse(coarse_u, coarse_u_halo, 9)
    grad_sums = lax.fori_loop(2, 4, convolve_grad, grad_sums)

    total_middle(3)

    mid_mix = jnp.concatenate(
        [mid_scaled(mid_value).astype(BF16), jnp.ones((128, 128), BF16)], axis=1
    )
    matrix_sum[...] = jnp.zeros((4, 256, 512), F32)

    @pl.loop(0, 9)
    def _(t):
        through = 0.0625 * dot(kernel_fine[8 - t], down_mid[...])
        for n in range(2):
            mixed = dot_first(window_sums[n, t].reshape(128, 256), mid_mix)
            plain = jnp.concatenate([mixed[:, 512:640]] * 4, axis=1)
            matrix_sum[2 * n] += through * plain
            matrix_sum[2 * n + 1] += through * mixed[:, 0:512]

    def iota(shape, axis):
        return lax.broadcasted_iota(jnp.int32, shape, axis)

    def one_hot(condition):
        return jnp.where(condition, 1.0, 0.0).astype(BF16)

    by_group = one_hot((iota((32, 256), 1) >> 3) == iota((32, 256), 0))
    matrix = jnp.zeros((32, 128), F32)
    for n in range(4):
        high, low = halves(matrix_sum[n] * mid_inverse)
        high, low = halves(dot(by_group, high) + dot(by_group, low))
        to_lane = one_hot(iota((512, 128), 1) == 32 * n + (iota((512, 128), 0) >> 4))
        matrix += dot(high, to_lane) + dot(low, to_lane)
    first_matrix[wide] = matrix
    total_send_wide(5)

    first_mean, second_mean = total_end(3, 512, 8 * wide_count * narrow_count)
    arrived(coarse_halo, 8)
    arrived(coarse_u_halo, 9)
    offset = coarse_inverse * first_mean
    factor = coarse_inverse * second_mean
    pieces = [coarse_u[...] - offset - scaled * factor]
    for d in range(8):
        piece = coarse_scaled(coarse_halo[d].astype(F32)[0:8])
        pieces.append(coarse_u_halo[d] - offset - piece * factor)
    pieces.append(jnp.zeros((56, 512), F32))
    coarse_in_grad = jnp.concatenate(pieces, axis=0).astype(BF16)

    mid_pool_grad = dot_t(dot(SPREAD[...], coarse_in_grad).astype(BF16), down_coarse[...])
    row = lax.broadcasted_iota(jnp.int32, (256, 128), 0)
    keep = jnp.where(row < ABOVE, 1.0, 0.0)
    bounds = ((ABOVE, 16, 1), (BELOW, 16, 2), (LEFT, 32, 3), (RIGHT, 32, 4)) + tuple(
        (CORNER + 4 * c, 4, 5 + c) for c in range(4)
    )
    for start, size, d in bounds:
        inside = jnp.logical_and(row >= start, row < start + size)
        keep = jnp.where(inside, jnp.where(exists[d], 1.0, 0.0).astype(F32), keep)
    mid_grad = (summed_grad[...] + 0.0625 * mid_pool_grad) * jnp.concatenate([keep] * 4, axis=1)
    mid_act_grad = mid_convolve(mid_grad, lambda t, part_: dot_t(part_, kernel_mid[8 - t]))
    scaled = mid_scaled(mid_value)
    normed_grad = mid_act_grad * slope(scaled, s_mid)
    mid_u = mid_grad[0:128].astype(BF16).astype(F32) + mid_inverse * normed_grad
    u_pack[...] = dot(PACK[...], mid_u.astype(BF16)).astype(BF16)
    send_mid(u_pack, u_halo, u_cor, 10)
    pulled = (0.0625 * dot_t(mid_u.astype(BF16), down_mid[...])).astype(BF16)
    fine_sums = [jnp.sum(value, axis=0, keepdims=True) for value in grad_sums]
    for t in range(9):
        term = dot_t(pulled, kernel_fine[8 - t])
        for n in range(2):
            fine_sums[n] += column_sums(window_sums[n, t].reshape(128, 256).astype(F32) * term)
    first_joint[wide, 8:16, :] = jnp.zeros((8, 128), F32)
    total_fill(4, 0, (column_sums(normed_grad), column_sums(normed_grad * scaled)))
    total_fill(4, 8, fine_sums)
    total_send_wide(4)
    total_middle(5)

    set_edges(
        fine_act(row_in[0, 0].astype(F32)),
        fine_act(row_in[1, 0].astype(F32)),
        fine_act(col_in[0, 0].astype(F32)),
        fine_act(col_in[1, 0].astype(F32)),
        corners(lambda c: cor_in[0, c], fine_act, True),
    )

    @pl.loop(0, 2)
    def _(f):
        fine_forward(f)

    coarse_block = (
        coarse_in.astype(F32)
        + coarse_convolve(
            coarse_extended(
                coarse_value,
                lambda d: coarse_halo[d].astype(F32)[0:8],
                silu(coarse_center, coarse_inverse, s_coarse),
                True,
            ),
            lambda t, part_: dot(part_, kernel_coarse[t]),
        )
    ).astype(BF16)
    coarse_up = dot(coarse_block, up_coarse[...]).astype(BF16)
    mid_sum = (mid_block.astype(F32) + dot(SPREAD[0:128, 0:16], coarse_up)).astype(BF16)
    mid_up = dot(mid_sum, up_mid[...]).astype(BF16)
    total_middle(4)

    @pl.loop(2, 4)
    def _(f):
        fine_forward(f)

    mid_up = dot(ENLARGE[:, 0:128], mid_up).reshape(4, 8, 1, 16, 256)
    for f in range(4):
        block = fine_block[f].astype(F32).reshape(8, 4, 16, 256)
        fine_block[f] = (block + mid_up[f]).astype(BF16).reshape(512, 256)
    out_copy = pltpu.make_async_copy(fine_block, out_ref, out_sem.at[0])
    out_copy.start()
    matrix = total_sum(5)

    joint = total_sum(4)
    t = group_lanes(joint[0:8], 16) * (1.0 / (16 * 128 * wide_count * narrow_count))
    first_mean, second_mean = row_of(t, 0, 512), row_of(t, 4, 512)
    arrived(u_halo, 10)
    arrived(u_cor, 11)
    offset = mid_inverse * first_mean
    factor = mid_inverse * second_mean
    mid_in_grad = mid_extended(
        mid_u, u_halo[...], lambda c: u_cor[c], lambda v: v - offset, False
    ) - factor * mid_extended(
        mid_value, mid_halo[...], lambda c: mid_cor[c], mid_scaled, False
    )

    pool_grad = 0.0625 * dot_t(mid_in_grad.astype(BF16), down_mid[...])
    pool_grad = pool_grad * jnp.concatenate([keep] * 2, axis=1)
    high, low = halves(pool_grad)
    added = dot(ENLARGE[...], jnp.concatenate([high[0:256], low[0:256]], axis=0))
    loads["stretch"].wait()
    for a in range(3):
        fields = [dot_t(high, kernel_fine[8 - 3 * a - b]).astype(BF16) for b in range(3)]
        stretched[a] = dot(stretch[...], jnp.concatenate(fields, axis=0)).reshape(4, 10, 16, 256)

    means = jnp.zeros((8, 128), F32)
    for n, mean in enumerate((first_mean, second_mean)):
        lane, row = iota((512, 128), 1), iota((512, 128), 0)
        inside = jnp.logical_and((lane & 31) == (row >> 4), ((lane >> 5) & 1) == n)
        to_lane = jnp.where(inside, 0.0625, 0.0).astype(BF16)
        high, low = halves(jnp.broadcast_to(mean, (8, 512)))
        means += dot(high, to_lane) + dot(low, to_lane)
    matrix_high, matrix_low = halves(matrix)
    spread_groups = one_hot((iota((256, 32), 0) >> 3) == iota((256, 32), 1))
    t = group_lanes(joint[8:16], 8)
    fine_means = []
    for n in range(2):
        half = jnp.where((iota((8, 128), 1) >> 6) == n, means, 0.0)
        high, low = halves(half)
        change = dot_t(high, matrix_high) + dot_t(low, matrix_high) + dot_t(high, matrix_low)
        high, low = halves(change)
        change = dot_t(high, spread_groups) + dot_t(low, spread_groups)
        fine_means.append(
            (row_of(t, 4 * n, 256) - change[0:1]) * (1.0 / (8 * 2048 * wide_count * narrow_count))
        )
    slant = -fine_inverse * fine_inverse * fine_means[1]
    shift = -fine_inverse * fine_means[0] - fine_center * slant

    added = added.reshape(4, 8, 1, 16, 256)
    grad_copies = []
    for f in range(4):
        above, here, below = stretched[0, f], stretched[1, f], stretched[2, f]
        centre = here[1:9] + above[1:9] + below[1:9]
        top = here[1:9] + above[0:8] + below[1:9]
        bottom = here[1:9] + above[1:9] + below[2:10]
        back = jnp.stack([top, centre, centre, bottom], axis=1).reshape(512, 256)
        normed_grad = (conv_grad[f] + back) * fine_slope[f]
        grad = xg[1, f].astype(F32).reshape(8, 4, 16, 256) + added[f]
        grad = grad.reshape(512, 256).astype(BF16).astype(F32)
        grad_buf[f] = grad + fine_inverse * normed_grad + (shift + fine_value(f) * slant)
        grad_copies.append(
            pltpu.make_async_copy(grad_buf.at[f], grad_ref.at[f], out_sem.at[1 + f])
        )
        grad_copies[f].start()

    for which in range(2):
        sent(row_in.at[:, which], 13 * which)
        sent(col_in.at[:, which], 13 * which + 1)
        sent(cor_in.at[which], 13 * which + 2)
    sent(sum_in, 3)
    sent(sum_cor, 4)
    sent(cgrad_in, 5)
    sent(mid_halo, 6)
    sent(mid_cor, 7)
    sent(coarse_halo, 8)
    sent(coarse_u_halo, 9)
    sent(u_halo, 10)
    sent(u_cor, 11)
    for phase in range(6):
        whole = firsts[phase].at[pl.ds(0, wide_count - 1)]
        pltpu.make_async_copy(whole, whole, total_send.at[2 * phase]).wait()
        whole = seconds[phase].at[pl.ds(0, narrow_count - 1)]
        pltpu.make_async_copy(whole, whole, total_send.at[2 * phase + 1]).wait()
    out_copy.wait()
    for copy in grad_copies:
        copy.wait()


def shards(*arguments):
    (
        fine_input,
        gain_fine,
        kernel_fine,
        down_mid,
        gain_mid,
        kernel_mid,
        down_coarse,
        gain_coarse,
        kernel_coarse,
        up_coarse,
        up_mid,
        grad_out,
    ) = arguments
    wide_count, narrow_count = lax.axis_size("wide"), lax.axis_size("narrow")
    anywhere = pl.BlockSpec(memory_space=pl.ANY)
    vmem = pltpu.VMEM
    scratch = [
        vmem((2, 4, 32, 16, 256), BF16),
        vmem((9, 256, 256), BF16),
        vmem((256, 512), BF16),
        vmem((9, 512, 512), BF16),
        vmem((512, 512), BF16),
        vmem((9, 512, 512), BF16),
        vmem((512, 512), BF16),
        vmem((512, 256), BF16),
        vmem((1, 256), F32),
        vmem((1, 512), F32),
        vmem((1, 512), F32),
        vmem((608, 512), BF16),
        vmem((1168, 256), BF16),
        vmem((1168, 128), BF16),
        vmem((288, 640), BF16),
        vmem((640, 768), BF16),
        vmem((9, 128, 512), BF16),
        vmem((9, 16, 512), BF16),
        vmem((4, 544, 768), BF16),
        vmem((4, 512, 256), BF16),
        vmem((4, 512, 256), F32),
        vmem((4, 512, 256), F32),
        vmem((128, 256), F32),
        vmem((128, 256), BF16),
        vmem((4, 512, 256), F32),
        vmem((2, 4, 16, 256), F32),
        vmem((4, 64, 256), BF16),
        vmem((16, 256), F32),
        vmem((256, 512), F32),
        vmem((4, wide_count, 8, 128), F32),
        vmem((4, narrow_count, 8, 128), F32),
        vmem((wide_count, 16, 128), F32),
        vmem((narrow_count, 16, 128), F32),
        vmem((wide_count, 32, 128), F32),
        vmem((narrow_count, 32, 128), F32),
        vmem((2, 9, 4, 32, 256), BF16),
        vmem((2, 2, 4, 16, 256), BF16),
        vmem((2, 2, 4, 32, 256), BF16),
        vmem((2, 4, 32, 256), BF16),
        vmem((4, 256, 512), F32),
        vmem((3, 4, 10, 16, 256), F32),
        vmem((2, 2, 128, 256), BF16),
        vmem((2, 16, 256), BF16),
        vmem((2, 2, 4, 16, 256), BF16),
        vmem((2, 2, 128, 256), BF16),
        vmem((2, 4, 16, 256), BF16),
        vmem((112, 256), BF16),
        vmem((96, 256), BF16),
        vmem((4, 16, 256), BF16),
        vmem((16, 512), BF16),
        vmem((8, 16, 512), BF16),
        vmem((112, 512), BF16),
        vmem((96, 512), BF16),
        vmem((4, 16, 512), BF16),
        vmem((16, 512), BF16),
        vmem((8, 16, 512), BF16),
        vmem((8, 512), F32),
        vmem((8, 8, 512), F32),
        vmem((112, 512), BF16),
        vmem((96, 512), BF16),
        vmem((4, 16, 512), BF16),
        pltpu.SemaphoreType.DMA((17,)),
        pltpu.SemaphoreType.DMA((5,)),
        pltpu.SemaphoreType.DMA((12,)),
        pltpu.SemaphoreType.DMA((12,)),
        pltpu.SemaphoreType.DMA((16,)),
        pltpu.SemaphoreType.DMA((16,)),
    ]
    output, grad = pl.pallas_call(
        functools.partial(kernel, wide_count, narrow_count),
        out_shape=(
            jax.ShapeDtypeStruct((4, 512, 256), BF16),
            jax.ShapeDtypeStruct((4, 512, 256), F32),
        ),
        in_specs=[anywhere] * 17,
        out_specs=(anywhere, anywhere),
        scratch_shapes=scratch,
        compiler_params=pltpu.CompilerParams(
            collective_id=0, has_side_effects=True, vmem_limit_bytes=56 * 2**20
        ),
        name="whole_net",
    )(
        fine_input,
        gain_fine.reshape(1, 256),
        kernel_fine.reshape(9, 256, 256),
        down_mid,
        gain_mid.reshape(1, 512),
        kernel_mid.reshape(9, 512, 512),
        down_coarse,
        gain_coarse.reshape(1, 512),
        kernel_coarse.reshape(9, 512, 512),
        up_coarse,
        up_mid,
        grad_out,
        *tables(),
    )
    return output.reshape(4, 32, 16, 256), grad.reshape(4, 32, 16, 256)


def solution(mesh):
    tile = P(None, "wide", "narrow", None)
    return jax.shard_map(
        shards,
        mesh=mesh,
        in_specs=(tile,) + (P(),) * 10 + (tile,),
        out_specs=(tile, tile),
        check_vma=False,
    )
```

```python
import functools

import jax
import jax.numpy as jnp
import numpy as np
from jax import lax
from jax.experimental import pallas as pl
from jax.experimental.pallas import tpu as pltpu
from jax.sharding import PartitionSpec as P

MESH = pl.DeviceIdType.MESH
GROUPS = 32
epsilon = 1e-05
F32 = jnp.float32
BF16 = jnp.bfloat16

DIRS = ((0, 0), (-1, 0), (1, 0), (0, -1), (0, 1), (-1, -1), (-1, 1), (1, -1), (1, 1))

ABOVE, BELOW, LEFT, RIGHT, CORNER = 128, 144, 160, 192, 224


def mid_row(f, i, j):
    if 0 <= i < 8 and 0 <= j < 4:
        return 32 * f + 4 * i + j
    if i < 0 and 0 <= j < 4:
        return ABOVE + 4 * f + j
    if i > 7 and 0 <= j < 4:
        return BELOW + 4 * f + j
    if 0 <= i < 8:
        return (LEFT if j < 0 else RIGHT) + 8 * f + i
    return CORNER + 4 * (2 * (i > 7) + (j > 3)) + f


def coarse_row(f, i, side):
    down = -1 if i < 0 else (1 if i > 1 else 0)
    return 8 * DIRS.index((down, side)) + 2 * f + i % 2


def tables():
    pick = np.zeros((96, 512), np.float32)
    for i in range(32):
        for j in range(16):
            pick[4 * (i // 4) + j // 4, 16 * i + j] = 1
        pick[32 + i, 16 * i + 15] = 1
        pick[64 + i, 16 * i] = 1
    enlarge = np.zeros((512, 256), np.float32)
    taps = np.zeros((1152, 256), np.float32)
    ends = np.zeros((16, 256), np.float32)
    pack = np.zeros((112, 128), np.float32)
    pool = np.zeros((16, 128), np.float32)
    coarse_taps = np.zeros((144, 128), np.float32)
    spread = np.zeros((256, 128), np.float32)
    for f in range(4):
        for i in range(8):
            for j in range(16):
                enlarge[128 * f + 16 * i + j, mid_row(f, i, j // 4)] = 1
        for c in range(4):
            low, first = c < 2, c % 2 == 1
            ends[4 * c + f, 128 * first + 32 * f + 31 * low] = 1
            pack[96 + 4 * c + f, mid_row(f, 7 * low, 3 * (not first))] = 1
        for i in range(8):
            for j in range(4):
                here = 32 * f + 4 * i + j
                pool[2 * f + i // 4, here] = 1
                for t in range(9):
                    taps[128 * t + here, mid_row(f, i + t // 3 - 1, j + t % 3 - 1)] = 1
            pack[32 + 8 * f + i, mid_row(f, i, 3)] = 1
            pack[64 + 8 * f + i, mid_row(f, i, 0)] = 1
        for j in range(4):
            pack[4 * f + j, mid_row(f, 7, j)] = 1
            pack[16 + 4 * f + j, mid_row(f, 0, j)] = 1
        for i in range(2):
            for t in range(9):
                coarse_taps[16 * t + 2 * f + i, coarse_row(f, i + t // 3 - 1, t % 3 - 1)] = 1
        for i in range(-1, 9):
            for j in range(-1, 5):
                side = -1 if j < 0 else (1 if j > 3 else 0)
                spread[mid_row(f, i, j), coarse_row(f, i // 4 if i < 8 else 2, side)] = 1
    windows = np.zeros((288, 640), np.float32)
    for t in range(9):
        for i in range(32):
            for j in range(16):
                p, q = i + 1 - t // 3, j + 1 - t % 3
                row = 32 * t + 4 * (i // 4) + j // 4
                if 0 <= p < 32 and 0 <= q < 16:
                    at = 16 * p + q
                elif 0 <= q < 16:
                    at = (512 if p < 0 else 528) + q
                elif 0 <= p < 32:
                    at = (544 if q < 0 else 576) + p
                else:
                    at = 608 + 2 * (p > 31) + (q > 15)
                windows[row, at] = 1
    stretch = np.zeros((640, 768), np.float32)
    for f in range(4):
        for i in range(10):
            for j in range(16):
                for b in range(3):
                    at = 256 * b + mid_row(f, i - 1, (j + b - 1) // 4)
                    stretch[160 * f + 16 * i + j, at] = 1
    by_frame = np.zeros((128, 128), np.float32)
    for f in range(4):
        for c in range(4):
            by_frame[32 * f + c, 4 * c + f] = 1
    sides = np.zeros((512, 128), np.float32)
    for i in range(32):
        sides[16 * i, i] = 1
        sides[16 * i + 15, 64 + i] = 1
    wide_table = np.concatenate([pick, np.concatenate([enlarge, enlarge], axis=1)])
    middle_table = np.concatenate([taps, ends])
    narrow_table = np.concatenate([pack, pool, coarse_taps, spread, sides, by_frame])
    result = (wide_table, middle_table, narrow_table, windows, stretch)
    return [jnp.asarray(t, BF16) for t in result]


def dot(a, b):
    return jnp.dot(a, b, preferred_element_type=F32)


def dot_t(a, b):
    return lax.dot_general(a, b, (((1,), (1,)), ((), ())), preferred_element_type=F32)


def dot_first(a, b):
    return lax.dot_general(a, b, (((0,), (0,)), ((), ())), preferred_element_type=F32)


def group_lanes(t, size):
    lane = lax.broadcasted_iota(jnp.int32, t.shape, 1)
    step = 1
    while step < size:
        t = t + jnp.where(
            (lane & step) != 0, pltpu.roll(t, step, 1), pltpu.roll(t, 128 - step, 1)
        )
        step *= 2
    return t


def halves(t):
    high = t.astype(BF16)
    return high, (t - high.astype(F32)).astype(BF16)


def kernel(
    wide_count,
    narrow_count,
    x_in,
    gain_fine_in,
    kernel_fine_in,
    down_mid_in,
    gain_mid_in,
    kernel_mid_in,
    down_coarse_in,
    gain_coarse_in,
    kernel_coarse_in,
    up_coarse_in,
    up_mid_in,
    grad_in,
    wide_table_in,
    middle_table_in,
    narrow_table_in,
    windows_in,
    stretch_in,
    out_ref,
    grad_ref,
    xg,
    kernel_fine,
    down_mid,
    kernel_mid,
    down_coarse,
    kernel_coarse,
    up_coarse,
    up_mid,
    gain_fine,
    gain_mid,
    gain_coarse,
    wide_table,
    middle_table,
    narrow_table,
    windows,
    stretch,
    columns,
    fine_block,
    grad_buf,
    conv_grad,
    pooled_x,
    summed,
    fine_slope,
    edge_rows,
    edge_sides,
    edge_ends,
    summed_grad,
    first,
    second,
    rows,
    first_matrix,
    second_matrix,
    window_sums,
    rim_rows,
    rim_sides,
    rim_ends,
    matrix_sum,
    through,
    stretched,
    col_pack,
    cor_pack,
    row_in,
    col_in,
    cor_in,
    sum_pack,
    sum_in,
    sum_cor,
    cgrad_own,
    cgrad_in,
    mid_pack,
    mid_halo,
    mid_cor,
    coarse_own,
    coarse_halo,
    coarse_u,
    coarse_u_halo,
    u_pack,
    u_halo,
    u_cor,
    load_sem,
    out_sem,
    total_send,
    total_recv,
    halo_send,
    halo_recv,
):
    wide, narrow = lax.axis_index("wide"), lax.axis_index("narrow")

    def around(index, step, count):
        moved = index + step
        if isinstance(step, int) and step < 0:
            return jnp.where(moved < 0, moved + count, moved)
        return jnp.where(moved >= count, moved - count, moved)

    def device(down, side):
        return (
            wide if isinstance(down, int) and down == 0 else around(wide, down, wide_count),
            narrow if isinstance(side, int) and side == 0 else around(narrow, side, narrow_count),
        )

    loads = {}
    pairs = (
        ("x", x_in, xg.at[0]),
        ("grad", grad_in, xg.at[1]),
        ("wide_table", wide_table_in, wide_table),
        ("middle_table", middle_table_in, middle_table),
        ("narrow_table", narrow_table_in, narrow_table),
        ("gain_fine", gain_fine_in, gain_fine),
        ("windows", windows_in, windows),
        ("kernel_fine", kernel_fine_in, kernel_fine),
        ("up_mid", up_mid_in, up_mid),
        ("up_coarse", up_coarse_in, up_coarse),
        ("down_mid", down_mid_in, down_mid),
        ("gain_mid", gain_mid_in, gain_mid),
        ("kernel_coarse", kernel_coarse_in, kernel_coarse),
        ("kernel_mid", kernel_mid_in, kernel_mid),
        ("down_coarse", down_coarse_in, down_coarse),
        ("gain_coarse", gain_coarse_in, gain_coarse),
        ("stretch", stretch_in, stretch),
    )
    for number, (name, source, target) in enumerate(pairs):
        loads[name] = pltpu.make_async_copy(source, target, load_sem.at[number])
    loads["x"].start()

    barrier = pltpu.get_barrier_semaphore()
    greeted = 0
    for down in range(wide_count):
        for side in range(-2, narrow_count - 2):
            near = (down <= 1 or down == wide_count - 1) and abs(side) <= 1
            if (down, side) != (0, 0) and (down == 0 or side == 0 or near):
                pl.semaphore_signal(
                    barrier, inc=1, device_id=device(down, side), device_id_type=MESH
                )
                greeted += 1

    def send(source, target, which, down, side):
        pltpu.make_async_remote_copy(
            src_ref=source,
            dst_ref=target,
            send_sem=halo_send.at[which],
            recv_sem=halo_recv.at[which],
            device_id=device(down, side),
            device_id_type=MESH,
        ).start()

    def arrived(buffer, which):
        pltpu.make_async_copy(buffer, buffer, halo_recv.at[which]).wait()

    def sent(buffer, which):
        pltpu.make_async_copy(buffer, buffer, halo_send.at[which]).wait()

    firsts = tuple(first.at[p] for p in range(6)) + (first_matrix,)
    seconds = tuple(second.at[p] for p in range(6)) + (second_matrix,)

    def total_send_wide(phase):
        mine = firsts[phase].at[wide]

        @pl.loop(1, wide_count)
        def _(step):
            pltpu.make_async_remote_copy(
                src_ref=mine,
                dst_ref=mine,
                send_sem=total_send.at[2 * phase],
                recv_sem=total_recv.at[2 * phase],
                device_id=device(step, 0),
                device_id_type=MESH,
            ).start()

    def diagonal(shape=(8, 128)):
        lane = lax.broadcasted_iota(jnp.int32, shape, 1) & 7
        return lane == lax.broadcasted_iota(jnp.int32, shape, 0)

    def total_begin(phase, one, two):
        channels = one.shape[1]
        if channels < 512:
            rows[...] = jnp.zeros((8, 128), F32)
        for n, value in enumerate((one, two)):
            for k in range(channels // 128):
                rows[4 * n + k : 4 * n + k + 1, :] = value[:, 128 * k : 128 * k + 128]
        grouped = group_lanes(rows[...], channels // GROUPS)
        grouped = jnp.where(diagonal(), grouped, 0.0)
        firsts[phase][wide] = jnp.sum(grouped, axis=0, keepdims=True)
        total_send_wide(phase)

    def total_middle(phase):
        whole = firsts[phase].at[pl.ds(0, wide_count - 1)]
        pltpu.make_async_copy(whole, whole, total_recv.at[2 * phase]).wait()
        summed_up = jnp.sum(firsts[phase][...].astype(F32), axis=0)
        seconds[phase][narrow] = summed_up.astype(seconds[phase].dtype)
        mine = seconds[phase].at[narrow]

        @pl.loop(1, narrow_count)
        def _(step):
            pltpu.make_async_remote_copy(
                src_ref=mine,
                dst_ref=mine,
                send_sem=total_send.at[2 * phase + 1],
                recv_sem=total_recv.at[2 * phase + 1],
                device_id=device(0, step),
                device_id_type=MESH,
            ).start()

    def total_sum(phase):
        whole = seconds[phase].at[pl.ds(0, narrow_count - 1)]
        pltpu.make_async_copy(whole, whole, total_recv.at[2 * phase + 1]).wait()
        return jnp.sum(seconds[phase][...].astype(F32), axis=0)

    def row_of(t, start, channels):
        return jnp.concatenate([t[start + k : start + k + 1] for k in range(channels // 128)], axis=1)

    def total_groups(phase, channels, scale):
        packed = jnp.broadcast_to(total_sum(phase), (8, 128))
        t = group_lanes(jnp.where(diagonal(), packed, 0.0), 8) * scale
        return row_of(t, 0, channels), row_of(t, 4, channels)

    def total_end(phase, channels, cells):
        return total_groups(phase, channels, 1.0 / (channels // GROUPS * cells))

    has_above, has_below = wide > 0, wide < wide_count - 1
    has_left, has_right = narrow > 0, narrow < narrow_count - 1
    has_corner = (
        jnp.logical_and(has_above, has_left),
        jnp.logical_and(has_above, has_right),
        jnp.logical_and(has_below, has_left),
        jnp.logical_and(has_below, has_right),
    )
    exists = (None, has_above, has_below, has_left, has_right) + has_corner

    def only(condition, value):
        return value * jnp.where(condition, 1.0, 0.0).astype(F32)

    def corners(read, change, masked):
        result = None
        for c in range(4):
            value = change(read(c).astype(F32))
            if masked:
                value = only(has_corner[c], value)
            cell = lax.broadcasted_iota(jnp.int32, value.shape, 0)
            result = value if result is None else jnp.where(cell >= 4 * c, value, result)
        return result

    def mid_extended(own, read_halo, read_cor, change, masked):
        pieces = [change(own)]
        halo = change(read_halo.astype(F32))
        for low, high, d in ((0, 16, 1), (16, 32, 2), (32, 64, 3), (64, 96, 4)):
            piece = halo[low:high]
            pieces.append(only(exists[d], piece) if masked else piece)
        pieces.append(corners(read_cor, change, masked))
        pieces.append(jnp.zeros((16, own.shape[1]), F32))
        return jnp.concatenate(pieces, axis=0)

    def send_mid(pack, halo, cor, which):
        send(pack.at[pl.ds(0, 16)], halo.at[pl.ds(0, 16)], which, 1, 0)
        send(pack.at[pl.ds(16, 16)], halo.at[pl.ds(16, 16)], which, -1, 0)
        send(pack.at[pl.ds(32, 32)], halo.at[pl.ds(32, 32)], which, 0, 1)
        send(pack.at[pl.ds(64, 32)], halo.at[pl.ds(64, 32)], which, 0, -1)
        for c in range(4):
            down, side = DIRS[5 + c]
            send(pack.at[pl.ds(96, 16)], cor.at[c], which + 1, -down, -side)

    def send_coarse(own, halo, which):
        for d in range(1, 9):
            down, side = DIRS[d]
            send(own, halo.at[d - 1], which, -down, -side)

    def coarse_extended(own, halo, change, masked):
        pieces = [change(own)]
        for d in range(1, 9):
            piece = change(halo(d - 1))
            pieces.append(only(exists[d], piece) if masked else piece)
        pieces.append(jnp.zeros((56, own.shape[1]), F32))
        return jnp.concatenate(pieces, axis=0)

    PICK = wide_table.at[pl.ds(0, 96)]
    ENLARGE = wide_table.at[pl.ds(96, 512)]
    TAPS = middle_table.at[pl.ds(0, 1152)]
    ENDS = middle_table.at[pl.ds(1152, 16)]
    PACK = narrow_table.at[pl.ds(0, 112)]
    POOL = narrow_table.at[pl.ds(112, 16)]
    COARSE_TAPS = narrow_table.at[pl.ds(128, 144)]
    SPREAD = narrow_table.at[pl.ds(272, 256)]
    SIDES = narrow_table.at[pl.ds(528, 512)]
    BY_FRAME = narrow_table.at[pl.ds(1040, 128)]

    def frame(which, f):
        return xg[which, f].reshape(512, 256)

    loads["x"].wait()
    for name in loads:
        if name != "x":
            loads[name].start()

    def add_frame(f, carry):
        value = frame(0, f).astype(F32)
        return (
            carry[0] + jnp.sum(value.reshape(64, 8, 256), axis=0),
            carry[1] + jnp.sum((value * value).reshape(64, 8, 256), axis=0),
        )

    blank = jnp.zeros((8, 256), F32)
    one, two = lax.fori_loop(0, 4, add_frame, (blank, blank))
    pl.semaphore_wait(barrier, greeted)
    total_begin(0, jnp.sum(one, axis=0, keepdims=True), jnp.sum(two, axis=0, keepdims=True))

    def rim(which):
        sem = 13 * which
        send(xg.at[which, :, 31], row_in.at[0, which], sem, 1, 0)
        send(xg.at[which, :, 0], row_in.at[1, which], sem, -1, 0)
        for f in range(4):
            picked = dot(PICK[...], frame(which, f))
            if which == 0:
                pooled_x[32 * f : 32 * f + 32] = picked[0:32]
            picked = picked.astype(BF16)
            col_pack[0, which, 32 * f : 32 * f + 32] = picked[32:64]
            col_pack[1, which, 32 * f : 32 * f + 32] = picked[64:96]
            if which == 1:
                summed[32 * f : 32 * f + 32] = picked[0:32]
        send(col_pack.at[0, which], col_in.at[0, which], sem + 1, 0, 1)
        send(col_pack.at[1, which], col_in.at[1, which], sem + 1, 0, -1)
        ends = jnp.concatenate([col_pack[0, which], col_pack[1, which]], axis=0)
        cor_pack[which] = dot(ENDS[...], ends).astype(BF16)
        for c in range(4):
            down, side = DIRS[5 + c]
            send(cor_pack.at[which], cor_in.at[which, c], sem + 2, -down, -side)

    loads["wide_table"].wait()
    loads["middle_table"].wait()
    rim(0)
    total_middle(0)
    loads["grad"].wait()
    rim(1)
    loads["narrow_table"].wait()

    up_mid_grad = summed[...]
    sum_pack[...] = dot(PACK[...], up_mid_grad).astype(BF16)
    send_mid(sum_pack, sum_in, sum_cor, 3)
    loads["up_mid"].wait()
    high, low = halves(dot_t(up_mid_grad, up_mid[...]))
    up_coarse_grad = (dot(POOL[...], high) + dot(POOL[...], low)).astype(BF16)
    loads["up_coarse"].wait()
    cgrad_own[...] = dot_t(up_coarse_grad, up_coarse[...]).astype(BF16)
    send_coarse(cgrad_own, cgrad_in, 5)

    loads["gain_fine"].wait()
    loads["kernel_fine"].wait()
    loads["down_mid"].wait()

    @pl.loop(0, 9)
    def _(t):
        through[t] = (0.0625 * dot(kernel_fine[8 - t], down_mid[...])).astype(BF16)

    fine_center, fine_square = total_end(0, 256, 2048 * wide_count * narrow_count)
    fine_inverse = lax.rsqrt(fine_square - fine_center * fine_center + epsilon)
    s_fine = gain_fine[...]

    def silu(center, inverse, scaling):
        gain = 0.5 * inverse * scaling
        shift = -center * gain

        def change(value):
            half = value * gain + shift
            return half * jnp.tanh(half) + half

        return change

    def slope(scaled, scaling):
        half = scaled * (0.5 * scaling)
        bend = jnp.tanh(half)
        return (0.5 * scaling) * (1.0 + bend) * (1.0 + half * (1.0 - bend))

    fine_act = silu(fine_center, fine_inverse, s_fine)

    arrived(row_in.at[:, 0], 0)
    arrived(col_in.at[:, 0], 1)
    arrived(cor_in.at[0], 2)

    def set_edges(kind, above, below, left, right, ends):
        edge_rows[kind, 0] = only(has_above, above)
        edge_rows[kind, 1] = only(has_below, below)
        left = only(has_left, left).astype(BF16)
        right = only(has_right, right).astype(BF16)
        for f in range(4):
            edge_sides[kind, f, 0:32] = left[32 * f : 32 * f + 32]
            edge_sides[kind, f, 32:64] = right[32 * f : 32 * f + 32]
        edge_ends[kind] = ends

    def place(kind, f, own):
        column = lax.broadcasted_iota(jnp.int32, (512, 256), 0) & 15
        sides = edge_sides[kind, f]
        low = jnp.where(
            column == 0, dot(SIDES[:, 0:64], sides), pltpu.roll(own, 1, 0)
        )
        columns[f, 16:528, 0:256] = low.astype(BF16)
        columns[f, 16:528, 256:512] = own.astype(BF16)
        high = jnp.where(
            column == 15, dot(SIDES[:, 32:96], sides), pltpu.roll(own, 511, 0)
        )
        columns[f, 16:528, 512:768] = high.astype(BF16)
        cell = lax.broadcasted_iota(jnp.int32, (16, 256), 0)
        for k in range(2):
            row = edge_rows[kind, k, f]
            at = slice(528 * k, 528 * k + 16)
            west = edge_ends[kind, pl.ds(8 * k + f, 1), :]
            east = edge_ends[kind, pl.ds(8 * k + 4 + f, 1), :]
            columns[f, at, 0:256] = jnp.where(cell == 0, west, pltpu.roll(row, 1, 0)).astype(BF16)
            columns[f, at, 256:512] = row.astype(BF16)
            columns[f, at, 512:768] = jnp.where(cell == 15, east, pltpu.roll(row, 15, 0)).astype(BF16)

    def side_by_side(pieces):
        return jnp.concatenate(list(pieces), axis=1)

    def fine_taps(f):
        return side_by_side(columns[f, 16 * a : 16 * a + 512, :] for a in range(3))

    def fine_convolve(f):
        return dot(fine_taps(f), kernel_fine[...].reshape(2304, 256))

    def fine_convolve_back(f):
        return dot_t(fine_taps(f), side_by_side(kernel_fine[8 - t] for t in range(9)))

    def fine_scaled(value):
        return (value - fine_center) * fine_inverse

    def fine_value(f):
        return frame(0, f).astype(F32)

    def set_fields(n, change):
        for k in range(2):
            rim_rows[n, k] = only(exists[1 + k], change(row_in[k, 0].astype(F32))).astype(BF16)
            sides = only(exists[3 + k], change(col_in[k, 0].astype(F32))).astype(BF16)
            rim_sides[n, k] = sides.reshape(4, 32, 256)
        ends = corners(lambda c: cor_in[0, c], change, True)
        ends = dot(BY_FRAME[:, 0:16], ends.astype(BF16)).astype(BF16)
        rim_ends[n] = ends.reshape(4, 32, 256)

    def window(n, f, own):
        field = jnp.concatenate(
            [
                own.astype(BF16),
                rim_rows[n, 0, f],
                rim_rows[n, 1, f],
                rim_sides[n, 0, f],
                rim_sides[n, 1, f],
                rim_ends[n, f],
            ],
            axis=0,
        )
        return dot(windows[...], field)

    set_fields(0, fine_act)
    loads["windows"].wait()

    @pl.loop(0, 4)
    def _(f):
        sums = window(0, f, fine_act(fine_value(f)))
        high, low = halves(sums)
        window_sums[0, :, f] = high.reshape(9, 32, 256)
        window_sums[1, :, f] = low.reshape(9, 32, 256)

    both = side_by_side(
        jnp.concatenate([window_sums[n, 8 - t].reshape(128, 256) for n in range(2)], axis=0)
        for t in range(9)
    )
    both = dot(both, kernel_fine[...].reshape(2304, 256))
    pooled = pooled_x[...] + both[0:128] + both[128:256]
    pooled = (pooled * 0.0625).astype(BF16)

    def fine_forward(f):
        value = fine_value(f)
        place(0, f, fine_act(value))
        fine_block[f] = (value + fine_convolve(f)).astype(BF16)

    def same(value):
        return value

    mid_in = dot(pooled, down_mid[...]).astype(BF16)
    mid_value = mid_in.astype(F32)

    def column_sums(value):
        return jnp.sum(value, axis=0, keepdims=True)

    total_begin(1, column_sums(mid_value), column_sums(mid_value * mid_value))
    mid_pack[...] = dot(PACK[...], mid_in).astype(BF16)
    send_mid(mid_pack, mid_halo, mid_cor, 6)

    @pl.loop(0, 4)
    def _(f):
        fine_slope[f] = slope(fine_scaled(fine_value(f)), s_fine)

    set_fields(0, lambda v: slope(fine_scaled(v), s_fine))
    set_fields(1, lambda v: slope(fine_scaled(v), s_fine) * fine_scaled(v))

    set_edges(
        0,
        fine_act(row_in[0, 0].astype(F32)),
        fine_act(row_in[1, 0].astype(F32)),
        fine_act(col_in[0, 0].astype(F32)),
        fine_act(col_in[1, 0].astype(F32)),
        corners(lambda c: cor_in[0, c], fine_act, True),
    )
    fine_forward(0)
    total_middle(1)
    fine_forward(1)

    @pl.loop(0, 4)
    def _(f):
        bent = fine_slope[f]
        window_sums[0, :, f] = window(0, f, bent).astype(BF16).reshape(9, 32, 256)
        bent = bent * fine_scaled(fine_value(f))
        window_sums[1, :, f] = window(1, f, bent).astype(BF16).reshape(9, 32, 256)

    loads["gain_mid"].wait()
    loads["kernel_mid"].wait()
    mid_center, mid_square = total_end(1, 512, 128 * wide_count * narrow_count)
    mid_inverse = lax.rsqrt(mid_square - mid_center * mid_center + epsilon)
    s_mid = gain_mid[...]

    mid_act = silu(mid_center, mid_inverse, s_mid)

    def mid_scaled(value):
        return (value - mid_center) * mid_inverse

    def mid_convolve(extended, product, weights):
        taps = dot(TAPS[...], extended.astype(BF16)).astype(BF16)
        return product(side_by_side(taps[128 * t : 128 * t + 128] for t in range(9)), weights)

    arrived(mid_halo, 6)
    arrived(mid_cor, 7)
    mid_block = (
        mid_value
        + mid_convolve(
            mid_extended(mid_value, mid_halo[...], lambda c: mid_cor[c], mid_act, True),
            dot,
            kernel_mid[...].reshape(4608, 512),
        )
    ).astype(BF16)

    loads["down_coarse"].wait()
    mid_pooled = (dot(POOL[...], mid_block) * 0.0625).astype(BF16)
    coarse_in = dot(mid_pooled, down_coarse[...]).astype(BF16)
    coarse_own[...] = coarse_in
    coarse_value = coarse_in.astype(F32)[0:8]
    total_begin(2, column_sums(coarse_value), column_sums(coarse_value * coarse_value))
    send_coarse(coarse_own, coarse_halo, 8)

    arrived(row_in.at[:, 1], 13)
    arrived(col_in.at[:, 1], 14)
    arrived(cor_in.at[1], 15)
    set_edges(
        1,
        row_in[0, 1].astype(F32),
        row_in[1, 1].astype(F32),
        col_in[0, 1].astype(F32),
        col_in[1, 1].astype(F32),
        corners(lambda c: cor_in[1, c], same, True),
    )

    def convolve_grad(f, carry):
        place(1, f, frame(1, f).astype(F32))
        result = fine_convolve_back(f)
        conv_grad[f] = result
        weighted = result * fine_slope[f]
        scaled = fine_scaled(fine_value(f))
        return (
            carry[0] + jnp.sum(weighted.reshape(64, 8, 256), axis=0),
            carry[1] + jnp.sum((weighted * scaled).reshape(64, 8, 256), axis=0),
        )

    grad_sums = lax.fori_loop(0, 2, convolve_grad, (blank, blank))
    total_middle(2)

    arrived(cgrad_in, 5)
    loads["kernel_coarse"].wait()

    def coarse_convolve(extended, product, weights):
        taps = dot(COARSE_TAPS[...], extended.astype(BF16)).astype(BF16)
        return product(side_by_side(taps[16 * t : 16 * t + 16] for t in range(9)), weights)

    cgrad = cgrad_own[...].astype(F32)[0:8]
    coarse_act_grad = coarse_convolve(
        coarse_extended(cgrad, lambda d: cgrad_in[d].astype(F32)[0:8], same, True),
        dot_t,
        side_by_side(kernel_coarse[8 - t] for t in range(9)),
    )[0:8]

    arrived(sum_in, 3)
    arrived(sum_cor, 4)
    sum_extended = mid_extended(
        up_mid_grad.astype(F32), sum_in[...], lambda c: sum_cor[c], same, True
    )
    summed_grad[...] = dot_t(sum_extended.astype(BF16), up_mid[...])

    loads["gain_coarse"].wait()
    coarse_center, coarse_square = total_end(2, 512, 8 * wide_count * narrow_count)
    coarse_inverse = lax.rsqrt(coarse_square - coarse_center * coarse_center + epsilon)
    s_coarse = gain_coarse[...]

    def coarse_scaled(value):
        return (value - coarse_center) * coarse_inverse

    scaled = coarse_scaled(coarse_value)
    normed_grad = coarse_act_grad * slope(scaled, s_coarse)
    total_begin(3, column_sums(normed_grad), column_sums(normed_grad * scaled))
    coarse_u[...] = cgrad + coarse_inverse * normed_grad
    send_coarse(coarse_u, coarse_u_halo, 9)
    grad_sums = lax.fori_loop(2, 4, convolve_grad, grad_sums)

    total_middle(3)

    mid_mix = jnp.concatenate(
        [mid_scaled(mid_value).astype(BF16), jnp.ones((128, 128), BF16)], axis=1
    )
    matrix_sum[...] = jnp.zeros((4, 256, 512), F32)

    @pl.loop(0, 9)
    def _(t):
        weight = through[t].astype(F32)
        for n in range(2):
            mixed = dot_first(window_sums[n, t].reshape(128, 256), mid_mix)
            plain = jnp.concatenate([mixed[:, 512:640]] * 4, axis=1)
            matrix_sum[2 * n] += weight * plain
            matrix_sum[2 * n + 1] += weight * mixed[:, 0:512]

    def iota(shape, axis):
        return lax.broadcasted_iota(jnp.int32, shape, axis)

    def one_hot(condition):
        return jnp.where(condition, 1.0, 0.0).astype(BF16)

    by_group = one_hot((iota((32, 256), 1) >> 3) == iota((32, 256), 0))
    matrix = jnp.zeros((32, 128), F32)
    for n in range(4):
        high, low = halves(matrix_sum[n] * mid_inverse)
        high, low = halves(dot(by_group, high) + dot(by_group, low))
        to_lane = one_hot(iota((512, 128), 1) == 32 * n + (iota((512, 128), 0) >> 4))
        matrix += dot(high, to_lane) + dot(low, to_lane)
    first_matrix[wide] = matrix.astype(BF16)
    total_send_wide(6)

    first_mean, second_mean = total_end(3, 512, 8 * wide_count * narrow_count)
    arrived(coarse_halo, 8)
    arrived(coarse_u_halo, 9)
    offset = coarse_inverse * first_mean
    factor = coarse_inverse * second_mean
    pieces = [coarse_u[...] - offset - scaled * factor]
    for d in range(8):
        piece = coarse_scaled(coarse_halo[d].astype(F32)[0:8])
        pieces.append(coarse_u_halo[d] - offset - piece * factor)
    pieces.append(jnp.zeros((56, 512), F32))
    coarse_in_grad = jnp.concatenate(pieces, axis=0).astype(BF16)

    mid_pool_grad = dot_t(dot(SPREAD[...], coarse_in_grad).astype(BF16), down_coarse[...])
    row = lax.broadcasted_iota(jnp.int32, (256, 128), 0)
    keep = jnp.where(row < ABOVE, 1.0, 0.0)
    bounds = ((ABOVE, 16, 1), (BELOW, 16, 2), (LEFT, 32, 3), (RIGHT, 32, 4)) + tuple(
        (CORNER + 4 * c, 4, 5 + c) for c in range(4)
    )
    for start, size, d in bounds:
        inside = jnp.logical_and(row >= start, row < start + size)
        keep = jnp.where(inside, jnp.where(exists[d], 1.0, 0.0).astype(F32), keep)
    mid_grad = (summed_grad[...] + 0.0625 * mid_pool_grad) * jnp.concatenate([keep] * 4, axis=1)
    mid_act_grad = mid_convolve(
        mid_grad, dot_t, side_by_side(kernel_mid[8 - t] for t in range(9))
    )
    scaled = mid_scaled(mid_value)
    normed_grad = mid_act_grad * slope(scaled, s_mid)
    total_begin(4, column_sums(normed_grad), column_sums(normed_grad * scaled))
    mid_u = mid_grad[0:128].astype(BF16).astype(F32) + mid_inverse * normed_grad
    u_pack[...] = dot(PACK[...], mid_u.astype(BF16)).astype(BF16)
    send_mid(u_pack, u_halo, u_cor, 10)
    pulled = (0.0625 * dot_t(mid_u.astype(BF16), down_mid[...])).astype(BF16)
    fine_sums = [jnp.sum(value, axis=0, keepdims=True) for value in grad_sums]
    for t in range(9):
        term = dot_t(pulled, kernel_fine[8 - t])
        for n in range(2):
            fine_sums[n] += column_sums(window_sums[n, t].reshape(128, 256).astype(F32) * term)
    total_begin(5, *fine_sums)
    total_middle(6)

    fine_forward(2)
    coarse_block = (
        coarse_in.astype(F32)
        + coarse_convolve(
            coarse_extended(
                coarse_value,
                lambda d: coarse_halo[d].astype(F32)[0:8],
                silu(coarse_center, coarse_inverse, s_coarse),
                True,
            ),
            dot,
            kernel_coarse[...].reshape(4608, 512),
        )
    ).astype(BF16)
    coarse_up = dot(coarse_block, up_coarse[...]).astype(BF16)
    mid_sum = (mid_block.astype(F32) + dot(SPREAD[0:128, 0:16], coarse_up)).astype(BF16)
    mid_up = dot(mid_sum, up_mid[...]).astype(BF16)
    total_middle(4)
    total_middle(5)

    fine_forward(3)
    mid_up = dot(ENLARGE[:, 0:128], mid_up).reshape(4, 8, 1, 16, 256)
    for f in range(4):
        block = fine_block[f].astype(F32).reshape(8, 4, 16, 256)
        fine_block[f] = (block + mid_up[f]).astype(BF16).reshape(512, 256)
    out_copy = pltpu.make_async_copy(fine_block, out_ref, out_sem.at[0])
    out_copy.start()
    first_mean, second_mean = total_end(4, 512, 128 * wide_count * narrow_count)
    arrived(u_halo, 10)
    arrived(u_cor, 11)
    offset = mid_inverse * first_mean
    factor = mid_inverse * second_mean
    mid_in_grad = mid_extended(
        mid_u, u_halo[...], lambda c: u_cor[c], lambda v: v - offset, False
    ) - factor * mid_extended(
        mid_value, mid_halo[...], lambda c: mid_cor[c], mid_scaled, False
    )

    pool_grad = 0.0625 * dot_t(mid_in_grad.astype(BF16), down_mid[...])
    pool_grad = pool_grad * jnp.concatenate([keep] * 2, axis=1)
    high, low = halves(pool_grad)
    added = dot(ENLARGE[...], jnp.concatenate([high[0:256], low[0:256]], axis=0))
    loads["stretch"].wait()
    for a in range(3):
        fields = [dot_t(high, kernel_fine[8 - 3 * a - b]).astype(BF16) for b in range(3)]
        stretched[a] = dot(stretch[...], jnp.concatenate(fields, axis=0)).reshape(4, 10, 16, 256)

    means = jnp.zeros((8, 128), F32)
    for n, mean in enumerate((first_mean, second_mean)):
        lane, row = iota((512, 128), 1), iota((512, 128), 0)
        inside = jnp.logical_and((lane & 31) == (row >> 4), ((lane >> 5) & 1) == n)
        to_lane = jnp.where(inside, 0.0625, 0.0).astype(BF16)
        high, low = halves(jnp.broadcast_to(mean, (8, 512)))
        means += dot(high, to_lane) + dot(low, to_lane)
    matrix_high, matrix_low = halves(total_sum(6))
    fine_totals = total_groups(5, 256, 1.0)
    spread_groups = one_hot((iota((256, 32), 0) >> 3) == iota((256, 32), 1))
    fine_means = []
    for n in range(2):
        half = jnp.where((iota((8, 128), 1) >> 6) == n, means, 0.0)
        high, low = halves(half)
        change = dot_t(high, matrix_high) + dot_t(low, matrix_high) + dot_t(high, matrix_low)
        high, low = halves(change)
        change = dot_t(high, spread_groups) + dot_t(low, spread_groups)
        fine_means.append(
            (fine_totals[n] - change[0:1]) * (1.0 / (8 * 2048 * wide_count * narrow_count))
        )
    slant = -fine_inverse * fine_inverse * fine_means[1]
    shift = -fine_inverse * fine_means[0] - fine_center * slant

    added = added.reshape(4, 8, 1, 16, 256)
    grad_copies = []
    for f in range(4):
        above, here, below = stretched[0, f], stretched[1, f], stretched[2, f]
        centre = here[1:9] + above[1:9] + below[1:9]
        top = here[1:9] + above[0:8] + below[1:9]
        bottom = here[1:9] + above[1:9] + below[2:10]
        back = jnp.stack([top, centre, centre, bottom], axis=1).reshape(512, 256)
        normed_grad = (conv_grad[f] + back) * fine_slope[f]
        grad = xg[1, f].astype(F32).reshape(8, 4, 16, 256) + added[f]
        grad = grad.reshape(512, 256).astype(BF16).astype(F32)
        grad_buf[f] = grad + fine_inverse * normed_grad + (shift + fine_value(f) * slant)
        grad_copies.append(
            pltpu.make_async_copy(grad_buf.at[f], grad_ref.at[f], out_sem.at[1 + f])
        )
        grad_copies[f].start()

    for which in range(2):
        sent(row_in.at[:, which], 13 * which)
        sent(col_in.at[:, which], 13 * which + 1)
        sent(cor_in.at[which], 13 * which + 2)
    sent(sum_in, 3)
    sent(sum_cor, 4)
    sent(cgrad_in, 5)
    sent(mid_halo, 6)
    sent(mid_cor, 7)
    sent(coarse_halo, 8)
    sent(coarse_u_halo, 9)
    sent(u_halo, 10)
    sent(u_cor, 11)
    for phase in range(7):
        whole = firsts[phase].at[pl.ds(0, wide_count - 1)]
        pltpu.make_async_copy(whole, whole, total_send.at[2 * phase]).wait()
        whole = seconds[phase].at[pl.ds(0, narrow_count - 1)]
        pltpu.make_async_copy(whole, whole, total_send.at[2 * phase + 1]).wait()
    out_copy.wait()
    for copy in grad_copies:
        copy.wait()


def shards(*arguments):
    (
        fine_input,
        gain_fine,
        kernel_fine,
        down_mid,
        gain_mid,
        kernel_mid,
        down_coarse,
        gain_coarse,
        kernel_coarse,
        up_coarse,
        up_mid,
        grad_out,
    ) = arguments
    wide_count, narrow_count = lax.axis_size("wide"), lax.axis_size("narrow")
    anywhere = pl.BlockSpec(memory_space=pl.ANY)
    vmem = pltpu.VMEM
    scratch = [
        vmem((2, 4, 32, 16, 256), BF16),
        vmem((9, 256, 256), BF16),
        vmem((256, 512), BF16),
        vmem((9, 512, 512), BF16),
        vmem((512, 512), BF16),
        vmem((9, 512, 512), BF16),
        vmem((512, 512), BF16),
        vmem((512, 256), BF16),
        vmem((1, 256), F32),
        vmem((1, 512), F32),
        vmem((1, 512), F32),
        vmem((608, 512), BF16),
        vmem((1168, 256), BF16),
        vmem((1168, 128), BF16),
        vmem((288, 640), BF16),
        vmem((640, 768), BF16),
        vmem((4, 544, 768), BF16),
        vmem((4, 512, 256), BF16),
        vmem((4, 512, 256), F32),
        vmem((4, 512, 256), F32),
        vmem((128, 256), F32),
        vmem((128, 256), BF16),
        vmem((4, 512, 256), F32),
        vmem((2, 2, 4, 16, 256), F32),
        vmem((2, 4, 64, 256), BF16),
        vmem((2, 16, 256), F32),
        vmem((256, 512), F32),
        vmem((6, wide_count, 1, 128), F32),
        vmem((6, narrow_count, 1, 128), F32),
        vmem((8, 128), F32),
        vmem((wide_count, 32, 128), BF16),
        vmem((narrow_count, 32, 128), BF16),
        vmem((2, 9, 4, 32, 256), BF16),
        vmem((2, 2, 4, 16, 256), BF16),
        vmem((2, 2, 4, 32, 256), BF16),
        vmem((2, 4, 32, 256), BF16),
        vmem((4, 256, 512), F32),
        vmem((9, 256, 512), BF16),
        vmem((3, 4, 10, 16, 256), F32),
        vmem((2, 2, 128, 256), BF16),
        vmem((2, 16, 256), BF16),
        vmem((2, 2, 4, 16, 256), BF16),
        vmem((2, 2, 128, 256), BF16),
        vmem((2, 4, 16, 256), BF16),
        vmem((112, 256), BF16),
        vmem((96, 256), BF16),
        vmem((4, 16, 256), BF16),
        vmem((16, 512), BF16),
        vmem((8, 16, 512), BF16),
        vmem((112, 512), BF16),
        vmem((96, 512), BF16),
        vmem((4, 16, 512), BF16),
        vmem((16, 512), BF16),
        vmem((8, 16, 512), BF16),
        vmem((8, 512), F32),
        vmem((8, 8, 512), F32),
        vmem((112, 512), BF16),
        vmem((96, 512), BF16),
        vmem((4, 16, 512), BF16),
        pltpu.SemaphoreType.DMA((17,)),
        pltpu.SemaphoreType.DMA((5,)),
        pltpu.SemaphoreType.DMA((14,)),
        pltpu.SemaphoreType.DMA((14,)),
        pltpu.SemaphoreType.DMA((16,)),
        pltpu.SemaphoreType.DMA((16,)),
    ]
    output, grad = pl.pallas_call(
        functools.partial(kernel, wide_count, narrow_count),
        out_shape=(
            jax.ShapeDtypeStruct((4, 512, 256), BF16),
            jax.ShapeDtypeStruct((4, 512, 256), F32),
        ),
        in_specs=[anywhere] * 17,
        out_specs=(anywhere, anywhere),
        scratch_shapes=scratch,
        compiler_params=pltpu.CompilerParams(
            collective_id=0, has_side_effects=True, vmem_limit_bytes=56 * 2**20
        ),
        name="whole_net",
    )(
        fine_input,
        gain_fine.reshape(1, 256),
        kernel_fine.reshape(9, 256, 256),
        down_mid,
        gain_mid.reshape(1, 512),
        kernel_mid.reshape(9, 512, 512),
        down_coarse,
        gain_coarse.reshape(1, 512),
        kernel_coarse.reshape(9, 512, 512),
        up_coarse,
        up_mid,
        grad_out,
        *tables(),
    )
    return output.reshape(4, 32, 16, 256), grad.reshape(4, 32, 16, 256)


def solution(mesh):
    tile = P(None, "wide", "narrow", None)
    return jax.shard_map(
        shards,
        mesh=mesh,
        in_specs=(tile,) + (P(),) * 10 + (tile,),
        out_specs=(tile, tile),
        check_vma=False,
    )
```

```python
import functools

import jax
import jax.numpy as jnp
import numpy as np
from jax import lax
from jax.experimental import pallas as pl
from jax.experimental.pallas import tpu as pltpu
from jax.sharding import PartitionSpec as P

MESH = pl.DeviceIdType.MESH
GROUPS = 32
epsilon = 1e-05
F32 = jnp.float32
BF16 = jnp.bfloat16

DIRS = ((0, 0), (-1, 0), (1, 0), (0, -1), (0, 1), (-1, -1), (-1, 1), (1, -1), (1, 1))

ABOVE, BELOW, LEFT, RIGHT, CORNER = 128, 144, 160, 192, 224


def mid_row(f, i, j):
    if 0 <= i < 8 and 0 <= j < 4:
        return 32 * f + 4 * i + j
    if i < 0 and 0 <= j < 4:
        return ABOVE + 4 * f + j
    if i > 7 and 0 <= j < 4:
        return BELOW + 4 * f + j
    if 0 <= i < 8:
        return (LEFT if j < 0 else RIGHT) + 8 * f + i
    return CORNER + 4 * (2 * (i > 7) + (j > 3)) + f


def coarse_row(f, i, side):
    down = -1 if i < 0 else (1 if i > 1 else 0)
    return 8 * DIRS.index((down, side)) + 2 * f + i % 2


def tables():
    pick = np.zeros((96, 512), np.float32)
    for i in range(32):
        for j in range(16):
            pick[4 * (i // 4) + j // 4, 16 * i + j] = 1
        pick[32 + i, 16 * i + 15] = 1
        pick[64 + i, 16 * i] = 1
    enlarge = np.zeros((512, 256), np.float32)
    taps = np.zeros((1152, 256), np.float32)
    ends = np.zeros((16, 256), np.float32)
    pack = np.zeros((112, 128), np.float32)
    pool = np.zeros((16, 128), np.float32)
    coarse_taps = np.zeros((144, 128), np.float32)
    spread = np.zeros((256, 128), np.float32)
    for f in range(4):
        for i in range(8):
            for j in range(16):
                enlarge[128 * f + 16 * i + j, mid_row(f, i, j // 4)] = 1
        for c in range(4):
            low, first = c < 2, c % 2 == 1
            ends[4 * c + f, 128 * first + 32 * f + 31 * low] = 1
            pack[96 + 4 * c + f, mid_row(f, 7 * low, 3 * (not first))] = 1
        for i in range(8):
            for j in range(4):
                here = 32 * f + 4 * i + j
                pool[2 * f + i // 4, here] = 1
                for t in range(9):
                    taps[128 * t + here, mid_row(f, i + t // 3 - 1, j + t % 3 - 1)] = 1
            pack[32 + 8 * f + i, mid_row(f, i, 3)] = 1
            pack[64 + 8 * f + i, mid_row(f, i, 0)] = 1
        for j in range(4):
            pack[4 * f + j, mid_row(f, 7, j)] = 1
            pack[16 + 4 * f + j, mid_row(f, 0, j)] = 1
        for i in range(2):
            for t in range(9):
                coarse_taps[16 * t + 2 * f + i, coarse_row(f, i + t // 3 - 1, t % 3 - 1)] = 1
        for i in range(-1, 9):
            for j in range(-1, 5):
                side = -1 if j < 0 else (1 if j > 3 else 0)
                spread[mid_row(f, i, j), coarse_row(f, i // 4 if i < 8 else 2, side)] = 1
    windows = np.zeros((288, 640), np.float32)
    for t in range(9):
        for i in range(32):
            for j in range(16):
                p, q = i + 1 - t // 3, j + 1 - t % 3
                row = 32 * t + 4 * (i // 4) + j // 4
                if 0 <= p < 32 and 0 <= q < 16:
                    at = 16 * p + q
                elif 0 <= q < 16:
                    at = (512 if p < 0 else 528) + q
                elif 0 <= p < 32:
                    at = (544 if q < 0 else 576) + p
                else:
                    at = 608 + 2 * (p > 31) + (q > 15)
                windows[row, at] = 1
    stretch = np.zeros((640, 768), np.float32)
    for f in range(4):
        for i in range(10):
            for j in range(16):
                for b in range(3):
                    at = 256 * b + mid_row(f, i - 1, (j + b - 1) // 4)
                    stretch[160 * f + 16 * i + j, at] = 1
    by_frame = np.zeros((128, 128), np.float32)
    for f in range(4):
        for c in range(4):
            by_frame[32 * f + c, 4 * c + f] = 1
    sides = np.zeros((512, 128), np.float32)
    for i in range(32):
        sides[16 * i, i] = 1
        sides[16 * i + 15, 64 + i] = 1
    wide_table = np.concatenate([pick, np.concatenate([enlarge, enlarge], axis=1)])
    middle_table = np.concatenate([taps, ends])
    narrow_table = np.concatenate([pack, pool, coarse_taps, spread, sides, by_frame])
    result = (wide_table, middle_table, narrow_table, windows, stretch)
    return [jnp.asarray(t, BF16) for t in result]


def dot(a, b):
    return jnp.dot(a, b, preferred_element_type=F32)


def dot_t(a, b):
    return lax.dot_general(a, b, (((1,), (1,)), ((), ())), preferred_element_type=F32)


def dot_first(a, b):
    return lax.dot_general(a, b, (((0,), (0,)), ((), ())), preferred_element_type=F32)


def group_lanes(t, size):
    lane = lax.broadcasted_iota(jnp.int32, t.shape, 1)
    step = 1
    while step < size:
        t = t + jnp.where(
            (lane & step) != 0, pltpu.roll(t, step, 1), pltpu.roll(t, 128 - step, 1)
        )
        step *= 2
    return t


def halves(t):
    high = t.astype(BF16)
    return high, (t - high.astype(F32)).astype(BF16)


def kernel(
    wide_count,
    narrow_count,
    x_in,
    gain_fine_in,
    kernel_fine_in,
    down_mid_in,
    gain_mid_in,
    kernel_mid_in,
    down_coarse_in,
    gain_coarse_in,
    kernel_coarse_in,
    up_coarse_in,
    up_mid_in,
    grad_in,
    wide_table_in,
    middle_table_in,
    narrow_table_in,
    windows_in,
    stretch_in,
    out_ref,
    grad_ref,
    xg,
    kernel_fine,
    down_mid,
    kernel_mid,
    down_coarse,
    kernel_coarse,
    up_coarse,
    up_mid,
    gain_fine,
    gain_mid,
    gain_coarse,
    wide_table,
    middle_table,
    narrow_table,
    windows,
    stretch,
    columns,
    fine_block,
    grad_buf,
    conv_grad,
    pooled_x,
    summed,
    fine_slope,
    edge_rows,
    edge_sides,
    edge_ends,
    summed_grad,
    first,
    second,
    rows,
    first_matrix,
    second_matrix,
    window_sums,
    rim_rows,
    rim_sides,
    rim_ends,
    matrix_sum,
    through,
    stretched,
    col_pack,
    cor_pack,
    row_in,
    col_in,
    cor_in,
    sum_pack,
    sum_in,
    sum_cor,
    cgrad_own,
    cgrad_in,
    mid_pack,
    mid_halo,
    mid_cor,
    coarse_own,
    coarse_halo,
    coarse_u,
    coarse_u_halo,
    u_pack,
    u_halo,
    u_cor,
    load_sem,
    out_sem,
    total_send,
    total_recv,
    halo_send,
    halo_recv,
):
    wide, narrow = lax.axis_index("wide"), lax.axis_index("narrow")

    def around(index, step, count):
        moved = index + step
        if isinstance(step, int) and step < 0:
            return jnp.where(moved < 0, moved + count, moved)
        return jnp.where(moved >= count, moved - count, moved)

    def device(down, side):
        return (
            wide if isinstance(down, int) and down == 0 else around(wide, down, wide_count),
            narrow if isinstance(side, int) and side == 0 else around(narrow, side, narrow_count),
        )

    loads = {}
    pairs = (
        ("x0", x_in.at[0], xg.at[0, 0]),
        ("x1", x_in.at[1], xg.at[0, 1]),
        ("x2", x_in.at[2], xg.at[0, 2]),
        ("x3", x_in.at[3], xg.at[0, 3]),
        ("grad", grad_in, xg.at[1]),
        ("wide_table", wide_table_in, wide_table),
        ("middle_table", middle_table_in, middle_table),
        ("narrow_table", narrow_table_in, narrow_table),
        ("gain_fine", gain_fine_in, gain_fine),
        ("windows", windows_in, windows),
        ("kernel_fine", kernel_fine_in, kernel_fine),
        ("up_mid", up_mid_in, up_mid),
        ("up_coarse", up_coarse_in, up_coarse),
        ("down_mid", down_mid_in, down_mid),
        ("gain_mid", gain_mid_in, gain_mid),
        ("kernel_coarse", kernel_coarse_in, kernel_coarse),
        ("kernel_mid", kernel_mid_in, kernel_mid),
        ("down_coarse", down_coarse_in, down_coarse),
        ("gain_coarse", gain_coarse_in, gain_coarse),
        ("stretch", stretch_in, stretch),
    )
    for number, (name, source, target) in enumerate(pairs):
        loads[name] = pltpu.make_async_copy(source, target, load_sem.at[number])

    def begin_loads(*names):
        for name in names:
            loads[name].start()

    begin_loads("x0", "x1", "x2", "x3", "wide_table", "middle_table")

    barrier = pltpu.get_barrier_semaphore()
    greeted = 0
    for down in range(wide_count):
        for side in range(-2, narrow_count - 2):
            near = (down <= 1 or down == wide_count - 1) and abs(side) <= 1
            if (down, side) != (0, 0) and (down == 0 or side == 0 or near):
                pl.semaphore_signal(
                    barrier, inc=1, device_id=device(down, side), device_id_type=MESH
                )
                greeted += 1

    def send(source, target, which, down, side):
        pltpu.make_async_remote_copy(
            src_ref=source,
            dst_ref=target,
            send_sem=halo_send.at[which],
            recv_sem=halo_recv.at[which],
            device_id=device(down, side),
            device_id_type=MESH,
        ).start()

    def arrived(buffer, which):
        pltpu.make_async_copy(buffer, buffer, halo_recv.at[which]).wait()

    def sent(buffer, which):
        pltpu.make_async_copy(buffer, buffer, halo_send.at[which]).wait()

    firsts = tuple(first.at[p] for p in range(6)) + (first_matrix,)
    seconds = tuple(second.at[p] for p in range(6)) + (second_matrix,)

    def total_send_wide(phase):
        mine = firsts[phase].at[wide]

        @pl.loop(1, wide_count)
        def _(step):
            pltpu.make_async_remote_copy(
                src_ref=mine,
                dst_ref=mine,
                send_sem=total_send.at[2 * phase],
                recv_sem=total_recv.at[2 * phase],
                device_id=device(step, 0),
                device_id_type=MESH,
            ).start()

    def diagonal(shape=(8, 128)):
        lane = lax.broadcasted_iota(jnp.int32, shape, 1) & 7
        return lane == lax.broadcasted_iota(jnp.int32, shape, 0)

    def total_begin(phase, one, two):
        channels = one.shape[1]
        if channels < 512:
            rows[...] = jnp.zeros((8, 128), F32)
        for n, value in enumerate((one, two)):
            for k in range(channels // 128):
                rows[4 * n + k : 4 * n + k + 1, :] = value[:, 128 * k : 128 * k + 128]
        grouped = group_lanes(rows[...], channels // GROUPS)
        grouped = jnp.where(diagonal(), grouped, 0.0)
        firsts[phase][wide] = jnp.sum(grouped, axis=0, keepdims=True)
        total_send_wide(phase)

    def total_middle(phase):
        whole = firsts[phase].at[pl.ds(0, wide_count - 1)]
        pltpu.make_async_copy(whole, whole, total_recv.at[2 * phase]).wait()
        summed_up = jnp.sum(firsts[phase][...].astype(F32), axis=0)
        seconds[phase][narrow] = summed_up.astype(seconds[phase].dtype)
        mine = seconds[phase].at[narrow]

        @pl.loop(1, narrow_count)
        def _(step):
            pltpu.make_async_remote_copy(
                src_ref=mine,
                dst_ref=mine,
                send_sem=total_send.at[2 * phase + 1],
                recv_sem=total_recv.at[2 * phase + 1],
                device_id=device(0, step),
                device_id_type=MESH,
            ).start()

    def total_sum(phase):
        whole = seconds[phase].at[pl.ds(0, narrow_count - 1)]
        pltpu.make_async_copy(whole, whole, total_recv.at[2 * phase + 1]).wait()
        return jnp.sum(seconds[phase][...].astype(F32), axis=0)

    def row_of(t, start, channels):
        return jnp.concatenate([t[start + k : start + k + 1] for k in range(channels // 128)], axis=1)

    def total_groups(phase, channels, scale):
        packed = jnp.broadcast_to(total_sum(phase), (8, 128))
        t = group_lanes(jnp.where(diagonal(), packed, 0.0), 8) * scale
        return row_of(t, 0, channels), row_of(t, 4, channels)

    def total_end(phase, channels, cells):
        return total_groups(phase, channels, 1.0 / (channels // GROUPS * cells))

    has_above, has_below = wide > 0, wide < wide_count - 1
    has_left, has_right = narrow > 0, narrow < narrow_count - 1
    has_corner = (
        jnp.logical_and(has_above, has_left),
        jnp.logical_and(has_above, has_right),
        jnp.logical_and(has_below, has_left),
        jnp.logical_and(has_below, has_right),
    )
    exists = (None, has_above, has_below, has_left, has_right) + has_corner

    def only(condition, value):
        return value * jnp.where(condition, 1.0, 0.0).astype(F32)

    def corners(read, change, masked):
        result = None
        for c in range(4):
            value = change(read(c).astype(F32))
            if masked:
                value = only(has_corner[c], value)
            cell = lax.broadcasted_iota(jnp.int32, value.shape, 0)
            result = value if result is None else jnp.where(cell >= 4 * c, value, result)
        return result

    def mid_extended(own, read_halo, read_cor, change, masked):
        pieces = [change(own)]
        halo = change(read_halo.astype(F32))
        for low, high, d in ((0, 16, 1), (16, 32, 2), (32, 64, 3), (64, 96, 4)):
            piece = halo[low:high]
            pieces.append(only(exists[d], piece) if masked else piece)
        pieces.append(corners(read_cor, change, masked))
        pieces.append(jnp.zeros((16, own.shape[1]), F32))
        return jnp.concatenate(pieces, axis=0)

    def send_mid(pack, halo, cor, which):
        send(pack.at[pl.ds(0, 16)], halo.at[pl.ds(0, 16)], which, 1, 0)
        send(pack.at[pl.ds(16, 16)], halo.at[pl.ds(16, 16)], which, -1, 0)
        send(pack.at[pl.ds(32, 32)], halo.at[pl.ds(32, 32)], which, 0, 1)
        send(pack.at[pl.ds(64, 32)], halo.at[pl.ds(64, 32)], which, 0, -1)
        for c in range(4):
            down, side = DIRS[5 + c]
            send(pack.at[pl.ds(96, 16)], cor.at[c], which + 1, -down, -side)

    def send_coarse(own, halo, which):
        for d in range(1, 9):
            down, side = DIRS[d]
            send(own, halo.at[d - 1], which, -down, -side)

    def coarse_extended(own, halo, change, masked):
        pieces = [change(own)]
        for d in range(1, 9):
            piece = change(halo(d - 1))
            pieces.append(only(exists[d], piece) if masked else piece)
        pieces.append(jnp.zeros((56, own.shape[1]), F32))
        return jnp.concatenate(pieces, axis=0)

    PICK = wide_table.at[pl.ds(0, 96)]
    ENLARGE = wide_table.at[pl.ds(96, 512)]
    TAPS = middle_table.at[pl.ds(0, 1152)]
    ENDS = middle_table.at[pl.ds(1152, 16)]
    PACK = narrow_table.at[pl.ds(0, 112)]
    POOL = narrow_table.at[pl.ds(112, 16)]
    COARSE_TAPS = narrow_table.at[pl.ds(128, 144)]
    SPREAD = narrow_table.at[pl.ds(272, 256)]
    SIDES = narrow_table.at[pl.ds(528, 512)]
    BY_FRAME = narrow_table.at[pl.ds(1040, 128)]

    def frame(which, f):
        return xg[which, f].reshape(512, 256)

    blank = jnp.zeros((8, 256), F32)
    one, two = blank, blank
    for f in range(4):
        loads["x%d" % f].wait()
        value = frame(0, f).astype(F32)
        one += jnp.sum(value.reshape(64, 8, 256), axis=0)
        two += jnp.sum((value * value).reshape(64, 8, 256), axis=0)
    pl.semaphore_wait(barrier, greeted)
    total_begin(0, jnp.sum(one, axis=0, keepdims=True), jnp.sum(two, axis=0, keepdims=True))

    begin_loads("grad", "narrow_table", "gain_fine", "windows", "kernel_fine")
    begin_loads("up_mid", "up_coarse", "down_mid", "gain_mid")

    def rim(which):
        sem = 13 * which
        send(xg.at[which, :, 31], row_in.at[0, which], sem, 1, 0)
        send(xg.at[which, :, 0], row_in.at[1, which], sem, -1, 0)
        for f in range(4):
            picked = dot(PICK[...], frame(which, f))
            if which == 0:
                pooled_x[32 * f : 32 * f + 32] = picked[0:32]
            picked = picked.astype(BF16)
            col_pack[0, which, 32 * f : 32 * f + 32] = picked[32:64]
            col_pack[1, which, 32 * f : 32 * f + 32] = picked[64:96]
            if which == 1:
                summed[32 * f : 32 * f + 32] = picked[0:32]
        send(col_pack.at[0, which], col_in.at[0, which], sem + 1, 0, 1)
        send(col_pack.at[1, which], col_in.at[1, which], sem + 1, 0, -1)
        ends = jnp.concatenate([col_pack[0, which], col_pack[1, which]], axis=0)
        cor_pack[which] = dot(ENDS[...], ends).astype(BF16)
        for c in range(4):
            down, side = DIRS[5 + c]
            send(cor_pack.at[which], cor_in.at[which, c], sem + 2, -down, -side)

    loads["wide_table"].wait()
    loads["middle_table"].wait()
    rim(0)
    total_middle(0)
    begin_loads("kernel_mid")
    loads["grad"].wait()
    rim(1)
    loads["narrow_table"].wait()

    up_mid_grad = summed[...]
    sum_pack[...] = dot(PACK[...], up_mid_grad).astype(BF16)
    send_mid(sum_pack, sum_in, sum_cor, 3)
    loads["up_mid"].wait()
    high, low = halves(dot_t(up_mid_grad, up_mid[...]))
    up_coarse_grad = (dot(POOL[...], high) + dot(POOL[...], low)).astype(BF16)
    loads["up_coarse"].wait()
    cgrad_own[...] = dot_t(up_coarse_grad, up_coarse[...]).astype(BF16)
    send_coarse(cgrad_own, cgrad_in, 5)

    loads["gain_fine"].wait()
    loads["kernel_fine"].wait()
    loads["down_mid"].wait()

    @pl.loop(0, 9)
    def _(t):
        through[t] = (0.0625 * dot(kernel_fine[8 - t], down_mid[...])).astype(BF16)

    fine_center, fine_square = total_end(0, 256, 2048 * wide_count * narrow_count)
    fine_inverse = lax.rsqrt(fine_square - fine_center * fine_center + epsilon)
    s_fine = gain_fine[...]

    def silu(center, inverse, scaling):
        gain = 0.5 * inverse * scaling
        shift = -center * gain

        def change(value):
            half = value * gain + shift
            return half * jnp.tanh(half) + half

        return change

    def slope(scaled, scaling):
        half = scaled * (0.5 * scaling)
        bend = jnp.tanh(half)
        return (0.5 * scaling) * (1.0 + bend) * (1.0 + half * (1.0 - bend))

    fine_act = silu(fine_center, fine_inverse, s_fine)

    arrived(row_in.at[:, 0], 0)
    arrived(col_in.at[:, 0], 1)
    arrived(cor_in.at[0], 2)

    def set_edges(kind, above, below, left, right, ends):
        edge_rows[kind, 0] = only(has_above, above)
        edge_rows[kind, 1] = only(has_below, below)
        left = only(has_left, left).astype(BF16)
        right = only(has_right, right).astype(BF16)
        for f in range(4):
            edge_sides[kind, f, 0:32] = left[32 * f : 32 * f + 32]
            edge_sides[kind, f, 32:64] = right[32 * f : 32 * f + 32]
        edge_ends[kind] = ends

    def place(kind, f, own):
        column = lax.broadcasted_iota(jnp.int32, (512, 256), 0) & 15
        sides = edge_sides[kind, f]
        low = jnp.where(
            column == 0, dot(SIDES[:, 0:64], sides), pltpu.roll(own, 1, 0)
        )
        columns[f, 16:528, 0:256] = low.astype(BF16)
        columns[f, 16:528, 256:512] = own.astype(BF16)
        high = jnp.where(
            column == 15, dot(SIDES[:, 32:96], sides), pltpu.roll(own, 511, 0)
        )
        columns[f, 16:528, 512:768] = high.astype(BF16)
        cell = lax.broadcasted_iota(jnp.int32, (16, 256), 0)
        for k in range(2):
            row = edge_rows[kind, k, f]
            at = slice(528 * k, 528 * k + 16)
            west = edge_ends[kind, pl.ds(8 * k + f, 1), :]
            east = edge_ends[kind, pl.ds(8 * k + 4 + f, 1), :]
            columns[f, at, 0:256] = jnp.where(cell == 0, west, pltpu.roll(row, 1, 0)).astype(BF16)
            columns[f, at, 256:512] = row.astype(BF16)
            columns[f, at, 512:768] = jnp.where(cell == 15, east, pltpu.roll(row, 15, 0)).astype(BF16)

    def side_by_side(pieces):
        return jnp.concatenate(list(pieces), axis=1)

    def fine_taps(f):
        return side_by_side(columns[f, 16 * a : 16 * a + 512, :] for a in range(3))

    def fine_convolve(f):
        return dot(fine_taps(f), kernel_fine[...].reshape(2304, 256))

    def fine_convolve_back(f):
        return dot_t(fine_taps(f), side_by_side(kernel_fine[8 - t] for t in range(9)))

    def fine_scaled(value):
        return (value - fine_center) * fine_inverse

    def fine_value(f):
        return frame(0, f).astype(F32)

    def set_fields(n, change):
        for k in range(2):
            rim_rows[n, k] = only(exists[1 + k], change(row_in[k, 0].astype(F32))).astype(BF16)
            sides = only(exists[3 + k], change(col_in[k, 0].astype(F32))).astype(BF16)
            rim_sides[n, k] = sides.reshape(4, 32, 256)
        ends = corners(lambda c: cor_in[0, c], change, True)
        ends = dot(BY_FRAME[:, 0:16], ends.astype(BF16)).astype(BF16)
        rim_ends[n] = ends.reshape(4, 32, 256)

    def window(n, f, own):
        field = jnp.concatenate(
            [
                own.astype(BF16),
                rim_rows[n, 0, f],
                rim_rows[n, 1, f],
                rim_sides[n, 0, f],
                rim_sides[n, 1, f],
                rim_ends[n, f],
            ],
            axis=0,
        )
        return dot(windows[...], field)

    set_fields(0, fine_act)
    loads["windows"].wait()

    @pl.loop(0, 4)
    def _(f):
        sums = window(0, f, fine_act(fine_value(f)))
        high, low = halves(sums)
        window_sums[0, :, f] = high.reshape(9, 32, 256)
        window_sums[1, :, f] = low.reshape(9, 32, 256)

    both = side_by_side(
        jnp.concatenate([window_sums[n, 8 - t].reshape(128, 256) for n in range(2)], axis=0)
        for t in range(9)
    )
    both = dot(both, kernel_fine[...].reshape(2304, 256))
    pooled = pooled_x[...] + both[0:128] + both[128:256]
    pooled = (pooled * 0.0625).astype(BF16)

    def fine_forward(f):
        value = fine_value(f)
        place(0, f, fine_act(value))
        fine_block[f] = (value + fine_convolve(f)).astype(BF16)

    def same(value):
        return value

    mid_in = dot(pooled, down_mid[...]).astype(BF16)
    mid_value = mid_in.astype(F32)

    def column_sums(value):
        return jnp.sum(value, axis=0, keepdims=True)

    total_begin(1, column_sums(mid_value), column_sums(mid_value * mid_value))
    mid_pack[...] = dot(PACK[...], mid_in).astype(BF16)
    send_mid(mid_pack, mid_halo, mid_cor, 6)
    begin_loads("down_coarse", "gain_coarse", "kernel_coarse", "stretch")

    @pl.loop(0, 4)
    def _(f):
        fine_slope[f] = slope(fine_scaled(fine_value(f)), s_fine)

    set_fields(0, lambda v: slope(fine_scaled(v), s_fine))
    set_fields(1, lambda v: slope(fine_scaled(v), s_fine) * fine_scaled(v))

    set_edges(
        0,
        fine_act(row_in[0, 0].astype(F32)),
        fine_act(row_in[1, 0].astype(F32)),
        fine_act(col_in[0, 0].astype(F32)),
        fine_act(col_in[1, 0].astype(F32)),
        corners(lambda c: cor_in[0, c], fine_act, True),
    )
    fine_forward(0)
    total_middle(1)
    fine_forward(1)

    @pl.loop(0, 4)
    def _(f):
        bent = fine_slope[f]
        window_sums[0, :, f] = window(0, f, bent).astype(BF16).reshape(9, 32, 256)
        bent = bent * fine_scaled(fine_value(f))
        window_sums[1, :, f] = window(1, f, bent).astype(BF16).reshape(9, 32, 256)

    loads["gain_mid"].wait()
    loads["kernel_mid"].wait()
    mid_center, mid_square = total_end(1, 512, 128 * wide_count * narrow_count)
    mid_inverse = lax.rsqrt(mid_square - mid_center * mid_center + epsilon)
    s_mid = gain_mid[...]

    mid_act = silu(mid_center, mid_inverse, s_mid)

    def mid_scaled(value):
        return (value - mid_center) * mid_inverse

    def mid_convolve(extended, product, weights):
        taps = dot(TAPS[...], extended.astype(BF16)).astype(BF16)
        return product(side_by_side(taps[128 * t : 128 * t + 128] for t in range(9)), weights)

    arrived(mid_halo, 6)
    arrived(mid_cor, 7)
    mid_block = (
        mid_value
        + mid_convolve(
            mid_extended(mid_value, mid_halo[...], lambda c: mid_cor[c], mid_act, True),
            dot,
            kernel_mid[...].reshape(4608, 512),
        )
    ).astype(BF16)

    loads["down_coarse"].wait()
    mid_pooled = (dot(POOL[...], mid_block) * 0.0625).astype(BF16)
    coarse_in = dot(mid_pooled, down_coarse[...]).astype(BF16)
    coarse_own[...] = coarse_in
    coarse_value = coarse_in.astype(F32)[0:8]
    total_begin(2, column_sums(coarse_value), column_sums(coarse_value * coarse_value))
    send_coarse(coarse_own, coarse_halo, 8)

    arrived(row_in.at[:, 1], 13)
    arrived(col_in.at[:, 1], 14)
    arrived(cor_in.at[1], 15)
    set_edges(
        1,
        row_in[0, 1].astype(F32),
        row_in[1, 1].astype(F32),
        col_in[0, 1].astype(F32),
        col_in[1, 1].astype(F32),
        corners(lambda c: cor_in[1, c], same, True),
    )

    def convolve_grad(f, carry):
        place(1, f, frame(1, f).astype(F32))
        result = fine_convolve_back(f)
        conv_grad[f] = result
        weighted = result * fine_slope[f]
        scaled = fine_scaled(fine_value(f))
        return (
            carry[0] + jnp.sum(weighted.reshape(64, 8, 256), axis=0),
            carry[1] + jnp.sum((weighted * scaled).reshape(64, 8, 256), axis=0),
        )

    grad_sums = lax.fori_loop(0, 2, convolve_grad, (blank, blank))
    total_middle(2)

    arrived(cgrad_in, 5)
    loads["kernel_coarse"].wait()

    def coarse_convolve(extended, product, weights):
        taps = dot(COARSE_TAPS[...], extended.astype(BF16)).astype(BF16)
        return product(side_by_side(taps[16 * t : 16 * t + 16] for t in range(9)), weights)

    cgrad = cgrad_own[...].astype(F32)[0:8]
    coarse_act_grad = coarse_convolve(
        coarse_extended(cgrad, lambda d: cgrad_in[d].astype(F32)[0:8], same, True),
        dot_t,
        side_by_side(kernel_coarse[8 - t] for t in range(9)),
    )[0:8]

    arrived(sum_in, 3)
    arrived(sum_cor, 4)
    sum_extended = mid_extended(
        up_mid_grad.astype(F32), sum_in[...], lambda c: sum_cor[c], same, True
    )
    summed_grad[...] = dot_t(sum_extended.astype(BF16), up_mid[...])

    loads["gain_coarse"].wait()
    coarse_center, coarse_square = total_end(2, 512, 8 * wide_count * narrow_count)
    coarse_inverse = lax.rsqrt(coarse_square - coarse_center * coarse_center + epsilon)
    s_coarse = gain_coarse[...]

    def coarse_scaled(value):
        return (value - coarse_center) * coarse_inverse

    scaled = coarse_scaled(coarse_value)
    normed_grad = coarse_act_grad * slope(scaled, s_coarse)
    total_begin(3, column_sums(normed_grad), column_sums(normed_grad * scaled))
    coarse_u[...] = cgrad + coarse_inverse * normed_grad
    send_coarse(coarse_u, coarse_u_halo, 9)
    grad_sums = lax.fori_loop(2, 4, convolve_grad, grad_sums)

    total_middle(3)

    mid_mix = jnp.concatenate(
        [mid_scaled(mid_value).astype(BF16), jnp.ones((128, 128), BF16)], axis=1
    )
    matrix_sum[...] = jnp.zeros((4, 256, 512), F32)

    @pl.loop(0, 9)
    def _(t):
        weight = through[t].astype(F32)
        for n in range(2):
            mixed = dot_first(window_sums[n, t].reshape(128, 256), mid_mix)
            plain = jnp.concatenate([mixed[:, 512:640]] * 4, axis=1)
            matrix_sum[2 * n] += weight * plain
            matrix_sum[2 * n + 1] += weight * mixed[:, 0:512]

    def iota(shape, axis):
        return lax.broadcasted_iota(jnp.int32, shape, axis)

    def one_hot(condition):
        return jnp.where(condition, 1.0, 0.0).astype(BF16)

    by_group = one_hot((iota((32, 256), 1) >> 3) == iota((32, 256), 0))
    matrix = jnp.zeros((32, 128), F32)
    for n in range(4):
        high, low = halves(matrix_sum[n] * mid_inverse)
        high, low = halves(dot(by_group, high) + dot(by_group, low))
        to_lane = one_hot(iota((512, 128), 1) == 32 * n + (iota((512, 128), 0) >> 4))
        matrix += dot(high, to_lane) + dot(low, to_lane)
    first_matrix[wide] = matrix.astype(BF16)
    total_send_wide(6)

    first_mean, second_mean = total_end(3, 512, 8 * wide_count * narrow_count)
    arrived(coarse_halo, 8)
    arrived(coarse_u_halo, 9)
    offset = coarse_inverse * first_mean
    factor = coarse_inverse * second_mean
    pieces = [coarse_u[...] - offset - scaled * factor]
    for d in range(8):
        piece = coarse_scaled(coarse_halo[d].astype(F32)[0:8])
        pieces.append(coarse_u_halo[d] - offset - piece * factor)
    pieces.append(jnp.zeros((56, 512), F32))
    coarse_in_grad = jnp.concatenate(pieces, axis=0).astype(BF16)

    mid_pool_grad = dot_t(dot(SPREAD[...], coarse_in_grad).astype(BF16), down_coarse[...])
    row = lax.broadcasted_iota(jnp.int32, (256, 128), 0)
    keep = jnp.where(row < ABOVE, 1.0, 0.0)
    bounds = ((ABOVE, 16, 1), (BELOW, 16, 2), (LEFT, 32, 3), (RIGHT, 32, 4)) + tuple(
        (CORNER + 4 * c, 4, 5 + c) for c in range(4)
    )
    for start, size, d in bounds:
        inside = jnp.logical_and(row >= start, row < start + size)
        keep = jnp.where(inside, jnp.where(exists[d], 1.0, 0.0).astype(F32), keep)
    mid_grad = (summed_grad[...] + 0.0625 * mid_pool_grad) * jnp.concatenate([keep] * 4, axis=1)
    mid_act_grad = mid_convolve(
        mid_grad, dot_t, side_by_side(kernel_mid[8 - t] for t in range(9))
    )
    scaled = mid_scaled(mid_value)
    normed_grad = mid_act_grad * slope(scaled, s_mid)
    total_begin(4, column_sums(normed_grad), column_sums(normed_grad * scaled))
    mid_u = mid_grad[0:128].astype(BF16).astype(F32) + mid_inverse * normed_grad
    u_pack[...] = dot(PACK[...], mid_u.astype(BF16)).astype(BF16)
    send_mid(u_pack, u_halo, u_cor, 10)
    pulled = (0.0625 * dot_t(mid_u.astype(BF16), down_mid[...])).astype(BF16)
    fine_sums = [jnp.sum(value, axis=0, keepdims=True) for value in grad_sums]
    for t in range(9):
        term = dot_t(pulled, kernel_fine[8 - t])
        for n in range(2):
            fine_sums[n] += column_sums(window_sums[n, t].reshape(128, 256).astype(F32) * term)
    total_begin(5, *fine_sums)
    total_middle(6)

    fine_forward(2)
    coarse_block = (
        coarse_in.astype(F32)
        + coarse_convolve(
            coarse_extended(
                coarse_value,
                lambda d: coarse_halo[d].astype(F32)[0:8],
                silu(coarse_center, coarse_inverse, s_coarse),
                True,
            ),
            dot,
            kernel_coarse[...].reshape(4608, 512),
        )
    ).astype(BF16)
    coarse_up = dot(coarse_block, up_coarse[...]).astype(BF16)
    mid_sum = (mid_block.astype(F32) + dot(SPREAD[0:128, 0:16], coarse_up)).astype(BF16)
    mid_up = dot(mid_sum, up_mid[...]).astype(BF16)
    total_middle(4)
    total_middle(5)

    fine_forward(3)
    mid_up = dot(ENLARGE[:, 0:128], mid_up).reshape(4, 8, 1, 16, 256)
    for f in range(4):
        block = fine_block[f].astype(F32).reshape(8, 4, 16, 256)
        fine_block[f] = (block + mid_up[f]).astype(BF16).reshape(512, 256)
    out_copy = pltpu.make_async_copy(fine_block, out_ref, out_sem.at[0])
    out_copy.start()
    first_mean, second_mean = total_end(4, 512, 128 * wide_count * narrow_count)
    arrived(u_halo, 10)
    arrived(u_cor, 11)
    offset = mid_inverse * first_mean
    factor = mid_inverse * second_mean
    mid_in_grad = mid_extended(
        mid_u, u_halo[...], lambda c: u_cor[c], lambda v: v - offset, False
    ) - factor * mid_extended(
        mid_value, mid_halo[...], lambda c: mid_cor[c], mid_scaled, False
    )

    pool_grad = 0.0625 * dot_t(mid_in_grad.astype(BF16), down_mid[...])
    pool_grad = pool_grad * jnp.concatenate([keep] * 2, axis=1)
    high, low = halves(pool_grad)
    added = dot(ENLARGE[...], jnp.concatenate([high[0:256], low[0:256]], axis=0))
    loads["stretch"].wait()
    for a in range(3):
        fields = [dot_t(high, kernel_fine[8 - 3 * a - b]).astype(BF16) for b in range(3)]
        stretched[a] = dot(stretch[...], jnp.concatenate(fields, axis=0)).reshape(4, 10, 16, 256)

    means = jnp.zeros((8, 128), F32)
    for n, mean in enumerate((first_mean, second_mean)):
        lane, row = iota((512, 128), 1), iota((512, 128), 0)
        inside = jnp.logical_and((lane & 31) == (row >> 4), ((lane >> 5) & 1) == n)
        to_lane = jnp.where(inside, 0.0625, 0.0).astype(BF16)
        high, low = halves(jnp.broadcast_to(mean, (8, 512)))
        means += dot(high, to_lane) + dot(low, to_lane)
    matrix_high, matrix_low = halves(total_sum(6))
    fine_totals = total_groups(5, 256, 1.0)
    spread_groups = one_hot((iota((256, 32), 0) >> 3) == iota((256, 32), 1))
    fine_means = []
    for n in range(2):
        half = jnp.where((iota((8, 128), 1) >> 6) == n, means, 0.0)
        high, low = halves(half)
        change = dot_t(high, matrix_high) + dot_t(low, matrix_high) + dot_t(high, matrix_low)
        high, low = halves(change)
        change = dot_t(high, spread_groups) + dot_t(low, spread_groups)
        fine_means.append(
            (fine_totals[n] - change[0:1]) * (1.0 / (8 * 2048 * wide_count * narrow_count))
        )
    slant = -fine_inverse * fine_inverse * fine_means[1]
    shift = -fine_inverse * fine_means[0] - fine_center * slant

    added = added.reshape(4, 8, 1, 16, 256)
    grad_copies = []
    for f in range(4):
        above, here, below = stretched[0, f], stretched[1, f], stretched[2, f]
        centre = here[1:9] + above[1:9] + below[1:9]
        top = here[1:9] + above[0:8] + below[1:9]
        bottom = here[1:9] + above[1:9] + below[2:10]
        back = jnp.stack([top, centre, centre, bottom], axis=1).reshape(512, 256)
        normed_grad = (conv_grad[f] + back) * fine_slope[f]
        grad = xg[1, f].astype(F32).reshape(8, 4, 16, 256) + added[f]
        grad = grad.reshape(512, 256).astype(BF16).astype(F32)
        grad_buf[f] = grad + fine_inverse * normed_grad + (shift + fine_value(f) * slant)
        grad_copies.append(
            pltpu.make_async_copy(grad_buf.at[f], grad_ref.at[f], out_sem.at[1 + f])
        )
        grad_copies[f].start()

    for which in range(2):
        sent(row_in.at[:, which], 13 * which)
        sent(col_in.at[:, which], 13 * which + 1)
        sent(cor_in.at[which], 13 * which + 2)
    sent(sum_in, 3)
    sent(sum_cor, 4)
    sent(cgrad_in, 5)
    sent(mid_halo, 6)
    sent(mid_cor, 7)
    sent(coarse_halo, 8)
    sent(coarse_u_halo, 9)
    sent(u_halo, 10)
    sent(u_cor, 11)
    for phase in range(7):
        whole = firsts[phase].at[pl.ds(0, wide_count - 1)]
        pltpu.make_async_copy(whole, whole, total_send.at[2 * phase]).wait()
        whole = seconds[phase].at[pl.ds(0, narrow_count - 1)]
        pltpu.make_async_copy(whole, whole, total_send.at[2 * phase + 1]).wait()
    out_copy.wait()
    for copy in grad_copies:
        copy.wait()


def shards(*arguments):
    (
        fine_input,
        gain_fine,
        kernel_fine,
        down_mid,
        gain_mid,
        kernel_mid,
        down_coarse,
        gain_coarse,
        kernel_coarse,
        up_coarse,
        up_mid,
        grad_out,
    ) = arguments
    wide_count, narrow_count = lax.axis_size("wide"), lax.axis_size("narrow")
    anywhere = pl.BlockSpec(memory_space=pl.ANY)
    vmem = pltpu.VMEM
    scratch = [
        vmem((2, 4, 32, 16, 256), BF16),
        vmem((9, 256, 256), BF16),
        vmem((256, 512), BF16),
        vmem((9, 512, 512), BF16),
        vmem((512, 512), BF16),
        vmem((9, 512, 512), BF16),
        vmem((512, 512), BF16),
        vmem((512, 256), BF16),
        vmem((1, 256), F32),
        vmem((1, 512), F32),
        vmem((1, 512), F32),
        vmem((608, 512), BF16),
        vmem((1168, 256), BF16),
        vmem((1168, 128), BF16),
        vmem((288, 640), BF16),
        vmem((640, 768), BF16),
        vmem((4, 544, 768), BF16),
        vmem((4, 512, 256), BF16),
        vmem((4, 512, 256), F32),
        vmem((4, 512, 256), F32),
        vmem((128, 256), F32),
        vmem((128, 256), BF16),
        vmem((4, 512, 256), F32),
        vmem((2, 2, 4, 16, 256), F32),
        vmem((2, 4, 64, 256), BF16),
        vmem((2, 16, 256), F32),
        vmem((256, 512), F32),
        vmem((6, wide_count, 1, 128), F32),
        vmem((6, narrow_count, 1, 128), F32),
        vmem((8, 128), F32),
        vmem((wide_count, 32, 128), BF16),
        vmem((narrow_count, 32, 128), BF16),
        vmem((2, 9, 4, 32, 256), BF16),
        vmem((2, 2, 4, 16, 256), BF16),
        vmem((2, 2, 4, 32, 256), BF16),
        vmem((2, 4, 32, 256), BF16),
        vmem((4, 256, 512), F32),
        vmem((9, 256, 512), BF16),
        vmem((3, 4, 10, 16, 256), F32),
        vmem((2, 2, 128, 256), BF16),
        vmem((2, 16, 256), BF16),
        vmem((2, 2, 4, 16, 256), BF16),
        vmem((2, 2, 128, 256), BF16),
        vmem((2, 4, 16, 256), BF16),
        vmem((112, 256), BF16),
        vmem((96, 256), BF16),
        vmem((4, 16, 256), BF16),
        vmem((16, 512), BF16),
        vmem((8, 16, 512), BF16),
        vmem((112, 512), BF16),
        vmem((96, 512), BF16),
        vmem((4, 16, 512), BF16),
        vmem((16, 512), BF16),
        vmem((8, 16, 512), BF16),
        vmem((8, 512), F32),
        vmem((8, 8, 512), F32),
        vmem((112, 512), BF16),
        vmem((96, 512), BF16),
        vmem((4, 16, 512), BF16),
        pltpu.SemaphoreType.DMA((20,)),
        pltpu.SemaphoreType.DMA((5,)),
        pltpu.SemaphoreType.DMA((14,)),
        pltpu.SemaphoreType.DMA((14,)),
        pltpu.SemaphoreType.DMA((16,)),
        pltpu.SemaphoreType.DMA((16,)),
    ]
    output, grad = pl.pallas_call(
        functools.partial(kernel, wide_count, narrow_count),
        out_shape=(
            jax.ShapeDtypeStruct((4, 512, 256), BF16),
            jax.ShapeDtypeStruct((4, 512, 256), F32),
        ),
        in_specs=[anywhere] * 17,
        out_specs=(anywhere, anywhere),
        scratch_shapes=scratch,
        compiler_params=pltpu.CompilerParams(
            collective_id=0, has_side_effects=True, vmem_limit_bytes=56 * 2**20
        ),
        name="whole_net",
    )(
        fine_input,
        gain_fine.reshape(1, 256),
        kernel_fine.reshape(9, 256, 256),
        down_mid,
        gain_mid.reshape(1, 512),
        kernel_mid.reshape(9, 512, 512),
        down_coarse,
        gain_coarse.reshape(1, 512),
        kernel_coarse.reshape(9, 512, 512),
        up_coarse,
        up_mid,
        grad_out,
        *tables(),
    )
    return output.reshape(4, 32, 16, 256), grad.reshape(4, 32, 16, 256)


def solution(mesh):
    tile = P(None, "wide", "narrow", None)
    return jax.shard_map(
        shards,
        mesh=mesh,
        in_specs=(tile,) + (P(),) * 10 + (tile,),
        out_specs=(tile, tile),
        check_vma=False,
    )
```

```python
import functools

import jax
import jax.numpy as jnp
import numpy as np
from jax import lax
from jax.experimental import pallas as pl
from jax.experimental.pallas import tpu as pltpu
from jax.sharding import PartitionSpec as P

MESH = pl.DeviceIdType.MESH
GROUPS = 32
epsilon = 1e-05
F32 = jnp.float32
BF16 = jnp.bfloat16

DIRS = ((0, 0), (-1, 0), (1, 0), (0, -1), (0, 1), (-1, -1), (-1, 1), (1, -1), (1, 1))

ABOVE, BELOW, LEFT, RIGHT, CORNER = 128, 144, 160, 192, 224


def mid_row(f, i, j):
    if 0 <= i < 8 and 0 <= j < 4:
        return 32 * f + 4 * i + j
    if i < 0 and 0 <= j < 4:
        return ABOVE + 4 * f + j
    if i > 7 and 0 <= j < 4:
        return BELOW + 4 * f + j
    if 0 <= i < 8:
        return (LEFT if j < 0 else RIGHT) + 8 * f + i
    return CORNER + 4 * (2 * (i > 7) + (j > 3)) + f


def coarse_row(f, i, side):
    down = -1 if i < 0 else (1 if i > 1 else 0)
    return 8 * DIRS.index((down, side)) + 2 * f + i % 2


def tables():
    pick = np.zeros((96, 512), np.float32)
    for i in range(32):
        for j in range(16):
            pick[4 * (i // 4) + j // 4, 16 * i + j] = 1
        pick[32 + i, 16 * i + 15] = 1
        pick[64 + i, 16 * i] = 1
    enlarge = np.zeros((512, 256), np.float32)
    taps = np.zeros((1152, 256), np.float32)
    ends = np.zeros((16, 256), np.float32)
    pack = np.zeros((112, 128), np.float32)
    pool = np.zeros((16, 128), np.float32)
    coarse_taps = np.zeros((144, 128), np.float32)
    spread = np.zeros((256, 128), np.float32)
    for f in range(4):
        for i in range(8):
            for j in range(16):
                enlarge[128 * f + 16 * i + j, mid_row(f, i, j // 4)] = 1
        for c in range(4):
            low, first = c < 2, c % 2 == 1
            ends[4 * c + f, 128 * first + 32 * f + 31 * low] = 1
            pack[96 + 4 * c + f, mid_row(f, 7 * low, 3 * (not first))] = 1
        for i in range(8):
            for j in range(4):
                here = 32 * f + 4 * i + j
                pool[2 * f + i // 4, here] = 1
                for t in range(9):
                    taps[128 * t + here, mid_row(f, i + t // 3 - 1, j + t % 3 - 1)] = 1
            pack[32 + 8 * f + i, mid_row(f, i, 3)] = 1
            pack[64 + 8 * f + i, mid_row(f, i, 0)] = 1
        for j in range(4):
            pack[4 * f + j, mid_row(f, 7, j)] = 1
            pack[16 + 4 * f + j, mid_row(f, 0, j)] = 1
        for i in range(2):
            for t in range(9):
                coarse_taps[16 * t + 2 * f + i, coarse_row(f, i + t // 3 - 1, t % 3 - 1)] = 1
        for i in range(-1, 9):
            for j in range(-1, 5):
                side = -1 if j < 0 else (1 if j > 3 else 0)
                spread[mid_row(f, i, j), coarse_row(f, i // 4 if i < 8 else 2, side)] = 1
    windows = np.zeros((288, 640), np.float32)
    for t in range(9):
        for i in range(32):
            for j in range(16):
                p, q = i + 1 - t // 3, j + 1 - t % 3
                row = 32 * t + 4 * (i // 4) + j // 4
                if 0 <= p < 32 and 0 <= q < 16:
                    at = 16 * p + q
                elif 0 <= q < 16:
                    at = (512 if p < 0 else 528) + q
                elif 0 <= p < 32:
                    at = (544 if q < 0 else 576) + p
                else:
                    at = 608 + 2 * (p > 31) + (q > 15)
                windows[row, at] = 1
    stretch = np.zeros((640, 768), np.float32)
    for f in range(4):
        for i in range(10):
            for j in range(16):
                for b in range(3):
                    at = 256 * b + mid_row(f, i - 1, (j + b - 1) // 4)
                    stretch[160 * f + 16 * i + j, at] = 1
    by_frame = np.zeros((128, 128), np.float32)
    for f in range(4):
        for c in range(4):
            by_frame[32 * f + c, 4 * c + f] = 1
    sides = np.zeros((512, 128), np.float32)
    for i in range(32):
        sides[16 * i, i] = 1
        sides[16 * i + 15, 64 + i] = 1
    wide_table = np.concatenate([pick, np.concatenate([enlarge, enlarge], axis=1)])
    middle_table = np.concatenate([taps, ends])
    narrow_table = np.concatenate([pack, pool, coarse_taps, spread, sides, by_frame])
    result = (wide_table, middle_table, narrow_table, windows, stretch)
    return [jnp.asarray(t, BF16) for t in result]


def dot(a, b):
    return jnp.dot(a, b, preferred_element_type=F32)


def dot_t(a, b):
    return lax.dot_general(a, b, (((1,), (1,)), ((), ())), preferred_element_type=F32)


def dot_first(a, b):
    return lax.dot_general(a, b, (((0,), (0,)), ((), ())), preferred_element_type=F32)


def group_lanes(t, size):
    lane = lax.broadcasted_iota(jnp.int32, t.shape, 1)
    step = 1
    while step < size:
        t = t + jnp.where(
            (lane & step) != 0, pltpu.roll(t, step, 1), pltpu.roll(t, 128 - step, 1)
        )
        step *= 2
    return t


def halves(t):
    high = t.astype(BF16)
    return high, (t - high.astype(F32)).astype(BF16)


def kernel(
    wide_count,
    narrow_count,
    x_in,
    gain_fine_in,
    kernel_fine_in,
    down_mid_in,
    gain_mid_in,
    kernel_mid_in,
    down_coarse_in,
    gain_coarse_in,
    kernel_coarse_in,
    up_coarse_in,
    up_mid_in,
    grad_in,
    wide_table_in,
    middle_table_in,
    narrow_table_in,
    windows_in,
    stretch_in,
    out_ref,
    grad_ref,
    xg,
    kernel_fine,
    down_mid,
    kernel_mid,
    down_coarse,
    kernel_coarse,
    up_coarse,
    up_mid,
    gain_fine,
    gain_mid,
    gain_coarse,
    wide_table,
    middle_table,
    narrow_table,
    windows,
    stretch,
    columns,
    fine_block,
    grad_buf,
    conv_grad,
    pooled_x,
    summed,
    fine_slope,
    edge_rows,
    edge_sides,
    edge_ends,
    summed_grad,
    first,
    second,
    rows,
    first_matrix,
    second_matrix,
    window_sums,
    rim_rows,
    rim_sides,
    rim_ends,
    matrix_sum,
    through,
    mixed,
    stretched,
    col_pack,
    cor_pack,
    row_in,
    col_in,
    cor_in,
    sum_pack,
    sum_in,
    sum_cor,
    cgrad_own,
    cgrad_in,
    mid_pack,
    mid_halo,
    mid_cor,
    coarse_own,
    coarse_halo,
    coarse_u,
    coarse_u_halo,
    u_pack,
    u_halo,
    u_cor,
    load_sem,
    out_sem,
    total_send,
    total_recv,
    halo_send,
    halo_recv,
):
    wide, narrow = lax.axis_index("wide"), lax.axis_index("narrow")

    def around(index, step, count):
        moved = index + step
        if isinstance(step, int) and step < 0:
            return jnp.where(moved < 0, moved + count, moved)
        return jnp.where(moved >= count, moved - count, moved)

    def device(down, side):
        return (
            wide if isinstance(down, int) and down == 0 else around(wide, down, wide_count),
            narrow if isinstance(side, int) and side == 0 else around(narrow, side, narrow_count),
        )

    loads = {}
    pairs = (
        ("x0", x_in.at[0], xg.at[0, 0]),
        ("x1", x_in.at[1], xg.at[0, 1]),
        ("x2", x_in.at[2], xg.at[0, 2]),
        ("x3", x_in.at[3], xg.at[0, 3]),
        ("grad", grad_in, xg.at[1]),
        ("wide_table", wide_table_in, wide_table),
        ("middle_table", middle_table_in, middle_table),
        ("narrow_table", narrow_table_in, narrow_table),
        ("gain_fine", gain_fine_in, gain_fine),
        ("windows", windows_in, windows),
        ("kernel_fine", kernel_fine_in, kernel_fine),
        ("up_mid", up_mid_in, up_mid),
        ("up_coarse", up_coarse_in, up_coarse),
        ("down_mid", down_mid_in, down_mid),
        ("gain_mid", gain_mid_in, gain_mid),
        ("kernel_coarse", kernel_coarse_in, kernel_coarse),
        ("kernel_mid", kernel_mid_in, kernel_mid),
        ("down_coarse", down_coarse_in, down_coarse),
        ("gain_coarse", gain_coarse_in, gain_coarse),
        ("stretch", stretch_in, stretch),
    )
    for number, (name, source, target) in enumerate(pairs):
        loads[name] = pltpu.make_async_copy(source, target, load_sem.at[number])

    def begin_loads(*names):
        for name in names:
            loads[name].start()

    begin_loads("x0", "x1", "x2", "x3", "wide_table", "middle_table")

    barrier = pltpu.get_barrier_semaphore()
    greeted = 0
    for down in range(wide_count):
        for side in range(-2, narrow_count - 2):
            near = (down <= 1 or down == wide_count - 1) and abs(side) <= 1
            if (down, side) != (0, 0) and (down == 0 or side == 0 or near):
                pl.semaphore_signal(
                    barrier, inc=1, device_id=device(down, side), device_id_type=MESH
                )
                greeted += 1

    def send(source, target, which, down, side):
        pltpu.make_async_remote_copy(
            src_ref=source,
            dst_ref=target,
            send_sem=halo_send.at[which],
            recv_sem=halo_recv.at[which],
            device_id=device(down, side),
            device_id_type=MESH,
        ).start()

    def arrived(buffer, which):
        pltpu.make_async_copy(buffer, buffer, halo_recv.at[which]).wait()

    def sent(buffer, which):
        pltpu.make_async_copy(buffer, buffer, halo_send.at[which]).wait()

    firsts = tuple(first.at[p] for p in range(6)) + (first_matrix,)
    seconds = tuple(second.at[p] for p in range(6)) + (second_matrix,)

    def total_send_wide(phase):
        mine = firsts[phase].at[wide]

        @pl.loop(1, wide_count)
        def _(step):
            pltpu.make_async_remote_copy(
                src_ref=mine,
                dst_ref=mine,
                send_sem=total_send.at[2 * phase],
                recv_sem=total_recv.at[2 * phase],
                device_id=device(step, 0),
                device_id_type=MESH,
            ).start()

    def diagonal(shape=(8, 128)):
        lane = lax.broadcasted_iota(jnp.int32, shape, 1) & 7
        return lane == lax.broadcasted_iota(jnp.int32, shape, 0)

    def total_begin(phase, one, two):
        channels = one.shape[1]
        if channels < 512:
            rows[...] = jnp.zeros((8, 128), F32)
        for n, value in enumerate((one, two)):
            for k in range(channels // 128):
                rows[4 * n + k : 4 * n + k + 1, :] = value[:, 128 * k : 128 * k + 128]
        grouped = group_lanes(rows[...], channels // GROUPS)
        grouped = jnp.where(diagonal(), grouped, 0.0)
        firsts[phase][wide] = jnp.sum(grouped, axis=0, keepdims=True)
        total_send_wide(phase)

    def total_middle(phase):
        whole = firsts[phase].at[pl.ds(0, wide_count - 1)]
        pltpu.make_async_copy(whole, whole, total_recv.at[2 * phase]).wait()
        summed_up = jnp.sum(firsts[phase][...].astype(F32), axis=0)
        seconds[phase][narrow] = summed_up.astype(seconds[phase].dtype)
        mine = seconds[phase].at[narrow]

        @pl.loop(1, narrow_count)
        def _(step):
            pltpu.make_async_remote_copy(
                src_ref=mine,
                dst_ref=mine,
                send_sem=total_send.at[2 * phase + 1],
                recv_sem=total_recv.at[2 * phase + 1],
                device_id=device(0, step),
                device_id_type=MESH,
            ).start()

    def total_sum(phase):
        whole = seconds[phase].at[pl.ds(0, narrow_count - 1)]
        pltpu.make_async_copy(whole, whole, total_recv.at[2 * phase + 1]).wait()
        return jnp.sum(seconds[phase][...].astype(F32), axis=0)

    def row_of(t, start, channels):
        return jnp.concatenate([t[start + k : start + k + 1] for k in range(channels // 128)], axis=1)

    def total_groups(phase, channels, scale):
        packed = jnp.broadcast_to(total_sum(phase), (8, 128))
        t = group_lanes(jnp.where(diagonal(), packed, 0.0), 8) * scale
        return row_of(t, 0, channels), row_of(t, 4, channels)

    def total_end(phase, channels, cells):
        return total_groups(phase, channels, 1.0 / (channels // GROUPS * cells))

    has_above, has_below = wide > 0, wide < wide_count - 1
    has_left, has_right = narrow > 0, narrow < narrow_count - 1
    has_corner = (
        jnp.logical_and(has_above, has_left),
        jnp.logical_and(has_above, has_right),
        jnp.logical_and(has_below, has_left),
        jnp.logical_and(has_below, has_right),
    )
    exists = (None, has_above, has_below, has_left, has_right) + has_corner

    def only(condition, value):
        return value * jnp.where(condition, 1.0, 0.0).astype(F32)

    def corners(read, change, masked):
        result = None
        for c in range(4):
            value = change(read(c).astype(F32))
            if masked:
                value = only(has_corner[c], value)
            cell = lax.broadcasted_iota(jnp.int32, value.shape, 0)
            result = value if result is None else jnp.where(cell >= 4 * c, value, result)
        return result

    def mid_extended(own, read_halo, read_cor, change, masked):
        pieces = [change(own)]
        halo = change(read_halo.astype(F32))
        for low, high, d in ((0, 16, 1), (16, 32, 2), (32, 64, 3), (64, 96, 4)):
            piece = halo[low:high]
            pieces.append(only(exists[d], piece) if masked else piece)
        pieces.append(corners(read_cor, change, masked))
        pieces.append(jnp.zeros((16, own.shape[1]), F32))
        return jnp.concatenate(pieces, axis=0)

    def send_mid(pack, halo, cor, which):
        send(pack.at[pl.ds(0, 16)], halo.at[pl.ds(0, 16)], which, 1, 0)
        send(pack.at[pl.ds(16, 16)], halo.at[pl.ds(16, 16)], which, -1, 0)
        send(pack.at[pl.ds(32, 32)], halo.at[pl.ds(32, 32)], which, 0, 1)
        send(pack.at[pl.ds(64, 32)], halo.at[pl.ds(64, 32)], which, 0, -1)
        for c in range(4):
            down, side = DIRS[5 + c]
            send(pack.at[pl.ds(96, 16)], cor.at[c], which + 1, -down, -side)

    def send_coarse(own, halo, which):
        for d in range(1, 9):
            down, side = DIRS[d]
            send(own, halo.at[d - 1], which, -down, -side)

    def coarse_extended(own, halo, change, masked):
        pieces = [change(own)]
        for d in range(1, 9):
            piece = change(halo(d - 1))
            pieces.append(only(exists[d], piece) if masked else piece)
        pieces.append(jnp.zeros((56, own.shape[1]), F32))
        return jnp.concatenate(pieces, axis=0)

    PICK = wide_table.at[pl.ds(0, 96)]
    ENLARGE = wide_table.at[pl.ds(96, 512)]
    TAPS = middle_table.at[pl.ds(0, 1152)]
    ENDS = middle_table.at[pl.ds(1152, 16)]
    PACK = narrow_table.at[pl.ds(0, 112)]
    POOL = narrow_table.at[pl.ds(112, 16)]
    COARSE_TAPS = narrow_table.at[pl.ds(128, 144)]
    SPREAD = narrow_table.at[pl.ds(272, 256)]
    SIDES = narrow_table.at[pl.ds(528, 512)]
    BY_FRAME = narrow_table.at[pl.ds(1040, 128)]

    def frame(which, f):
        return xg[which, f].reshape(512, 256)

    blank = jnp.zeros((8, 256), F32)
    one, two = blank, blank
    for f in range(4):
        loads["x%d" % f].wait()
        value = frame(0, f).astype(F32)
        one += jnp.sum(value.reshape(64, 8, 256), axis=0)
        two += jnp.sum((value * value).reshape(64, 8, 256), axis=0)
    pl.semaphore_wait(barrier, greeted)
    total_begin(0, jnp.sum(one, axis=0, keepdims=True), jnp.sum(two, axis=0, keepdims=True))

    begin_loads("grad", "narrow_table", "gain_fine", "windows", "kernel_fine")
    begin_loads("up_mid", "up_coarse", "down_mid", "gain_mid")

    def rim_rows_out(which):
        send(xg.at[which, :, 31], row_in.at[0, which], 13 * which, 1, 0)
        send(xg.at[which, :, 0], row_in.at[1, which], 13 * which, -1, 0)

    def rim_pick(which):
        for f in range(4):
            picked = dot(PICK[...], frame(which, f))
            if which == 0:
                pooled_x[32 * f : 32 * f + 32] = picked[0:32]
            picked = picked.astype(BF16)
            col_pack[0, which, 32 * f : 32 * f + 32] = picked[32:64]
            col_pack[1, which, 32 * f : 32 * f + 32] = picked[64:96]
            if which == 1:
                summed[32 * f : 32 * f + 32] = picked[0:32]

    def rim_sides_out(which):
        send(col_pack.at[0, which], col_in.at[0, which], 13 * which + 1, 0, 1)
        send(col_pack.at[1, which], col_in.at[1, which], 13 * which + 1, 0, -1)

    def rim_ends_out(which):
        ends = jnp.concatenate([col_pack[0, which], col_pack[1, which]], axis=0)
        cor_pack[which] = dot(ENDS[...], ends).astype(BF16)
        for c in range(4):
            down, side = DIRS[5 + c]
            send(cor_pack.at[which], cor_in.at[which, c], 13 * which + 2, -down, -side)

    loads["wide_table"].wait()
    loads["middle_table"].wait()
    rim_rows_out(0)
    rim_pick(0)
    rim_sides_out(0)
    rim_ends_out(0)
    loads["grad"].wait()
    rim_pick(1)
    total_middle(0)
    begin_loads("kernel_mid")
    rim_rows_out(1)
    rim_sides_out(1)
    rim_ends_out(1)
    loads["narrow_table"].wait()

    up_mid_grad = summed[...]
    sum_pack[...] = dot(PACK[...], up_mid_grad).astype(BF16)
    send_mid(sum_pack, sum_in, sum_cor, 3)
    loads["up_mid"].wait()
    high, low = halves(dot_t(up_mid_grad, up_mid[...]))
    up_coarse_grad = (dot(POOL[...], high) + dot(POOL[...], low)).astype(BF16)
    loads["up_coarse"].wait()
    cgrad_own[...] = dot_t(up_coarse_grad, up_coarse[...]).astype(BF16)
    send_coarse(cgrad_own, cgrad_in, 5)

    loads["gain_fine"].wait()
    loads["kernel_fine"].wait()
    loads["down_mid"].wait()

    fine_center, fine_square = total_end(0, 256, 2048 * wide_count * narrow_count)
    fine_inverse = lax.rsqrt(fine_square - fine_center * fine_center + epsilon)
    s_fine = gain_fine[...]

    def silu(center, inverse, scaling):
        gain = 0.5 * inverse * scaling
        shift = -center * gain

        def change(value):
            half = value * gain + shift
            return half * jnp.tanh(half) + half

        return change

    def slope(scaled, scaling):
        half = scaled * (0.5 * scaling)
        bend = jnp.tanh(half)
        return (0.5 * scaling) * (1.0 + bend) * (1.0 + half * (1.0 - bend))

    fine_act = silu(fine_center, fine_inverse, s_fine)

    arrived(row_in.at[:, 0], 0)
    arrived(col_in.at[:, 0], 1)
    arrived(cor_in.at[0], 2)

    def set_edges(kind, above, below, left, right, ends):
        edge_rows[kind, 0] = only(has_above, above)
        edge_rows[kind, 1] = only(has_below, below)
        left = only(has_left, left)
        right = only(has_right, right)
        for f in range(4):
            edge_sides[kind, f, 0:32] = left[32 * f : 32 * f + 32]
            edge_sides[kind, f, 32:64] = right[32 * f : 32 * f + 32]
        edge_ends[kind] = ends

    def place(kind, f, own):
        column = lax.broadcasted_iota(jnp.int32, (32, 16, 256), 1)
        west, east = (
            jnp.broadcast_to(edge_sides[kind, f, 32 * k : 32 * k + 32].reshape(32, 1, 256), (32, 16, 256))
            for k in range(2)
        )
        low = jnp.where(column == 0, west, pltpu.roll(own, 1, 0).reshape(32, 16, 256))
        columns[f, 16:528, 0:256] = low.reshape(512, 256).astype(BF16)
        columns[f, 16:528, 256:512] = own.astype(BF16)
        high = jnp.where(column == 15, east, pltpu.roll(own, 511, 0).reshape(32, 16, 256))
        columns[f, 16:528, 512:768] = high.reshape(512, 256).astype(BF16)
        cell = lax.broadcasted_iota(jnp.int32, (16, 256), 0)
        for k in range(2):
            row = edge_rows[kind, k, f]
            at = slice(528 * k, 528 * k + 16)
            west = edge_ends[kind, pl.ds(8 * k + f, 1), :]
            east = edge_ends[kind, pl.ds(8 * k + 4 + f, 1), :]
            columns[f, at, 0:256] = jnp.where(cell == 0, west, pltpu.roll(row, 1, 0)).astype(BF16)
            columns[f, at, 256:512] = row.astype(BF16)
            columns[f, at, 512:768] = jnp.where(cell == 15, east, pltpu.roll(row, 15, 0)).astype(BF16)

    def side_by_side(pieces):
        return jnp.concatenate(list(pieces), axis=1)

    def fine_taps(f):
        return side_by_side(
            columns[f : f + 2, 16 * a : 16 * a + 512, :].reshape(1024, 768) for a in range(3)
        )

    def fine_convolve(f):
        taps = side_by_side(columns[f, 16 * a : 16 * a + 512, :] for a in range(3))
        return dot(taps, kernel_fine[...].reshape(2304, 256))

    def fine_convolve_back(f):
        return dot_t(fine_taps(f), side_by_side(kernel_fine[8 - t] for t in range(9)))

    def fine_scaled(value):
        return (value - fine_center) * fine_inverse

    def fine_value(f):
        return frame(0, f).astype(F32)

    def set_fields(n, change):
        for k in range(2):
            rim_rows[n, k] = only(exists[1 + k], change(row_in[k, 0].astype(F32))).astype(BF16)
            sides = only(exists[3 + k], change(col_in[k, 0].astype(F32))).astype(BF16)
            rim_sides[n, k] = sides.reshape(4, 32, 256)
        ends = corners(lambda c: cor_in[0, c], change, True)
        ends = dot(BY_FRAME[:, 0:16], ends.astype(BF16)).astype(BF16)
        rim_ends[n] = ends.reshape(4, 32, 256)

    def window(n, f, own):
        field = jnp.concatenate(
            [
                own.astype(BF16),
                rim_rows[n, 0, f],
                rim_rows[n, 1, f],
                rim_sides[n, 0, f],
                rim_sides[n, 1, f],
                rim_ends[n, f],
            ],
            axis=0,
        )
        return dot(windows[...], field)

    set_fields(0, fine_act)
    loads["windows"].wait()

    @pl.loop(0, 4)
    def _(f):
        sums = window(0, f, fine_act(fine_value(f)))
        high, low = halves(sums)
        window_sums[0, :, f] = high.reshape(9, 32, 256)
        window_sums[1, :, f] = low.reshape(9, 32, 256)

    both = side_by_side(
        jnp.concatenate([window_sums[n, 8 - t].reshape(128, 256) for n in range(2)], axis=0)
        for t in range(9)
    )
    both = dot(both, kernel_fine[...].reshape(2304, 256))
    pooled = pooled_x[...] + both[0:128] + both[128:256]
    pooled = (pooled * 0.0625).astype(BF16)

    def fine_forward(f):
        value = fine_value(f)
        place(0, f, fine_act(value))
        fine_block[f] = (value + fine_convolve(f)).astype(BF16)

    def same(value):
        return value

    mid_in = dot(pooled, down_mid[...]).astype(BF16)
    mid_value = mid_in.astype(F32)

    def column_sums(value):
        return jnp.sum(value, axis=0, keepdims=True)

    total_begin(1, column_sums(mid_value), column_sums(mid_value * mid_value))
    mid_pack[...] = dot(PACK[...], mid_in).astype(BF16)
    send_mid(mid_pack, mid_halo, mid_cor, 6)
    begin_loads("down_coarse", "gain_coarse", "kernel_coarse", "stretch")

    @pl.loop(0, 4)
    def _(f):
        fine_slope[f] = slope(fine_scaled(fine_value(f)), s_fine)

    set_fields(0, lambda v: slope(fine_scaled(v), s_fine))
    set_fields(1, lambda v: slope(fine_scaled(v), s_fine) * fine_scaled(v))

    set_edges(
        0,
        fine_act(row_in[0, 0].astype(F32)),
        fine_act(row_in[1, 0].astype(F32)),
        fine_act(col_in[0, 0].astype(F32)),
        fine_act(col_in[1, 0].astype(F32)),
        corners(lambda c: cor_in[0, c], fine_act, True),
    )
    fine_forward(0)
    total_middle(1)
    fine_forward(1)

    @pl.loop(0, 4)
    def _(f):
        bent = fine_slope[f]
        window_sums[0, :, f] = window(0, f, bent).astype(BF16).reshape(9, 32, 256)
        bent = bent * fine_scaled(fine_value(f))
        window_sums[1, :, f] = window(1, f, bent).astype(BF16).reshape(9, 32, 256)

    loads["gain_mid"].wait()
    loads["kernel_mid"].wait()
    mid_center, mid_square = total_end(1, 512, 128 * wide_count * narrow_count)
    mid_inverse = lax.rsqrt(mid_square - mid_center * mid_center + epsilon)
    s_mid = gain_mid[...]

    mid_act = silu(mid_center, mid_inverse, s_mid)

    def mid_scaled(value):
        return (value - mid_center) * mid_inverse

    def mid_convolve(extended, product, weights):
        taps = dot(TAPS[...], extended.astype(BF16)).astype(BF16)
        return product(side_by_side(taps[128 * t : 128 * t + 128] for t in range(9)), weights)

    arrived(mid_halo, 6)
    arrived(mid_cor, 7)
    mid_block = (
        mid_value
        + mid_convolve(
            mid_extended(mid_value, mid_halo[...], lambda c: mid_cor[c], mid_act, True),
            dot,
            kernel_mid[...].reshape(4608, 512),
        )
    ).astype(BF16)

    loads["down_coarse"].wait()
    mid_pooled = (dot(POOL[...], mid_block) * 0.0625).astype(BF16)
    coarse_in = dot(mid_pooled, down_coarse[...]).astype(BF16)
    coarse_own[...] = coarse_in
    coarse_value = coarse_in.astype(F32)[0:8]
    total_begin(2, column_sums(coarse_value), column_sums(coarse_value * coarse_value))
    send_coarse(coarse_own, coarse_halo, 8)

    arrived(row_in.at[:, 1], 13)
    arrived(col_in.at[:, 1], 14)
    arrived(cor_in.at[1], 15)
    set_edges(
        1,
        row_in[0, 1].astype(F32),
        row_in[1, 1].astype(F32),
        col_in[0, 1].astype(F32),
        col_in[1, 1].astype(F32),
        corners(lambda c: cor_in[1, c], same, True),
    )

    def convolve_grad(f):
        for k in range(2):
            place(1, f + k, frame(1, f + k).astype(F32))
        result = fine_convolve_back(f).reshape(2, 512, 256)
        for k in range(2):
            conv_grad[f + k] = result[k]
            weighted = result[k] * fine_slope[f + k]
            scaled = fine_scaled(fine_value(f + k))
            grad_sums[0] += jnp.sum(weighted.reshape(64, 8, 256), axis=0)
            grad_sums[1] += jnp.sum((weighted * scaled).reshape(64, 8, 256), axis=0)

    grad_sums = [blank, blank]
    convolve_grad(0)
    total_middle(2)

    arrived(cgrad_in, 5)
    loads["kernel_coarse"].wait()

    def coarse_convolve(extended, product, weights):
        taps = dot(COARSE_TAPS[...], extended.astype(BF16)).astype(BF16)
        return product(side_by_side(taps[16 * t : 16 * t + 16] for t in range(9)), weights)

    cgrad = cgrad_own[...].astype(F32)[0:8]
    coarse_act_grad = coarse_convolve(
        coarse_extended(cgrad, lambda d: cgrad_in[d].astype(F32)[0:8], same, True),
        dot_t,
        side_by_side(kernel_coarse[8 - t] for t in range(9)),
    )[0:8]

    @pl.loop(0, 9)
    def _(t):
        through[t] = (0.0625 * dot(kernel_fine[8 - t], down_mid[...])).astype(BF16)

    arrived(sum_in, 3)
    arrived(sum_cor, 4)
    sum_extended = mid_extended(
        up_mid_grad.astype(F32), sum_in[...], lambda c: sum_cor[c], same, True
    )
    summed_grad[...] = dot_t(sum_extended.astype(BF16), up_mid[...])

    loads["gain_coarse"].wait()
    coarse_center, coarse_square = total_end(2, 512, 8 * wide_count * narrow_count)
    coarse_inverse = lax.rsqrt(coarse_square - coarse_center * coarse_center + epsilon)
    s_coarse = gain_coarse[...]

    def coarse_scaled(value):
        return (value - coarse_center) * coarse_inverse

    scaled = coarse_scaled(coarse_value)
    normed_grad = coarse_act_grad * slope(scaled, s_coarse)
    total_begin(3, column_sums(normed_grad), column_sums(normed_grad * scaled))
    coarse_u[...] = cgrad + coarse_inverse * normed_grad
    send_coarse(coarse_u, coarse_u_halo, 9)
    convolve_grad(2)

    total_middle(3)

    mid_mix = jnp.concatenate(
        [mid_scaled(mid_value).astype(BF16), jnp.ones((128, 128), BF16)], axis=1
    )
    for n in range(2):
        sums = side_by_side(window_sums[n, t].reshape(128, 256) for t in range(9))
        mixed[n] = dot_first(sums, mid_mix).astype(BF16).reshape(9, 256, 640)

    @pl.loop(0, 16)
    def _(part):
        here = pl.ds(pl.multiple_of(16 * part, 16), 16)
        totals = [jnp.zeros((16, 512), F32) for _ in range(4)]
        for t in range(9):
            weight = through[t, here, :].astype(F32)
            for n in range(2):
                value = mixed[n, t, here, :].astype(F32)
                totals[2 * n] += weight * side_by_side([value[:, 512:640]] * 4)
                totals[2 * n + 1] += weight * value[:, 0:512]
        for n in range(4):
            matrix_sum[n, here, :] = totals[n]

    def iota(shape, axis):
        return lax.broadcasted_iota(jnp.int32, shape, axis)

    def one_hot(condition):
        return jnp.where(condition, 1.0, 0.0).astype(BF16)

    by_group = one_hot((iota((32, 256), 1) >> 3) == iota((32, 256), 0))
    matrix = jnp.zeros((32, 128), F32)
    for n in range(4):
        high, low = halves(matrix_sum[n] * mid_inverse)
        high, low = halves(dot(by_group, high) + dot(by_group, low))
        to_lane = one_hot(iota((512, 128), 1) == 32 * n + (iota((512, 128), 0) >> 4))
        matrix += dot(high, to_lane) + dot(low, to_lane)
    first_matrix[wide] = matrix.astype(BF16)
    total_send_wide(6)

    first_mean, second_mean = total_end(3, 512, 8 * wide_count * narrow_count)
    arrived(coarse_halo, 8)
    arrived(coarse_u_halo, 9)
    offset = coarse_inverse * first_mean
    factor = coarse_inverse * second_mean
    pieces = [coarse_u[...] - offset - scaled * factor]
    for d in range(8):
        piece = coarse_scaled(coarse_halo[d].astype(F32)[0:8])
        pieces.append(coarse_u_halo[d] - offset - piece * factor)
    pieces.append(jnp.zeros((56, 512), F32))
    coarse_in_grad = jnp.concatenate(pieces, axis=0).astype(BF16)

    mid_pool_grad = dot_t(dot(SPREAD[...], coarse_in_grad).astype(BF16), down_coarse[...])
    row = lax.broadcasted_iota(jnp.int32, (256, 128), 0)
    keep = jnp.where(row < ABOVE, 1.0, 0.0)
    bounds = ((ABOVE, 16, 1), (BELOW, 16, 2), (LEFT, 32, 3), (RIGHT, 32, 4)) + tuple(
        (CORNER + 4 * c, 4, 5 + c) for c in range(4)
    )
    for start, size, d in bounds:
        inside = jnp.logical_and(row >= start, row < start + size)
        keep = jnp.where(inside, jnp.where(exists[d], 1.0, 0.0).astype(F32), keep)
    mid_grad = (summed_grad[...] + 0.0625 * mid_pool_grad) * jnp.concatenate([keep] * 4, axis=1)
    mid_act_grad = mid_convolve(
        mid_grad, dot_t, side_by_side(kernel_mid[8 - t] for t in range(9))
    )
    scaled = mid_scaled(mid_value)
    normed_grad = mid_act_grad * slope(scaled, s_mid)
    total_begin(4, column_sums(normed_grad), column_sums(normed_grad * scaled))
    mid_u = mid_grad[0:128].astype(BF16).astype(F32) + mid_inverse * normed_grad
    u_pack[...] = dot(PACK[...], mid_u.astype(BF16)).astype(BF16)
    send_mid(u_pack, u_halo, u_cor, 10)
    pulled = (0.0625 * dot_t(mid_u.astype(BF16), down_mid[...])).astype(BF16)
    fine_sums = [jnp.sum(value, axis=0, keepdims=True) for value in grad_sums]
    for t in range(9):
        term = dot_t(pulled, kernel_fine[8 - t])
        for n in range(2):
            fine_sums[n] += column_sums(window_sums[n, t].reshape(128, 256).astype(F32) * term)
    total_begin(5, *fine_sums)
    total_middle(6)

    coarse_block = (
        coarse_in.astype(F32)
        + coarse_convolve(
            coarse_extended(
                coarse_value,
                lambda d: coarse_halo[d].astype(F32)[0:8],
                silu(coarse_center, coarse_inverse, s_coarse),
                True,
            ),
            dot,
            kernel_coarse[...].reshape(4608, 512),
        )
    ).astype(BF16)
    coarse_up = dot(coarse_block, up_coarse[...]).astype(BF16)
    mid_sum = (mid_block.astype(F32) + dot(SPREAD[0:128, 0:16], coarse_up)).astype(BF16)
    mid_up = dot(mid_sum, up_mid[...]).astype(BF16)
    total_middle(4)
    total_middle(5)

    fine_forward(2)
    fine_forward(3)
    mid_up = dot(ENLARGE[:, 0:128], mid_up).reshape(4, 8, 1, 16, 256)
    for f in range(4):
        block = fine_block[f].astype(F32).reshape(8, 4, 16, 256)
        fine_block[f] = (block + mid_up[f]).astype(BF16).reshape(512, 256)
    out_copy = pltpu.make_async_copy(fine_block, out_ref, out_sem.at[0])
    out_copy.start()
    first_mean, second_mean = total_end(4, 512, 128 * wide_count * narrow_count)
    arrived(u_halo, 10)
    arrived(u_cor, 11)
    offset = mid_inverse * first_mean
    factor = mid_inverse * second_mean
    mid_in_grad = mid_extended(
        mid_u, u_halo[...], lambda c: u_cor[c], lambda v: v - offset, False
    ) - factor * mid_extended(
        mid_value, mid_halo[...], lambda c: mid_cor[c], mid_scaled, False
    )

    pool_grad = 0.0625 * dot_t(mid_in_grad.astype(BF16), down_mid[...])
    pool_grad = pool_grad * jnp.concatenate([keep] * 2, axis=1)
    high, low = halves(pool_grad)
    added = dot(ENLARGE[...], jnp.concatenate([high[0:256], low[0:256]], axis=0))
    loads["stretch"].wait()
    for a in range(3):
        fields = [dot_t(high, kernel_fine[8 - 3 * a - b]).astype(BF16) for b in range(3)]
        stretched[a] = dot(stretch[...], jnp.concatenate(fields, axis=0)).reshape(4, 10, 16, 256)

    means = jnp.zeros((8, 128), F32)
    for n, mean in enumerate((first_mean, second_mean)):
        lane, row = iota((512, 128), 1), iota((512, 128), 0)
        inside = jnp.logical_and((lane & 31) == (row >> 4), ((lane >> 5) & 1) == n)
        to_lane = jnp.where(inside, 0.0625, 0.0).astype(BF16)
        high, low = halves(jnp.broadcast_to(mean, (8, 512)))
        means += dot(high, to_lane) + dot(low, to_lane)
    matrix_high, matrix_low = halves(total_sum(6))
    fine_totals = total_groups(5, 256, 1.0)
    spread_groups = one_hot((iota((256, 32), 0) >> 3) == iota((256, 32), 1))
    fine_means = []
    for n in range(2):
        half = jnp.where((iota((8, 128), 1) >> 6) == n, means, 0.0)
        high, low = halves(half)
        change = dot_t(high, matrix_high) + dot_t(low, matrix_high) + dot_t(high, matrix_low)
        high, low = halves(change)
        change = dot_t(high, spread_groups) + dot_t(low, spread_groups)
        fine_means.append(
            (fine_totals[n] - change[0:1]) * (1.0 / (8 * 2048 * wide_count * narrow_count))
        )
    slant = -fine_inverse * fine_inverse * fine_means[1]
    shift = -fine_inverse * fine_means[0] - fine_center * slant

    added = added.reshape(4, 8, 1, 16, 256)
    grad_copies = []
    for f in range(4):
        above, here, below = stretched[0, f], stretched[1, f], stretched[2, f]
        centre = here[1:9] + above[1:9] + below[1:9]
        top = here[1:9] + above[0:8] + below[1:9]
        bottom = here[1:9] + above[1:9] + below[2:10]
        back = jnp.stack([top, centre, centre, bottom], axis=1).reshape(512, 256)
        normed_grad = (conv_grad[f] + back) * fine_slope[f]
        grad = xg[1, f].astype(F32).reshape(8, 4, 16, 256) + added[f]
        grad = grad.reshape(512, 256).astype(BF16).astype(F32)
        grad_buf[f] = grad + fine_inverse * normed_grad + (shift + fine_value(f) * slant)
        grad_copies.append(
            pltpu.make_async_copy(grad_buf.at[f], grad_ref.at[f], out_sem.at[1 + f])
        )
        grad_copies[f].start()

    for which in range(2):
        sent(row_in.at[:, which], 13 * which)
        sent(col_in.at[:, which], 13 * which + 1)
        sent(cor_in.at[which], 13 * which + 2)
    sent(sum_in, 3)
    sent(sum_cor, 4)
    sent(cgrad_in, 5)
    sent(mid_halo, 6)
    sent(mid_cor, 7)
    sent(coarse_halo, 8)
    sent(coarse_u_halo, 9)
    sent(u_halo, 10)
    sent(u_cor, 11)
    for phase in range(7):
        whole = firsts[phase].at[pl.ds(0, wide_count - 1)]
        pltpu.make_async_copy(whole, whole, total_send.at[2 * phase]).wait()
        whole = seconds[phase].at[pl.ds(0, narrow_count - 1)]
        pltpu.make_async_copy(whole, whole, total_send.at[2 * phase + 1]).wait()
    out_copy.wait()
    for copy in grad_copies:
        copy.wait()


def shards(*arguments):
    (
        fine_input,
        gain_fine,
        kernel_fine,
        down_mid,
        gain_mid,
        kernel_mid,
        down_coarse,
        gain_coarse,
        kernel_coarse,
        up_coarse,
        up_mid,
        grad_out,
    ) = arguments
    wide_count, narrow_count = lax.axis_size("wide"), lax.axis_size("narrow")
    anywhere = pl.BlockSpec(memory_space=pl.ANY)
    vmem = pltpu.VMEM
    scratch = [
        vmem((2, 4, 32, 16, 256), BF16),
        vmem((9, 256, 256), BF16),
        vmem((256, 512), BF16),
        vmem((9, 512, 512), BF16),
        vmem((512, 512), BF16),
        vmem((9, 512, 512), BF16),
        vmem((512, 512), BF16),
        vmem((512, 256), BF16),
        vmem((1, 256), F32),
        vmem((1, 512), F32),
        vmem((1, 512), F32),
        vmem((608, 512), BF16),
        vmem((1168, 256), BF16),
        vmem((1168, 128), BF16),
        vmem((288, 640), BF16),
        vmem((640, 768), BF16),
        vmem((4, 544, 768), BF16),
        vmem((4, 512, 256), BF16),
        vmem((4, 512, 256), F32),
        vmem((4, 512, 256), F32),
        vmem((128, 256), F32),
        vmem((128, 256), BF16),
        vmem((4, 512, 256), F32),
        vmem((2, 2, 4, 16, 256), F32),
        vmem((2, 4, 64, 256), F32),
        vmem((2, 16, 256), F32),
        vmem((256, 512), F32),
        vmem((6, wide_count, 1, 128), F32),
        vmem((6, narrow_count, 1, 128), F32),
        vmem((8, 128), F32),
        vmem((wide_count, 32, 128), BF16),
        vmem((narrow_count, 32, 128), BF16),
        vmem((2, 9, 4, 32, 256), BF16),
        vmem((2, 2, 4, 16, 256), BF16),
        vmem((2, 2, 4, 32, 256), BF16),
        vmem((2, 4, 32, 256), BF16),
        vmem((4, 256, 512), F32),
        vmem((9, 256, 512), BF16),
        vmem((2, 9, 256, 640), BF16),
        vmem((3, 4, 10, 16, 256), F32),
        vmem((2, 2, 128, 256), BF16),
        vmem((2, 16, 256), BF16),
        vmem((2, 2, 4, 16, 256), BF16),
        vmem((2, 2, 128, 256), BF16),
        vmem((2, 4, 16, 256), BF16),
        vmem((112, 256), BF16),
        vmem((96, 256), BF16),
        vmem((4, 16, 256), BF16),
        vmem((16, 512), BF16),
        vmem((8, 16, 512), BF16),
        vmem((112, 512), BF16),
        vmem((96, 512), BF16),
        vmem((4, 16, 512), BF16),
        vmem((16, 512), BF16),
        vmem((8, 16, 512), BF16),
        vmem((8, 512), F32),
        vmem((8, 8, 512), F32),
        vmem((112, 512), BF16),
        vmem((96, 512), BF16),
        vmem((4, 16, 512), BF16),
        pltpu.SemaphoreType.DMA((20,)),
        pltpu.SemaphoreType.DMA((5,)),
        pltpu.SemaphoreType.DMA((14,)),
        pltpu.SemaphoreType.DMA((14,)),
        pltpu.SemaphoreType.DMA((16,)),
        pltpu.SemaphoreType.DMA((16,)),
    ]
    output, grad = pl.pallas_call(
        functools.partial(kernel, wide_count, narrow_count),
        out_shape=(
            jax.ShapeDtypeStruct((4, 512, 256), BF16),
            jax.ShapeDtypeStruct((4, 512, 256), F32),
        ),
        in_specs=[anywhere] * 17,
        out_specs=(anywhere, anywhere),
        scratch_shapes=scratch,
        compiler_params=pltpu.CompilerParams(
            collective_id=0, has_side_effects=True, vmem_limit_bytes=56 * 2**20
        ),
        name="whole_net",
    )(
        fine_input,
        gain_fine.reshape(1, 256),
        kernel_fine.reshape(9, 256, 256),
        down_mid,
        gain_mid.reshape(1, 512),
        kernel_mid.reshape(9, 512, 512),
        down_coarse,
        gain_coarse.reshape(1, 512),
        kernel_coarse.reshape(9, 512, 512),
        up_coarse,
        up_mid,
        grad_out,
        *tables(),
    )
    return output.reshape(4, 32, 16, 256), grad.reshape(4, 32, 16, 256)


def solution(mesh):
    tile = P(None, "wide", "narrow", None)
    return jax.shard_map(
        shards,
        mesh=mesh,
        in_specs=(tile,) + (P(),) * 10 + (tile,),
        out_specs=(tile, tile),
        check_vma=False,
    )
```

```python
import functools

import jax
import jax.numpy as jnp
import numpy as np
from jax import lax
from jax.experimental import pallas as pl
from jax.experimental.pallas import tpu as pltpu
from jax.sharding import PartitionSpec as P

MESH = pl.DeviceIdType.MESH
GROUPS = 32
epsilon = 1e-05
F32 = jnp.float32
BF16 = jnp.bfloat16

DIRS = ((0, 0), (-1, 0), (1, 0), (0, -1), (0, 1), (-1, -1), (-1, 1), (1, -1), (1, 1))

ABOVE, BELOW, LEFT, RIGHT, CORNER = 128, 144, 160, 192, 224


def mid_row(f, i, j):
    if 0 <= i < 8 and 0 <= j < 4:
        return 32 * f + 4 * i + j
    if i < 0 and 0 <= j < 4:
        return ABOVE + 4 * f + j
    if i > 7 and 0 <= j < 4:
        return BELOW + 4 * f + j
    if 0 <= i < 8:
        return (LEFT if j < 0 else RIGHT) + 8 * f + i
    return CORNER + 4 * (2 * (i > 7) + (j > 3)) + f


def coarse_row(f, i, side):
    down = -1 if i < 0 else (1 if i > 1 else 0)
    return 8 * DIRS.index((down, side)) + 2 * f + i % 2


def tables():
    pick = np.zeros((96, 512), np.float32)
    for i in range(32):
        for j in range(16):
            pick[4 * (i // 4) + j // 4, 16 * i + j] = 1
        pick[32 + i, 16 * i + 15] = 1
        pick[64 + i, 16 * i] = 1
    enlarge = np.zeros((512, 256), np.float32)
    taps = np.zeros((1152, 256), np.float32)
    ends = np.zeros((16, 256), np.float32)
    pack = np.zeros((112, 128), np.float32)
    pool = np.zeros((16, 128), np.float32)
    coarse_taps = np.zeros((144, 128), np.float32)
    spread = np.zeros((256, 128), np.float32)
    for f in range(4):
        for i in range(8):
            for j in range(16):
                enlarge[128 * f + 16 * i + j, mid_row(f, i, j // 4)] = 1
        for c in range(4):
            low, first = c < 2, c % 2 == 1
            ends[4 * c + f, 128 * first + 32 * f + 31 * low] = 1
            pack[96 + 4 * c + f, mid_row(f, 7 * low, 3 * (not first))] = 1
        for i in range(8):
            for j in range(4):
                here = 32 * f + 4 * i + j
                pool[2 * f + i // 4, here] = 1
                for t in range(9):
                    taps[128 * t + here, mid_row(f, i + t // 3 - 1, j + t % 3 - 1)] = 1
            pack[32 + 8 * f + i, mid_row(f, i, 3)] = 1
            pack[64 + 8 * f + i, mid_row(f, i, 0)] = 1
        for j in range(4):
            pack[4 * f + j, mid_row(f, 7, j)] = 1
            pack[16 + 4 * f + j, mid_row(f, 0, j)] = 1
        for i in range(2):
            for t in range(9):
                coarse_taps[16 * t + 2 * f + i, coarse_row(f, i + t // 3 - 1, t % 3 - 1)] = 1
        for i in range(-1, 9):
            for j in range(-1, 5):
                side = -1 if j < 0 else (1 if j > 3 else 0)
                spread[mid_row(f, i, j), coarse_row(f, i // 4 if i < 8 else 2, side)] = 1
    windows = np.zeros((288, 640), np.float32)
    for t in range(9):
        for i in range(32):
            for j in range(16):
                p, q = i + 1 - t // 3, j + 1 - t % 3
                row = 32 * t + 4 * (i // 4) + j // 4
                if 0 <= p < 32 and 0 <= q < 16:
                    at = 16 * p + q
                elif 0 <= q < 16:
                    at = (512 if p < 0 else 528) + q
                elif 0 <= p < 32:
                    at = (544 if q < 0 else 576) + p
                else:
                    at = 608 + 2 * (p > 31) + (q > 15)
                windows[row, at] = 1
    stretch = np.zeros((640, 768), np.float32)
    for f in range(4):
        for i in range(10):
            for j in range(16):
                for b in range(3):
                    at = 256 * b + mid_row(f, i - 1, (j + b - 1) // 4)
                    stretch[160 * f + 16 * i + j, at] = 1
    by_frame = np.zeros((128, 128), np.float32)
    for f in range(4):
        for c in range(4):
            by_frame[32 * f + c, 4 * c + f] = 1
    sides = np.zeros((512, 128), np.float32)
    for i in range(32):
        sides[16 * i, i] = 1
        sides[16 * i + 15, 64 + i] = 1
    wide_table = np.concatenate([pick, np.concatenate([enlarge, enlarge], axis=1)])
    middle_table = np.concatenate([taps, ends])
    narrow_table = np.concatenate([pack, pool, coarse_taps, spread, sides, by_frame])
    result = (wide_table, middle_table, narrow_table, windows, stretch)
    return [jnp.asarray(t, BF16) for t in result]


def dot(a, b):
    return jnp.dot(a, b, preferred_element_type=F32)


def dot_t(a, b):
    return lax.dot_general(a, b, (((1,), (1,)), ((), ())), preferred_element_type=F32)


def dot_first(a, b):
    return lax.dot_general(a, b, (((0,), (0,)), ((), ())), preferred_element_type=F32)


def group_lanes(t, size):
    lane = lax.broadcasted_iota(jnp.int32, t.shape, 1)
    step = 1
    while step < size:
        t = t + jnp.where(
            (lane & step) != 0, pltpu.roll(t, step, 1), pltpu.roll(t, 128 - step, 1)
        )
        step *= 2
    return t


def halves(t):
    high = t.astype(BF16)
    return high, (t - high.astype(F32)).astype(BF16)


def kernel(
    wide_count,
    narrow_count,
    x_in,
    gain_fine_in,
    kernel_fine_in,
    down_mid_in,
    gain_mid_in,
    kernel_mid_in,
    down_coarse_in,
    gain_coarse_in,
    kernel_coarse_in,
    up_coarse_in,
    up_mid_in,
    grad_in,
    wide_table_in,
    middle_table_in,
    narrow_table_in,
    windows_in,
    stretch_in,
    out_ref,
    grad_ref,
    xg,
    kernel_fine,
    down_mid,
    kernel_mid,
    down_coarse,
    kernel_coarse,
    up_coarse,
    up_mid,
    gain_fine,
    gain_mid,
    gain_coarse,
    wide_table,
    middle_table,
    narrow_table,
    windows,
    stretch,
    columns,
    fine_block,
    grad_buf,
    conv_grad,
    pooled_x,
    summed,
    fine_slope,
    edge_rows,
    edge_sides,
    edge_ends,
    summed_grad,
    first,
    second,
    rows,
    first_matrix,
    second_matrix,
    window_sums,
    rim_rows,
    rim_sides,
    rim_ends,
    matrix_sum,
    through,
    stretched,
    col_pack,
    cor_pack,
    row_in,
    col_in,
    cor_in,
    sum_pack,
    sum_in,
    sum_cor,
    cgrad_own,
    cgrad_in,
    mid_pack,
    mid_halo,
    mid_cor,
    coarse_own,
    coarse_halo,
    coarse_u,
    coarse_u_halo,
    u_pack,
    u_halo,
    u_cor,
    load_sem,
    out_sem,
    total_send,
    total_recv,
    halo_send,
    halo_recv,
):
    wide, narrow = lax.axis_index("wide"), lax.axis_index("narrow")

    def around(index, step, count):
        moved = index + step
        if isinstance(step, int) and step < 0:
            return jnp.where(moved < 0, moved + count, moved)
        return jnp.where(moved >= count, moved - count, moved)

    def device(down, side):
        return (
            wide if isinstance(down, int) and down == 0 else around(wide, down, wide_count),
            narrow if isinstance(side, int) and side == 0 else around(narrow, side, narrow_count),
        )

    loads = {}
    pairs = (
        ("x0", x_in.at[0], xg.at[0, 0]),
        ("x1", x_in.at[1], xg.at[0, 1]),
        ("x2", x_in.at[2], xg.at[0, 2]),
        ("x3", x_in.at[3], xg.at[0, 3]),
        ("grad", grad_in, xg.at[1]),
        ("wide_table", wide_table_in, wide_table),
        ("middle_table", middle_table_in, middle_table),
        ("narrow_table", narrow_table_in, narrow_table),
        ("gain_fine", gain_fine_in, gain_fine),
        ("windows", windows_in, windows),
        ("kernel_fine", kernel_fine_in, kernel_fine),
        ("up_mid", up_mid_in, up_mid),
        ("up_coarse", up_coarse_in, up_coarse),
        ("down_mid", down_mid_in, down_mid),
        ("gain_mid", gain_mid_in, gain_mid),
        ("kernel_coarse", kernel_coarse_in, kernel_coarse),
        ("kernel_mid", kernel_mid_in, kernel_mid),
        ("down_coarse", down_coarse_in, down_coarse),
        ("gain_coarse", gain_coarse_in, gain_coarse),
        ("stretch", stretch_in, stretch),
    )
    for number, (name, source, target) in enumerate(pairs):
        loads[name] = pltpu.make_async_copy(source, target, load_sem.at[number])

    def begin_loads(*names):
        for name in names:
            loads[name].start()

    begin_loads("x0", "x1", "x2", "x3", "wide_table", "middle_table")

    barrier = pltpu.get_barrier_semaphore()
    greeted = 0
    for down in range(wide_count):
        for side in range(-2, narrow_count - 2):
            near = (down <= 1 or down == wide_count - 1) and abs(side) <= 1
            if (down, side) != (0, 0) and (down == 0 or side == 0 or near):
                pl.semaphore_signal(
                    barrier, inc=1, device_id=device(down, side), device_id_type=MESH
                )
                greeted += 1

    def send(source, target, which, down, side):
        pltpu.make_async_remote_copy(
            src_ref=source,
            dst_ref=target,
            send_sem=halo_send.at[which],
            recv_sem=halo_recv.at[which],
            device_id=device(down, side),
            device_id_type=MESH,
        ).start()

    def arrived(buffer, which):
        pltpu.make_async_copy(buffer, buffer, halo_recv.at[which]).wait()

    def sent(buffer, which):
        pltpu.make_async_copy(buffer, buffer, halo_send.at[which]).wait()

    firsts = tuple(first.at[p] for p in range(6)) + (first_matrix,)
    seconds = tuple(second.at[p] for p in range(6)) + (second_matrix,)

    def total_send_wide(phase):
        mine = firsts[phase].at[wide]

        for step in sorted(range(1, wide_count), key=lambda k: -min(k & 7, 8 - (k & 7))):
            pltpu.make_async_remote_copy(
                src_ref=mine,
                dst_ref=mine,
                send_sem=total_send.at[2 * phase],
                recv_sem=total_recv.at[2 * phase],
                device_id=device(step, 0),
                device_id_type=MESH,
            ).start()

    def diagonal(shape=(8, 128)):
        lane = lax.broadcasted_iota(jnp.int32, shape, 1) & 7
        return lane == lax.broadcasted_iota(jnp.int32, shape, 0)

    def total_begin(phase, one, two):
        channels = one.shape[1]
        if channels < 512:
            rows[...] = jnp.zeros((8, 128), F32)
        for n, value in enumerate((one, two)):
            for k in range(channels // 128):
                rows[4 * n + k : 4 * n + k + 1, :] = value[:, 128 * k : 128 * k + 128]
        grouped = group_lanes(rows[...], channels // GROUPS)
        grouped = jnp.where(diagonal(), grouped, 0.0)
        firsts[phase][wide] = jnp.sum(grouped, axis=0, keepdims=True)
        total_send_wide(phase)

    def total_middle(phase):
        whole = firsts[phase].at[pl.ds(0, wide_count - 1)]
        pltpu.make_async_copy(whole, whole, total_recv.at[2 * phase]).wait()
        summed_up = jnp.sum(firsts[phase][...].astype(F32), axis=0)
        seconds[phase][narrow] = summed_up.astype(seconds[phase].dtype)
        mine = seconds[phase].at[narrow]

        for step in sorted(range(1, narrow_count), key=lambda k: -min(k & 3, 4 - (k & 3))):
            pltpu.make_async_remote_copy(
                src_ref=mine,
                dst_ref=mine,
                send_sem=total_send.at[2 * phase + 1],
                recv_sem=total_recv.at[2 * phase + 1],
                device_id=device(0, step),
                device_id_type=MESH,
            ).start()

    def total_sum(phase):
        whole = seconds[phase].at[pl.ds(0, narrow_count - 1)]
        pltpu.make_async_copy(whole, whole, total_recv.at[2 * phase + 1]).wait()
        return jnp.sum(seconds[phase][...].astype(F32), axis=0)

    def row_of(t, start, channels):
        return jnp.concatenate([t[start + k : start + k + 1] for k in range(channels // 128)], axis=1)

    def total_groups(phase, channels, scale):
        packed = jnp.broadcast_to(total_sum(phase), (8, 128))
        t = group_lanes(jnp.where(diagonal(), packed, 0.0), 8) * scale
        return row_of(t, 0, channels), row_of(t, 4, channels)

    def total_end(phase, channels, cells):
        return total_groups(phase, channels, 1.0 / (channels // GROUPS * cells))

    has_above, has_below = wide > 0, wide < wide_count - 1
    has_left, has_right = narrow > 0, narrow < narrow_count - 1
    has_corner = (
        jnp.logical_and(has_above, has_left),
        jnp.logical_and(has_above, has_right),
        jnp.logical_and(has_below, has_left),
        jnp.logical_and(has_below, has_right),
    )
    exists = (None, has_above, has_below, has_left, has_right) + has_corner

    def only(condition, value):
        return value * jnp.where(condition, 1.0, 0.0).astype(F32)

    def corners(read, change, masked):
        result = None
        for c in range(4):
            value = change(read(c).astype(F32))
            if masked:
                value = only(has_corner[c], value)
            cell = lax.broadcasted_iota(jnp.int32, value.shape, 0)
            result = value if result is None else jnp.where(cell >= 4 * c, value, result)
        return result

    def mid_extended(own, read_halo, read_cor, change, masked):
        pieces = [change(own)]
        halo = change(read_halo.astype(F32))
        for low, high, d in ((0, 16, 1), (16, 32, 2), (32, 64, 3), (64, 96, 4)):
            piece = halo[low:high]
            pieces.append(only(exists[d], piece) if masked else piece)
        pieces.append(corners(read_cor, change, masked))
        pieces.append(jnp.zeros((16, own.shape[1]), F32))
        return jnp.concatenate(pieces, axis=0)

    def send_mid(pack, halo, cor, which):
        send(pack.at[pl.ds(0, 16)], halo.at[pl.ds(0, 16)], which, 1, 0)
        send(pack.at[pl.ds(16, 16)], halo.at[pl.ds(16, 16)], which, -1, 0)
        send(pack.at[pl.ds(32, 32)], halo.at[pl.ds(32, 32)], which, 0, 1)
        send(pack.at[pl.ds(64, 32)], halo.at[pl.ds(64, 32)], which, 0, -1)
        for c in range(4):
            down, side = DIRS[5 + c]
            send(pack.at[pl.ds(96, 16)], cor.at[c], which + 1, -down, -side)

    def send_coarse(own, halo, which):
        for d in range(1, 9):
            down, side = DIRS[d]
            send(own, halo.at[d - 1], which, -down, -side)

    def coarse_extended(own, halo, change, masked):
        pieces = [change(own)]
        for d in range(1, 9):
            piece = change(halo(d - 1))
            pieces.append(only(exists[d], piece) if masked else piece)
        pieces.append(jnp.zeros((56, own.shape[1]), F32))
        return jnp.concatenate(pieces, axis=0)

    PICK = wide_table.at[pl.ds(0, 96)]
    ENLARGE = wide_table.at[pl.ds(96, 512)]
    TAPS = middle_table.at[pl.ds(0, 1152)]
    ENDS = middle_table.at[pl.ds(1152, 16)]
    PACK = narrow_table.at[pl.ds(0, 112)]
    POOL = narrow_table.at[pl.ds(112, 16)]
    COARSE_TAPS = narrow_table.at[pl.ds(128, 144)]
    SPREAD = narrow_table.at[pl.ds(272, 256)]
    SIDES = narrow_table.at[pl.ds(528, 512)]
    BY_FRAME = narrow_table.at[pl.ds(1040, 128)]

    def frame(which, f):
        return xg[which, f].reshape(512, 256)

    blank = jnp.zeros((8, 256), F32)
    one, two = blank, blank
    for f in range(4):
        loads["x%d" % f].wait()
        value = frame(0, f).astype(F32)
        one += jnp.sum(value.reshape(64, 8, 256), axis=0)
        two += jnp.sum((value * value).reshape(64, 8, 256), axis=0)
    pl.semaphore_wait(barrier, greeted)
    total_begin(0, jnp.sum(one, axis=0, keepdims=True), jnp.sum(two, axis=0, keepdims=True))

    begin_loads("grad", "narrow_table", "gain_fine", "windows", "kernel_fine")
    begin_loads("up_mid", "up_coarse", "down_mid", "gain_mid")

    def rim_rows_out(which):
        send(xg.at[which, :, 31], row_in.at[0, which], 13 * which, 1, 0)
        send(xg.at[which, :, 0], row_in.at[1, which], 13 * which, -1, 0)

    def rim_pick(which):
        for f in range(4):
            picked = dot(PICK[...], frame(which, f))
            if which == 0:
                pooled_x[32 * f : 32 * f + 32] = picked[0:32]
            picked = picked.astype(BF16)
            col_pack[0, which, 32 * f : 32 * f + 32] = picked[32:64]
            col_pack[1, which, 32 * f : 32 * f + 32] = picked[64:96]
            if which == 1:
                summed[32 * f : 32 * f + 32] = picked[0:32]

    def rim_sides_out(which):
        send(col_pack.at[0, which], col_in.at[0, which], 13 * which + 1, 0, 1)
        send(col_pack.at[1, which], col_in.at[1, which], 13 * which + 1, 0, -1)

    def rim_ends_out(which):
        ends = jnp.concatenate([col_pack[0, which], col_pack[1, which]], axis=0)
        cor_pack[which] = dot(ENDS[...], ends).astype(BF16)
        for c in range(4):
            down, side = DIRS[5 + c]
            send(cor_pack.at[which], cor_in.at[which, c], 13 * which + 2, -down, -side)

    loads["wide_table"].wait()
    loads["middle_table"].wait()
    rim_rows_out(0)
    rim_pick(0)
    rim_sides_out(0)
    rim_ends_out(0)
    loads["grad"].wait()
    rim_pick(1)
    total_middle(0)
    begin_loads("kernel_mid")
    rim_rows_out(1)
    rim_sides_out(1)
    rim_ends_out(1)
    loads["narrow_table"].wait()

    up_mid_grad = summed[...]
    sum_pack[...] = dot(PACK[...], up_mid_grad).astype(BF16)
    send_mid(sum_pack, sum_in, sum_cor, 3)
    loads["up_mid"].wait()
    high, low = halves(dot_t(up_mid_grad, up_mid[...]))
    up_coarse_grad = (dot(POOL[...], high) + dot(POOL[...], low)).astype(BF16)
    loads["up_coarse"].wait()
    cgrad_own[...] = dot_t(up_coarse_grad, up_coarse[...]).astype(BF16)
    send_coarse(cgrad_own, cgrad_in, 5)

    loads["gain_fine"].wait()
    loads["kernel_fine"].wait()
    loads["down_mid"].wait()

    fine_center, fine_square = total_end(0, 256, 2048 * wide_count * narrow_count)
    fine_inverse = lax.rsqrt(fine_square - fine_center * fine_center + epsilon)
    s_fine = gain_fine[...]

    def silu(center, inverse, scaling):
        gain = 0.5 * inverse * scaling
        shift = -center * gain

        def change(value):
            half = value * gain + shift
            return half * jnp.tanh(half) + half

        return change

    def slope(scaled, scaling):
        half = scaled * (0.5 * scaling)
        bend = jnp.tanh(half)
        return (0.5 * scaling) * (1.0 + bend) * (1.0 + half * (1.0 - bend))

    fine_act = silu(fine_center, fine_inverse, s_fine)

    arrived(row_in.at[:, 0], 0)
    arrived(col_in.at[:, 0], 1)
    arrived(cor_in.at[0], 2)

    def set_edges(kind, above, below, left, right, ends):
        edge_rows[kind, 0] = only(has_above, above)
        edge_rows[kind, 1] = only(has_below, below)
        left = only(has_left, left)
        right = only(has_right, right)
        for f in range(4):
            edge_sides[kind, f, 0:32] = left[32 * f : 32 * f + 32]
            edge_sides[kind, f, 32:64] = right[32 * f : 32 * f + 32]
        edge_ends[kind] = ends

    def place(kind, f, own):
        column = lax.broadcasted_iota(jnp.int32, (32, 16, 256), 1)
        west, east = (
            jnp.broadcast_to(edge_sides[kind, f, 32 * k : 32 * k + 32].reshape(32, 1, 256), (32, 16, 256))
            for k in range(2)
        )
        low = jnp.where(column == 0, west, pltpu.roll(own, 1, 0).reshape(32, 16, 256))
        columns[f, 16:528, 0:256] = low.reshape(512, 256).astype(BF16)
        columns[f, 16:528, 256:512] = own.astype(BF16)
        high = jnp.where(column == 15, east, pltpu.roll(own, 511, 0).reshape(32, 16, 256))
        columns[f, 16:528, 512:768] = high.reshape(512, 256).astype(BF16)
        cell = lax.broadcasted_iota(jnp.int32, (16, 256), 0)
        for k in range(2):
            row = edge_rows[kind, k, f]
            at = slice(528 * k, 528 * k + 16)
            west = edge_ends[kind, pl.ds(8 * k + f, 1), :]
            east = edge_ends[kind, pl.ds(8 * k + 4 + f, 1), :]
            columns[f, at, 0:256] = jnp.where(cell == 0, west, pltpu.roll(row, 1, 0)).astype(BF16)
            columns[f, at, 256:512] = row.astype(BF16)
            columns[f, at, 512:768] = jnp.where(cell == 15, east, pltpu.roll(row, 15, 0)).astype(BF16)

    def side_by_side(pieces):
        return jnp.concatenate(list(pieces), axis=1)

    def fine_taps(f):
        return side_by_side(columns[f, 16 * a : 16 * a + 512, :] for a in range(3))

    def fine_convolve(f):
        return dot(fine_taps(f), kernel_fine[...].reshape(2304, 256))

    def fine_convolve_back(f):
        return dot_t(fine_taps(f), side_by_side(kernel_fine[8 - t] for t in range(9)))

    def fine_scaled(value):
        return (value - fine_center) * fine_inverse

    def fine_value(f):
        return frame(0, f).astype(F32)

    def set_fields(n, change):
        for k in range(2):
            rim_rows[n, k] = only(exists[1 + k], change(row_in[k, 0].astype(F32))).astype(BF16)
            sides = only(exists[3 + k], change(col_in[k, 0].astype(F32))).astype(BF16)
            rim_sides[n, k] = sides.reshape(4, 32, 256)
        ends = corners(lambda c: cor_in[0, c], change, True)
        ends = dot(BY_FRAME[:, 0:16], ends.astype(BF16)).astype(BF16)
        rim_ends[n] = ends.reshape(4, 32, 256)

    def window(n, f, own):
        field = jnp.concatenate(
            [
                own.astype(BF16),
                rim_rows[n, 0, f],
                rim_rows[n, 1, f],
                rim_sides[n, 0, f],
                rim_sides[n, 1, f],
                rim_ends[n, f],
            ],
            axis=0,
        )
        return dot(windows[...], field)

    set_fields(0, fine_act)
    loads["windows"].wait()

    @pl.loop(0, 4)
    def _(f):
        sums = window(0, f, fine_act(fine_value(f)))
        high, low = halves(sums)
        window_sums[0, :, f] = high.reshape(9, 32, 256)
        window_sums[1, :, f] = low.reshape(9, 32, 256)

    both = side_by_side(
        jnp.concatenate([window_sums[n, 8 - t].reshape(128, 256) for n in range(2)], axis=0)
        for t in range(9)
    )
    both = dot(both, kernel_fine[...].reshape(2304, 256))
    pooled = pooled_x[...] + both[0:128] + both[128:256]
    pooled = (pooled * 0.0625).astype(BF16)

    def fine_forward(f):
        value = fine_value(f)
        place(0, f, fine_act(value))
        fine_block[f] = (value + fine_convolve(f)).astype(BF16)

    def same(value):
        return value

    mid_in = dot(pooled, down_mid[...]).astype(BF16)
    mid_value = mid_in.astype(F32)

    def column_sums(value):
        return jnp.sum(value, axis=0, keepdims=True)

    total_begin(1, column_sums(mid_value), column_sums(mid_value * mid_value))
    mid_pack[...] = dot(PACK[...], mid_in).astype(BF16)
    send_mid(mid_pack, mid_halo, mid_cor, 6)
    begin_loads("down_coarse", "gain_coarse", "kernel_coarse", "stretch")

    @pl.loop(0, 4)
    def _(f):
        fine_slope[f] = slope(fine_scaled(fine_value(f)), s_fine)

    set_fields(0, lambda v: slope(fine_scaled(v), s_fine))
    set_fields(1, lambda v: slope(fine_scaled(v), s_fine) * fine_scaled(v))

    set_edges(
        0,
        fine_act(row_in[0, 0].astype(F32)),
        fine_act(row_in[1, 0].astype(F32)),
        fine_act(col_in[0, 0].astype(F32)),
        fine_act(col_in[1, 0].astype(F32)),
        corners(lambda c: cor_in[0, c], fine_act, True),
    )
    fine_forward(0)
    total_middle(1)
    fine_forward(1)

    @pl.loop(0, 4)
    def _(f):
        bent = fine_slope[f]
        window_sums[0, :, f] = window(0, f, bent).astype(BF16).reshape(9, 32, 256)
        bent = bent * fine_scaled(fine_value(f))
        window_sums[1, :, f] = window(1, f, bent).astype(BF16).reshape(9, 32, 256)

    loads["gain_mid"].wait()
    loads["kernel_mid"].wait()
    mid_center, mid_square = total_end(1, 512, 128 * wide_count * narrow_count)
    mid_inverse = lax.rsqrt(mid_square - mid_center * mid_center + epsilon)
    s_mid = gain_mid[...]

    mid_act = silu(mid_center, mid_inverse, s_mid)

    def mid_scaled(value):
        return (value - mid_center) * mid_inverse

    def mid_convolve(extended, product, weights):
        taps = dot(TAPS[...], extended.astype(BF16)).astype(BF16)
        return product(side_by_side(taps[128 * t : 128 * t + 128] for t in range(9)), weights)

    arrived(mid_halo, 6)
    arrived(mid_cor, 7)
    mid_block = (
        mid_value
        + mid_convolve(
            mid_extended(mid_value, mid_halo[...], lambda c: mid_cor[c], mid_act, True),
            dot,
            kernel_mid[...].reshape(4608, 512),
        )
    ).astype(BF16)

    loads["down_coarse"].wait()
    mid_pooled = (dot(POOL[...], mid_block) * 0.0625).astype(BF16)
    coarse_in = dot(mid_pooled, down_coarse[...]).astype(BF16)
    coarse_own[...] = coarse_in
    coarse_value = coarse_in.astype(F32)[0:8]
    total_begin(2, column_sums(coarse_value), column_sums(coarse_value * coarse_value))
    send_coarse(coarse_own, coarse_halo, 8)

    arrived(row_in.at[:, 1], 13)
    arrived(col_in.at[:, 1], 14)
    arrived(cor_in.at[1], 15)
    set_edges(
        1,
        row_in[0, 1].astype(F32),
        row_in[1, 1].astype(F32),
        col_in[0, 1].astype(F32),
        col_in[1, 1].astype(F32),
        corners(lambda c: cor_in[1, c], same, True),
    )

    def convolve_grad(f, carry):
        place(1, f, frame(1, f).astype(F32))
        result = fine_convolve_back(f)
        conv_grad[f] = result
        weighted = result * fine_slope[f]
        scaled = fine_scaled(fine_value(f))
        return (
            carry[0] + jnp.sum(weighted.reshape(64, 8, 256), axis=0),
            carry[1] + jnp.sum((weighted * scaled).reshape(64, 8, 256), axis=0),
        )

    grad_sums = lax.fori_loop(0, 2, convolve_grad, (blank, blank))
    total_middle(2)

    arrived(cgrad_in, 5)
    loads["kernel_coarse"].wait()

    def coarse_convolve(extended, product, weights):
        taps = dot(COARSE_TAPS[...], extended.astype(BF16)).astype(BF16)
        return product(side_by_side(taps[16 * t : 16 * t + 16] for t in range(9)), weights)

    cgrad = cgrad_own[...].astype(F32)[0:8]
    coarse_act_grad = coarse_convolve(
        coarse_extended(cgrad, lambda d: cgrad_in[d].astype(F32)[0:8], same, True),
        dot_t,
        side_by_side(kernel_coarse[8 - t] for t in range(9)),
    )[0:8]

    @pl.loop(0, 9)
    def _(t):
        through[t] = (0.0625 * dot(kernel_fine[8 - t], down_mid[...])).astype(BF16)

    arrived(sum_in, 3)
    arrived(sum_cor, 4)
    sum_extended = mid_extended(
        up_mid_grad.astype(F32), sum_in[...], lambda c: sum_cor[c], same, True
    )
    summed_grad[...] = dot_t(sum_extended.astype(BF16), up_mid[...])

    loads["gain_coarse"].wait()
    coarse_center, coarse_square = total_end(2, 512, 8 * wide_count * narrow_count)
    coarse_inverse = lax.rsqrt(coarse_square - coarse_center * coarse_center + epsilon)
    s_coarse = gain_coarse[...]

    def coarse_scaled(value):
        return (value - coarse_center) * coarse_inverse

    scaled = coarse_scaled(coarse_value)
    normed_grad = coarse_act_grad * slope(scaled, s_coarse)
    total_begin(3, column_sums(normed_grad), column_sums(normed_grad * scaled))
    coarse_u[...] = cgrad + coarse_inverse * normed_grad
    send_coarse(coarse_u, coarse_u_halo, 9)
    grad_sums = lax.fori_loop(2, 4, convolve_grad, grad_sums)

    total_middle(3)

    mid_mix = jnp.concatenate(
        [mid_scaled(mid_value).astype(BF16), jnp.ones((128, 128), BF16)], axis=1
    )
    matrix_sum[...] = jnp.zeros((4, 256, 512), F32)

    @pl.loop(0, 9)
    def _(t):
        weight = through[t].astype(F32)
        for n in range(2):
            mixed = dot_first(window_sums[n, t].reshape(128, 256), mid_mix)
            plain = jnp.concatenate([mixed[:, 512:640]] * 4, axis=1)
            matrix_sum[2 * n] += weight * plain
            matrix_sum[2 * n + 1] += weight * mixed[:, 0:512]

    def iota(shape, axis):
        return lax.broadcasted_iota(jnp.int32, shape, axis)

    def one_hot(condition):
        return jnp.where(condition, 1.0, 0.0).astype(BF16)

    by_group = one_hot((iota((32, 256), 1) >> 3) == iota((32, 256), 0))
    matrix = jnp.zeros((32, 128), F32)
    for n in range(4):
        high, low = halves(matrix_sum[n] * mid_inverse)
        high, low = halves(dot(by_group, high) + dot(by_group, low))
        to_lane = one_hot(iota((512, 128), 1) == 32 * n + (iota((512, 128), 0) >> 4))
        matrix += dot(high, to_lane) + dot(low, to_lane)
    first_matrix[wide] = matrix.astype(BF16)
    total_send_wide(6)

    first_mean, second_mean = total_end(3, 512, 8 * wide_count * narrow_count)
    arrived(coarse_halo, 8)
    arrived(coarse_u_halo, 9)
    offset = coarse_inverse * first_mean
    factor = coarse_inverse * second_mean
    pieces = [coarse_u[...] - offset - scaled * factor]
    for d in range(8):
        piece = coarse_scaled(coarse_halo[d].astype(F32)[0:8])
        pieces.append(coarse_u_halo[d] - offset - piece * factor)
    pieces.append(jnp.zeros((56, 512), F32))
    coarse_in_grad = jnp.concatenate(pieces, axis=0).astype(BF16)

    mid_pool_grad = dot_t(dot(SPREAD[...], coarse_in_grad).astype(BF16), down_coarse[...])
    row = lax.broadcasted_iota(jnp.int32, (256, 128), 0)
    keep = jnp.where(row < ABOVE, 1.0, 0.0)
    bounds = ((ABOVE, 16, 1), (BELOW, 16, 2), (LEFT, 32, 3), (RIGHT, 32, 4)) + tuple(
        (CORNER + 4 * c, 4, 5 + c) for c in range(4)
    )
    for start, size, d in bounds:
        inside = jnp.logical_and(row >= start, row < start + size)
        keep = jnp.where(inside, jnp.where(exists[d], 1.0, 0.0).astype(F32), keep)
    mid_grad = (summed_grad[...] + 0.0625 * mid_pool_grad) * jnp.concatenate([keep] * 4, axis=1)
    mid_act_grad = mid_convolve(
        mid_grad, dot_t, side_by_side(kernel_mid[8 - t] for t in range(9))
    )
    scaled = mid_scaled(mid_value)
    normed_grad = mid_act_grad * slope(scaled, s_mid)
    total_begin(4, column_sums(normed_grad), column_sums(normed_grad * scaled))
    mid_u = mid_grad[0:128].astype(BF16).astype(F32) + mid_inverse * normed_grad
    u_pack[...] = dot(PACK[...], mid_u.astype(BF16)).astype(BF16)
    send_mid(u_pack, u_halo, u_cor, 10)
    pulled = (0.0625 * dot_t(mid_u.astype(BF16), down_mid[...])).astype(BF16)
    fine_sums = [jnp.sum(value, axis=0, keepdims=True) for value in grad_sums]
    for t in range(9):
        term = dot_t(pulled, kernel_fine[8 - t])
        for n in range(2):
            fine_sums[n] += column_sums(window_sums[n, t].reshape(128, 256).astype(F32) * term)
    total_begin(5, *fine_sums)
    total_middle(6)

    fine_forward(2)
    coarse_block = (
        coarse_in.astype(F32)
        + coarse_convolve(
            coarse_extended(
                coarse_value,
                lambda d: coarse_halo[d].astype(F32)[0:8],
                silu(coarse_center, coarse_inverse, s_coarse),
                True,
            ),
            dot,
            kernel_coarse[...].reshape(4608, 512),
        )
    ).astype(BF16)
    coarse_up = dot(coarse_block, up_coarse[...]).astype(BF16)
    mid_sum = (mid_block.astype(F32) + dot(SPREAD[0:128, 0:16], coarse_up)).astype(BF16)
    mid_up = dot(mid_sum, up_mid[...]).astype(BF16)
    total_middle(4)
    total_middle(5)

    fine_forward(3)
    mid_up = dot(ENLARGE[:, 0:128], mid_up).reshape(4, 8, 1, 16, 256)
    for f in range(4):
        block = fine_block[f].astype(F32).reshape(8, 4, 16, 256)
        fine_block[f] = (block + mid_up[f]).astype(BF16).reshape(512, 256)
    out_copy = pltpu.make_async_copy(fine_block, out_ref, out_sem.at[0])
    out_copy.start()
    first_mean, second_mean = total_end(4, 512, 128 * wide_count * narrow_count)
    arrived(u_halo, 10)
    arrived(u_cor, 11)
    offset = mid_inverse * first_mean
    factor = mid_inverse * second_mean
    mid_in_grad = mid_extended(
        mid_u, u_halo[...], lambda c: u_cor[c], lambda v: v - offset, False
    ) - factor * mid_extended(
        mid_value, mid_halo[...], lambda c: mid_cor[c], mid_scaled, False
    )

    pool_grad = 0.0625 * dot_t(mid_in_grad.astype(BF16), down_mid[...])
    pool_grad = pool_grad * jnp.concatenate([keep] * 2, axis=1)
    high, low = halves(pool_grad)
    added = dot(ENLARGE[...], jnp.concatenate([high[0:256], low[0:256]], axis=0))
    loads["stretch"].wait()
    for a in range(3):
        fields = [dot_t(high, kernel_fine[8 - 3 * a - b]).astype(BF16) for b in range(3)]
        stretched[a] = dot(stretch[...], jnp.concatenate(fields, axis=0)).reshape(4, 10, 16, 256)

    means = jnp.zeros((8, 128), F32)
    for n, mean in enumerate((first_mean, second_mean)):
        lane, row = iota((512, 128), 1), iota((512, 128), 0)
        inside = jnp.logical_and((lane & 31) == (row >> 4), ((lane >> 5) & 1) == n)
        to_lane = jnp.where(inside, 0.0625, 0.0).astype(BF16)
        high, low = halves(jnp.broadcast_to(mean, (8, 512)))
        means += dot(high, to_lane) + dot(low, to_lane)
    matrix_high, matrix_low = halves(total_sum(6))
    fine_totals = total_groups(5, 256, 1.0)
    spread_groups = one_hot((iota((256, 32), 0) >> 3) == iota((256, 32), 1))
    fine_means = []
    for n in range(2):
        half = jnp.where((iota((8, 128), 1) >> 6) == n, means, 0.0)
        high, low = halves(half)
        change = dot_t(high, matrix_high) + dot_t(low, matrix_high) + dot_t(high, matrix_low)
        high, low = halves(change)
        change = dot_t(high, spread_groups) + dot_t(low, spread_groups)
        fine_means.append(
            (fine_totals[n] - change[0:1]) * (1.0 / (8 * 2048 * wide_count * narrow_count))
        )
    slant = -fine_inverse * fine_inverse * fine_means[1]
    shift = -fine_inverse * fine_means[0] - fine_center * slant

    added = added.reshape(4, 8, 1, 16, 256)
    grad_copies = []
    for f in range(4):
        above, here, below = stretched[0, f], stretched[1, f], stretched[2, f]
        centre = here[1:9] + above[1:9] + below[1:9]
        top = here[1:9] + above[0:8] + below[1:9]
        bottom = here[1:9] + above[1:9] + below[2:10]
        back = jnp.stack([top, centre, centre, bottom], axis=1).reshape(512, 256)
        normed_grad = (conv_grad[f] + back) * fine_slope[f]
        grad = xg[1, f].astype(F32).reshape(8, 4, 16, 256) + added[f]
        grad = grad.reshape(512, 256).astype(BF16).astype(F32)
        grad_buf[f] = grad + fine_inverse * normed_grad + (shift + fine_value(f) * slant)
        grad_copies.append(
            pltpu.make_async_copy(grad_buf.at[f], grad_ref.at[f], out_sem.at[1 + f])
        )
        grad_copies[f].start()

    for which in range(2):
        sent(row_in.at[:, which], 13 * which)
        sent(col_in.at[:, which], 13 * which + 1)
        sent(cor_in.at[which], 13 * which + 2)
    sent(sum_in, 3)
    sent(sum_cor, 4)
    sent(cgrad_in, 5)
    sent(mid_halo, 6)
    sent(mid_cor, 7)
    sent(coarse_halo, 8)
    sent(coarse_u_halo, 9)
    sent(u_halo, 10)
    sent(u_cor, 11)
    for phase in range(7):
        whole = firsts[phase].at[pl.ds(0, wide_count - 1)]
        pltpu.make_async_copy(whole, whole, total_send.at[2 * phase]).wait()
        whole = seconds[phase].at[pl.ds(0, narrow_count - 1)]
        pltpu.make_async_copy(whole, whole, total_send.at[2 * phase + 1]).wait()
    out_copy.wait()
    for copy in grad_copies:
        copy.wait()


def shards(*arguments):
    (
        fine_input,
        gain_fine,
        kernel_fine,
        down_mid,
        gain_mid,
        kernel_mid,
        down_coarse,
        gain_coarse,
        kernel_coarse,
        up_coarse,
        up_mid,
        grad_out,
    ) = arguments
    wide_count, narrow_count = lax.axis_size("wide"), lax.axis_size("narrow")
    anywhere = pl.BlockSpec(memory_space=pl.ANY)
    vmem = pltpu.VMEM
    scratch = [
        vmem((2, 4, 32, 16, 256), BF16),
        vmem((9, 256, 256), BF16),
        vmem((256, 512), BF16),
        vmem((9, 512, 512), BF16),
        vmem((512, 512), BF16),
        vmem((9, 512, 512), BF16),
        vmem((512, 512), BF16),
        vmem((512, 256), BF16),
        vmem((1, 256), F32),
        vmem((1, 512), F32),
        vmem((1, 512), F32),
        vmem((608, 512), BF16),
        vmem((1168, 256), BF16),
        vmem((1168, 128), BF16),
        vmem((288, 640), BF16),
        vmem((640, 768), BF16),
        vmem((4, 544, 768), BF16),
        vmem((4, 512, 256), BF16),
        vmem((4, 512, 256), F32),
        vmem((4, 512, 256), F32),
        vmem((128, 256), F32),
        vmem((128, 256), BF16),
        vmem((4, 512, 256), F32),
        vmem((2, 2, 4, 16, 256), F32),
        vmem((2, 4, 64, 256), F32),
        vmem((2, 16, 256), F32),
        vmem((256, 512), F32),
        vmem((6, wide_count, 1, 128), F32),
        vmem((6, narrow_count, 1, 128), F32),
        vmem((8, 128), F32),
        vmem((wide_count, 32, 128), BF16),
        vmem((narrow_count, 32, 128), BF16),
        vmem((2, 9, 4, 32, 256), BF16),
        vmem((2, 2, 4, 16, 256), BF16),
        vmem((2, 2, 4, 32, 256), BF16),
        vmem((2, 4, 32, 256), BF16),
        vmem((4, 256, 512), F32),
        vmem((9, 256, 512), BF16),
        vmem((3, 4, 10, 16, 256), F32),
        vmem((2, 2, 128, 256), BF16),
        vmem((2, 16, 256), BF16),
        vmem((2, 2, 4, 16, 256), BF16),
        vmem((2, 2, 128, 256), BF16),
        vmem((2, 4, 16, 256), BF16),
        vmem((112, 256), BF16),
        vmem((96, 256), BF16),
        vmem((4, 16, 256), BF16),
        vmem((16, 512), BF16),
        vmem((8, 16, 512), BF16),
        vmem((112, 512), BF16),
        vmem((96, 512), BF16),
        vmem((4, 16, 512), BF16),
        vmem((16, 512), BF16),
        vmem((8, 16, 512), BF16),
        vmem((8, 512), F32),
        vmem((8, 8, 512), F32),
        vmem((112, 512), BF16),
        vmem((96, 512), BF16),
        vmem((4, 16, 512), BF16),
        pltpu.SemaphoreType.DMA((20,)),
        pltpu.SemaphoreType.DMA((5,)),
        pltpu.SemaphoreType.DMA((14,)),
        pltpu.SemaphoreType.DMA((14,)),
        pltpu.SemaphoreType.DMA((16,)),
        pltpu.SemaphoreType.DMA((16,)),
    ]
    output, grad = pl.pallas_call(
        functools.partial(kernel, wide_count, narrow_count),
        out_shape=(
            jax.ShapeDtypeStruct((4, 512, 256), BF16),
            jax.ShapeDtypeStruct((4, 512, 256), F32),
        ),
        in_specs=[anywhere] * 17,
        out_specs=(anywhere, anywhere),
        scratch_shapes=scratch,
        compiler_params=pltpu.CompilerParams(
            collective_id=0, has_side_effects=True, vmem_limit_bytes=56 * 2**20
        ),
        name="whole_net",
    )(
        fine_input,
        gain_fine.reshape(1, 256),
        kernel_fine.reshape(9, 256, 256),
        down_mid,
        gain_mid.reshape(1, 512),
        kernel_mid.reshape(9, 512, 512),
        down_coarse,
        gain_coarse.reshape(1, 512),
        kernel_coarse.reshape(9, 512, 512),
        up_coarse,
        up_mid,
        grad_out,
        *tables(),
    )
    return output.reshape(4, 32, 16, 256), grad.reshape(4, 32, 16, 256)


def solution(mesh):
    tile = P(None, "wide", "narrow", None)
    return jax.shard_map(
        shards,
        mesh=mesh,
        in_specs=(tile,) + (P(),) * 10 + (tile,),
        out_specs=(tile, tile),
        check_vma=False,
    )
```

```python
import functools

import jax
import jax.numpy as jnp
import numpy as np
from jax import lax
from jax.experimental import pallas as pl
from jax.experimental.pallas import tpu as pltpu
from jax.sharding import PartitionSpec as P

MESH = pl.DeviceIdType.MESH
GROUPS = 32
epsilon = 1e-05
F32 = jnp.float32
BF16 = jnp.bfloat16

DIRS = ((0, 0), (-1, 0), (1, 0), (0, -1), (0, 1), (-1, -1), (-1, 1), (1, -1), (1, 1))

ABOVE, BELOW, LEFT, RIGHT, CORNER = 128, 144, 160, 192, 224


def mid_row(f, i, j):
    if 0 <= i < 8 and 0 <= j < 4:
        return 32 * f + 4 * i + j
    if i < 0 and 0 <= j < 4:
        return ABOVE + 4 * f + j
    if i > 7 and 0 <= j < 4:
        return BELOW + 4 * f + j
    if 0 <= i < 8:
        return (LEFT if j < 0 else RIGHT) + 8 * f + i
    return CORNER + 4 * (2 * (i > 7) + (j > 3)) + f


def coarse_row(f, i, side):
    down = -1 if i < 0 else (1 if i > 1 else 0)
    return 8 * DIRS.index((down, side)) + 2 * f + i % 2


def tables():
    pick = np.zeros((96, 512), np.float32)
    for i in range(32):
        for j in range(16):
            pick[4 * (i // 4) + j // 4, 16 * i + j] = 1
        pick[32 + i, 16 * i + 15] = 1
        pick[64 + i, 16 * i] = 1
    enlarge = np.zeros((512, 256), np.float32)
    taps = np.zeros((1152, 256), np.float32)
    ends = np.zeros((16, 256), np.float32)
    pack = np.zeros((112, 128), np.float32)
    pool = np.zeros((16, 128), np.float32)
    coarse_taps = np.zeros((144, 128), np.float32)
    spread = np.zeros((256, 128), np.float32)
    for f in range(4):
        for i in range(8):
            for j in range(16):
                enlarge[128 * f + 16 * i + j, mid_row(f, i, j // 4)] = 1
        for c in range(4):
            low, first = c < 2, c % 2 == 1
            ends[4 * c + f, 128 * first + 32 * f + 31 * low] = 1
            pack[96 + 4 * c + f, mid_row(f, 7 * low, 3 * (not first))] = 1
        for i in range(8):
            for j in range(4):
                here = 32 * f + 4 * i + j
                pool[2 * f + i // 4, here] = 1
                for t in range(9):
                    taps[128 * t + here, mid_row(f, i + t // 3 - 1, j + t % 3 - 1)] = 1
            pack[32 + 8 * f + i, mid_row(f, i, 3)] = 1
            pack[64 + 8 * f + i, mid_row(f, i, 0)] = 1
        for j in range(4):
            pack[4 * f + j, mid_row(f, 7, j)] = 1
            pack[16 + 4 * f + j, mid_row(f, 0, j)] = 1
        for i in range(2):
            for t in range(9):
                coarse_taps[16 * t + 2 * f + i, coarse_row(f, i + t // 3 - 1, t % 3 - 1)] = 1
        for i in range(-1, 9):
            for j in range(-1, 5):
                side = -1 if j < 0 else (1 if j > 3 else 0)
                spread[mid_row(f, i, j), coarse_row(f, i // 4 if i < 8 else 2, side)] = 1
    windows = np.zeros((288, 640), np.float32)
    for t in range(9):
        for i in range(32):
            for j in range(16):
                p, q = i + 1 - t // 3, j + 1 - t % 3
                row = 32 * t + 4 * (i // 4) + j // 4
                if 0 <= p < 32 and 0 <= q < 16:
                    at = 16 * p + q
                elif 0 <= q < 16:
                    at = (512 if p < 0 else 528) + q
                elif 0 <= p < 32:
                    at = (544 if q < 0 else 576) + p
                else:
                    at = 608 + 2 * (p > 31) + (q > 15)
                windows[row, at] = 1
    stretch = np.zeros((640, 768), np.float32)
    for f in range(4):
        for i in range(10):
            for j in range(16):
                for b in range(3):
                    at = 256 * b + mid_row(f, i - 1, (j + b - 1) // 4)
                    stretch[160 * f + 16 * i + j, at] = 1
    by_frame = np.zeros((128, 128), np.float32)
    for f in range(4):
        for c in range(4):
            by_frame[32 * f + c, 4 * c + f] = 1
    sides = np.zeros((512, 128), np.float32)
    for i in range(32):
        sides[16 * i, i] = 1
        sides[16 * i + 15, 64 + i] = 1
    wide_table = np.concatenate([pick, np.concatenate([enlarge, enlarge], axis=1)])
    middle_table = np.concatenate([taps, ends])
    narrow_table = np.concatenate([pack, pool, coarse_taps, spread, sides, by_frame])
    result = (wide_table, middle_table, narrow_table, windows, stretch)
    return [jnp.asarray(t, BF16) for t in result]


def dot(a, b):
    return jnp.dot(a, b, preferred_element_type=F32)


def dot_t(a, b):
    return lax.dot_general(a, b, (((1,), (1,)), ((), ())), preferred_element_type=F32)


def dot_first(a, b):
    return lax.dot_general(a, b, (((0,), (0,)), ((), ())), preferred_element_type=F32)


def group_lanes(t, size):
    lane = lax.broadcasted_iota(jnp.int32, t.shape, 1)
    step = 1
    while step < size:
        t = t + jnp.where(
            (lane & step) != 0, pltpu.roll(t, step, 1), pltpu.roll(t, 128 - step, 1)
        )
        step *= 2
    return t


def halves(t):
    high = t.astype(BF16)
    return high, (t - high.astype(F32)).astype(BF16)


def kernel(
    wide_count,
    narrow_count,
    x_in,
    gain_fine_in,
    kernel_fine_in,
    down_mid_in,
    gain_mid_in,
    kernel_mid_in,
    down_coarse_in,
    gain_coarse_in,
    kernel_coarse_in,
    up_coarse_in,
    up_mid_in,
    grad_in,
    wide_table_in,
    middle_table_in,
    narrow_table_in,
    windows_in,
    stretch_in,
    out_ref,
    grad_ref,
    xg,
    kernel_fine,
    down_mid,
    kernel_mid,
    down_coarse,
    kernel_coarse,
    up_coarse,
    up_mid,
    gain_fine,
    gain_mid,
    gain_coarse,
    wide_table,
    middle_table,
    narrow_table,
    windows,
    stretch,
    columns,
    fine_block,
    grad_buf,
    conv_grad,
    pooled_x,
    summed,
    fine_slope,
    edge_rows,
    edge_sides,
    edge_ends,
    summed_grad,
    first,
    second,
    rows,
    first_matrix,
    second_matrix,
    window_sums,
    rim_rows,
    rim_sides,
    rim_ends,
    matrix_sum,
    through,
    mixed,
    stretched,
    col_pack,
    cor_pack,
    row_in,
    col_in,
    cor_in,
    sum_pack,
    sum_in,
    sum_cor,
    cgrad_own,
    cgrad_in,
    mid_pack,
    mid_halo,
    mid_cor,
    coarse_own,
    coarse_halo,
    coarse_u,
    coarse_u_halo,
    u_pack,
    u_halo,
    u_cor,
    load_sem,
    out_sem,
    total_send,
    total_recv,
    halo_send,
    halo_recv,
):
    wide, narrow = lax.axis_index("wide"), lax.axis_index("narrow")

    def around(index, step, count):
        moved = index + step
        if isinstance(step, int) and step < 0:
            return jnp.where(moved < 0, moved + count, moved)
        return jnp.where(moved >= count, moved - count, moved)

    def device(down, side):
        return (
            wide if isinstance(down, int) and down == 0 else around(wide, down, wide_count),
            narrow if isinstance(side, int) and side == 0 else around(narrow, side, narrow_count),
        )

    loads = {}
    pairs = (
        ("x0", x_in.at[0], xg.at[0, 0]),
        ("x1", x_in.at[1], xg.at[0, 1]),
        ("x2", x_in.at[2], xg.at[0, 2]),
        ("x3", x_in.at[3], xg.at[0, 3]),
        ("grad", grad_in, xg.at[1]),
        ("wide_table", wide_table_in, wide_table),
        ("middle_table", middle_table_in, middle_table),
        ("narrow_table", narrow_table_in, narrow_table),
        ("gain_fine", gain_fine_in, gain_fine),
        ("windows", windows_in, windows),
        ("kernel_fine", kernel_fine_in, kernel_fine),
        ("up_mid", up_mid_in, up_mid),
        ("up_coarse", up_coarse_in, up_coarse),
        ("down_mid", down_mid_in, down_mid),
        ("gain_mid", gain_mid_in, gain_mid),
        ("kernel_coarse", kernel_coarse_in, kernel_coarse),
        ("kernel_mid", kernel_mid_in, kernel_mid),
        ("down_coarse", down_coarse_in, down_coarse),
        ("gain_coarse", gain_coarse_in, gain_coarse),
        ("stretch", stretch_in, stretch),
    )
    for number, (name, source, target) in enumerate(pairs):
        loads[name] = pltpu.make_async_copy(source, target, load_sem.at[number])

    def begin_loads(*names):
        for name in names:
            loads[name].start()

    begin_loads("x0", "x1", "x2", "x3", "wide_table", "middle_table")

    barrier = pltpu.get_barrier_semaphore()
    greeted = 0
    for down in range(wide_count):
        for side in range(-2, narrow_count - 2):
            near = (down <= 1 or down == wide_count - 1) and abs(side) <= 1
            if (down, side) != (0, 0) and (down == 0 or side == 0 or near):
                pl.semaphore_signal(
                    barrier, inc=1, device_id=device(down, side), device_id_type=MESH
                )
                greeted += 1

    def send(source, target, which, down, side):
        pltpu.make_async_remote_copy(
            src_ref=source,
            dst_ref=target,
            send_sem=halo_send.at[which],
            recv_sem=halo_recv.at[which],
            device_id=device(down, side),
            device_id_type=MESH,
        ).start()

    def arrived(buffer, which):
        pltpu.make_async_copy(buffer, buffer, halo_recv.at[which]).wait()

    def sent(buffer, which):
        pltpu.make_async_copy(buffer, buffer, halo_send.at[which]).wait()

    firsts = tuple(first.at[p] for p in range(6)) + (first_matrix,)
    seconds = tuple(second.at[p] for p in range(6)) + (second_matrix,)

    def total_send_wide(phase):
        mine = firsts[phase].at[wide]

        for step in sorted(range(1, wide_count), key=lambda k: -min(k & 7, 8 - (k & 7))):
            pltpu.make_async_remote_copy(
                src_ref=mine,
                dst_ref=mine,
                send_sem=total_send.at[2 * phase],
                recv_sem=total_recv.at[2 * phase],
                device_id=device(step, 0),
                device_id_type=MESH,
            ).start()

    def diagonal(shape=(8, 128)):
        lane = lax.broadcasted_iota(jnp.int32, shape, 1) & 7
        return lane == lax.broadcasted_iota(jnp.int32, shape, 0)

    def total_begin(phase, one, two):
        channels = one.shape[1]
        if channels < 512:
            rows[...] = jnp.zeros((8, 128), F32)
        for n, value in enumerate((one, two)):
            for k in range(channels // 128):
                rows[4 * n + k : 4 * n + k + 1, :] = value[:, 128 * k : 128 * k + 128]
        grouped = group_lanes(rows[...], channels // GROUPS)
        grouped = jnp.where(diagonal(), grouped, 0.0)
        firsts[phase][wide] = jnp.sum(grouped, axis=0, keepdims=True)
        total_send_wide(phase)

    def total_middle(phase):
        whole = firsts[phase].at[pl.ds(0, wide_count - 1)]
        pltpu.make_async_copy(whole, whole, total_recv.at[2 * phase]).wait()
        summed_up = jnp.sum(firsts[phase][...].astype(F32), axis=0)
        seconds[phase][narrow] = summed_up.astype(seconds[phase].dtype)
        mine = seconds[phase].at[narrow]

        for step in sorted(range(1, narrow_count), key=lambda k: -min(k & 3, 4 - (k & 3))):
            pltpu.make_async_remote_copy(
                src_ref=mine,
                dst_ref=mine,
                send_sem=total_send.at[2 * phase + 1],
                recv_sem=total_recv.at[2 * phase + 1],
                device_id=device(0, step),
                device_id_type=MESH,
            ).start()

    def total_sum(phase):
        whole = seconds[phase].at[pl.ds(0, narrow_count - 1)]
        pltpu.make_async_copy(whole, whole, total_recv.at[2 * phase + 1]).wait()
        return jnp.sum(seconds[phase][...].astype(F32), axis=0)

    def row_of(t, start, channels):
        return jnp.concatenate([t[start + k : start + k + 1] for k in range(channels // 128)], axis=1)

    def total_groups(phase, channels, scale):
        packed = jnp.broadcast_to(total_sum(phase), (8, 128))
        t = group_lanes(jnp.where(diagonal(), packed, 0.0), 8) * scale
        return row_of(t, 0, channels), row_of(t, 4, channels)

    def total_end(phase, channels, cells):
        return total_groups(phase, channels, 1.0 / (channels // GROUPS * cells))

    has_above, has_below = wide > 0, wide < wide_count - 1
    has_left, has_right = narrow > 0, narrow < narrow_count - 1
    has_corner = (
        jnp.logical_and(has_above, has_left),
        jnp.logical_and(has_above, has_right),
        jnp.logical_and(has_below, has_left),
        jnp.logical_and(has_below, has_right),
    )
    exists = (None, has_above, has_below, has_left, has_right) + has_corner

    def only(condition, value):
        return value * jnp.where(condition, 1.0, 0.0).astype(F32)

    def corners(read, change, masked):
        result = None
        for c in range(4):
            value = change(read(c).astype(F32))
            if masked:
                value = only(has_corner[c], value)
            cell = lax.broadcasted_iota(jnp.int32, value.shape, 0)
            result = value if result is None else jnp.where(cell >= 4 * c, value, result)
        return result

    def mid_extended(own, read_halo, read_cor, change, masked):
        pieces = [change(own)]
        halo = change(read_halo.astype(F32))
        for low, high, d in ((0, 16, 1), (16, 32, 2), (32, 64, 3), (64, 96, 4)):
            piece = halo[low:high]
            pieces.append(only(exists[d], piece) if masked else piece)
        pieces.append(corners(read_cor, change, masked))
        pieces.append(jnp.zeros((16, own.shape[1]), F32))
        return jnp.concatenate(pieces, axis=0)

    def send_mid(pack, halo, cor, which):
        send(pack.at[pl.ds(0, 16)], halo.at[pl.ds(0, 16)], which, 1, 0)
        send(pack.at[pl.ds(16, 16)], halo.at[pl.ds(16, 16)], which, -1, 0)
        send(pack.at[pl.ds(32, 32)], halo.at[pl.ds(32, 32)], which, 0, 1)
        send(pack.at[pl.ds(64, 32)], halo.at[pl.ds(64, 32)], which, 0, -1)
        for c in range(4):
            down, side = DIRS[5 + c]
            send(pack.at[pl.ds(96, 16)], cor.at[c], which + 1, -down, -side)

    def send_coarse(own, halo, which):
        for d in range(1, 9):
            down, side = DIRS[d]
            send(own, halo.at[d - 1], which, -down, -side)

    def coarse_extended(own, halo, change, masked):
        pieces = [change(own)]
        for d in range(1, 9):
            piece = change(halo(d - 1))
            pieces.append(only(exists[d], piece) if masked else piece)
        pieces.append(jnp.zeros((56, own.shape[1]), F32))
        return jnp.concatenate(pieces, axis=0)

    PICK = wide_table.at[pl.ds(0, 96)]
    ENLARGE = wide_table.at[pl.ds(96, 512)]
    TAPS = middle_table.at[pl.ds(0, 1152)]
    ENDS = middle_table.at[pl.ds(1152, 16)]
    PACK = narrow_table.at[pl.ds(0, 112)]
    POOL = narrow_table.at[pl.ds(112, 16)]
    COARSE_TAPS = narrow_table.at[pl.ds(128, 144)]
    SPREAD = narrow_table.at[pl.ds(272, 256)]
    SIDES = narrow_table.at[pl.ds(528, 512)]
    BY_FRAME = narrow_table.at[pl.ds(1040, 128)]

    def frame(which, f):
        return xg[which, f].reshape(512, 256)

    blank = jnp.zeros((8, 256), F32)
    one, two = blank, blank
    for f in range(4):
        loads["x%d" % f].wait()
        value = frame(0, f).astype(F32)
        one += jnp.sum(value.reshape(64, 8, 256), axis=0)
        two += jnp.sum((value * value).reshape(64, 8, 256), axis=0)
    pl.semaphore_wait(barrier, greeted)
    total_begin(0, jnp.sum(one, axis=0, keepdims=True), jnp.sum(two, axis=0, keepdims=True))

    begin_loads("grad", "narrow_table", "gain_fine", "windows", "kernel_fine")
    begin_loads("up_mid", "up_coarse", "down_mid", "gain_mid")

    def rim_rows_out(which):
        send(xg.at[which, :, 31], row_in.at[0, which], 13 * which, 1, 0)
        send(xg.at[which, :, 0], row_in.at[1, which], 13 * which, -1, 0)

    def rim_pick(which):
        for f in range(4):
            picked = dot(PICK[...], frame(which, f))
            if which == 0:
                pooled_x[32 * f : 32 * f + 32] = picked[0:32]
            picked = picked.astype(BF16)
            col_pack[0, which, 32 * f : 32 * f + 32] = picked[32:64]
            col_pack[1, which, 32 * f : 32 * f + 32] = picked[64:96]
            if which == 1:
                summed[32 * f : 32 * f + 32] = picked[0:32]

    def rim_sides_out(which):
        send(col_pack.at[0, which], col_in.at[0, which], 13 * which + 1, 0, 1)
        send(col_pack.at[1, which], col_in.at[1, which], 13 * which + 1, 0, -1)

    def rim_ends_out(which):
        ends = jnp.concatenate([col_pack[0, which], col_pack[1, which]], axis=0)
        cor_pack[which] = dot(ENDS[...], ends).astype(BF16)
        for c in range(4):
            down, side = DIRS[5 + c]
            send(cor_pack.at[which], cor_in.at[which, c], 13 * which + 2, -down, -side)

    loads["wide_table"].wait()
    loads["middle_table"].wait()
    rim_rows_out(0)
    rim_pick(0)
    rim_sides_out(0)
    rim_ends_out(0)
    loads["grad"].wait()
    rim_pick(1)
    total_middle(0)
    begin_loads("kernel_mid")
    rim_rows_out(1)
    rim_sides_out(1)
    rim_ends_out(1)
    loads["narrow_table"].wait()

    up_mid_grad = summed[...]
    sum_pack[...] = dot(PACK[...], up_mid_grad).astype(BF16)
    send_mid(sum_pack, sum_in, sum_cor, 3)
    loads["up_mid"].wait()
    high, low = halves(dot_t(up_mid_grad, up_mid[...]))
    up_coarse_grad = (dot(POOL[...], high) + dot(POOL[...], low)).astype(BF16)
    loads["up_coarse"].wait()
    cgrad_own[...] = dot_t(up_coarse_grad, up_coarse[...]).astype(BF16)
    send_coarse(cgrad_own, cgrad_in, 5)

    loads["gain_fine"].wait()
    loads["kernel_fine"].wait()
    loads["down_mid"].wait()

    fine_center, fine_square = total_end(0, 256, 2048 * wide_count * narrow_count)
    fine_inverse = lax.rsqrt(fine_square - fine_center * fine_center + epsilon)
    s_fine = gain_fine[...]

    def silu(center, inverse, scaling):
        gain = 0.5 * inverse * scaling
        shift = -center * gain

        def change(value):
            half = value * gain + shift
            return half * jnp.tanh(half) + half

        return change

    def slope(scaled, scaling):
        half = scaled * (0.5 * scaling)
        bend = jnp.tanh(half)
        return (0.5 * scaling) * (1.0 + bend) * (1.0 + half * (1.0 - bend))

    fine_act = silu(fine_center, fine_inverse, s_fine)

    arrived(row_in.at[:, 0], 0)
    arrived(col_in.at[:, 0], 1)
    arrived(cor_in.at[0], 2)

    def set_edges(kind, above, below, left, right, ends):
        edge_rows[kind, 0] = only(has_above, above)
        edge_rows[kind, 1] = only(has_below, below)
        left = only(has_left, left)
        right = only(has_right, right)
        for f in range(4):
            edge_sides[kind, f, 0:32] = left[32 * f : 32 * f + 32]
            edge_sides[kind, f, 32:64] = right[32 * f : 32 * f + 32]
        edge_ends[kind] = ends

    def place(kind, f, own):
        column = lax.broadcasted_iota(jnp.int32, (32, 16, 256), 1)
        west, east = (
            jnp.broadcast_to(edge_sides[kind, f, 32 * k : 32 * k + 32].reshape(32, 1, 256), (32, 16, 256))
            for k in range(2)
        )
        low = jnp.where(column == 0, west, pltpu.roll(own, 1, 0).reshape(32, 16, 256))
        columns[f, 16:528, 0:256] = low.reshape(512, 256).astype(BF16)
        columns[f, 16:528, 256:512] = own.astype(BF16)
        high = jnp.where(column == 15, east, pltpu.roll(own, 511, 0).reshape(32, 16, 256))
        columns[f, 16:528, 512:768] = high.reshape(512, 256).astype(BF16)
        cell = lax.broadcasted_iota(jnp.int32, (16, 256), 0)
        for k in range(2):
            row = edge_rows[kind, k, f]
            at = slice(528 * k, 528 * k + 16)
            west = edge_ends[kind, pl.ds(8 * k + f, 1), :]
            east = edge_ends[kind, pl.ds(8 * k + 4 + f, 1), :]
            columns[f, at, 0:256] = jnp.where(cell == 0, west, pltpu.roll(row, 1, 0)).astype(BF16)
            columns[f, at, 256:512] = row.astype(BF16)
            columns[f, at, 512:768] = jnp.where(cell == 15, east, pltpu.roll(row, 15, 0)).astype(BF16)

    def side_by_side(pieces):
        return jnp.concatenate(list(pieces), axis=1)

    def fine_taps(f):
        return side_by_side(columns[f, 16 * a : 16 * a + 512, :] for a in range(3))

    def fine_convolve(f):
        return dot(fine_taps(f), kernel_fine[...].reshape(2304, 256))

    def fine_convolve_back(f):
        return dot_t(fine_taps(f), side_by_side(kernel_fine[8 - t] for t in range(9)))

    def fine_scaled(value):
        return (value - fine_center) * fine_inverse

    def fine_value(f):
        return frame(0, f).astype(F32)

    def set_fields(n, change):
        for k in range(2):
            rim_rows[n, k] = only(exists[1 + k], change(row_in[k, 0].astype(F32))).astype(BF16)
            sides = only(exists[3 + k], change(col_in[k, 0].astype(F32))).astype(BF16)
            rim_sides[n, k] = sides.reshape(4, 32, 256)
        ends = corners(lambda c: cor_in[0, c], change, True)
        ends = dot(BY_FRAME[:, 0:16], ends.astype(BF16)).astype(BF16)
        rim_ends[n] = ends.reshape(4, 32, 256)

    def window(n, f, own):
        field = jnp.concatenate(
            [
                own.astype(BF16),
                rim_rows[n, 0, f],
                rim_rows[n, 1, f],
                rim_sides[n, 0, f],
                rim_sides[n, 1, f],
                rim_ends[n, f],
            ],
            axis=0,
        )
        return dot(windows[...], field)

    set_fields(0, fine_act)
    loads["windows"].wait()

    @pl.loop(0, 4)
    def _(f):
        sums = window(0, f, fine_act(fine_value(f)))
        high, low = halves(sums)
        window_sums[0, :, f] = high.reshape(9, 32, 256)
        window_sums[1, :, f] = low.reshape(9, 32, 256)

    both = side_by_side(
        jnp.concatenate([window_sums[n, 8 - t].reshape(128, 256) for n in range(2)], axis=0)
        for t in range(9)
    )
    both = dot(both, kernel_fine[...].reshape(2304, 256))
    pooled = pooled_x[...] + both[0:128] + both[128:256]
    pooled = (pooled * 0.0625).astype(BF16)

    def fine_forward(f):
        value = fine_value(f)
        place(0, f, fine_act(value))
        fine_block[f] = (value + fine_convolve(f)).astype(BF16)

    def same(value):
        return value

    mid_in = dot(pooled, down_mid[...]).astype(BF16)
    mid_value = mid_in.astype(F32)

    def column_sums(value):
        return jnp.sum(value, axis=0, keepdims=True)

    total_begin(1, column_sums(mid_value), column_sums(mid_value * mid_value))
    mid_pack[...] = dot(PACK[...], mid_in).astype(BF16)
    send_mid(mid_pack, mid_halo, mid_cor, 6)
    begin_loads("down_coarse", "gain_coarse", "kernel_coarse", "stretch")

    @pl.loop(0, 4)
    def _(f):
        fine_slope[f] = slope(fine_scaled(fine_value(f)), s_fine)

    set_fields(0, lambda v: slope(fine_scaled(v), s_fine))
    set_fields(1, lambda v: slope(fine_scaled(v), s_fine) * fine_scaled(v))

    set_edges(
        0,
        fine_act(row_in[0, 0].astype(F32)),
        fine_act(row_in[1, 0].astype(F32)),
        fine_act(col_in[0, 0].astype(F32)),
        fine_act(col_in[1, 0].astype(F32)),
        corners(lambda c: cor_in[0, c], fine_act, True),
    )
    fine_forward(0)
    total_middle(1)
    fine_forward(1)

    @pl.loop(0, 4)
    def _(f):
        bent = fine_slope[f]
        window_sums[0, :, f] = window(0, f, bent).astype(BF16).reshape(9, 32, 256)
        bent = bent * fine_scaled(fine_value(f))
        window_sums[1, :, f] = window(1, f, bent).astype(BF16).reshape(9, 32, 256)

    loads["gain_mid"].wait()
    loads["kernel_mid"].wait()
    mid_center, mid_square = total_end(1, 512, 128 * wide_count * narrow_count)
    mid_inverse = lax.rsqrt(mid_square - mid_center * mid_center + epsilon)
    s_mid = gain_mid[...]

    mid_act = silu(mid_center, mid_inverse, s_mid)

    def mid_scaled(value):
        return (value - mid_center) * mid_inverse

    def mid_convolve(extended, product, weights):
        taps = dot(TAPS[...], extended.astype(BF16)).astype(BF16)
        return product(side_by_side(taps[128 * t : 128 * t + 128] for t in range(9)), weights)

    arrived(mid_halo, 6)
    arrived(mid_cor, 7)
    mid_block = (
        mid_value
        + mid_convolve(
            mid_extended(mid_value, mid_halo[...], lambda c: mid_cor[c], mid_act, True),
            dot,
            kernel_mid[...].reshape(4608, 512),
        )
    ).astype(BF16)

    loads["down_coarse"].wait()
    mid_pooled = (dot(POOL[...], mid_block) * 0.0625).astype(BF16)
    coarse_in = dot(mid_pooled, down_coarse[...]).astype(BF16)
    coarse_own[...] = coarse_in
    coarse_value = coarse_in.astype(F32)[0:8]
    total_begin(2, column_sums(coarse_value), column_sums(coarse_value * coarse_value))
    send_coarse(coarse_own, coarse_halo, 8)

    arrived(row_in.at[:, 1], 13)
    arrived(col_in.at[:, 1], 14)
    arrived(cor_in.at[1], 15)
    set_edges(
        1,
        row_in[0, 1].astype(F32),
        row_in[1, 1].astype(F32),
        col_in[0, 1].astype(F32),
        col_in[1, 1].astype(F32),
        corners(lambda c: cor_in[1, c], same, True),
    )

    def convolve_grad(f, carry):
        place(1, f, frame(1, f).astype(F32))
        result = fine_convolve_back(f)
        conv_grad[f] = result
        weighted = result * fine_slope[f]
        scaled = fine_scaled(fine_value(f))
        return (
            carry[0] + jnp.sum(weighted.reshape(64, 8, 256), axis=0),
            carry[1] + jnp.sum((weighted * scaled).reshape(64, 8, 256), axis=0),
        )

    grad_sums = lax.fori_loop(0, 2, convolve_grad, (blank, blank))
    total_middle(2)

    arrived(cgrad_in, 5)
    loads["kernel_coarse"].wait()

    def coarse_convolve(extended, product, weights):
        taps = dot(COARSE_TAPS[...], extended.astype(BF16)).astype(BF16)
        return product(side_by_side(taps[16 * t : 16 * t + 16] for t in range(9)), weights)

    cgrad = cgrad_own[...].astype(F32)[0:8]
    coarse_act_grad = coarse_convolve(
        coarse_extended(cgrad, lambda d: cgrad_in[d].astype(F32)[0:8], same, True),
        dot_t,
        side_by_side(kernel_coarse[8 - t] for t in range(9)),
    )[0:8]

    @pl.loop(0, 9)
    def _(t):
        through[t] = (0.0625 * dot(kernel_fine[8 - t], down_mid[...])).astype(BF16)

    arrived(sum_in, 3)
    arrived(sum_cor, 4)
    sum_extended = mid_extended(
        up_mid_grad.astype(F32), sum_in[...], lambda c: sum_cor[c], same, True
    )
    summed_grad[...] = dot_t(sum_extended.astype(BF16), up_mid[...])

    loads["gain_coarse"].wait()
    coarse_center, coarse_square = total_end(2, 512, 8 * wide_count * narrow_count)
    coarse_inverse = lax.rsqrt(coarse_square - coarse_center * coarse_center + epsilon)
    s_coarse = gain_coarse[...]

    def coarse_scaled(value):
        return (value - coarse_center) * coarse_inverse

    scaled = coarse_scaled(coarse_value)
    normed_grad = coarse_act_grad * slope(scaled, s_coarse)
    total_begin(3, column_sums(normed_grad), column_sums(normed_grad * scaled))
    coarse_u[...] = cgrad + coarse_inverse * normed_grad
    send_coarse(coarse_u, coarse_u_halo, 9)
    grad_sums = lax.fori_loop(2, 4, convolve_grad, grad_sums)

    total_middle(3)

    mid_mix = jnp.concatenate(
        [mid_scaled(mid_value).astype(BF16), jnp.ones((128, 128), BF16)], axis=1
    )
    for n in range(2):
        sums = side_by_side(window_sums[n, t].reshape(128, 256) for t in range(9))
        mixed[n] = dot_first(sums, mid_mix).astype(BF16).reshape(9, 256, 640)

    @pl.loop(0, 16)
    def _(part):
        here = pl.ds(pl.multiple_of(16 * part, 16), 16)
        totals = [jnp.zeros((16, 512), F32) for _ in range(4)]
        for t in range(9):
            weight = through[t, here, :].astype(F32)
            for n in range(2):
                value = mixed[n, t, here, :].astype(F32)
                totals[2 * n] += weight * side_by_side([value[:, 512:640]] * 4)
                totals[2 * n + 1] += weight * value[:, 0:512]
        for n in range(4):
            matrix_sum[n, here, :] = totals[n]

    def iota(shape, axis):
        return lax.broadcasted_iota(jnp.int32, shape, axis)

    def one_hot(condition):
        return jnp.where(condition, 1.0, 0.0).astype(BF16)

    by_group = one_hot((iota((32, 256), 1) >> 3) == iota((32, 256), 0))
    matrix = jnp.zeros((32, 128), F32)
    for n in range(4):
        high, low = halves(matrix_sum[n] * mid_inverse)
        high, low = halves(dot(by_group, high) + dot(by_group, low))
        to_lane = one_hot(iota((512, 128), 1) == 32 * n + (iota((512, 128), 0) >> 4))
        matrix += dot(high, to_lane) + dot(low, to_lane)
    first_matrix[wide] = matrix.astype(BF16)
    total_send_wide(6)

    first_mean, second_mean = total_end(3, 512, 8 * wide_count * narrow_count)
    arrived(coarse_halo, 8)
    arrived(coarse_u_halo, 9)
    offset = coarse_inverse * first_mean
    factor = coarse_inverse * second_mean
    pieces = [coarse_u[...] - offset - scaled * factor]
    for d in range(8):
        piece = coarse_scaled(coarse_halo[d].astype(F32)[0:8])
        pieces.append(coarse_u_halo[d] - offset - piece * factor)
    pieces.append(jnp.zeros((56, 512), F32))
    coarse_in_grad = jnp.concatenate(pieces, axis=0).astype(BF16)

    mid_pool_grad = dot_t(dot(SPREAD[...], coarse_in_grad).astype(BF16), down_coarse[...])
    row = lax.broadcasted_iota(jnp.int32, (256, 128), 0)
    keep = jnp.where(row < ABOVE, 1.0, 0.0)
    bounds = ((ABOVE, 16, 1), (BELOW, 16, 2), (LEFT, 32, 3), (RIGHT, 32, 4)) + tuple(
        (CORNER + 4 * c, 4, 5 + c) for c in range(4)
    )
    for start, size, d in bounds:
        inside = jnp.logical_and(row >= start, row < start + size)
        keep = jnp.where(inside, jnp.where(exists[d], 1.0, 0.0).astype(F32), keep)
    mid_grad = (summed_grad[...] + 0.0625 * mid_pool_grad) * jnp.concatenate([keep] * 4, axis=1)
    mid_act_grad = mid_convolve(
        mid_grad, dot_t, side_by_side(kernel_mid[8 - t] for t in range(9))
    )
    scaled = mid_scaled(mid_value)
    normed_grad = mid_act_grad * slope(scaled, s_mid)
    total_begin(4, column_sums(normed_grad), column_sums(normed_grad * scaled))
    mid_u = mid_grad[0:128].astype(BF16).astype(F32) + mid_inverse * normed_grad
    u_pack[...] = dot(PACK[...], mid_u.astype(BF16)).astype(BF16)
    send_mid(u_pack, u_halo, u_cor, 10)
    pulled = (0.0625 * dot_t(mid_u.astype(BF16), down_mid[...])).astype(BF16)
    fine_sums = [jnp.sum(value, axis=0, keepdims=True) for value in grad_sums]
    for t in range(9):
        term = dot_t(pulled, kernel_fine[8 - t])
        for n in range(2):
            fine_sums[n] += column_sums(window_sums[n, t].reshape(128, 256).astype(F32) * term)
    total_begin(5, *fine_sums)
    total_middle(6)

    coarse_block = (
        coarse_in.astype(F32)
        + coarse_convolve(
            coarse_extended(
                coarse_value,
                lambda d: coarse_halo[d].astype(F32)[0:8],
                silu(coarse_center, coarse_inverse, s_coarse),
                True,
            ),
            dot,
            kernel_coarse[...].reshape(4608, 512),
        )
    ).astype(BF16)
    coarse_up = dot(coarse_block, up_coarse[...]).astype(BF16)
    mid_sum = (mid_block.astype(F32) + dot(SPREAD[0:128, 0:16], coarse_up)).astype(BF16)
    mid_up = dot(mid_sum, up_mid[...]).astype(BF16)
    total_middle(4)
    total_middle(5)

    fine_forward(2)
    fine_forward(3)
    mid_up = dot(ENLARGE[:, 0:128], mid_up).reshape(4, 8, 1, 16, 256)
    for f in range(4):
        block = fine_block[f].astype(F32).reshape(8, 4, 16, 256)
        fine_block[f] = (block + mid_up[f]).astype(BF16).reshape(512, 256)
    out_copy = pltpu.make_async_copy(fine_block, out_ref, out_sem.at[0])
    out_copy.start()
    first_mean, second_mean = total_end(4, 512, 128 * wide_count * narrow_count)
    arrived(u_halo, 10)
    arrived(u_cor, 11)
    offset = mid_inverse * first_mean
    factor = mid_inverse * second_mean
    mid_in_grad = mid_extended(
        mid_u, u_halo[...], lambda c: u_cor[c], lambda v: v - offset, False
    ) - factor * mid_extended(
        mid_value, mid_halo[...], lambda c: mid_cor[c], mid_scaled, False
    )

    pool_grad = 0.0625 * dot_t(mid_in_grad.astype(BF16), down_mid[...])
    pool_grad = pool_grad * jnp.concatenate([keep] * 2, axis=1)
    high, low = halves(pool_grad)
    added = dot(ENLARGE[...], jnp.concatenate([high[0:256], low[0:256]], axis=0))
    loads["stretch"].wait()
    for a in range(3):
        fields = [dot_t(high, kernel_fine[8 - 3 * a - b]).astype(BF16) for b in range(3)]
        stretched[a] = dot(stretch[...], jnp.concatenate(fields, axis=0)).reshape(4, 10, 16, 256)

    means = jnp.zeros((8, 128), F32)
    for n, mean in enumerate((first_mean, second_mean)):
        lane, row = iota((512, 128), 1), iota((512, 128), 0)
        inside = jnp.logical_and((lane & 31) == (row >> 4), ((lane >> 5) & 1) == n)
        to_lane = jnp.where(inside, 0.0625, 0.0).astype(BF16)
        high, low = halves(jnp.broadcast_to(mean, (8, 512)))
        means += dot(high, to_lane) + dot(low, to_lane)
    matrix_high, matrix_low = halves(total_sum(6))
    fine_totals = total_groups(5, 256, 1.0)
    spread_groups = one_hot((iota((256, 32), 0) >> 3) == iota((256, 32), 1))
    fine_means = []
    for n in range(2):
        half = jnp.where((iota((8, 128), 1) >> 6) == n, means, 0.0)
        high, low = halves(half)
        change = dot_t(high, matrix_high) + dot_t(low, matrix_high) + dot_t(high, matrix_low)
        high, low = halves(change)
        change = dot_t(high, spread_groups) + dot_t(low, spread_groups)
        fine_means.append(
            (fine_totals[n] - change[0:1]) * (1.0 / (8 * 2048 * wide_count * narrow_count))
        )
    slant = -fine_inverse * fine_inverse * fine_means[1]
    shift = -fine_inverse * fine_means[0] - fine_center * slant

    added = added.reshape(4, 8, 1, 16, 256)
    grad_copies = []
    for f in range(4):
        above, here, below = stretched[0, f], stretched[1, f], stretched[2, f]
        centre = here[1:9] + above[1:9] + below[1:9]
        top = here[1:9] + above[0:8] + below[1:9]
        bottom = here[1:9] + above[1:9] + below[2:10]
        back = jnp.stack([top, centre, centre, bottom], axis=1).reshape(512, 256)
        normed_grad = (conv_grad[f] + back) * fine_slope[f]
        grad = xg[1, f].astype(F32).reshape(8, 4, 16, 256) + added[f]
        grad = grad.reshape(512, 256).astype(BF16).astype(F32)
        grad_buf[f] = grad + fine_inverse * normed_grad + (shift + fine_value(f) * slant)
        grad_copies.append(
            pltpu.make_async_copy(grad_buf.at[f], grad_ref.at[f], out_sem.at[1 + f])
        )
        grad_copies[f].start()

    for which in range(2):
        sent(row_in.at[:, which], 13 * which)
        sent(col_in.at[:, which], 13 * which + 1)
        sent(cor_in.at[which], 13 * which + 2)
    sent(sum_in, 3)
    sent(sum_cor, 4)
    sent(cgrad_in, 5)
    sent(mid_halo, 6)
    sent(mid_cor, 7)
    sent(coarse_halo, 8)
    sent(coarse_u_halo, 9)
    sent(u_halo, 10)
    sent(u_cor, 11)
    for phase in range(7):
        whole = firsts[phase].at[pl.ds(0, wide_count - 1)]
        pltpu.make_async_copy(whole, whole, total_send.at[2 * phase]).wait()
        whole = seconds[phase].at[pl.ds(0, narrow_count - 1)]
        pltpu.make_async_copy(whole, whole, total_send.at[2 * phase + 1]).wait()
    out_copy.wait()
    for copy in grad_copies:
        copy.wait()


def shards(*arguments):
    (
        fine_input,
        gain_fine,
        kernel_fine,
        down_mid,
        gain_mid,
        kernel_mid,
        down_coarse,
        gain_coarse,
        kernel_coarse,
        up_coarse,
        up_mid,
        grad_out,
    ) = arguments
    wide_count, narrow_count = lax.axis_size("wide"), lax.axis_size("narrow")
    anywhere = pl.BlockSpec(memory_space=pl.ANY)
    vmem = pltpu.VMEM
    scratch = [
        vmem((2, 4, 32, 16, 256), BF16),
        vmem((9, 256, 256), BF16),
        vmem((256, 512), BF16),
        vmem((9, 512, 512), BF16),
        vmem((512, 512), BF16),
        vmem((9, 512, 512), BF16),
        vmem((512, 512), BF16),
        vmem((512, 256), BF16),
        vmem((1, 256), F32),
        vmem((1, 512), F32),
        vmem((1, 512), F32),
        vmem((608, 512), BF16),
        vmem((1168, 256), BF16),
        vmem((1168, 128), BF16),
        vmem((288, 640), BF16),
        vmem((640, 768), BF16),
        vmem((4, 544, 768), BF16),
        vmem((4, 512, 256), BF16),
        vmem((4, 512, 256), F32),
        vmem((4, 512, 256), F32),
        vmem((128, 256), F32),
        vmem((128, 256), BF16),
        vmem((4, 512, 256), F32),
        vmem((2, 2, 4, 16, 256), F32),
        vmem((2, 4, 64, 256), F32),
        vmem((2, 16, 256), F32),
        vmem((256, 512), F32),
        vmem((6, wide_count, 1, 128), F32),
        vmem((6, narrow_count, 1, 128), F32),
        vmem((8, 128), F32),
        vmem((wide_count, 32, 128), BF16),
        vmem((narrow_count, 32, 128), BF16),
        vmem((2, 9, 4, 32, 256), BF16),
        vmem((2, 2, 4, 16, 256), BF16),
        vmem((2, 2, 4, 32, 256), BF16),
        vmem((2, 4, 32, 256), BF16),
        vmem((4, 256, 512), F32),
        vmem((9, 256, 512), BF16),
        vmem((2, 9, 256, 640), BF16),
        vmem((3, 4, 10, 16, 256), F32),
        vmem((2, 2, 128, 256), BF16),
        vmem((2, 16, 256), BF16),
        vmem((2, 2, 4, 16, 256), BF16),
        vmem((2, 2, 128, 256), BF16),
        vmem((2, 4, 16, 256), BF16),
        vmem((112, 256), BF16),
        vmem((96, 256), BF16),
        vmem((4, 16, 256), BF16),
        vmem((16, 512), BF16),
        vmem((8, 16, 512), BF16),
        vmem((112, 512), BF16),
        vmem((96, 512), BF16),
        vmem((4, 16, 512), BF16),
        vmem((16, 512), BF16),
        vmem((8, 16, 512), BF16),
        vmem((8, 512), F32),
        vmem((8, 8, 512), F32),
        vmem((112, 512), BF16),
        vmem((96, 512), BF16),
        vmem((4, 16, 512), BF16),
        pltpu.SemaphoreType.DMA((20,)),
        pltpu.SemaphoreType.DMA((5,)),
        pltpu.SemaphoreType.DMA((14,)),
        pltpu.SemaphoreType.DMA((14,)),
        pltpu.SemaphoreType.DMA((16,)),
        pltpu.SemaphoreType.DMA((16,)),
    ]
    output, grad = pl.pallas_call(
        functools.partial(kernel, wide_count, narrow_count),
        out_shape=(
            jax.ShapeDtypeStruct((4, 512, 256), BF16),
            jax.ShapeDtypeStruct((4, 512, 256), F32),
        ),
        in_specs=[anywhere] * 17,
        out_specs=(anywhere, anywhere),
        scratch_shapes=scratch,
        compiler_params=pltpu.CompilerParams(
            collective_id=0, has_side_effects=True, vmem_limit_bytes=56 * 2**20
        ),
        name="whole_net",
    )(
        fine_input,
        gain_fine.reshape(1, 256),
        kernel_fine.reshape(9, 256, 256),
        down_mid,
        gain_mid.reshape(1, 512),
        kernel_mid.reshape(9, 512, 512),
        down_coarse,
        gain_coarse.reshape(1, 512),
        kernel_coarse.reshape(9, 512, 512),
        up_coarse,
        up_mid,
        grad_out,
        *tables(),
    )
    return output.reshape(4, 32, 16, 256), grad.reshape(4, 32, 16, 256)


def solution(mesh):
    tile = P(None, "wide", "narrow", None)
    return jax.shard_map(
        shards,
        mesh=mesh,
        in_specs=(tile,) + (P(),) * 10 + (tile,),
        out_specs=(tile, tile),
        check_vma=False,
    )
```

```python
import functools

import jax
import jax.numpy as jnp
import numpy as np
from jax import lax
from jax.experimental import pallas as pl
from jax.experimental.pallas import tpu as pltpu
from jax.sharding import PartitionSpec as P

MESH = pl.DeviceIdType.MESH
GROUPS = 32
epsilon = 1e-05
F32 = jnp.float32
BF16 = jnp.bfloat16

DIRS = ((0, 0), (-1, 0), (1, 0), (0, -1), (0, 1), (-1, -1), (-1, 1), (1, -1), (1, 1))

ABOVE, BELOW, LEFT, RIGHT, CORNER = 128, 144, 160, 192, 224


def mid_row(f, i, j):
    if 0 <= i < 8 and 0 <= j < 4:
        return 32 * f + 4 * i + j
    if i < 0 and 0 <= j < 4:
        return ABOVE + 4 * f + j
    if i > 7 and 0 <= j < 4:
        return BELOW + 4 * f + j
    if 0 <= i < 8:
        return (LEFT if j < 0 else RIGHT) + 8 * f + i
    return CORNER + 4 * (2 * (i > 7) + (j > 3)) + f


def coarse_row(f, i, side):
    down = -1 if i < 0 else (1 if i > 1 else 0)
    return 8 * DIRS.index((down, side)) + 2 * f + i % 2


def tables():
    pick = np.zeros((96, 512), np.float32)
    for i in range(32):
        for j in range(16):
            pick[4 * (i // 4) + j // 4, 16 * i + j] = 1
        pick[32 + i, 16 * i + 15] = 1
        pick[64 + i, 16 * i] = 1
    enlarge = np.zeros((512, 256), np.float32)
    taps = np.zeros((1152, 256), np.float32)
    ends = np.zeros((16, 256), np.float32)
    pack = np.zeros((112, 128), np.float32)
    pool = np.zeros((16, 128), np.float32)
    coarse_taps = np.zeros((144, 128), np.float32)
    spread = np.zeros((256, 128), np.float32)
    for f in range(4):
        for i in range(8):
            for j in range(16):
                enlarge[128 * f + 16 * i + j, mid_row(f, i, j // 4)] = 1
        for c in range(4):
            low, first = c < 2, c % 2 == 1
            ends[4 * c + f, 128 * first + 32 * f + 31 * low] = 1
            pack[96 + 4 * c + f, mid_row(f, 7 * low, 3 * (not first))] = 1
        for i in range(8):
            for j in range(4):
                here = 32 * f + 4 * i + j
                pool[2 * f + i // 4, here] = 1
                for t in range(9):
                    taps[128 * t + here, mid_row(f, i + t // 3 - 1, j + t % 3 - 1)] = 1
            pack[32 + 8 * f + i, mid_row(f, i, 3)] = 1
            pack[64 + 8 * f + i, mid_row(f, i, 0)] = 1
        for j in range(4):
            pack[4 * f + j, mid_row(f, 7, j)] = 1
            pack[16 + 4 * f + j, mid_row(f, 0, j)] = 1
        for i in range(2):
            for t in range(9):
                coarse_taps[16 * t + 2 * f + i, coarse_row(f, i + t // 3 - 1, t % 3 - 1)] = 1
        for i in range(-1, 9):
            for j in range(-1, 5):
                side = -1 if j < 0 else (1 if j > 3 else 0)
                spread[mid_row(f, i, j), coarse_row(f, i // 4 if i < 8 else 2, side)] = 1
    windows = np.zeros((288, 640), np.float32)
    for t in range(9):
        for i in range(32):
            for j in range(16):
                p, q = i + 1 - t // 3, j + 1 - t % 3
                row = 32 * t + 4 * (i // 4) + j // 4
                if 0 <= p < 32 and 0 <= q < 16:
                    at = 16 * p + q
                elif 0 <= q < 16:
                    at = (512 if p < 0 else 528) + q
                elif 0 <= p < 32:
                    at = (544 if q < 0 else 576) + p
                else:
                    at = 608 + 2 * (p > 31) + (q > 15)
                windows[row, at] = 1
    stretch = np.zeros((640, 768), np.float32)
    for f in range(4):
        for i in range(10):
            for j in range(16):
                for b in range(3):
                    at = 256 * b + mid_row(f, i - 1, (j + b - 1) // 4)
                    stretch[160 * f + 16 * i + j, at] = 1
    by_frame = np.zeros((128, 128), np.float32)
    for f in range(4):
        for c in range(4):
            by_frame[32 * f + c, 4 * c + f] = 1
    sides = np.zeros((512, 128), np.float32)
    for i in range(32):
        sides[16 * i, i] = 1
        sides[16 * i + 15, 64 + i] = 1
    wide_table = np.concatenate([pick, np.concatenate([enlarge, enlarge], axis=1)])
    middle_table = np.concatenate([taps, ends])
    narrow_table = np.concatenate([pack, pool, coarse_taps, spread, sides, by_frame])
    result = (wide_table, middle_table, narrow_table, windows, stretch)
    return [jnp.asarray(t, BF16) for t in result]


def dot(a, b):
    return jnp.dot(a, b, preferred_element_type=F32)


def dot_t(a, b):
    return lax.dot_general(a, b, (((1,), (1,)), ((), ())), preferred_element_type=F32)


def dot_first(a, b):
    return lax.dot_general(a, b, (((0,), (0,)), ((), ())), preferred_element_type=F32)


def group_lanes(t, size):
    lane = lax.broadcasted_iota(jnp.int32, t.shape, 1)
    step = 1
    while step < size:
        t = t + jnp.where(
            (lane & step) != 0, pltpu.roll(t, step, 1), pltpu.roll(t, 128 - step, 1)
        )
        step *= 2
    return t


def halves(t):
    high = t.astype(BF16)
    return high, (t - high.astype(F32)).astype(BF16)


def kernel(
    wide_count,
    narrow_count,
    x_in,
    gain_fine_in,
    kernel_fine_in,
    down_mid_in,
    gain_mid_in,
    kernel_mid_in,
    down_coarse_in,
    gain_coarse_in,
    kernel_coarse_in,
    up_coarse_in,
    up_mid_in,
    grad_in,
    wide_table_in,
    middle_table_in,
    narrow_table_in,
    windows_in,
    stretch_in,
    out_ref,
    grad_ref,
    xg,
    kernel_fine,
    down_mid,
    kernel_mid,
    down_coarse,
    kernel_coarse,
    up_coarse,
    up_mid,
    gain_fine,
    gain_mid,
    gain_coarse,
    wide_table,
    middle_table,
    narrow_table,
    windows,
    stretch,
    columns,
    fine_block,
    grad_buf,
    conv_grad,
    pooled_x,
    summed,
    fine_slope,
    edge_rows,
    edge_sides,
    edge_ends,
    summed_grad,
    first,
    second,
    rows,
    first_matrix,
    second_matrix,
    window_sums,
    rim_rows,
    rim_sides,
    rim_ends,
    matrix_sum,
    through,
    mixed,
    stretched,
    col_pack,
    cor_pack,
    row_in,
    col_in,
    cor_in,
    sum_pack,
    sum_in,
    sum_cor,
    cgrad_own,
    cgrad_in,
    mid_pack,
    mid_halo,
    mid_cor,
    coarse_own,
    coarse_halo,
    coarse_u,
    coarse_u_halo,
    u_pack,
    u_halo,
    u_cor,
    load_sem,
    out_sem,
    total_send,
    total_recv,
    halo_send,
    halo_recv,
):
    wide, narrow = lax.axis_index("wide"), lax.axis_index("narrow")

    def around(index, step, count):
        moved = index + step
        if isinstance(step, int) and step < 0:
            return jnp.where(moved < 0, moved + count, moved)
        return jnp.where(moved >= count, moved - count, moved)

    def device(down, side):
        return (
            wide if isinstance(down, int) and down == 0 else around(wide, down, wide_count),
            narrow if isinstance(side, int) and side == 0 else around(narrow, side, narrow_count),
        )

    loads = {}
    pairs = (
        ("x0", x_in.at[0], xg.at[0, 0]),
        ("x1", x_in.at[1], xg.at[0, 1]),
        ("x2", x_in.at[2], xg.at[0, 2]),
        ("x3", x_in.at[3], xg.at[0, 3]),
        ("grad", grad_in, xg.at[1]),
        ("wide_table", wide_table_in, wide_table),
        ("middle_table", middle_table_in, middle_table),
        ("narrow_table", narrow_table_in, narrow_table),
        ("gain_fine", gain_fine_in, gain_fine),
        ("windows", windows_in, windows),
        ("kernel_fine", kernel_fine_in, kernel_fine),
        ("up_mid", up_mid_in, up_mid),
        ("up_coarse", up_coarse_in, up_coarse),
        ("down_mid", down_mid_in, down_mid),
        ("gain_mid", gain_mid_in, gain_mid),
        ("kernel_coarse", kernel_coarse_in, kernel_coarse),
        ("kernel_mid", kernel_mid_in, kernel_mid),
        ("down_coarse", down_coarse_in, down_coarse),
        ("gain_coarse", gain_coarse_in, gain_coarse),
        ("stretch", stretch_in, stretch),
    )
    for number, (name, source, target) in enumerate(pairs):
        loads[name] = pltpu.make_async_copy(source, target, load_sem.at[number])

    def begin_loads(*names):
        for name in names:
            loads[name].start()

    begin_loads("x0", "x1", "x2", "x3", "wide_table", "middle_table")

    barrier = pltpu.get_barrier_semaphore()
    greeted = 0
    for down in range(wide_count):
        for side in range(-2, narrow_count - 2):
            near = (down <= 1 or down == wide_count - 1) and abs(side) <= 1
            if (down, side) != (0, 0) and (down == 0 or side == 0 or near):
                pl.semaphore_signal(
                    barrier, inc=1, device_id=device(down, side), device_id_type=MESH
                )
                greeted += 1

    def send(source, target, which, down, side):
        pltpu.make_async_remote_copy(
            src_ref=source,
            dst_ref=target,
            send_sem=halo_send.at[which],
            recv_sem=halo_recv.at[which],
            device_id=device(down, side),
            device_id_type=MESH,
        ).start()

    def arrived(buffer, which):
        pltpu.make_async_copy(buffer, buffer, halo_recv.at[which]).wait()

    def sent(buffer, which):
        pltpu.make_async_copy(buffer, buffer, halo_send.at[which]).wait()

    firsts = tuple(first.at[p] for p in range(6)) + (first_matrix,)
    seconds = tuple(second.at[p] for p in range(6)) + (second_matrix,)

    def total_send_wide(phase):
        mine = firsts[phase].at[wide]

        for step in sorted(range(1, wide_count), key=lambda k: -min(k & 7, 8 - (k & 7))):
            pltpu.make_async_remote_copy(
                src_ref=mine,
                dst_ref=mine,
                send_sem=total_send.at[2 * phase],
                recv_sem=total_recv.at[2 * phase],
                device_id=device(step, 0),
                device_id_type=MESH,
            ).start()

    def diagonal(shape=(8, 128)):
        lane = lax.broadcasted_iota(jnp.int32, shape, 1) & 7
        return lane == lax.broadcasted_iota(jnp.int32, shape, 0)

    def total_begin(phase, one, two):
        channels = one.shape[1]
        if channels < 512:
            rows[...] = jnp.zeros((8, 128), F32)
        for n, value in enumerate((one, two)):
            for k in range(channels // 128):
                rows[4 * n + k : 4 * n + k + 1, :] = value[:, 128 * k : 128 * k + 128]
        grouped = group_lanes(rows[...], channels // GROUPS)
        grouped = jnp.where(diagonal(), grouped, 0.0)
        firsts[phase][wide] = jnp.sum(grouped, axis=0, keepdims=True)
        total_send_wide(phase)

    def total_middle(phase):
        whole = firsts[phase].at[pl.ds(0, wide_count - 1)]
        pltpu.make_async_copy(whole, whole, total_recv.at[2 * phase]).wait()
        summed_up = jnp.sum(firsts[phase][...].astype(F32), axis=0)
        seconds[phase][narrow] = summed_up.astype(seconds[phase].dtype)
        mine = seconds[phase].at[narrow]

        for step in sorted(range(1, narrow_count), key=lambda k: -min(k & 3, 4 - (k & 3))):
            pltpu.make_async_remote_copy(
                src_ref=mine,
                dst_ref=mine,
                send_sem=total_send.at[2 * phase + 1],
                recv_sem=total_recv.at[2 * phase + 1],
                device_id=device(0, step),
                device_id_type=MESH,
            ).start()

    def total_sum(phase):
        whole = seconds[phase].at[pl.ds(0, narrow_count - 1)]
        pltpu.make_async_copy(whole, whole, total_recv.at[2 * phase + 1]).wait()
        return jnp.sum(seconds[phase][...].astype(F32), axis=0)

    def row_of(t, start, channels):
        return jnp.concatenate([t[start + k : start + k + 1] for k in range(channels // 128)], axis=1)

    def total_groups(phase, channels, scale):
        packed = jnp.broadcast_to(total_sum(phase), (8, 128))
        t = group_lanes(jnp.where(diagonal(), packed, 0.0), 8) * scale
        return row_of(t, 0, channels), row_of(t, 4, channels)

    def total_end(phase, channels, cells):
        return total_groups(phase, channels, 1.0 / (channels // GROUPS * cells))

    has_above, has_below = wide > 0, wide < wide_count - 1
    has_left, has_right = narrow > 0, narrow < narrow_count - 1
    has_corner = (
        jnp.logical_and(has_above, has_left),
        jnp.logical_and(has_above, has_right),
        jnp.logical_and(has_below, has_left),
        jnp.logical_and(has_below, has_right),
    )
    exists = (None, has_above, has_below, has_left, has_right) + has_corner

    def only(condition, value):
        return value * jnp.where(condition, 1.0, 0.0).astype(F32)

    def corners(read, change, masked):
        result = None
        for c in range(4):
            value = change(read(c).astype(F32))
            if masked:
                value = only(has_corner[c], value)
            cell = lax.broadcasted_iota(jnp.int32, value.shape, 0)
            result = value if result is None else jnp.where(cell >= 4 * c, value, result)
        return result

    def mid_extended(own, read_halo, read_cor, change, masked):
        pieces = [change(own)]
        halo = change(read_halo.astype(F32))
        for low, high, d in ((0, 16, 1), (16, 32, 2), (32, 64, 3), (64, 96, 4)):
            piece = halo[low:high]
            pieces.append(only(exists[d], piece) if masked else piece)
        pieces.append(corners(read_cor, change, masked))
        pieces.append(jnp.zeros((16, own.shape[1]), F32))
        return jnp.concatenate(pieces, axis=0)

    def send_mid(pack, halo, cor, which):
        send(pack.at[pl.ds(0, 16)], halo.at[pl.ds(0, 16)], which, 1, 0)
        send(pack.at[pl.ds(16, 16)], halo.at[pl.ds(16, 16)], which, -1, 0)
        send(pack.at[pl.ds(32, 32)], halo.at[pl.ds(32, 32)], which, 0, 1)
        send(pack.at[pl.ds(64, 32)], halo.at[pl.ds(64, 32)], which, 0, -1)
        for c in range(4):
            down, side = DIRS[5 + c]
            send(pack.at[pl.ds(96, 16)], cor.at[c], which + 1, -down, -side)

    def send_coarse(own, halo, which):
        for d in range(1, 9):
            down, side = DIRS[d]
            send(own, halo.at[d - 1], which, -down, -side)

    def coarse_extended(own, halo, change, masked):
        pieces = [change(own)]
        for d in range(1, 9):
            piece = change(halo(d - 1))
            pieces.append(only(exists[d], piece) if masked else piece)
        pieces.append(jnp.zeros((56, own.shape[1]), F32))
        return jnp.concatenate(pieces, axis=0)

    PICK = wide_table.at[pl.ds(0, 96)]
    ENLARGE = wide_table.at[pl.ds(96, 512)]
    TAPS = middle_table.at[pl.ds(0, 1152)]
    ENDS = middle_table.at[pl.ds(1152, 16)]
    PACK = narrow_table.at[pl.ds(0, 112)]
    POOL = narrow_table.at[pl.ds(112, 16)]
    COARSE_TAPS = narrow_table.at[pl.ds(128, 144)]
    SPREAD = narrow_table.at[pl.ds(272, 256)]
    SIDES = narrow_table.at[pl.ds(528, 512)]
    BY_FRAME = narrow_table.at[pl.ds(1040, 128)]

    def frame(which, f):
        return xg[which, f].reshape(512, 256)

    blank = jnp.zeros((8, 256), F32)
    one, two = blank, blank
    for f in range(4):
        loads["x%d" % f].wait()
        value = frame(0, f).astype(F32)
        one += jnp.sum(value.reshape(64, 8, 256), axis=0)
        two += jnp.sum((value * value).reshape(64, 8, 256), axis=0)
    pl.semaphore_wait(barrier, greeted)
    total_begin(0, jnp.sum(one, axis=0, keepdims=True), jnp.sum(two, axis=0, keepdims=True))

    begin_loads("grad", "narrow_table", "gain_fine", "windows", "kernel_fine")
    begin_loads("up_mid", "up_coarse", "down_mid", "gain_mid")

    def rim_rows_out(which):
        send(xg.at[which, :, 31], row_in.at[0, which], 13 * which, 1, 0)
        send(xg.at[which, :, 0], row_in.at[1, which], 13 * which, -1, 0)

    def rim_pick(which):
        for f in range(4):
            picked = dot(PICK[...], frame(which, f))
            if which == 0:
                pooled_x[32 * f : 32 * f + 32] = picked[0:32]
            picked = picked.astype(BF16)
            col_pack[0, which, 32 * f : 32 * f + 32] = picked[32:64]
            col_pack[1, which, 32 * f : 32 * f + 32] = picked[64:96]
            if which == 1:
                summed[32 * f : 32 * f + 32] = picked[0:32]

    def rim_sides_out(which):
        send(col_pack.at[0, which], col_in.at[0, which], 13 * which + 1, 0, 1)
        send(col_pack.at[1, which], col_in.at[1, which], 13 * which + 1, 0, -1)

    def rim_ends_out(which):
        ends = jnp.concatenate([col_pack[0, which], col_pack[1, which]], axis=0)
        cor_pack[which] = dot(ENDS[...], ends).astype(BF16)
        for c in range(4):
            down, side = DIRS[5 + c]
            send(cor_pack.at[which], cor_in.at[which, c], 13 * which + 2, -down, -side)

    loads["wide_table"].wait()
    loads["middle_table"].wait()
    rim_rows_out(0)
    rim_pick(0)
    rim_sides_out(0)
    rim_ends_out(0)
    loads["grad"].wait()
    rim_pick(1)
    total_middle(0)
    begin_loads("kernel_mid")
    rim_rows_out(1)
    rim_sides_out(1)
    rim_ends_out(1)
    loads["narrow_table"].wait()

    up_mid_grad = summed[...]
    sum_pack[...] = dot(PACK[...], up_mid_grad).astype(BF16)
    send_mid(sum_pack, sum_in, sum_cor, 3)
    loads["up_mid"].wait()
    high, low = halves(dot_t(up_mid_grad, up_mid[...]))
    up_coarse_grad = (dot(POOL[...], high) + dot(POOL[...], low)).astype(BF16)
    loads["up_coarse"].wait()
    cgrad_own[...] = dot_t(up_coarse_grad, up_coarse[...]).astype(BF16)
    send_coarse(cgrad_own, cgrad_in, 5)

    loads["gain_fine"].wait()
    loads["kernel_fine"].wait()
    loads["down_mid"].wait()

    fine_center, fine_square = total_end(0, 256, 2048 * wide_count * narrow_count)
    fine_inverse = lax.rsqrt(fine_square - fine_center * fine_center + epsilon)
    s_fine = gain_fine[...]

    def silu(center, inverse, scaling):
        gain = 0.5 * inverse * scaling
        shift = -center * gain

        def change(value):
            half = value * gain + shift
            return half * jnp.tanh(half) + half

        return change

    def slope(scaled, scaling):
        half = scaled * (0.5 * scaling)
        bend = jnp.tanh(half)
        return (0.5 * scaling) * (1.0 + bend) * (1.0 + half * (1.0 - bend))

    fine_act = silu(fine_center, fine_inverse, s_fine)

    arrived(row_in.at[:, 0], 0)
    arrived(col_in.at[:, 0], 1)
    arrived(cor_in.at[0], 2)

    def set_edges(kind, above, below, left, right, ends):
        edge_rows[kind, 0] = only(has_above, above)
        edge_rows[kind, 1] = only(has_below, below)
        left = only(has_left, left)
        right = only(has_right, right)
        for f in range(4):
            edge_sides[kind, f, 0:32] = left[32 * f : 32 * f + 32]
            edge_sides[kind, f, 32:64] = right[32 * f : 32 * f + 32]
        edge_ends[kind] = ends

    def place(kind, f, own):
        column = lax.broadcasted_iota(jnp.int32, (32, 16, 256), 1)
        west, east = (
            jnp.broadcast_to(edge_sides[kind, f, 32 * k : 32 * k + 32].reshape(32, 1, 256), (32, 16, 256))
            for k in range(2)
        )
        low = jnp.where(column == 0, west, pltpu.roll(own, 1, 0).reshape(32, 16, 256))
        columns[f, 16:528, 0:256] = low.reshape(512, 256).astype(BF16)
        columns[f, 16:528, 256:512] = own.astype(BF16)
        high = jnp.where(column == 15, east, pltpu.roll(own, 511, 0).reshape(32, 16, 256))
        columns[f, 16:528, 512:768] = high.reshape(512, 256).astype(BF16)
        cell = lax.broadcasted_iota(jnp.int32, (16, 256), 0)
        for k in range(2):
            row = edge_rows[kind, k, f]
            at = slice(528 * k, 528 * k + 16)
            west = edge_ends[kind, pl.ds(8 * k + f, 1), :]
            east = edge_ends[kind, pl.ds(8 * k + 4 + f, 1), :]
            columns[f, at, 0:256] = jnp.where(cell == 0, west, pltpu.roll(row, 1, 0)).astype(BF16)
            columns[f, at, 256:512] = row.astype(BF16)
            columns[f, at, 512:768] = jnp.where(cell == 15, east, pltpu.roll(row, 15, 0)).astype(BF16)

    def side_by_side(pieces):
        return jnp.concatenate(list(pieces), axis=1)

    def fine_taps(f):
        return side_by_side(columns[f, 16 * a : 16 * a + 512, :] for a in range(3))

    def fine_convolve(f):
        return dot(fine_taps(f), kernel_fine[...].reshape(2304, 256))

    def fine_convolve_back(f):
        return dot_t(fine_taps(f), side_by_side(kernel_fine[8 - t] for t in range(9)))

    def fine_scaled(value):
        return (value - fine_center) * fine_inverse

    def fine_value(f):
        return frame(0, f).astype(F32)

    def set_fields(n, change):
        for k in range(2):
            rim_rows[n, k] = only(exists[1 + k], change(row_in[k, 0].astype(F32))).astype(BF16)
            sides = only(exists[3 + k], change(col_in[k, 0].astype(F32))).astype(BF16)
            rim_sides[n, k] = sides.reshape(4, 32, 256)
        ends = corners(lambda c: cor_in[0, c], change, True)
        ends = dot(BY_FRAME[:, 0:16], ends.astype(BF16)).astype(BF16)
        rim_ends[n] = ends.reshape(4, 32, 256)

    def window(n, f, own):
        field = jnp.concatenate(
            [
                own.astype(BF16),
                rim_rows[n, 0, f],
                rim_rows[n, 1, f],
                rim_sides[n, 0, f],
                rim_sides[n, 1, f],
                rim_ends[n, f],
            ],
            axis=0,
        )
        return dot(windows[...], field)

    set_fields(0, fine_act)
    loads["windows"].wait()

    @pl.loop(0, 4)
    def _(f):
        sums = window(0, f, fine_act(fine_value(f)))
        high, low = halves(sums)
        window_sums[0, :, f] = high.reshape(9, 32, 256)
        window_sums[1, :, f] = low.reshape(9, 32, 256)

    both = side_by_side(
        jnp.concatenate([window_sums[n, 8 - t].reshape(128, 256) for n in range(2)], axis=0)
        for t in range(9)
    )
    both = dot(both, kernel_fine[...].reshape(2304, 256))
    pooled = pooled_x[...] + both[0:128] + both[128:256]
    pooled = (pooled * 0.0625).astype(BF16)

    def fine_forward(f):
        value = fine_value(f)
        place(0, f, fine_act(value))
        fine_block[f] = (value + fine_convolve(f)).astype(BF16)

    def same(value):
        return value

    mid_in = dot(pooled, down_mid[...]).astype(BF16)
    mid_value = mid_in.astype(F32)

    def column_sums(value):
        return jnp.sum(value, axis=0, keepdims=True)

    total_begin(1, column_sums(mid_value), column_sums(mid_value * mid_value))
    mid_pack[...] = dot(PACK[...], mid_in).astype(BF16)
    send_mid(mid_pack, mid_halo, mid_cor, 6)
    begin_loads("down_coarse", "gain_coarse", "kernel_coarse", "stretch")

    @pl.loop(0, 4)
    def _(f):
        fine_slope[f] = slope(fine_scaled(fine_value(f)), s_fine)

    set_fields(0, lambda v: slope(fine_scaled(v), s_fine))
    set_fields(1, lambda v: slope(fine_scaled(v), s_fine) * fine_scaled(v))

    set_edges(
        0,
        fine_act(row_in[0, 0].astype(F32)),
        fine_act(row_in[1, 0].astype(F32)),
        fine_act(col_in[0, 0].astype(F32)),
        fine_act(col_in[1, 0].astype(F32)),
        corners(lambda c: cor_in[0, c], fine_act, True),
    )
    fine_forward(0)
    total_middle(1)
    fine_forward(1)

    @pl.loop(0, 4)
    def _(f):
        bent = fine_slope[f]
        window_sums[0, :, f] = window(0, f, bent).astype(BF16).reshape(9, 32, 256)
        bent = bent * fine_scaled(fine_value(f))
        window_sums[1, :, f] = window(1, f, bent).astype(BF16).reshape(9, 32, 256)

    loads["gain_mid"].wait()
    loads["kernel_mid"].wait()
    mid_center, mid_square = total_end(1, 512, 128 * wide_count * narrow_count)
    mid_inverse = lax.rsqrt(mid_square - mid_center * mid_center + epsilon)
    s_mid = gain_mid[...]

    mid_act = silu(mid_center, mid_inverse, s_mid)

    def mid_scaled(value):
        return (value - mid_center) * mid_inverse

    def mid_convolve(extended, product, weights):
        taps = dot(TAPS[...], extended.astype(BF16)).astype(BF16)
        return product(side_by_side(taps[128 * t : 128 * t + 128] for t in range(9)), weights)

    arrived(mid_halo, 6)
    arrived(mid_cor, 7)
    mid_block = (
        mid_value
        + mid_convolve(
            mid_extended(mid_value, mid_halo[...], lambda c: mid_cor[c], mid_act, True),
            dot,
            kernel_mid[...].reshape(4608, 512),
        )
    ).astype(BF16)

    loads["down_coarse"].wait()
    mid_pooled = (dot(POOL[...], mid_block) * 0.0625).astype(BF16)
    coarse_in = dot(mid_pooled, down_coarse[...]).astype(BF16)
    coarse_own[...] = coarse_in
    coarse_value = coarse_in.astype(F32)[0:8]
    total_begin(2, column_sums(coarse_value), column_sums(coarse_value * coarse_value))
    send_coarse(coarse_own, coarse_halo, 8)

    arrived(row_in.at[:, 1], 13)
    arrived(col_in.at[:, 1], 14)
    arrived(cor_in.at[1], 15)
    set_edges(
        1,
        row_in[0, 1].astype(F32),
        row_in[1, 1].astype(F32),
        col_in[0, 1].astype(F32),
        col_in[1, 1].astype(F32),
        corners(lambda c: cor_in[1, c], same, True),
    )

    def convolve_grad(f, carry):
        place(1, f, frame(1, f).astype(F32))
        result = fine_convolve_back(f)
        conv_grad[f] = result
        weighted = result * fine_slope[f]
        scaled = fine_scaled(fine_value(f))
        return (
            carry[0] + jnp.sum(weighted.reshape(64, 8, 256), axis=0),
            carry[1] + jnp.sum((weighted * scaled).reshape(64, 8, 256), axis=0),
        )

    grad_sums = lax.fori_loop(0, 2, convolve_grad, (blank, blank))
    total_middle(2)

    arrived(cgrad_in, 5)
    loads["kernel_coarse"].wait()

    def coarse_convolve(extended, product, weights):
        taps = dot(COARSE_TAPS[...], extended.astype(BF16)).astype(BF16)
        return product(side_by_side(taps[16 * t : 16 * t + 16] for t in range(9)), weights)

    cgrad = cgrad_own[...].astype(F32)[0:8]
    coarse_act_grad = coarse_convolve(
        coarse_extended(cgrad, lambda d: cgrad_in[d].astype(F32)[0:8], same, True),
        dot_t,
        side_by_side(kernel_coarse[8 - t] for t in range(9)),
    )[0:8]

    @pl.loop(0, 9)
    def _(t):
        through[t] = (0.0625 * dot(kernel_fine[8 - t], down_mid[...])).astype(BF16)

    arrived(sum_in, 3)
    arrived(sum_cor, 4)
    sum_extended = mid_extended(
        up_mid_grad.astype(F32), sum_in[...], lambda c: sum_cor[c], same, True
    )
    summed_grad[...] = dot_t(sum_extended.astype(BF16), up_mid[...])

    loads["gain_coarse"].wait()
    coarse_center, coarse_square = total_end(2, 512, 8 * wide_count * narrow_count)
    coarse_inverse = lax.rsqrt(coarse_square - coarse_center * coarse_center + epsilon)
    s_coarse = gain_coarse[...]

    def coarse_scaled(value):
        return (value - coarse_center) * coarse_inverse

    scaled = coarse_scaled(coarse_value)
    normed_grad = coarse_act_grad * slope(scaled, s_coarse)
    total_begin(3, column_sums(normed_grad), column_sums(normed_grad * scaled))
    coarse_u[...] = cgrad + coarse_inverse * normed_grad
    send_coarse(coarse_u, coarse_u_halo, 9)
    grad_sums = lax.fori_loop(2, 4, convolve_grad, grad_sums)

    total_middle(3)

    mid_mix = jnp.concatenate(
        [mid_scaled(mid_value).astype(BF16), jnp.ones((128, 128), BF16)], axis=1
    )
    for n in range(2):
        sums = side_by_side(window_sums[n, t].reshape(128, 256) for t in range(9))
        mixed[n] = dot_first(sums, mid_mix).astype(BF16).reshape(9, 256, 640)

    @pl.loop(0, 16)
    def _(part):
        here = pl.ds(pl.multiple_of(16 * part, 16), 16)
        totals = [jnp.zeros((16, 512), F32) for _ in range(4)]
        for t in range(9):
            weight = through[t, here, :].astype(F32)
            for n in range(2):
                value = mixed[n, t, here, :].astype(F32)
                totals[2 * n] += weight * side_by_side([value[:, 512:640]] * 4)
                totals[2 * n + 1] += weight * value[:, 0:512]
        for n in range(4):
            matrix_sum[n, here, :] = totals[n]

    def iota(shape, axis):
        return lax.broadcasted_iota(jnp.int32, shape, axis)

    def one_hot(condition):
        return jnp.where(condition, 1.0, 0.0).astype(BF16)

    by_group = one_hot((iota((32, 256), 1) >> 3) == iota((32, 256), 0))
    matrix = jnp.zeros((32, 128), F32)
    for n in range(4):
        high, low = halves(matrix_sum[n] * mid_inverse)
        high, low = halves(dot(by_group, high) + dot(by_group, low))
        to_lane = one_hot(iota((512, 128), 1) == 32 * n + (iota((512, 128), 0) >> 4))
        matrix += dot(high, to_lane) + dot(low, to_lane)
    first_matrix[wide] = matrix.astype(BF16)
    total_send_wide(6)

    row = lax.broadcasted_iota(jnp.int32, (256, 128), 0)
    keep = jnp.where(row < ABOVE, 1.0, 0.0)
    bounds = ((ABOVE, 16, 1), (BELOW, 16, 2), (LEFT, 32, 3), (RIGHT, 32, 4)) + tuple(
        (CORNER + 4 * c, 4, 5 + c) for c in range(4)
    )
    for start, size, d in bounds:
        inside = jnp.logical_and(row >= start, row < start + size)
        keep = jnp.where(inside, jnp.where(exists[d], 1.0, 0.0).astype(F32), keep)
    mid_scaled_own = mid_scaled(mid_value)
    mid_bend = slope(mid_scaled_own, s_mid)
    first_mean, second_mean = total_end(3, 512, 8 * wide_count * narrow_count)
    arrived(coarse_halo, 8)
    arrived(coarse_u_halo, 9)
    offset = coarse_inverse * first_mean
    factor = coarse_inverse * second_mean
    pieces = [coarse_u[...] - offset - scaled * factor]
    for d in range(8):
        piece = coarse_scaled(coarse_halo[d].astype(F32)[0:8])
        pieces.append(coarse_u_halo[d] - offset - piece * factor)
    pieces.append(jnp.zeros((56, 512), F32))
    coarse_in_grad = jnp.concatenate(pieces, axis=0).astype(BF16)

    mid_pool_grad = dot_t(dot(SPREAD[...], coarse_in_grad).astype(BF16), down_coarse[...])
    mid_grad = (summed_grad[...] + 0.0625 * mid_pool_grad) * jnp.concatenate([keep] * 4, axis=1)
    mid_act_grad = mid_convolve(
        mid_grad, dot_t, side_by_side(kernel_mid[8 - t] for t in range(9))
    )
    scaled = mid_scaled_own
    normed_grad = mid_act_grad * mid_bend
    total_begin(4, column_sums(normed_grad), column_sums(normed_grad * scaled))
    mid_u = mid_grad[0:128].astype(BF16).astype(F32) + mid_inverse * normed_grad
    u_pack[...] = dot(PACK[...], mid_u.astype(BF16)).astype(BF16)
    send_mid(u_pack, u_halo, u_cor, 10)
    pulled = (0.0625 * dot_t(mid_u.astype(BF16), down_mid[...])).astype(BF16)
    fine_sums = [jnp.sum(value, axis=0, keepdims=True) for value in grad_sums]
    terms = dot_t(pulled, kernel_fine[...].reshape(2304, 256))
    for t in range(9):
        term = terms[:, 256 * (8 - t) : 256 * (9 - t)]
        for n in range(2):
            fine_sums[n] += column_sums(window_sums[n, t].reshape(128, 256).astype(F32) * term)
    total_begin(5, *fine_sums)
    total_middle(6)

    coarse_block = (
        coarse_in.astype(F32)
        + coarse_convolve(
            coarse_extended(
                coarse_value,
                lambda d: coarse_halo[d].astype(F32)[0:8],
                silu(coarse_center, coarse_inverse, s_coarse),
                True,
            ),
            dot,
            kernel_coarse[...].reshape(4608, 512),
        )
    ).astype(BF16)
    coarse_up = dot(coarse_block, up_coarse[...]).astype(BF16)
    mid_sum = (mid_block.astype(F32) + dot(SPREAD[0:128, 0:16], coarse_up)).astype(BF16)
    mid_up = dot(mid_sum, up_mid[...]).astype(BF16)
    total_middle(4)
    total_middle(5)

    fine_forward(2)
    fine_forward(3)
    mid_up = dot(ENLARGE[:, 0:128], mid_up).reshape(4, 8, 1, 16, 256)
    for f in range(4):
        block = fine_block[f].astype(F32).reshape(8, 4, 16, 256)
        fine_block[f] = (block + mid_up[f]).astype(BF16).reshape(512, 256)
    out_copy = pltpu.make_async_copy(fine_block, out_ref, out_sem.at[0])
    out_copy.start()
    scaled_around = mid_extended(
        mid_value, mid_halo[...], lambda c: mid_cor[c], mid_scaled, False
    )
    to_lanes = []
    for n in range(2):
        lane, row = iota((512, 128), 1), iota((512, 128), 0)
        inside = jnp.logical_and((lane & 31) == (row >> 4), ((lane >> 5) & 1) == n)
        to_lanes.append(jnp.where(inside, 0.0625, 0.0).astype(BF16))
    first_mean, second_mean = total_end(4, 512, 128 * wide_count * narrow_count)
    arrived(u_halo, 10)
    arrived(u_cor, 11)
    offset = mid_inverse * first_mean
    factor = mid_inverse * second_mean
    mid_in_grad = mid_extended(
        mid_u, u_halo[...], lambda c: u_cor[c], lambda v: v - offset, False
    ) - factor * scaled_around

    pool_grad = 0.0625 * dot_t(mid_in_grad.astype(BF16), down_mid[...])
    pool_grad = pool_grad * jnp.concatenate([keep] * 2, axis=1)
    high, low = halves(pool_grad)
    added = dot(ENLARGE[...], jnp.concatenate([high[0:256], low[0:256]], axis=0))
    loads["stretch"].wait()
    all_fields = dot_t(high, kernel_fine[...].reshape(2304, 256)).astype(BF16)
    for a in range(3):
        fields = [all_fields[:, 256 * k : 256 * k + 256] for k in range(8 - 3 * a, 5 - 3 * a, -1)]
        stretched[a] = dot(stretch[...], jnp.concatenate(fields, axis=0)).reshape(4, 10, 16, 256)

    means = jnp.zeros((8, 128), F32)
    for n, mean in enumerate((first_mean, second_mean)):
        to_lane = to_lanes[n]
        high, low = halves(jnp.broadcast_to(mean, (8, 512)))
        means += dot(high, to_lane) + dot(low, to_lane)
    matrix_high, matrix_low = halves(total_sum(6))
    fine_totals = total_groups(5, 256, 1.0)
    spread_groups = one_hot((iota((256, 32), 0) >> 3) == iota((256, 32), 1))
    fine_means = []
    for n in range(2):
        half = jnp.where((iota((8, 128), 1) >> 6) == n, means, 0.0)
        high, low = halves(half)
        change = dot_t(high, matrix_high) + dot_t(low, matrix_high) + dot_t(high, matrix_low)
        high, low = halves(change)
        change = dot_t(high, spread_groups) + dot_t(low, spread_groups)
        fine_means.append(
            (fine_totals[n] - change[0:1]) * (1.0 / (8 * 2048 * wide_count * narrow_count))
        )
    slant = -fine_inverse * fine_inverse * fine_means[1]
    shift = -fine_inverse * fine_means[0] - fine_center * slant

    added = added.reshape(4, 8, 1, 16, 256)
    grad_copies = []
    for f in range(4):
        above, here, below = stretched[0, f], stretched[1, f], stretched[2, f]
        centre = here[1:9] + above[1:9] + below[1:9]
        top = here[1:9] + above[0:8] + below[1:9]
        bottom = here[1:9] + above[1:9] + below[2:10]
        back = jnp.stack([top, centre, centre, bottom], axis=1).reshape(512, 256)
        normed_grad = (conv_grad[f] + back) * fine_slope[f]
        grad = xg[1, f].astype(F32).reshape(8, 4, 16, 256) + added[f]
        grad = grad.reshape(512, 256).astype(BF16).astype(F32)
        grad_buf[f] = grad + fine_inverse * normed_grad + (shift + fine_value(f) * slant)
        grad_copies.append(
            pltpu.make_async_copy(grad_buf.at[f], grad_ref.at[f], out_sem.at[1 + f])
        )
        grad_copies[f].start()

    for which in range(2):
        sent(row_in.at[:, which], 13 * which)
        sent(col_in.at[:, which], 13 * which + 1)
        sent(cor_in.at[which], 13 * which + 2)
    sent(sum_in, 3)
    sent(sum_cor, 4)
    sent(cgrad_in, 5)
    sent(mid_halo, 6)
    sent(mid_cor, 7)
    sent(coarse_halo, 8)
    sent(coarse_u_halo, 9)
    sent(u_halo, 10)
    sent(u_cor, 11)
    for phase in range(7):
        whole = firsts[phase].at[pl.ds(0, wide_count - 1)]
        pltpu.make_async_copy(whole, whole, total_send.at[2 * phase]).wait()
        whole = seconds[phase].at[pl.ds(0, narrow_count - 1)]
        pltpu.make_async_copy(whole, whole, total_send.at[2 * phase + 1]).wait()
    out_copy.wait()
    for copy in grad_copies:
        copy.wait()


def shards(*arguments):
    (
        fine_input,
        gain_fine,
        kernel_fine,
        down_mid,
        gain_mid,
        kernel_mid,
        down_coarse,
        gain_coarse,
        kernel_coarse,
        up_coarse,
        up_mid,
        grad_out,
    ) = arguments
    wide_count, narrow_count = lax.axis_size("wide"), lax.axis_size("narrow")
    anywhere = pl.BlockSpec(memory_space=pl.ANY)
    vmem = pltpu.VMEM
    scratch = [
        vmem((2, 4, 32, 16, 256), BF16),
        vmem((9, 256, 256), BF16),
        vmem((256, 512), BF16),
        vmem((9, 512, 512), BF16),
        vmem((512, 512), BF16),
        vmem((9, 512, 512), BF16),
        vmem((512, 512), BF16),
        vmem((512, 256), BF16),
        vmem((1, 256), F32),
        vmem((1, 512), F32),
        vmem((1, 512), F32),
        vmem((608, 512), BF16),
        vmem((1168, 256), BF16),
        vmem((1168, 128), BF16),
        vmem((288, 640), BF16),
        vmem((640, 768), BF16),
        vmem((4, 544, 768), BF16),
        vmem((4, 512, 256), BF16),
        vmem((4, 512, 256), F32),
        vmem((4, 512, 256), F32),
        vmem((128, 256), F32),
        vmem((128, 256), BF16),
        vmem((4, 512, 256), F32),
        vmem((2, 2, 4, 16, 256), F32),
        vmem((2, 4, 64, 256), F32),
        vmem((2, 16, 256), F32),
        vmem((256, 512), F32),
        vmem((6, wide_count, 1, 128), F32),
        vmem((6, narrow_count, 1, 128), F32),
        vmem((8, 128), F32),
        vmem((wide_count, 32, 128), BF16),
        vmem((narrow_count, 32, 128), BF16),
        vmem((2, 9, 4, 32, 256), BF16),
        vmem((2, 2, 4, 16, 256), BF16),
        vmem((2, 2, 4, 32, 256), BF16),
        vmem((2, 4, 32, 256), BF16),
        vmem((4, 256, 512), F32),
        vmem((9, 256, 512), BF16),
        vmem((2, 9, 256, 640), BF16),
        vmem((3, 4, 10, 16, 256), F32),
        vmem((2, 2, 128, 256), BF16),
        vmem((2, 16, 256), BF16),
        vmem((2, 2, 4, 16, 256), BF16),
        vmem((2, 2, 128, 256), BF16),
        vmem((2, 4, 16, 256), BF16),
        vmem((112, 256), BF16),
        vmem((96, 256), BF16),
        vmem((4, 16, 256), BF16),
        vmem((16, 512), BF16),
        vmem((8, 16, 512), BF16),
        vmem((112, 512), BF16),
        vmem((96, 512), BF16),
        vmem((4, 16, 512), BF16),
        vmem((16, 512), BF16),
        vmem((8, 16, 512), BF16),
        vmem((8, 512), F32),
        vmem((8, 8, 512), F32),
        vmem((112, 512), BF16),
        vmem((96, 512), BF16),
        vmem((4, 16, 512), BF16),
        pltpu.SemaphoreType.DMA((20,)),
        pltpu.SemaphoreType.DMA((5,)),
        pltpu.SemaphoreType.DMA((14,)),
        pltpu.SemaphoreType.DMA((14,)),
        pltpu.SemaphoreType.DMA((16,)),
        pltpu.SemaphoreType.DMA((16,)),
    ]
    output, grad = pl.pallas_call(
        functools.partial(kernel, wide_count, narrow_count),
        out_shape=(
            jax.ShapeDtypeStruct((4, 512, 256), BF16),
            jax.ShapeDtypeStruct((4, 512, 256), F32),
        ),
        in_specs=[anywhere] * 17,
        out_specs=(anywhere, anywhere),
        scratch_shapes=scratch,
        compiler_params=pltpu.CompilerParams(
            collective_id=0, has_side_effects=True, vmem_limit_bytes=56 * 2**20
        ),
        name="whole_net",
    )(
        fine_input,
        gain_fine.reshape(1, 256),
        kernel_fine.reshape(9, 256, 256),
        down_mid,
        gain_mid.reshape(1, 512),
        kernel_mid.reshape(9, 512, 512),
        down_coarse,
        gain_coarse.reshape(1, 512),
        kernel_coarse.reshape(9, 512, 512),
        up_coarse,
        up_mid,
        grad_out,
        *tables(),
    )
    return output.reshape(4, 32, 16, 256), grad.reshape(4, 32, 16, 256)


def solution(mesh):
    tile = P(None, "wide", "narrow", None)
    return jax.shard_map(
        shards,
        mesh=mesh,
        in_specs=(tile,) + (P(),) * 10 + (tile,),
        out_specs=(tile, tile),
        check_vma=False,
    )
```

```python
import functools

import jax
import jax.numpy as jnp
import numpy as np
from jax import lax
from jax.experimental import pallas as pl
from jax.experimental.pallas import tpu as pltpu
from jax.sharding import PartitionSpec as P

MESH = pl.DeviceIdType.MESH
GROUPS = 32
epsilon = 1e-05
F32 = jnp.float32
BF16 = jnp.bfloat16

DIRS = ((0, 0), (-1, 0), (1, 0), (0, -1), (0, 1), (-1, -1), (-1, 1), (1, -1), (1, 1))

ABOVE, BELOW, LEFT, RIGHT, CORNER = 128, 144, 160, 192, 224


def mid_row(f, i, j):
    if 0 <= i < 8 and 0 <= j < 4:
        return 32 * f + 4 * i + j
    if i < 0 and 0 <= j < 4:
        return ABOVE + 4 * f + j
    if i > 7 and 0 <= j < 4:
        return BELOW + 4 * f + j
    if 0 <= i < 8:
        return (LEFT if j < 0 else RIGHT) + 8 * f + i
    return CORNER + 4 * (2 * (i > 7) + (j > 3)) + f


def coarse_row(f, i, side):
    down = -1 if i < 0 else (1 if i > 1 else 0)
    return 8 * DIRS.index((down, side)) + 2 * f + i % 2


def tables():
    pick = np.zeros((96, 512), np.float32)
    for i in range(32):
        for j in range(16):
            pick[4 * (i // 4) + j // 4, 16 * i + j] = 1
        pick[32 + i, 16 * i + 15] = 1
        pick[64 + i, 16 * i] = 1
    enlarge = np.zeros((512, 256), np.float32)
    taps = np.zeros((1152, 256), np.float32)
    ends = np.zeros((16, 256), np.float32)
    pack = np.zeros((112, 128), np.float32)
    pool = np.zeros((16, 128), np.float32)
    coarse_taps = np.zeros((144, 128), np.float32)
    spread = np.zeros((256, 128), np.float32)
    for f in range(4):
        for i in range(8):
            for j in range(16):
                enlarge[128 * f + 16 * i + j, mid_row(f, i, j // 4)] = 1
        for c in range(4):
            low, first = c < 2, c % 2 == 1
            ends[4 * c + f, 128 * first + 32 * f + 31 * low] = 1
            pack[96 + 4 * c + f, mid_row(f, 7 * low, 3 * (not first))] = 1
        for i in range(8):
            for j in range(4):
                here = 32 * f + 4 * i + j
                pool[2 * f + i // 4, here] = 1
                for t in range(9):
                    taps[128 * t + here, mid_row(f, i + t // 3 - 1, j + t % 3 - 1)] = 1
            pack[32 + 8 * f + i, mid_row(f, i, 3)] = 1
            pack[64 + 8 * f + i, mid_row(f, i, 0)] = 1
        for j in range(4):
            pack[4 * f + j, mid_row(f, 7, j)] = 1
            pack[16 + 4 * f + j, mid_row(f, 0, j)] = 1
        for i in range(2):
            for t in range(9):
                coarse_taps[16 * t + 2 * f + i, coarse_row(f, i + t // 3 - 1, t % 3 - 1)] = 1
        for i in range(-1, 9):
            for j in range(-1, 5):
                side = -1 if j < 0 else (1 if j > 3 else 0)
                spread[mid_row(f, i, j), coarse_row(f, i // 4 if i < 8 else 2, side)] = 1
    windows = np.zeros((288, 640), np.float32)
    for t in range(9):
        for i in range(32):
            for j in range(16):
                p, q = i + 1 - t // 3, j + 1 - t % 3
                row = 32 * t + 4 * (i // 4) + j // 4
                if 0 <= p < 32 and 0 <= q < 16:
                    at = 16 * p + q
                elif 0 <= q < 16:
                    at = (512 if p < 0 else 528) + q
                elif 0 <= p < 32:
                    at = (544 if q < 0 else 576) + p
                else:
                    at = 608 + 2 * (p > 31) + (q > 15)
                windows[row, at] = 1
    stretch = np.zeros((640, 768), np.float32)
    for f in range(4):
        for i in range(10):
            for j in range(16):
                for b in range(3):
                    at = 256 * b + mid_row(f, i - 1, (j + b - 1) // 4)
                    stretch[160 * f + 16 * i + j, at] = 1
    by_frame = np.zeros((128, 128), np.float32)
    for f in range(4):
        for c in range(4):
            by_frame[32 * f + c, 4 * c + f] = 1
    sides = np.zeros((512, 128), np.float32)
    for i in range(32):
        sides[16 * i, i] = 1
        sides[16 * i + 15, 64 + i] = 1
    wide_table = np.concatenate([pick, np.concatenate([enlarge, enlarge], axis=1)])
    middle_table = np.concatenate([taps, ends])
    narrow_table = np.concatenate([pack, pool, coarse_taps, spread, sides, by_frame])
    result = (wide_table, middle_table, narrow_table, windows, stretch)
    return [jnp.asarray(t, BF16) for t in result]


def dot(a, b):
    return jnp.dot(a, b, preferred_element_type=F32)


def dot_t(a, b):
    return lax.dot_general(a, b, (((1,), (1,)), ((), ())), preferred_element_type=F32)


def dot_first(a, b):
    return lax.dot_general(a, b, (((0,), (0,)), ((), ())), preferred_element_type=F32)


def group_lanes(t, size):
    lane = lax.broadcasted_iota(jnp.int32, t.shape, 1)
    step = 1
    while step < size:
        t = t + jnp.where(
            (lane & step) != 0, pltpu.roll(t, step, 1), pltpu.roll(t, 128 - step, 1)
        )
        step *= 2
    return t


def halves(t):
    high = t.astype(BF16)
    return high, (t - high.astype(F32)).astype(BF16)


def kernel(
    wide_count,
    narrow_count,
    x_in,
    gain_fine_in,
    kernel_fine_in,
    down_mid_in,
    gain_mid_in,
    kernel_mid_in,
    down_coarse_in,
    gain_coarse_in,
    kernel_coarse_in,
    up_coarse_in,
    up_mid_in,
    grad_in,
    wide_table_in,
    middle_table_in,
    narrow_table_in,
    windows_in,
    stretch_in,
    out_ref,
    grad_ref,
    xg,
    kernel_fine,
    down_mid,
    kernel_mid,
    down_coarse,
    kernel_coarse,
    up_coarse,
    up_mid,
    gain_fine,
    gain_mid,
    gain_coarse,
    wide_table,
    middle_table,
    narrow_table,
    windows,
    stretch,
    columns,
    fine_block,
    grad_buf,
    conv_grad,
    pooled_x,
    summed,
    fine_slope,
    edge_rows,
    edge_sides,
    edge_ends,
    summed_grad,
    first,
    second,
    rows,
    first_matrix,
    second_matrix,
    window_sums,
    rim_rows,
    rim_sides,
    rim_ends,
    matrix_sum,
    through,
    mixed,
    stretched,
    col_pack,
    cor_pack,
    row_in,
    col_in,
    cor_in,
    sum_pack,
    sum_in,
    sum_cor,
    cgrad_own,
    cgrad_in,
    mid_pack,
    mid_halo,
    mid_cor,
    coarse_own,
    coarse_halo,
    coarse_u,
    coarse_u_halo,
    u_pack,
    u_halo,
    u_cor,
    load_sem,
    out_sem,
    total_send,
    total_recv,
    halo_send,
    halo_recv,
):
    wide, narrow = lax.axis_index("wide"), lax.axis_index("narrow")

    def around(index, step, count):
        moved = index + step
        if isinstance(step, int) and step < 0:
            return jnp.where(moved < 0, moved + count, moved)
        return jnp.where(moved >= count, moved - count, moved)

    def device(down, side):
        return (
            wide if isinstance(down, int) and down == 0 else around(wide, down, wide_count),
            narrow if isinstance(side, int) and side == 0 else around(narrow, side, narrow_count),
        )

    loads = {}
    pairs = (
        ("x0", x_in.at[0], xg.at[0, 0]),
        ("x1", x_in.at[1], xg.at[0, 1]),
        ("x2", x_in.at[2], xg.at[0, 2]),
        ("x3", x_in.at[3], xg.at[0, 3]),
        ("grad", grad_in, xg.at[1]),
        ("wide_table", wide_table_in, wide_table),
        ("middle_table", middle_table_in, middle_table),
        ("narrow_table", narrow_table_in, narrow_table),
        ("gain_fine", gain_fine_in, gain_fine),
        ("windows", windows_in, windows),
        ("kernel_fine", kernel_fine_in, kernel_fine),
        ("up_mid", up_mid_in, up_mid),
        ("up_coarse", up_coarse_in, up_coarse),
        ("down_mid", down_mid_in, down_mid),
        ("gain_mid", gain_mid_in, gain_mid),
        ("kernel_coarse", kernel_coarse_in, kernel_coarse),
        ("kernel_mid", kernel_mid_in, kernel_mid),
        ("down_coarse", down_coarse_in, down_coarse),
        ("gain_coarse", gain_coarse_in, gain_coarse),
        ("stretch", stretch_in, stretch),
    )
    for number, (name, source, target) in enumerate(pairs):
        loads[name] = pltpu.make_async_copy(source, target, load_sem.at[number])

    def begin_loads(*names):
        for name in names:
            loads[name].start()

    begin_loads("x0", "x1", "x2", "x3", "wide_table", "middle_table")

    barrier = pltpu.get_barrier_semaphore()
    greeted = 0
    for down in range(wide_count):
        for side in range(-2, narrow_count - 2):
            near = (down <= 1 or down == wide_count - 1) and abs(side) <= 1
            if (down, side) != (0, 0) and (down == 0 or side == 0 or near):
                pl.semaphore_signal(
                    barrier, inc=1, device_id=device(down, side), device_id_type=MESH
                )
                greeted += 1

    def send(source, target, which, down, side):
        pltpu.make_async_remote_copy(
            src_ref=source,
            dst_ref=target,
            send_sem=halo_send.at[which],
            recv_sem=halo_recv.at[which],
            device_id=device(down, side),
            device_id_type=MESH,
        ).start()

    def arrived(buffer, which):
        pltpu.make_async_copy(buffer, buffer, halo_recv.at[which]).wait()

    def sent(buffer, which):
        pltpu.make_async_copy(buffer, buffer, halo_send.at[which]).wait()

    firsts = tuple(first.at[p] for p in range(6)) + (first_matrix,)
    seconds = tuple(second.at[p] for p in range(6)) + (second_matrix,)

    def total_send_wide(phase):
        mine = firsts[phase].at[wide]

        for step in sorted(range(1, wide_count), key=lambda k: -min(k & 7, 8 - (k & 7))):
            pltpu.make_async_remote_copy(
                src_ref=mine,
                dst_ref=mine,
                send_sem=total_send.at[2 * phase],
                recv_sem=total_recv.at[2 * phase],
                device_id=device(step, 0),
                device_id_type=MESH,
            ).start()

    def diagonal(shape=(8, 128)):
        lane = lax.broadcasted_iota(jnp.int32, shape, 1) & 7
        return lane == lax.broadcasted_iota(jnp.int32, shape, 0)

    def total_begin(phase, one, two):
        channels = one.shape[1]
        if channels < 512:
            rows[...] = jnp.zeros((8, 128), F32)
        for n, value in enumerate((one, two)):
            for k in range(channels // 128):
                rows[4 * n + k : 4 * n + k + 1, :] = value[:, 128 * k : 128 * k + 128]
        grouped = group_lanes(rows[...], channels // GROUPS)
        grouped = jnp.where(diagonal(), grouped, 0.0)
        firsts[phase][wide] = jnp.sum(grouped, axis=0, keepdims=True)
        total_send_wide(phase)

    def total_middle(phase):
        whole = firsts[phase].at[pl.ds(0, wide_count - 1)]
        pltpu.make_async_copy(whole, whole, total_recv.at[2 * phase]).wait()
        summed_up = jnp.sum(firsts[phase][...].astype(F32), axis=0)
        seconds[phase][narrow] = summed_up.astype(seconds[phase].dtype)
        mine = seconds[phase].at[narrow]

        for step in sorted(range(1, narrow_count), key=lambda k: -min(k & 3, 4 - (k & 3))):
            pltpu.make_async_remote_copy(
                src_ref=mine,
                dst_ref=mine,
                send_sem=total_send.at[2 * phase + 1],
                recv_sem=total_recv.at[2 * phase + 1],
                device_id=device(0, step),
                device_id_type=MESH,
            ).start()

    def total_sum(phase):
        whole = seconds[phase].at[pl.ds(0, narrow_count - 1)]
        pltpu.make_async_copy(whole, whole, total_recv.at[2 * phase + 1]).wait()
        return jnp.sum(seconds[phase][...].astype(F32), axis=0)

    def row_of(t, start, channels):
        return jnp.concatenate([t[start + k : start + k + 1] for k in range(channels // 128)], axis=1)

    def total_groups(phase, channels, scale):
        packed = jnp.broadcast_to(total_sum(phase), (8, 128))
        t = group_lanes(jnp.where(diagonal(), packed, 0.0), 8) * scale
        return row_of(t, 0, channels), row_of(t, 4, channels)

    def total_end(phase, channels, cells):
        return total_groups(phase, channels, 1.0 / (channels // GROUPS * cells))

    has_above, has_below = wide > 0, wide < wide_count - 1
    has_left, has_right = narrow > 0, narrow < narrow_count - 1
    has_corner = (
        jnp.logical_and(has_above, has_left),
        jnp.logical_and(has_above, has_right),
        jnp.logical_and(has_below, has_left),
        jnp.logical_and(has_below, has_right),
    )
    exists = (None, has_above, has_below, has_left, has_right) + has_corner

    def only(condition, value):
        return value * jnp.where(condition, 1.0, 0.0).astype(F32)

    def corners(read, change, masked):
        result = None
        for c in range(4):
            value = change(read(c).astype(F32))
            if masked:
                value = only(has_corner[c], value)
            cell = lax.broadcasted_iota(jnp.int32, value.shape, 0)
            result = value if result is None else jnp.where(cell >= 4 * c, value, result)
        return result

    def mid_extended(own, read_halo, read_cor, change, masked):
        pieces = [change(own)]
        halo = change(read_halo.astype(F32))
        for low, high, d in ((0, 16, 1), (16, 32, 2), (32, 64, 3), (64, 96, 4)):
            piece = halo[low:high]
            pieces.append(only(exists[d], piece) if masked else piece)
        pieces.append(corners(read_cor, change, masked))
        pieces.append(jnp.zeros((16, own.shape[1]), F32))
        return jnp.concatenate(pieces, axis=0)

    def send_mid(pack, halo, cor, which):
        send(pack.at[pl.ds(0, 16)], halo.at[pl.ds(0, 16)], which, 1, 0)
        send(pack.at[pl.ds(16, 16)], halo.at[pl.ds(16, 16)], which, -1, 0)
        send(pack.at[pl.ds(32, 32)], halo.at[pl.ds(32, 32)], which, 0, 1)
        send(pack.at[pl.ds(64, 32)], halo.at[pl.ds(64, 32)], which, 0, -1)
        for c in range(4):
            down, side = DIRS[5 + c]
            send(pack.at[pl.ds(96, 16)], cor.at[c], which + 1, -down, -side)

    def send_coarse(own, halo, which):
        for d in range(1, 9):
            down, side = DIRS[d]
            send(own, halo.at[d - 1], which, -down, -side)

    def coarse_extended(own, halo, change, masked):
        pieces = [change(own)]
        for d in range(1, 9):
            piece = change(halo(d - 1))
            pieces.append(only(exists[d], piece) if masked else piece)
        pieces.append(jnp.zeros((56, own.shape[1]), F32))
        return jnp.concatenate(pieces, axis=0)

    PICK = wide_table.at[pl.ds(0, 96)]
    ENLARGE = wide_table.at[pl.ds(96, 512)]
    TAPS = middle_table.at[pl.ds(0, 1152)]
    ENDS = middle_table.at[pl.ds(1152, 16)]
    PACK = narrow_table.at[pl.ds(0, 112)]
    POOL = narrow_table.at[pl.ds(112, 16)]
    COARSE_TAPS = narrow_table.at[pl.ds(128, 144)]
    SPREAD = narrow_table.at[pl.ds(272, 256)]
    SIDES = narrow_table.at[pl.ds(528, 512)]
    BY_FRAME = narrow_table.at[pl.ds(1040, 128)]

    def frame(which, f):
        return xg[which, f].reshape(512, 256)

    blank = jnp.zeros((8, 256), F32)
    one, two = blank, blank
    for f in range(4):
        loads["x%d" % f].wait()
        value = frame(0, f).astype(F32)
        one += jnp.sum(value.reshape(64, 8, 256), axis=0)
        two += jnp.sum((value * value).reshape(64, 8, 256), axis=0)
    pl.semaphore_wait(barrier, greeted)
    total_begin(0, jnp.sum(one, axis=0, keepdims=True), jnp.sum(two, axis=0, keepdims=True))

    begin_loads("grad", "narrow_table", "gain_fine", "windows", "kernel_fine")
    begin_loads("up_mid", "up_coarse", "down_mid", "gain_mid")

    def rim_rows_out(which):
        send(xg.at[which, :, 31], row_in.at[0, which], 13 * which, 1, 0)
        send(xg.at[which, :, 0], row_in.at[1, which], 13 * which, -1, 0)

    def rim_pick(which):
        for f in range(4):
            picked = dot(PICK[...], frame(which, f))
            if which == 0:
                pooled_x[32 * f : 32 * f + 32] = picked[0:32]
            picked = picked.astype(BF16)
            col_pack[0, which, 32 * f : 32 * f + 32] = picked[32:64]
            col_pack[1, which, 32 * f : 32 * f + 32] = picked[64:96]
            if which == 1:
                summed[32 * f : 32 * f + 32] = picked[0:32]

    def rim_sides_out(which):
        send(col_pack.at[0, which], col_in.at[0, which], 13 * which + 1, 0, 1)
        send(col_pack.at[1, which], col_in.at[1, which], 13 * which + 1, 0, -1)

    def rim_ends_out(which):
        ends = jnp.concatenate([col_pack[0, which], col_pack[1, which]], axis=0)
        cor_pack[which] = dot(ENDS[...], ends).astype(BF16)
        for c in range(4):
            down, side = DIRS[5 + c]
            send(cor_pack.at[which], cor_in.at[which, c], 13 * which + 2, -down, -side)

    loads["wide_table"].wait()
    loads["middle_table"].wait()
    rim_rows_out(0)
    rim_pick(0)
    rim_sides_out(0)
    rim_ends_out(0)
    loads["grad"].wait()
    rim_pick(1)
    total_middle(0)
    begin_loads("kernel_mid")
    rim_rows_out(1)
    rim_sides_out(1)
    rim_ends_out(1)
    loads["narrow_table"].wait()

    up_mid_grad = summed[...]
    sum_pack[...] = dot(PACK[...], up_mid_grad).astype(BF16)
    send_mid(sum_pack, sum_in, sum_cor, 3)
    loads["up_mid"].wait()
    high, low = halves(dot_t(up_mid_grad, up_mid[...]))
    up_coarse_grad = (dot(POOL[...], high) + dot(POOL[...], low)).astype(BF16)
    loads["up_coarse"].wait()
    cgrad_own[...] = dot_t(up_coarse_grad, up_coarse[...]).astype(BF16)
    send_coarse(cgrad_own, cgrad_in, 5)

    loads["gain_fine"].wait()
    loads["kernel_fine"].wait()
    loads["down_mid"].wait()

    fine_center, fine_square = total_end(0, 256, 2048 * wide_count * narrow_count)
    fine_inverse = lax.rsqrt(fine_square - fine_center * fine_center + epsilon)
    s_fine = gain_fine[...]

    def silu(center, inverse, scaling):
        gain = 0.5 * inverse * scaling
        shift = -center * gain

        def change(value):
            half = value * gain + shift
            return half * jnp.tanh(half) + half

        return change

    def slope(scaled, scaling):
        half = scaled * (0.5 * scaling)
        bend = jnp.tanh(half)
        return (0.5 * scaling) * (1.0 + bend) * (1.0 + half * (1.0 - bend))

    fine_act = silu(fine_center, fine_inverse, s_fine)

    arrived(row_in.at[:, 0], 0)
    arrived(col_in.at[:, 0], 1)
    arrived(cor_in.at[0], 2)

    def set_edges(kind, above, below, left, right, ends):
        edge_rows[kind, 0] = only(has_above, above)
        edge_rows[kind, 1] = only(has_below, below)
        left = only(has_left, left)
        right = only(has_right, right)
        for f in range(4):
            edge_sides[kind, f, 0:32] = left[32 * f : 32 * f + 32]
            edge_sides[kind, f, 32:64] = right[32 * f : 32 * f + 32]
        edge_ends[kind] = ends

    def place(kind, f, own):
        column = lax.broadcasted_iota(jnp.int32, (32, 16, 256), 1)
        west, east = (
            jnp.broadcast_to(edge_sides[kind, f, 32 * k : 32 * k + 32].reshape(32, 1, 256), (32, 16, 256))
            for k in range(2)
        )
        low = jnp.where(column == 0, west, pltpu.roll(own, 1, 0).reshape(32, 16, 256))
        columns[f, 16:528, 0:256] = low.reshape(512, 256).astype(BF16)
        columns[f, 16:528, 256:512] = own.astype(BF16)
        high = jnp.where(column == 15, east, pltpu.roll(own, 511, 0).reshape(32, 16, 256))
        columns[f, 16:528, 512:768] = high.reshape(512, 256).astype(BF16)
        cell = lax.broadcasted_iota(jnp.int32, (16, 256), 0)
        for k in range(2):
            row = edge_rows[kind, k, f]
            at = slice(528 * k, 528 * k + 16)
            west = edge_ends[kind, pl.ds(8 * k + f, 1), :]
            east = edge_ends[kind, pl.ds(8 * k + 4 + f, 1), :]
            columns[f, at, 0:256] = jnp.where(cell == 0, west, pltpu.roll(row, 1, 0)).astype(BF16)
            columns[f, at, 256:512] = row.astype(BF16)
            columns[f, at, 512:768] = jnp.where(cell == 15, east, pltpu.roll(row, 15, 0)).astype(BF16)

    def side_by_side(pieces):
        return jnp.concatenate(list(pieces), axis=1)

    def fine_taps(f):
        return side_by_side(columns[f, 16 * a : 16 * a + 512, :] for a in range(3))

    def fine_convolve(f):
        return dot(fine_taps(f), kernel_fine[...].reshape(2304, 256))

    def fine_convolve_back(f):
        return dot_t(fine_taps(f), side_by_side(kernel_fine[8 - t] for t in range(9)))

    def fine_scaled(value):
        return (value - fine_center) * fine_inverse

    def fine_value(f):
        return frame(0, f).astype(F32)

    def set_fields(n, change):
        for k in range(2):
            rim_rows[n, k] = only(exists[1 + k], change(row_in[k, 0].astype(F32))).astype(BF16)
            sides = only(exists[3 + k], change(col_in[k, 0].astype(F32))).astype(BF16)
            rim_sides[n, k] = sides.reshape(4, 32, 256)
        ends = corners(lambda c: cor_in[0, c], change, True)
        ends = dot(BY_FRAME[:, 0:16], ends.astype(BF16)).astype(BF16)
        rim_ends[n] = ends.reshape(4, 32, 256)

    def window(n, f, own):
        field = jnp.concatenate(
            [
                own.astype(BF16),
                rim_rows[n, 0, f],
                rim_rows[n, 1, f],
                rim_sides[n, 0, f],
                rim_sides[n, 1, f],
                rim_ends[n, f],
            ],
            axis=0,
        )
        return dot(windows[...], field)

    set_fields(0, fine_act)
    loads["windows"].wait()

    for f in range(4):
        sums = window(0, f, fine_act(fine_value(f)))
        high, low = halves(sums)
        window_sums[0, :, f] = high.reshape(9, 32, 256)
        window_sums[1, :, f] = low.reshape(9, 32, 256)

    both = side_by_side(
        jnp.concatenate([window_sums[n, 8 - t].reshape(128, 256) for n in range(2)], axis=0)
        for t in range(9)
    )
    both = dot(both, kernel_fine[...].reshape(2304, 256))
    pooled = pooled_x[...] + both[0:128] + both[128:256]
    pooled = (pooled * 0.0625).astype(BF16)

    def fine_forward(f):
        value = fine_value(f)
        place(0, f, fine_act(value))
        fine_block[f] = (value + fine_convolve(f)).astype(BF16)

    def same(value):
        return value

    mid_in = dot(pooled, down_mid[...]).astype(BF16)
    mid_value = mid_in.astype(F32)

    def column_sums(value):
        return jnp.sum(value, axis=0, keepdims=True)

    total_begin(1, column_sums(mid_value), column_sums(mid_value * mid_value))
    mid_pack[...] = dot(PACK[...], mid_in).astype(BF16)
    send_mid(mid_pack, mid_halo, mid_cor, 6)
    begin_loads("down_coarse", "gain_coarse", "kernel_coarse", "stretch")

    @pl.loop(0, 4)
    def _(f):
        fine_slope[f] = slope(fine_scaled(fine_value(f)), s_fine)

    set_fields(0, lambda v: slope(fine_scaled(v), s_fine))
    set_fields(1, lambda v: slope(fine_scaled(v), s_fine) * fine_scaled(v))

    set_edges(
        0,
        fine_act(row_in[0, 0].astype(F32)),
        fine_act(row_in[1, 0].astype(F32)),
        fine_act(col_in[0, 0].astype(F32)),
        fine_act(col_in[1, 0].astype(F32)),
        corners(lambda c: cor_in[0, c], fine_act, True),
    )
    fine_forward(0)
    total_middle(1)
    fine_forward(1)

    for f in range(4):
        bent = fine_slope[f]
        window_sums[0, :, f] = window(0, f, bent).astype(BF16).reshape(9, 32, 256)
        bent = bent * fine_scaled(fine_value(f))
        window_sums[1, :, f] = window(1, f, bent).astype(BF16).reshape(9, 32, 256)

    loads["gain_mid"].wait()
    loads["kernel_mid"].wait()
    mid_center, mid_square = total_end(1, 512, 128 * wide_count * narrow_count)
    mid_inverse = lax.rsqrt(mid_square - mid_center * mid_center + epsilon)
    s_mid = gain_mid[...]

    mid_act = silu(mid_center, mid_inverse, s_mid)

    def mid_scaled(value):
        return (value - mid_center) * mid_inverse

    def mid_convolve(extended, product, weights):
        taps = dot(TAPS[...], extended.astype(BF16)).astype(BF16)
        return product(side_by_side(taps[128 * t : 128 * t + 128] for t in range(9)), weights)

    arrived(mid_halo, 6)
    arrived(mid_cor, 7)
    mid_block = (
        mid_value
        + mid_convolve(
            mid_extended(mid_value, mid_halo[...], lambda c: mid_cor[c], mid_act, True),
            dot,
            kernel_mid[...].reshape(4608, 512),
        )
    ).astype(BF16)

    loads["down_coarse"].wait()
    mid_pooled = (dot(POOL[...], mid_block) * 0.0625).astype(BF16)
    coarse_in = dot(mid_pooled, down_coarse[...]).astype(BF16)
    coarse_own[...] = coarse_in
    coarse_value = coarse_in.astype(F32)[0:8]
    total_begin(2, column_sums(coarse_value), column_sums(coarse_value * coarse_value))
    send_coarse(coarse_own, coarse_halo, 8)

    arrived(row_in.at[:, 1], 13)
    arrived(col_in.at[:, 1], 14)
    arrived(cor_in.at[1], 15)
    set_edges(
        1,
        row_in[0, 1].astype(F32),
        row_in[1, 1].astype(F32),
        col_in[0, 1].astype(F32),
        col_in[1, 1].astype(F32),
        corners(lambda c: cor_in[1, c], same, True),
    )

    def convolve_grad(f, carry):
        place(1, f, frame(1, f).astype(F32))
        result = fine_convolve_back(f)
        conv_grad[f] = result
        weighted = result * fine_slope[f]
        scaled = fine_scaled(fine_value(f))
        return (
            carry[0] + jnp.sum(weighted.reshape(64, 8, 256), axis=0),
            carry[1] + jnp.sum((weighted * scaled).reshape(64, 8, 256), axis=0),
        )

    grad_sums = lax.fori_loop(0, 2, convolve_grad, (blank, blank))
    total_middle(2)

    arrived(cgrad_in, 5)
    loads["kernel_coarse"].wait()

    def coarse_convolve(extended, product, weights):
        taps = dot(COARSE_TAPS[...], extended.astype(BF16)).astype(BF16)
        return product(side_by_side(taps[16 * t : 16 * t + 16] for t in range(9)), weights)

    cgrad = cgrad_own[...].astype(F32)[0:8]
    coarse_act_grad = coarse_convolve(
        coarse_extended(cgrad, lambda d: cgrad_in[d].astype(F32)[0:8], same, True),
        dot_t,
        side_by_side(kernel_coarse[8 - t] for t in range(9)),
    )[0:8]

    @pl.loop(0, 9)
    def _(t):
        through[t] = (0.0625 * dot(kernel_fine[8 - t], down_mid[...])).astype(BF16)

    arrived(sum_in, 3)
    arrived(sum_cor, 4)
    sum_extended = mid_extended(
        up_mid_grad.astype(F32), sum_in[...], lambda c: sum_cor[c], same, True
    )
    summed_grad[...] = dot_t(sum_extended.astype(BF16), up_mid[...])

    loads["gain_coarse"].wait()
    coarse_center, coarse_square = total_end(2, 512, 8 * wide_count * narrow_count)
    coarse_inverse = lax.rsqrt(coarse_square - coarse_center * coarse_center + epsilon)
    s_coarse = gain_coarse[...]

    def coarse_scaled(value):
        return (value - coarse_center) * coarse_inverse

    scaled = coarse_scaled(coarse_value)
    normed_grad = coarse_act_grad * slope(scaled, s_coarse)
    total_begin(3, column_sums(normed_grad), column_sums(normed_grad * scaled))
    coarse_u[...] = cgrad + coarse_inverse * normed_grad
    send_coarse(coarse_u, coarse_u_halo, 9)
    grad_sums = lax.fori_loop(2, 4, convolve_grad, grad_sums)

    total_middle(3)

    mid_mix = jnp.concatenate(
        [mid_scaled(mid_value).astype(BF16), jnp.ones((128, 128), BF16)], axis=1
    )
    for n in range(2):
        sums = side_by_side(window_sums[n, t].reshape(128, 256) for t in range(9))
        mixed[n] = dot_first(sums, mid_mix).astype(BF16).reshape(9, 256, 640)

    @pl.loop(0, 16)
    def _(part):
        here = pl.ds(pl.multiple_of(16 * part, 16), 16)
        totals = [jnp.zeros((16, 512), F32) for _ in range(4)]
        for t in range(9):
            weight = through[t, here, :].astype(F32)
            for n in range(2):
                value = mixed[n, t, here, :].astype(F32)
                totals[2 * n] += weight * side_by_side([value[:, 512:640]] * 4)
                totals[2 * n + 1] += weight * value[:, 0:512]
        for n in range(4):
            matrix_sum[n, here, :] = totals[n]

    def iota(shape, axis):
        return lax.broadcasted_iota(jnp.int32, shape, axis)

    def one_hot(condition):
        return jnp.where(condition, 1.0, 0.0).astype(BF16)

    by_group = one_hot((iota((32, 256), 1) >> 3) == iota((32, 256), 0))
    matrix = jnp.zeros((32, 128), F32)
    for n in range(4):
        high, low = halves(matrix_sum[n] * mid_inverse)
        high, low = halves(dot(by_group, high) + dot(by_group, low))
        to_lane = one_hot(iota((512, 128), 1) == 32 * n + (iota((512, 128), 0) >> 4))
        matrix += dot(high, to_lane) + dot(low, to_lane)
    first_matrix[wide] = matrix.astype(BF16)
    total_send_wide(6)

    first_mean, second_mean = total_end(3, 512, 8 * wide_count * narrow_count)
    arrived(coarse_halo, 8)
    arrived(coarse_u_halo, 9)
    offset = coarse_inverse * first_mean
    factor = coarse_inverse * second_mean
    pieces = [coarse_u[...] - offset - scaled * factor]
    for d in range(8):
        piece = coarse_scaled(coarse_halo[d].astype(F32)[0:8])
        pieces.append(coarse_u_halo[d] - offset - piece * factor)
    pieces.append(jnp.zeros((56, 512), F32))
    coarse_in_grad = jnp.concatenate(pieces, axis=0).astype(BF16)

    mid_pool_grad = dot_t(dot(SPREAD[...], coarse_in_grad).astype(BF16), down_coarse[...])
    row = lax.broadcasted_iota(jnp.int32, (256, 128), 0)
    keep = jnp.where(row < ABOVE, 1.0, 0.0)
    bounds = ((ABOVE, 16, 1), (BELOW, 16, 2), (LEFT, 32, 3), (RIGHT, 32, 4)) + tuple(
        (CORNER + 4 * c, 4, 5 + c) for c in range(4)
    )
    for start, size, d in bounds:
        inside = jnp.logical_and(row >= start, row < start + size)
        keep = jnp.where(inside, jnp.where(exists[d], 1.0, 0.0).astype(F32), keep)
    mid_grad = (summed_grad[...] + 0.0625 * mid_pool_grad) * jnp.concatenate([keep] * 4, axis=1)
    mid_act_grad = mid_convolve(
        mid_grad, dot_t, side_by_side(kernel_mid[8 - t] for t in range(9))
    )
    scaled = mid_scaled(mid_value)
    normed_grad = mid_act_grad * slope(scaled, s_mid)
    total_begin(4, column_sums(normed_grad), column_sums(normed_grad * scaled))
    mid_u = mid_grad[0:128].astype(BF16).astype(F32) + mid_inverse * normed_grad
    u_pack[...] = dot(PACK[...], mid_u.astype(BF16)).astype(BF16)
    send_mid(u_pack, u_halo, u_cor, 10)
    pulled = (0.0625 * dot_t(mid_u.astype(BF16), down_mid[...])).astype(BF16)
    fine_sums = [jnp.sum(value, axis=0, keepdims=True) for value in grad_sums]
    for t in range(9):
        term = dot_t(pulled, kernel_fine[8 - t])
        for n in range(2):
            fine_sums[n] += column_sums(window_sums[n, t].reshape(128, 256).astype(F32) * term)
    total_begin(5, *fine_sums)
    total_middle(6)

    coarse_block = (
        coarse_in.astype(F32)
        + coarse_convolve(
            coarse_extended(
                coarse_value,
                lambda d: coarse_halo[d].astype(F32)[0:8],
                silu(coarse_center, coarse_inverse, s_coarse),
                True,
            ),
            dot,
            kernel_coarse[...].reshape(4608, 512),
        )
    ).astype(BF16)
    coarse_up = dot(coarse_block, up_coarse[...]).astype(BF16)
    mid_sum = (mid_block.astype(F32) + dot(SPREAD[0:128, 0:16], coarse_up)).astype(BF16)
    mid_up = dot(mid_sum, up_mid[...]).astype(BF16)
    total_middle(4)
    total_middle(5)

    fine_forward(2)
    fine_forward(3)
    mid_up = dot(ENLARGE[:, 0:128], mid_up).reshape(4, 8, 1, 16, 256)
    for f in range(4):
        block = fine_block[f].astype(F32).reshape(8, 4, 16, 256)
        fine_block[f] = (block + mid_up[f]).astype(BF16).reshape(512, 256)
    out_copy = pltpu.make_async_copy(fine_block, out_ref, out_sem.at[0])
    out_copy.start()
    first_mean, second_mean = total_end(4, 512, 128 * wide_count * narrow_count)
    arrived(u_halo, 10)
    arrived(u_cor, 11)
    offset = mid_inverse * first_mean
    factor = mid_inverse * second_mean
    mid_in_grad = mid_extended(
        mid_u, u_halo[...], lambda c: u_cor[c], lambda v: v - offset, False
    ) - factor * mid_extended(
        mid_value, mid_halo[...], lambda c: mid_cor[c], mid_scaled, False
    )

    pool_grad = 0.0625 * dot_t(mid_in_grad.astype(BF16), down_mid[...])
    pool_grad = pool_grad * jnp.concatenate([keep] * 2, axis=1)
    high, low = halves(pool_grad)
    added = dot(ENLARGE[...], jnp.concatenate([high[0:256], low[0:256]], axis=0))
    loads["stretch"].wait()
    for a in range(3):
        fields = [dot_t(high, kernel_fine[8 - 3 * a - b]).astype(BF16) for b in range(3)]
        stretched[a] = dot(stretch[...], jnp.concatenate(fields, axis=0)).reshape(4, 10, 16, 256)

    means = jnp.zeros((8, 128), F32)
    for n, mean in enumerate((first_mean, second_mean)):
        lane, row = iota((512, 128), 1), iota((512, 128), 0)
        inside = jnp.logical_and((lane & 31) == (row >> 4), ((lane >> 5) & 1) == n)
        to_lane = jnp.where(inside, 0.0625, 0.0).astype(BF16)
        high, low = halves(jnp.broadcast_to(mean, (8, 512)))
        means += dot(high, to_lane) + dot(low, to_lane)
    matrix_high, matrix_low = halves(total_sum(6))
    fine_totals = total_groups(5, 256, 1.0)
    spread_groups = one_hot((iota((256, 32), 0) >> 3) == iota((256, 32), 1))
    fine_means = []
    for n in range(2):
        half = jnp.where((iota((8, 128), 1) >> 6) == n, means, 0.0)
        high, low = halves(half)
        change = dot_t(high, matrix_high) + dot_t(low, matrix_high) + dot_t(high, matrix_low)
        high, low = halves(change)
        change = dot_t(high, spread_groups) + dot_t(low, spread_groups)
        fine_means.append(
            (fine_totals[n] - change[0:1]) * (1.0 / (8 * 2048 * wide_count * narrow_count))
        )
    slant = -fine_inverse * fine_inverse * fine_means[1]
    shift = -fine_inverse * fine_means[0] - fine_center * slant

    added = added.reshape(4, 8, 1, 16, 256)
    grad_copies = []
    for f in range(4):
        above, here, below = stretched[0, f], stretched[1, f], stretched[2, f]
        centre = here[1:9] + above[1:9] + below[1:9]
        top = here[1:9] + above[0:8] + below[1:9]
        bottom = here[1:9] + above[1:9] + below[2:10]
        back = jnp.stack([top, centre, centre, bottom], axis=1).reshape(512, 256)
        normed_grad = (conv_grad[f] + back) * fine_slope[f]
        grad = xg[1, f].astype(F32).reshape(8, 4, 16, 256) + added[f]
        grad = grad.reshape(512, 256).astype(BF16).astype(F32)
        grad_buf[f] = grad + fine_inverse * normed_grad + (shift + fine_value(f) * slant)
        grad_copies.append(
            pltpu.make_async_copy(grad_buf.at[f], grad_ref.at[f], out_sem.at[1 + f])
        )
        grad_copies[f].start()

    for which in range(2):
        sent(row_in.at[:, which], 13 * which)
        sent(col_in.at[:, which], 13 * which + 1)
        sent(cor_in.at[which], 13 * which + 2)
    sent(sum_in, 3)
    sent(sum_cor, 4)
    sent(cgrad_in, 5)
    sent(mid_halo, 6)
    sent(mid_cor, 7)
    sent(coarse_halo, 8)
    sent(coarse_u_halo, 9)
    sent(u_halo, 10)
    sent(u_cor, 11)
    for phase in range(7):
        whole = firsts[phase].at[pl.ds(0, wide_count - 1)]
        pltpu.make_async_copy(whole, whole, total_send.at[2 * phase]).wait()
        whole = seconds[phase].at[pl.ds(0, narrow_count - 1)]
        pltpu.make_async_copy(whole, whole, total_send.at[2 * phase + 1]).wait()
    out_copy.wait()
    for copy in grad_copies:
        copy.wait()


def shards(*arguments):
    (
        fine_input,
        gain_fine,
        kernel_fine,
        down_mid,
        gain_mid,
        kernel_mid,
        down_coarse,
        gain_coarse,
        kernel_coarse,
        up_coarse,
        up_mid,
        grad_out,
    ) = arguments
    wide_count, narrow_count = lax.axis_size("wide"), lax.axis_size("narrow")
    anywhere = pl.BlockSpec(memory_space=pl.ANY)
    vmem = pltpu.VMEM
    scratch = [
        vmem((2, 4, 32, 16, 256), BF16),
        vmem((9, 256, 256), BF16),
        vmem((256, 512), BF16),
        vmem((9, 512, 512), BF16),
        vmem((512, 512), BF16),
        vmem((9, 512, 512), BF16),
        vmem((512, 512), BF16),
        vmem((512, 256), BF16),
        vmem((1, 256), F32),
        vmem((1, 512), F32),
        vmem((1, 512), F32),
        vmem((608, 512), BF16),
        vmem((1168, 256), BF16),
        vmem((1168, 128), BF16),
        vmem((288, 640), BF16),
        vmem((640, 768), BF16),
        vmem((4, 544, 768), BF16),
        vmem((4, 512, 256), BF16),
        vmem((4, 512, 256), F32),
        vmem((4, 512, 256), F32),
        vmem((128, 256), F32),
        vmem((128, 256), BF16),
        vmem((4, 512, 256), F32),
        vmem((2, 2, 4, 16, 256), F32),
        vmem((2, 4, 64, 256), F32),
        vmem((2, 16, 256), F32),
        vmem((256, 512), F32),
        vmem((6, wide_count, 1, 128), F32),
        vmem((6, narrow_count, 1, 128), F32),
        vmem((8, 128), F32),
        vmem((wide_count, 32, 128), BF16),
        vmem((narrow_count, 32, 128), BF16),
        vmem((2, 9, 4, 32, 256), BF16),
        vmem((2, 2, 4, 16, 256), BF16),
        vmem((2, 2, 4, 32, 256), BF16),
        vmem((2, 4, 32, 256), BF16),
        vmem((4, 256, 512), F32),
        vmem((9, 256, 512), BF16),
        vmem((2, 9, 256, 640), BF16),
        vmem((3, 4, 10, 16, 256), F32),
        vmem((2, 2, 128, 256), BF16),
        vmem((2, 16, 256), BF16),
        vmem((2, 2, 4, 16, 256), BF16),
        vmem((2, 2, 128, 256), BF16),
        vmem((2, 4, 16, 256), BF16),
        vmem((112, 256), BF16),
        vmem((96, 256), BF16),
        vmem((4, 16, 256), BF16),
        vmem((16, 512), BF16),
        vmem((8, 16, 512), BF16),
        vmem((112, 512), BF16),
        vmem((96, 512), BF16),
        vmem((4, 16, 512), BF16),
        vmem((16, 512), BF16),
        vmem((8, 16, 512), BF16),
        vmem((8, 512), F32),
        vmem((8, 8, 512), F32),
        vmem((112, 512), BF16),
        vmem((96, 512), BF16),
        vmem((4, 16, 512), BF16),
        pltpu.SemaphoreType.DMA((20,)),
        pltpu.SemaphoreType.DMA((5,)),
        pltpu.SemaphoreType.DMA((14,)),
        pltpu.SemaphoreType.DMA((14,)),
        pltpu.SemaphoreType.DMA((16,)),
        pltpu.SemaphoreType.DMA((16,)),
    ]
    output, grad = pl.pallas_call(
        functools.partial(kernel, wide_count, narrow_count),
        out_shape=(
            jax.ShapeDtypeStruct((4, 512, 256), BF16),
            jax.ShapeDtypeStruct((4, 512, 256), F32),
        ),
        in_specs=[anywhere] * 17,
        out_specs=(anywhere, anywhere),
        scratch_shapes=scratch,
        compiler_params=pltpu.CompilerParams(
            collective_id=0, has_side_effects=True, vmem_limit_bytes=56 * 2**20
        ),
        name="whole_net",
    )(
        fine_input,
        gain_fine.reshape(1, 256),
        kernel_fine.reshape(9, 256, 256),
        down_mid,
        gain_mid.reshape(1, 512),
        kernel_mid.reshape(9, 512, 512),
        down_coarse,
        gain_coarse.reshape(1, 512),
        kernel_coarse.reshape(9, 512, 512),
        up_coarse,
        up_mid,
        grad_out,
        *tables(),
    )
    return output.reshape(4, 32, 16, 256), grad.reshape(4, 32, 16, 256)


def solution(mesh):
    tile = P(None, "wide", "narrow", None)
    return jax.shard_map(
        shards,
        mesh=mesh,
        in_specs=(tile,) + (P(),) * 10 + (tile,),
        out_specs=(tile, tile),
        check_vma=False,
    )
```

```python
import functools

import jax
import jax.numpy as jnp
import numpy as np
from jax import lax
from jax.experimental import pallas as pl
from jax.experimental.pallas import tpu as pltpu
from jax.sharding import PartitionSpec as P

MESH = pl.DeviceIdType.MESH
GROUPS = 32
epsilon = 1e-05
F32 = jnp.float32
BF16 = jnp.bfloat16

DIRS = ((0, 0), (-1, 0), (1, 0), (0, -1), (0, 1), (-1, -1), (-1, 1), (1, -1), (1, 1))

ABOVE, BELOW, LEFT, RIGHT, CORNER = 128, 144, 160, 192, 224


def mid_row(f, i, j):
    if 0 <= i < 8 and 0 <= j < 4:
        return 32 * f + 4 * i + j
    if i < 0 and 0 <= j < 4:
        return ABOVE + 4 * f + j
    if i > 7 and 0 <= j < 4:
        return BELOW + 4 * f + j
    if 0 <= i < 8:
        return (LEFT if j < 0 else RIGHT) + 8 * f + i
    return CORNER + 4 * (2 * (i > 7) + (j > 3)) + f


def coarse_row(f, i, side):
    down = -1 if i < 0 else (1 if i > 1 else 0)
    return 8 * DIRS.index((down, side)) + 2 * f + i % 2


def tables():
    pick = np.zeros((96, 512), np.float32)
    for i in range(32):
        for j in range(16):
            pick[4 * (i // 4) + j // 4, 16 * i + j] = 1
        pick[32 + i, 16 * i + 15] = 1
        pick[64 + i, 16 * i] = 1
    enlarge = np.zeros((512, 256), np.float32)
    taps = np.zeros((1152, 256), np.float32)
    ends = np.zeros((16, 256), np.float32)
    pack = np.zeros((112, 128), np.float32)
    pool = np.zeros((16, 128), np.float32)
    coarse_taps = np.zeros((144, 128), np.float32)
    spread = np.zeros((256, 128), np.float32)
    for f in range(4):
        for i in range(8):
            for j in range(16):
                enlarge[128 * f + 16 * i + j, mid_row(f, i, j // 4)] = 1
        for c in range(4):
            low, first = c < 2, c % 2 == 1
            ends[4 * c + f, 128 * first + 32 * f + 31 * low] = 1
            pack[96 + 4 * c + f, mid_row(f, 7 * low, 3 * (not first))] = 1
        for i in range(8):
            for j in range(4):
                here = 32 * f + 4 * i + j
                pool[2 * f + i // 4, here] = 1
                for t in range(9):
                    taps[128 * t + here, mid_row(f, i + t // 3 - 1, j + t % 3 - 1)] = 1
            pack[32 + 8 * f + i, mid_row(f, i, 3)] = 1
            pack[64 + 8 * f + i, mid_row(f, i, 0)] = 1
        for j in range(4):
            pack[4 * f + j, mid_row(f, 7, j)] = 1
            pack[16 + 4 * f + j, mid_row(f, 0, j)] = 1
        for i in range(2):
            for t in range(9):
                coarse_taps[16 * t + 2 * f + i, coarse_row(f, i + t // 3 - 1, t % 3 - 1)] = 1
        for i in range(-1, 9):
            for j in range(-1, 5):
                side = -1 if j < 0 else (1 if j > 3 else 0)
                spread[mid_row(f, i, j), coarse_row(f, i // 4 if i < 8 else 2, side)] = 1
    windows = np.zeros((288, 640), np.float32)
    for t in range(9):
        for i in range(32):
            for j in range(16):
                p, q = i + 1 - t // 3, j + 1 - t % 3
                row = 32 * t + 4 * (i // 4) + j // 4
                if 0 <= p < 32 and 0 <= q < 16:
                    at = 16 * p + q
                elif 0 <= q < 16:
                    at = (512 if p < 0 else 528) + q
                elif 0 <= p < 32:
                    at = (544 if q < 0 else 576) + p
                else:
                    at = 608 + 2 * (p > 31) + (q > 15)
                windows[row, at] = 1
    stretch = np.zeros((640, 768), np.float32)
    for f in range(4):
        for i in range(10):
            for j in range(16):
                for b in range(3):
                    at = 256 * b + mid_row(f, i - 1, (j + b - 1) // 4)
                    stretch[160 * f + 16 * i + j, at] = 1
    by_frame = np.zeros((128, 128), np.float32)
    for f in range(4):
        for c in range(4):
            by_frame[32 * f + c, 4 * c + f] = 1
    sides = np.zeros((512, 128), np.float32)
    for i in range(32):
        sides[16 * i, i] = 1
        sides[16 * i + 15, 64 + i] = 1
    wide_table = np.concatenate([pick, np.concatenate([enlarge, enlarge], axis=1)])
    middle_table = np.concatenate([taps, ends])
    narrow_table = np.concatenate([pack, pool, coarse_taps, spread, sides, by_frame])
    result = (wide_table, middle_table, narrow_table, windows, stretch)
    return [jnp.asarray(t, BF16) for t in result]


def dot(a, b):
    return jnp.dot(a, b, preferred_element_type=F32)


def dot_t(a, b):
    return lax.dot_general(a, b, (((1,), (1,)), ((), ())), preferred_element_type=F32)


def dot_first(a, b):
    return lax.dot_general(a, b, (((0,), (0,)), ((), ())), preferred_element_type=F32)


def group_lanes(t, size):
    lane = lax.broadcasted_iota(jnp.int32, t.shape, 1)
    step = 1
    while step < size:
        t = t + jnp.where(
            (lane & step) != 0, pltpu.roll(t, step, 1), pltpu.roll(t, 128 - step, 1)
        )
        step *= 2
    return t


def halves(t):
    high = t.astype(BF16)
    return high, (t - high.astype(F32)).astype(BF16)


def kernel(
    wide_count,
    narrow_count,
    x_in,
    gain_fine_in,
    kernel_fine_in,
    down_mid_in,
    gain_mid_in,
    kernel_mid_in,
    down_coarse_in,
    gain_coarse_in,
    kernel_coarse_in,
    up_coarse_in,
    up_mid_in,
    grad_in,
    wide_table_in,
    middle_table_in,
    narrow_table_in,
    windows_in,
    stretch_in,
    out_ref,
    grad_ref,
    xg,
    kernel_fine,
    down_mid,
    kernel_mid,
    down_coarse,
    kernel_coarse,
    up_coarse,
    up_mid,
    gain_fine,
    gain_mid,
    gain_coarse,
    wide_table,
    middle_table,
    narrow_table,
    windows,
    stretch,
    columns,
    fine_block,
    grad_buf,
    conv_grad,
    pooled_x,
    summed,
    fine_slope,
    edge_rows,
    edge_sides,
    edge_ends,
    summed_grad,
    first,
    second,
    rows,
    first_matrix,
    second_matrix,
    window_sums,
    rim_rows,
    rim_sides,
    rim_ends,
    matrix_sum,
    through,
    mixed,
    stretched,
    col_pack,
    cor_pack,
    row_in,
    col_in,
    cor_in,
    sum_pack,
    sum_in,
    sum_cor,
    cgrad_own,
    cgrad_in,
    mid_pack,
    mid_halo,
    mid_cor,
    coarse_own,
    coarse_halo,
    coarse_u,
    coarse_u_halo,
    u_pack,
    u_halo,
    u_cor,
    load_sem,
    out_sem,
    total_send,
    total_recv,
    halo_send,
    halo_recv,
):
    wide, narrow = lax.axis_index("wide"), lax.axis_index("narrow")

    def around(index, step, count):
        moved = index + step
        if isinstance(step, int) and step < 0:
            return jnp.where(moved < 0, moved + count, moved)
        return jnp.where(moved >= count, moved - count, moved)

    def device(down, side):
        return (
            wide if isinstance(down, int) and down == 0 else around(wide, down, wide_count),
            narrow if isinstance(side, int) and side == 0 else around(narrow, side, narrow_count),
        )

    loads = {}
    pairs = (
        ("x0", x_in.at[0], xg.at[0, 0]),
        ("x1", x_in.at[1], xg.at[0, 1]),
        ("x2", x_in.at[2], xg.at[0, 2]),
        ("x3", x_in.at[3], xg.at[0, 3]),
        ("grad", grad_in, xg.at[1]),
        ("wide_table", wide_table_in, wide_table),
        ("middle_table", middle_table_in, middle_table),
        ("narrow_table", narrow_table_in, narrow_table),
        ("gain_fine", gain_fine_in, gain_fine),
        ("windows", windows_in, windows),
        ("kernel_fine", kernel_fine_in, kernel_fine),
        ("up_mid", up_mid_in, up_mid),
        ("up_coarse", up_coarse_in, up_coarse),
        ("down_mid", down_mid_in, down_mid),
        ("gain_mid", gain_mid_in, gain_mid),
        ("kernel_coarse", kernel_coarse_in, kernel_coarse),
        ("kernel_mid", kernel_mid_in, kernel_mid),
        ("down_coarse", down_coarse_in, down_coarse),
        ("gain_coarse", gain_coarse_in, gain_coarse),
        ("stretch", stretch_in, stretch),
    )
    for number, (name, source, target) in enumerate(pairs):
        loads[name] = pltpu.make_async_copy(source, target, load_sem.at[number])

    def begin_loads(*names):
        for name in names:
            loads[name].start()

    begin_loads("x0", "x1", "x2", "x3", "wide_table", "middle_table")

    barrier = pltpu.get_barrier_semaphore()
    greeted = 0
    for down in range(wide_count):
        for side in range(-2, narrow_count - 2):
            near = (down <= 1 or down == wide_count - 1) and abs(side) <= 1
            if (down, side) != (0, 0) and (down == 0 or side == 0 or near):
                pl.semaphore_signal(
                    barrier, inc=1, device_id=device(down, side), device_id_type=MESH
                )
                greeted += 1

    def send(source, target, which, down, side):
        pltpu.make_async_remote_copy(
            src_ref=source,
            dst_ref=target,
            send_sem=halo_send.at[which],
            recv_sem=halo_recv.at[which],
            device_id=device(down, side),
            device_id_type=MESH,
        ).start()

    def arrived(buffer, which):
        pltpu.make_async_copy(buffer, buffer, halo_recv.at[which]).wait()

    def sent(buffer, which):
        pltpu.make_async_copy(buffer, buffer, halo_send.at[which]).wait()

    firsts = tuple(first.at[p] for p in range(6)) + (first_matrix,)
    seconds = tuple(second.at[p] for p in range(6)) + (second_matrix,)

    def total_send_wide(phase):
        mine = firsts[phase].at[wide]

        for step in sorted(range(1, wide_count), key=lambda k: -min(k & 7, 8 - (k & 7))):
            pltpu.make_async_remote_copy(
                src_ref=mine,
                dst_ref=mine,
                send_sem=total_send.at[2 * phase],
                recv_sem=total_recv.at[2 * phase],
                device_id=device(step, 0),
                device_id_type=MESH,
            ).start()

    def diagonal(shape=(8, 128)):
        lane = lax.broadcasted_iota(jnp.int32, shape, 1) & 7
        return lane == lax.broadcasted_iota(jnp.int32, shape, 0)

    def total_begin(phase, one, two):
        channels = one.shape[1]
        if channels < 512:
            rows[...] = jnp.zeros((8, 128), F32)
        for n, value in enumerate((one, two)):
            for k in range(channels // 128):
                rows[4 * n + k : 4 * n + k + 1, :] = value[:, 128 * k : 128 * k + 128]
        grouped = group_lanes(rows[...], channels // GROUPS)
        grouped = jnp.where(diagonal(), grouped, 0.0)
        firsts[phase][wide] = jnp.sum(grouped, axis=0, keepdims=True)
        total_send_wide(phase)

    def total_middle(phase):
        whole = firsts[phase].at[pl.ds(0, wide_count - 1)]
        pltpu.make_async_copy(whole, whole, total_recv.at[2 * phase]).wait()
        summed_up = jnp.sum(firsts[phase][...].astype(F32), axis=0)
        seconds[phase][narrow] = summed_up.astype(seconds[phase].dtype)
        mine = seconds[phase].at[narrow]

        for step in sorted(range(1, narrow_count), key=lambda k: -min(k & 3, 4 - (k & 3))):
            pltpu.make_async_remote_copy(
                src_ref=mine,
                dst_ref=mine,
                send_sem=total_send.at[2 * phase + 1],
                recv_sem=total_recv.at[2 * phase + 1],
                device_id=device(0, step),
                device_id_type=MESH,
            ).start()

    def total_sum(phase):
        whole = seconds[phase].at[pl.ds(0, narrow_count - 1)]
        pltpu.make_async_copy(whole, whole, total_recv.at[2 * phase + 1]).wait()
        return jnp.sum(seconds[phase][...].astype(F32), axis=0)

    def row_of(t, start, channels):
        return jnp.concatenate([t[start + k : start + k + 1] for k in range(channels // 128)], axis=1)

    def total_groups(phase, channels, scale):
        packed = jnp.broadcast_to(total_sum(phase), (8, 128))
        t = group_lanes(jnp.where(diagonal(), packed, 0.0), 8) * scale
        return row_of(t, 0, channels), row_of(t, 4, channels)

    def total_end(phase, channels, cells):
        return total_groups(phase, channels, 1.0 / (channels // GROUPS * cells))

    has_above, has_below = wide > 0, wide < wide_count - 1
    has_left, has_right = narrow > 0, narrow < narrow_count - 1
    has_corner = (
        jnp.logical_and(has_above, has_left),
        jnp.logical_and(has_above, has_right),
        jnp.logical_and(has_below, has_left),
        jnp.logical_and(has_below, has_right),
    )
    exists = (None, has_above, has_below, has_left, has_right) + has_corner

    def only(condition, value):
        return value * jnp.where(condition, 1.0, 0.0).astype(F32)

    def corners(read, change, masked):
        result = None
        for c in range(4):
            value = change(read(c).astype(F32))
            if masked:
                value = only(has_corner[c], value)
            cell = lax.broadcasted_iota(jnp.int32, value.shape, 0)
            result = value if result is None else jnp.where(cell >= 4 * c, value, result)
        return result

    def mid_extended(own, read_halo, read_cor, change, masked):
        pieces = [change(own)]
        halo = change(read_halo.astype(F32))
        for low, high, d in ((0, 16, 1), (16, 32, 2), (32, 64, 3), (64, 96, 4)):
            piece = halo[low:high]
            pieces.append(only(exists[d], piece) if masked else piece)
        pieces.append(corners(read_cor, change, masked))
        pieces.append(jnp.zeros((16, own.shape[1]), F32))
        return jnp.concatenate(pieces, axis=0)

    def send_mid(pack, halo, cor, which):
        send(pack.at[pl.ds(0, 16)], halo.at[pl.ds(0, 16)], which, 1, 0)
        send(pack.at[pl.ds(16, 16)], halo.at[pl.ds(16, 16)], which, -1, 0)
        send(pack.at[pl.ds(32, 32)], halo.at[pl.ds(32, 32)], which, 0, 1)
        send(pack.at[pl.ds(64, 32)], halo.at[pl.ds(64, 32)], which, 0, -1)
        for c in range(4):
            down, side = DIRS[5 + c]
            send(pack.at[pl.ds(96, 16)], cor.at[c], which + 1, -down, -side)

    def send_coarse(own, halo, which):
        for d in range(1, 9):
            down, side = DIRS[d]
            send(own, halo.at[d - 1], which, -down, -side)

    def coarse_extended(own, halo, change, masked):
        pieces = [change(own)]
        for d in range(1, 9):
            piece = change(halo(d - 1))
            pieces.append(only(exists[d], piece) if masked else piece)
        pieces.append(jnp.zeros((56, own.shape[1]), F32))
        return jnp.concatenate(pieces, axis=0)

    PICK = wide_table.at[pl.ds(0, 96)]
    ENLARGE = wide_table.at[pl.ds(96, 512)]
    TAPS = middle_table.at[pl.ds(0, 1152)]
    ENDS = middle_table.at[pl.ds(1152, 16)]
    PACK = narrow_table.at[pl.ds(0, 112)]
    POOL = narrow_table.at[pl.ds(112, 16)]
    COARSE_TAPS = narrow_table.at[pl.ds(128, 144)]
    SPREAD = narrow_table.at[pl.ds(272, 256)]
    SIDES = narrow_table.at[pl.ds(528, 512)]
    BY_FRAME = narrow_table.at[pl.ds(1040, 128)]

    def frame(which, f):
        return xg[which, f].reshape(512, 256)

    blank = jnp.zeros((8, 256), F32)
    one, two = blank, blank
    for f in range(4):
        loads["x%d" % f].wait()
        value = frame(0, f).astype(F32)
        one += jnp.sum(value.reshape(64, 8, 256), axis=0)
        two += jnp.sum((value * value).reshape(64, 8, 256), axis=0)
    pl.semaphore_wait(barrier, greeted)
    total_begin(0, jnp.sum(one, axis=0, keepdims=True), jnp.sum(two, axis=0, keepdims=True))

    begin_loads("grad", "narrow_table", "gain_fine", "windows", "kernel_fine")
    begin_loads("up_mid", "up_coarse", "down_mid", "gain_mid")

    def rim_rows_out(which):
        send(xg.at[which, :, 31], row_in.at[0, which], 13 * which, 1, 0)
        send(xg.at[which, :, 0], row_in.at[1, which], 13 * which, -1, 0)

    def rim_pick(which):
        for f in range(4):
            picked = dot(PICK[...], frame(which, f))
            if which == 0:
                pooled_x[32 * f : 32 * f + 32] = picked[0:32]
            picked = picked.astype(BF16)
            col_pack[0, which, 32 * f : 32 * f + 32] = picked[32:64]
            col_pack[1, which, 32 * f : 32 * f + 32] = picked[64:96]
            if which == 1:
                summed[32 * f : 32 * f + 32] = picked[0:32]

    def rim_sides_out(which):
        send(col_pack.at[0, which], col_in.at[0, which], 13 * which + 1, 0, 1)
        send(col_pack.at[1, which], col_in.at[1, which], 13 * which + 1, 0, -1)

    def rim_ends_out(which):
        ends = jnp.concatenate([col_pack[0, which], col_pack[1, which]], axis=0)
        cor_pack[which] = dot(ENDS[...], ends).astype(BF16)
        for c in range(4):
            down, side = DIRS[5 + c]
            send(cor_pack.at[which], cor_in.at[which, c], 13 * which + 2, -down, -side)

    loads["wide_table"].wait()
    loads["middle_table"].wait()
    rim_rows_out(0)
    rim_pick(0)
    rim_sides_out(0)
    rim_ends_out(0)
    loads["grad"].wait()
    rim_pick(1)
    total_middle(0)
    begin_loads("kernel_mid")
    rim_rows_out(1)
    rim_sides_out(1)
    rim_ends_out(1)
    loads["narrow_table"].wait()

    up_mid_grad = summed[...]
    sum_pack[...] = dot(PACK[...], up_mid_grad).astype(BF16)
    send_mid(sum_pack, sum_in, sum_cor, 3)
    loads["up_mid"].wait()
    high, low = halves(dot_t(up_mid_grad, up_mid[...]))
    up_coarse_grad = (dot(POOL[...], high) + dot(POOL[...], low)).astype(BF16)
    loads["up_coarse"].wait()
    cgrad_own[...] = dot_t(up_coarse_grad, up_coarse[...]).astype(BF16)
    send_coarse(cgrad_own, cgrad_in, 5)

    loads["gain_fine"].wait()
    loads["kernel_fine"].wait()
    loads["down_mid"].wait()

    fine_center, fine_square = total_end(0, 256, 2048 * wide_count * narrow_count)
    fine_inverse = lax.rsqrt(fine_square - fine_center * fine_center + epsilon)
    s_fine = gain_fine[...]

    def silu(center, inverse, scaling):
        gain = 0.5 * inverse * scaling
        shift = -center * gain

        def change(value):
            half = value * gain + shift
            return half * jnp.tanh(half) + half

        return change

    def slope(scaled, scaling):
        half = scaled * (0.5 * scaling)
        bend = jnp.tanh(half)
        return (0.5 * scaling) * (1.0 + bend) * (1.0 + half * (1.0 - bend))

    fine_act = silu(fine_center, fine_inverse, s_fine)

    arrived(row_in.at[:, 0], 0)
    arrived(col_in.at[:, 0], 1)
    arrived(cor_in.at[0], 2)

    def set_edges(kind, above, below, left, right, ends):
        edge_rows[kind, 0] = only(has_above, above)
        edge_rows[kind, 1] = only(has_below, below)
        left = only(has_left, left)
        right = only(has_right, right)
        for f in range(4):
            edge_sides[kind, f, 0:32] = left[32 * f : 32 * f + 32]
            edge_sides[kind, f, 32:64] = right[32 * f : 32 * f + 32]
        edge_ends[kind] = ends

    def place(kind, f, own):
        column = lax.broadcasted_iota(jnp.int32, (32, 16, 256), 1)
        west, east = (
            jnp.broadcast_to(edge_sides[kind, f, 32 * k : 32 * k + 32].reshape(32, 1, 256), (32, 16, 256))
            for k in range(2)
        )
        low = jnp.where(column == 0, west, pltpu.roll(own, 1, 0).reshape(32, 16, 256))
        columns[f, 16:528, 0:256] = low.reshape(512, 256).astype(BF16)
        columns[f, 16:528, 256:512] = own.astype(BF16)
        high = jnp.where(column == 15, east, pltpu.roll(own, 511, 0).reshape(32, 16, 256))
        columns[f, 16:528, 512:768] = high.reshape(512, 256).astype(BF16)
        cell = lax.broadcasted_iota(jnp.int32, (16, 256), 0)
        for k in range(2):
            row = edge_rows[kind, k, f]
            at = slice(528 * k, 528 * k + 16)
            west = edge_ends[kind, pl.ds(8 * k + f, 1), :]
            east = edge_ends[kind, pl.ds(8 * k + 4 + f, 1), :]
            columns[f, at, 0:256] = jnp.where(cell == 0, west, pltpu.roll(row, 1, 0)).astype(BF16)
            columns[f, at, 256:512] = row.astype(BF16)
            columns[f, at, 512:768] = jnp.where(cell == 15, east, pltpu.roll(row, 15, 0)).astype(BF16)

    def side_by_side(pieces):
        return jnp.concatenate(list(pieces), axis=1)

    def fine_taps(f):
        return side_by_side(columns[f, 16 * a : 16 * a + 512, :] for a in range(3))

    def fine_convolve(f):
        return dot(fine_taps(f), kernel_fine[...].reshape(2304, 256))

    def fine_convolve_back(f):
        return dot_t(fine_taps(f), side_by_side(kernel_fine[8 - t] for t in range(9)))

    def fine_scaled(value):
        return (value - fine_center) * fine_inverse

    def fine_value(f):
        return frame(0, f).astype(F32)

    def set_fields(n, change):
        for k in range(2):
            rim_rows[n, k] = only(exists[1 + k], change(row_in[k, 0].astype(F32))).astype(BF16)
            sides = only(exists[3 + k], change(col_in[k, 0].astype(F32))).astype(BF16)
            rim_sides[n, k] = sides.reshape(4, 32, 256)
        ends = corners(lambda c: cor_in[0, c], change, True)
        ends = dot(BY_FRAME[:, 0:16], ends.astype(BF16)).astype(BF16)
        rim_ends[n] = ends.reshape(4, 32, 256)

    def window(n, f, own):
        field = jnp.concatenate(
            [
                own.astype(BF16),
                rim_rows[n, 0, f],
                rim_rows[n, 1, f],
                rim_sides[n, 0, f],
                rim_sides[n, 1, f],
                rim_ends[n, f],
            ],
            axis=0,
        )
        return dot(windows[...], field)

    set_fields(0, fine_act)
    loads["windows"].wait()

    for f in range(4):
        sums = window(0, f, fine_act(fine_value(f)))
        high, low = halves(sums)
        window_sums[0, :, f] = high.reshape(9, 32, 256)
        window_sums[1, :, f] = low.reshape(9, 32, 256)

    both = side_by_side(
        jnp.concatenate([window_sums[n, 8 - t].reshape(128, 256) for n in range(2)], axis=0)
        for t in range(9)
    )
    both = dot(both, kernel_fine[...].reshape(2304, 256))
    pooled = pooled_x[...] + both[0:128] + both[128:256]
    pooled = (pooled * 0.0625).astype(BF16)

    def fine_forward(f):
        value = fine_value(f)
        place(0, f, fine_act(value))
        fine_block[f] = (value + fine_convolve(f)).astype(BF16)

    def same(value):
        return value

    mid_in = dot(pooled, down_mid[...]).astype(BF16)
    mid_value = mid_in.astype(F32)

    def column_sums(value):
        return jnp.sum(value, axis=0, keepdims=True)

    total_begin(1, column_sums(mid_value), column_sums(mid_value * mid_value))
    mid_pack[...] = dot(PACK[...], mid_in).astype(BF16)
    send_mid(mid_pack, mid_halo, mid_cor, 6)
    begin_loads("down_coarse", "gain_coarse", "kernel_coarse", "stretch")

    for f in range(4):
        fine_slope[f] = slope(fine_scaled(fine_value(f)), s_fine)

    set_fields(0, lambda v: slope(fine_scaled(v), s_fine))
    set_fields(1, lambda v: slope(fine_scaled(v), s_fine) * fine_scaled(v))

    set_edges(
        0,
        fine_act(row_in[0, 0].astype(F32)),
        fine_act(row_in[1, 0].astype(F32)),
        fine_act(col_in[0, 0].astype(F32)),
        fine_act(col_in[1, 0].astype(F32)),
        corners(lambda c: cor_in[0, c], fine_act, True),
    )
    fine_forward(0)
    total_middle(1)
    fine_forward(1)

    for f in range(4):
        bent = fine_slope[f]
        window_sums[0, :, f] = window(0, f, bent).astype(BF16).reshape(9, 32, 256)
        bent = bent * fine_scaled(fine_value(f))
        window_sums[1, :, f] = window(1, f, bent).astype(BF16).reshape(9, 32, 256)

    loads["gain_mid"].wait()
    loads["kernel_mid"].wait()
    mid_center, mid_square = total_end(1, 512, 128 * wide_count * narrow_count)
    mid_inverse = lax.rsqrt(mid_square - mid_center * mid_center + epsilon)
    s_mid = gain_mid[...]

    mid_act = silu(mid_center, mid_inverse, s_mid)

    def mid_scaled(value):
        return (value - mid_center) * mid_inverse

    def mid_convolve(extended, product, weights):
        taps = dot(TAPS[...], extended.astype(BF16)).astype(BF16)
        return product(side_by_side(taps[128 * t : 128 * t + 128] for t in range(9)), weights)

    arrived(mid_halo, 6)
    arrived(mid_cor, 7)
    mid_block = (
        mid_value
        + mid_convolve(
            mid_extended(mid_value, mid_halo[...], lambda c: mid_cor[c], mid_act, True),
            dot,
            kernel_mid[...].reshape(4608, 512),
        )
    ).astype(BF16)

    loads["down_coarse"].wait()
    mid_pooled = (dot(POOL[...], mid_block) * 0.0625).astype(BF16)
    coarse_in = dot(mid_pooled, down_coarse[...]).astype(BF16)
    coarse_own[...] = coarse_in
    coarse_value = coarse_in.astype(F32)[0:8]
    total_begin(2, column_sums(coarse_value), column_sums(coarse_value * coarse_value))
    send_coarse(coarse_own, coarse_halo, 8)

    arrived(row_in.at[:, 1], 13)
    arrived(col_in.at[:, 1], 14)
    arrived(cor_in.at[1], 15)
    set_edges(
        1,
        row_in[0, 1].astype(F32),
        row_in[1, 1].astype(F32),
        col_in[0, 1].astype(F32),
        col_in[1, 1].astype(F32),
        corners(lambda c: cor_in[1, c], same, True),
    )

    def convolve_grad(f, carry):
        place(1, f, frame(1, f).astype(F32))
        result = fine_convolve_back(f)
        conv_grad[f] = result
        weighted = result * fine_slope[f]
        scaled = fine_scaled(fine_value(f))
        return (
            carry[0] + jnp.sum(weighted.reshape(64, 8, 256), axis=0),
            carry[1] + jnp.sum((weighted * scaled).reshape(64, 8, 256), axis=0),
        )

    grad_sums = lax.fori_loop(0, 2, convolve_grad, (blank, blank))
    total_middle(2)

    arrived(cgrad_in, 5)
    loads["kernel_coarse"].wait()

    def coarse_convolve(extended, product, weights):
        taps = dot(COARSE_TAPS[...], extended.astype(BF16)).astype(BF16)
        return product(side_by_side(taps[16 * t : 16 * t + 16] for t in range(9)), weights)

    cgrad = cgrad_own[...].astype(F32)[0:8]
    coarse_act_grad = coarse_convolve(
        coarse_extended(cgrad, lambda d: cgrad_in[d].astype(F32)[0:8], same, True),
        dot_t,
        side_by_side(kernel_coarse[8 - t] for t in range(9)),
    )[0:8]

    @pl.loop(0, 9)
    def _(t):
        through[t] = (0.0625 * dot(kernel_fine[8 - t], down_mid[...])).astype(BF16)

    arrived(sum_in, 3)
    arrived(sum_cor, 4)
    sum_extended = mid_extended(
        up_mid_grad.astype(F32), sum_in[...], lambda c: sum_cor[c], same, True
    )
    summed_grad[...] = dot_t(sum_extended.astype(BF16), up_mid[...])

    loads["gain_coarse"].wait()
    coarse_center, coarse_square = total_end(2, 512, 8 * wide_count * narrow_count)
    coarse_inverse = lax.rsqrt(coarse_square - coarse_center * coarse_center + epsilon)
    s_coarse = gain_coarse[...]

    def coarse_scaled(value):
        return (value - coarse_center) * coarse_inverse

    scaled = coarse_scaled(coarse_value)
    normed_grad = coarse_act_grad * slope(scaled, s_coarse)
    total_begin(3, column_sums(normed_grad), column_sums(normed_grad * scaled))
    coarse_u[...] = cgrad + coarse_inverse * normed_grad
    send_coarse(coarse_u, coarse_u_halo, 9)
    grad_sums = lax.fori_loop(2, 4, convolve_grad, grad_sums)

    total_middle(3)

    mid_mix = jnp.concatenate(
        [mid_scaled(mid_value).astype(BF16), jnp.ones((128, 128), BF16)], axis=1
    )
    for n in range(2):
        sums = side_by_side(window_sums[n, t].reshape(128, 256) for t in range(9))
        mixed[n] = dot_first(sums, mid_mix).astype(BF16).reshape(9, 256, 640)

    @pl.loop(0, 16)
    def _(part):
        here = pl.ds(pl.multiple_of(16 * part, 16), 16)
        totals = [jnp.zeros((16, 512), F32) for _ in range(4)]
        for t in range(9):
            weight = through[t, here, :].astype(F32)
            for n in range(2):
                value = mixed[n, t, here, :].astype(F32)
                totals[2 * n] += weight * side_by_side([value[:, 512:640]] * 4)
                totals[2 * n + 1] += weight * value[:, 0:512]
        for n in range(4):
            matrix_sum[n, here, :] = totals[n]

    def iota(shape, axis):
        return lax.broadcasted_iota(jnp.int32, shape, axis)

    def one_hot(condition):
        return jnp.where(condition, 1.0, 0.0).astype(BF16)

    by_group = one_hot((iota((32, 256), 1) >> 3) == iota((32, 256), 0))
    matrix = jnp.zeros((32, 128), F32)
    for n in range(4):
        high, low = halves(matrix_sum[n] * mid_inverse)
        high, low = halves(dot(by_group, high) + dot(by_group, low))
        to_lane = one_hot(iota((512, 128), 1) == 32 * n + (iota((512, 128), 0) >> 4))
        matrix += dot(high, to_lane) + dot(low, to_lane)
    first_matrix[wide] = matrix.astype(BF16)
    total_send_wide(6)

    first_mean, second_mean = total_end(3, 512, 8 * wide_count * narrow_count)
    arrived(coarse_halo, 8)
    arrived(coarse_u_halo, 9)
    offset = coarse_inverse * first_mean
    factor = coarse_inverse * second_mean
    pieces = [coarse_u[...] - offset - scaled * factor]
    for d in range(8):
        piece = coarse_scaled(coarse_halo[d].astype(F32)[0:8])
        pieces.append(coarse_u_halo[d] - offset - piece * factor)
    pieces.append(jnp.zeros((56, 512), F32))
    coarse_in_grad = jnp.concatenate(pieces, axis=0).astype(BF16)

    mid_pool_grad = dot_t(dot(SPREAD[...], coarse_in_grad).astype(BF16), down_coarse[...])
    row = lax.broadcasted_iota(jnp.int32, (256, 128), 0)
    keep = jnp.where(row < ABOVE, 1.0, 0.0)
    bounds = ((ABOVE, 16, 1), (BELOW, 16, 2), (LEFT, 32, 3), (RIGHT, 32, 4)) + tuple(
        (CORNER + 4 * c, 4, 5 + c) for c in range(4)
    )
    for start, size, d in bounds:
        inside = jnp.logical_and(row >= start, row < start + size)
        keep = jnp.where(inside, jnp.where(exists[d], 1.0, 0.0).astype(F32), keep)
    mid_grad = (summed_grad[...] + 0.0625 * mid_pool_grad) * jnp.concatenate([keep] * 4, axis=1)
    mid_act_grad = mid_convolve(
        mid_grad, dot_t, side_by_side(kernel_mid[8 - t] for t in range(9))
    )
    scaled = mid_scaled(mid_value)
    normed_grad = mid_act_grad * slope(scaled, s_mid)
    total_begin(4, column_sums(normed_grad), column_sums(normed_grad * scaled))
    mid_u = mid_grad[0:128].astype(BF16).astype(F32) + mid_inverse * normed_grad
    u_pack[...] = dot(PACK[...], mid_u.astype(BF16)).astype(BF16)
    send_mid(u_pack, u_halo, u_cor, 10)
    pulled = (0.0625 * dot_t(mid_u.astype(BF16), down_mid[...])).astype(BF16)
    fine_sums = [jnp.sum(value, axis=0, keepdims=True) for value in grad_sums]
    for t in range(9):
        term = dot_t(pulled, kernel_fine[8 - t])
        for n in range(2):
            fine_sums[n] += column_sums(window_sums[n, t].reshape(128, 256).astype(F32) * term)
    total_begin(5, *fine_sums)
    total_middle(6)

    coarse_block = (
        coarse_in.astype(F32)
        + coarse_convolve(
            coarse_extended(
                coarse_value,
                lambda d: coarse_halo[d].astype(F32)[0:8],
                silu(coarse_center, coarse_inverse, s_coarse),
                True,
            ),
            dot,
            kernel_coarse[...].reshape(4608, 512),
        )
    ).astype(BF16)
    coarse_up = dot(coarse_block, up_coarse[...]).astype(BF16)
    mid_sum = (mid_block.astype(F32) + dot(SPREAD[0:128, 0:16], coarse_up)).astype(BF16)
    mid_up = dot(mid_sum, up_mid[...]).astype(BF16)
    total_middle(4)
    total_middle(5)

    fine_forward(2)
    fine_forward(3)
    mid_up = dot(ENLARGE[:, 0:128], mid_up).reshape(4, 8, 1, 16, 256)
    for f in range(4):
        block = fine_block[f].astype(F32).reshape(8, 4, 16, 256)
        fine_block[f] = (block + mid_up[f]).astype(BF16).reshape(512, 256)
    out_copy = pltpu.make_async_copy(fine_block, out_ref, out_sem.at[0])
    out_copy.start()
    first_mean, second_mean = total_end(4, 512, 128 * wide_count * narrow_count)
    arrived(u_halo, 10)
    arrived(u_cor, 11)
    offset = mid_inverse * first_mean
    factor = mid_inverse * second_mean
    mid_in_grad = mid_extended(
        mid_u, u_halo[...], lambda c: u_cor[c], lambda v: v - offset, False
    ) - factor * mid_extended(
        mid_value, mid_halo[...], lambda c: mid_cor[c], mid_scaled, False
    )

    pool_grad = 0.0625 * dot_t(mid_in_grad.astype(BF16), down_mid[...])
    pool_grad = pool_grad * jnp.concatenate([keep] * 2, axis=1)
    high, low = halves(pool_grad)
    added = dot(ENLARGE[...], jnp.concatenate([high[0:256], low[0:256]], axis=0))
    loads["stretch"].wait()
    for a in range(3):
        fields = [dot_t(high, kernel_fine[8 - 3 * a - b]).astype(BF16) for b in range(3)]
        stretched[a] = dot(stretch[...], jnp.concatenate(fields, axis=0)).reshape(4, 10, 16, 256)

    means = jnp.zeros((8, 128), F32)
    for n, mean in enumerate((first_mean, second_mean)):
        lane, row = iota((512, 128), 1), iota((512, 128), 0)
        inside = jnp.logical_and((lane & 31) == (row >> 4), ((lane >> 5) & 1) == n)
        to_lane = jnp.where(inside, 0.0625, 0.0).astype(BF16)
        high, low = halves(jnp.broadcast_to(mean, (8, 512)))
        means += dot(high, to_lane) + dot(low, to_lane)
    matrix_high, matrix_low = halves(total_sum(6))
    fine_totals = total_groups(5, 256, 1.0)
    spread_groups = one_hot((iota((256, 32), 0) >> 3) == iota((256, 32), 1))
    fine_means = []
    for n in range(2):
        half = jnp.where((iota((8, 128), 1) >> 6) == n, means, 0.0)
        high, low = halves(half)
        change = dot_t(high, matrix_high) + dot_t(low, matrix_high) + dot_t(high, matrix_low)
        high, low = halves(change)
        change = dot_t(high, spread_groups) + dot_t(low, spread_groups)
        fine_means.append(
            (fine_totals[n] - change[0:1]) * (1.0 / (8 * 2048 * wide_count * narrow_count))
        )
    slant = -fine_inverse * fine_inverse * fine_means[1]
    shift = -fine_inverse * fine_means[0] - fine_center * slant

    added = added.reshape(4, 8, 1, 16, 256)
    grad_copies = []
    for f in range(4):
        above, here, below = stretched[0, f], stretched[1, f], stretched[2, f]
        centre = here[1:9] + above[1:9] + below[1:9]
        top = here[1:9] + above[0:8] + below[1:9]
        bottom = here[1:9] + above[1:9] + below[2:10]
        back = jnp.stack([top, centre, centre, bottom], axis=1).reshape(512, 256)
        normed_grad = (conv_grad[f] + back) * fine_slope[f]
        grad = xg[1, f].astype(F32).reshape(8, 4, 16, 256) + added[f]
        grad = grad.reshape(512, 256).astype(BF16).astype(F32)
        grad_buf[f] = grad + fine_inverse * normed_grad + (shift + fine_value(f) * slant)
        grad_copies.append(
            pltpu.make_async_copy(grad_buf.at[f], grad_ref.at[f], out_sem.at[1 + f])
        )
        grad_copies[f].start()

    for which in range(2):
        sent(row_in.at[:, which], 13 * which)
        sent(col_in.at[:, which], 13 * which + 1)
        sent(cor_in.at[which], 13 * which + 2)
    sent(sum_in, 3)
    sent(sum_cor, 4)
    sent(cgrad_in, 5)
    sent(mid_halo, 6)
    sent(mid_cor, 7)
    sent(coarse_halo, 8)
    sent(coarse_u_halo, 9)
    sent(u_halo, 10)
    sent(u_cor, 11)
    for phase in range(7):
        whole = firsts[phase].at[pl.ds(0, wide_count - 1)]
        pltpu.make_async_copy(whole, whole, total_send.at[2 * phase]).wait()
        whole = seconds[phase].at[pl.ds(0, narrow_count - 1)]
        pltpu.make_async_copy(whole, whole, total_send.at[2 * phase + 1]).wait()
    out_copy.wait()
    for copy in grad_copies:
        copy.wait()


def shards(*arguments):
    (
        fine_input,
        gain_fine,
        kernel_fine,
        down_mid,
        gain_mid,
        kernel_mid,
        down_coarse,
        gain_coarse,
        kernel_coarse,
        up_coarse,
        up_mid,
        grad_out,
    ) = arguments
    wide_count, narrow_count = lax.axis_size("wide"), lax.axis_size("narrow")
    anywhere = pl.BlockSpec(memory_space=pl.ANY)
    vmem = pltpu.VMEM
    scratch = [
        vmem((2, 4, 32, 16, 256), BF16),
        vmem((9, 256, 256), BF16),
        vmem((256, 512), BF16),
        vmem((9, 512, 512), BF16),
        vmem((512, 512), BF16),
        vmem((9, 512, 512), BF16),
        vmem((512, 512), BF16),
        vmem((512, 256), BF16),
        vmem((1, 256), F32),
        vmem((1, 512), F32),
        vmem((1, 512), F32),
        vmem((608, 512), BF16),
        vmem((1168, 256), BF16),
        vmem((1168, 128), BF16),
        vmem((288, 640), BF16),
        vmem((640, 768), BF16),
        vmem((4, 544, 768), BF16),
        vmem((4, 512, 256), BF16),
        vmem((4, 512, 256), F32),
        vmem((4, 512, 256), F32),
        vmem((128, 256), F32),
        vmem((128, 256), BF16),
        vmem((4, 512, 256), F32),
        vmem((2, 2, 4, 16, 256), F32),
        vmem((2, 4, 64, 256), F32),
        vmem((2, 16, 256), F32),
        vmem((256, 512), F32),
        vmem((6, wide_count, 1, 128), F32),
        vmem((6, narrow_count, 1, 128), F32),
        vmem((8, 128), F32),
        vmem((wide_count, 32, 128), BF16),
        vmem((narrow_count, 32, 128), BF16),
        vmem((2, 9, 4, 32, 256), BF16),
        vmem((2, 2, 4, 16, 256), BF16),
        vmem((2, 2, 4, 32, 256), BF16),
        vmem((2, 4, 32, 256), BF16),
        vmem((4, 256, 512), F32),
        vmem((9, 256, 512), BF16),
        vmem((2, 9, 256, 640), BF16),
        vmem((3, 4, 10, 16, 256), F32),
        vmem((2, 2, 128, 256), BF16),
        vmem((2, 16, 256), BF16),
        vmem((2, 2, 4, 16, 256), BF16),
        vmem((2, 2, 128, 256), BF16),
        vmem((2, 4, 16, 256), BF16),
        vmem((112, 256), BF16),
        vmem((96, 256), BF16),
        vmem((4, 16, 256), BF16),
        vmem((16, 512), BF16),
        vmem((8, 16, 512), BF16),
        vmem((112, 512), BF16),
        vmem((96, 512), BF16),
        vmem((4, 16, 512), BF16),
        vmem((16, 512), BF16),
        vmem((8, 16, 512), BF16),
        vmem((8, 512), F32),
        vmem((8, 8, 512), F32),
        vmem((112, 512), BF16),
        vmem((96, 512), BF16),
        vmem((4, 16, 512), BF16),
        pltpu.SemaphoreType.DMA((20,)),
        pltpu.SemaphoreType.DMA((5,)),
        pltpu.SemaphoreType.DMA((14,)),
        pltpu.SemaphoreType.DMA((14,)),
        pltpu.SemaphoreType.DMA((16,)),
        pltpu.SemaphoreType.DMA((16,)),
    ]
    output, grad = pl.pallas_call(
        functools.partial(kernel, wide_count, narrow_count),
        out_shape=(
            jax.ShapeDtypeStruct((4, 512, 256), BF16),
            jax.ShapeDtypeStruct((4, 512, 256), F32),
        ),
        in_specs=[anywhere] * 17,
        out_specs=(anywhere, anywhere),
        scratch_shapes=scratch,
        compiler_params=pltpu.CompilerParams(
            collective_id=0, has_side_effects=True, vmem_limit_bytes=56 * 2**20
        ),
        name="whole_net",
    )(
        fine_input,
        gain_fine.reshape(1, 256),
        kernel_fine.reshape(9, 256, 256),
        down_mid,
        gain_mid.reshape(1, 512),
        kernel_mid.reshape(9, 512, 512),
        down_coarse,
        gain_coarse.reshape(1, 512),
        kernel_coarse.reshape(9, 512, 512),
        up_coarse,
        up_mid,
        grad_out,
        *tables(),
    )
    return output.reshape(4, 32, 16, 256), grad.reshape(4, 32, 16, 256)


def solution(mesh):
    tile = P(None, "wide", "narrow", None)
    return jax.shard_map(
        shards,
        mesh=mesh,
        in_specs=(tile,) + (P(),) * 10 + (tile,),
        out_specs=(tile, tile),
        check_vma=False,
    )
```
